32 devices in a mesh: ka: 4 (over z), band: 8 (over y, x, core).
Axes of the slice: x: 2, y: 2, z: 4, core: 2. Of those that a mesh axis runs over, the one named last changes fastest.
Arguments:
- start_vec: float32 [12, 4096], P('ka', 'band'), may hold values from -360 to 360
- val_energy: float32 [12, 64], P('ka', 'band'), may hold values from -3 to -0.5
- cond_energy: float32 [12, 64], P('ka'), may hold values from 0.5 to 3
- val_orb: bfloat16 [12, 64, 8192], P('ka', 'band'), may hold values from -6 to 6
- cond_orb: bfloat16 [12, 64, 8192], P('ka'), may hold values from -6 to 6
- coulomb: bfloat16 [8192, 8192], P(('ka', 'band')), may hold values from -3 to 3
- screened: bfloat16 [8192, 8192], P('band', 'ka'), may hold values from -6 to 6
Outputs:
- next_vec: float32 [12, 4096], P('ka', 'band')
- coeffs: float32 [4], replicated
The draws below stay inside these ranges and needn't reach their ends.
All inputs are finite; a program needn't handle non-finite values.
Results may differ from the reference program's by a relative error of at most 0.0075.
Values may be sent and summed in bfloat16 or wider, within the bound.
No kernel may reach another device: no remote copies, remote signals or barrier semaphores. Data moves between devices by JAX's collectives and lax.ppermute only.
A program may use at most 128 MiB of HBM per device.

```python
import math
import jax
import jax.numpy as jnp
from jax import lax

NV = 64
NC = 64
NPT = 8192
STEPS = 2
K = 12


def draw_start_vec(key, part):
    key = jax.random.fold_in(key, 11)
    key_rows, key_cols, key_base = jax.random.split(key, 3)
    ramp = jnp.float32(3.0) ** (jnp.arange(K, dtype=jnp.float32) / max(K - 1, 1))
    row_scale = ramp * jnp.exp(jax.random.uniform(key_rows, (K,), jnp.float32, 0.0, math.log(3.0)))
    col_scale = jnp.exp(jax.random.uniform(key_cols, (NV * NC,), jnp.float32, 0.0, math.log(10.0)))
    base_vals = jnp.clip(jax.random.normal(key_base, (K, NV * NC), jnp.float32), -4.0, 4.0)
    return (base_vals * row_scale[:, None] * col_scale[None, :]).astype(jnp.float32)


def draw_coulomb(key, part):
    key = jax.random.fold_in(key, 23)
    raw_vals = jnp.clip(jax.random.normal(key, (NPT, NPT), jnp.float32), -3.0, 3.0)
    return ((raw_vals + raw_vals.T) * 0.5).astype(jnp.bfloat16)


def block_levels(own_key, shape, shards, low, high):
    level, own = 1.0, jax.random.fold_in(own_key, 6)
    for dim, blocks in shards:
        steps = jnp.exp(jax.random.uniform(jax.random.fold_in(own, dim), (blocks,), jnp.float32, low / len(shards), high / len(shards)))
        level = level * jnp.repeat(steps, shape[dim] // blocks).reshape([-1 if axis == dim else 1 for axis in range(len(shape))])
    return level


def noise(key, dims, scale, bound, cuts=(), kind=jnp.bfloat16):
    level = block_levels(key, dims, cuts, -0.22, 0.18) if cuts else 1.0
    drawn = jax.random.normal(key, dims, jnp.float32) * scale * level
    return jnp.minimum(jnp.maximum(drawn, -bound), bound).astype(kind)


def setup_inputs(seed: int = 0) -> dict:
    keys = jax.random.split(jax.random.key(seed), 8)
    return {
        "start_vec": draw_start_vec(jax.random.fold_in(keys[7], 71), 0),
        "val_energy": jnp.clip(-3.0 + 2.5 * jax.random.uniform(keys[1], (K, NV), jnp.float32) ** block_levels(keys[1], (K, NV), ((0, 4), (1, 8)), -0.2, 0.2), -3.0, -0.5),
        "cond_energy": jnp.clip(0.5 + 2.5 * jax.random.uniform(keys[2], (K, NC), jnp.float32) ** block_levels(keys[2], (K, NC), ((0, 4),), -0.2, 0.2), 0.5, 3.0),
        "val_orb": noise(keys[3], (K, NV, NPT), 1.0, 6.0, ((0, 4), (1, 8))),
        "cond_orb": noise(keys[4], (K, NC, NPT), 1.0, 6.0, ((0, 4),)),
        "coulomb": draw_coulomb(jax.random.fold_in(keys[7], 71), 0),
        "screened": noise(keys[6], (NPT, NPT), 1.0, 6.0, ((0, 8), (1, 4))),
    }


def hamiltonian(vector, val_energy, cond_energy, val_orb, cond_orb, coulomb, screened):
    kernel_scale = 1.0 / (NPT * math.sqrt(K * NV * NC))
    vec_bf = vector.astype(jnp.bfloat16).reshape(K, NV, NC).astype(jnp.float32)
    val_f = val_orb.astype(jnp.float32)
    cond_f = cond_orb.astype(jnp.float32)
    hi_prec = lax.Precision.HIGHEST
    pair_part = jnp.einsum('kvc,kcp->kvp', vec_bf, cond_f, precision=hi_prec)
    density = lax.optimization_barrier(jnp.sum(val_f * pair_part, axis=(0, 1)))
    potential = kernel_scale * jnp.dot(coulomb, density.astype(jnp.bfloat16), preferred_element_type=jnp.float32)
    weighted = (val_f * potential).astype(jnp.bfloat16).astype(jnp.float32)
    exchange_term = jnp.einsum('kvp,kcp->kvc', weighted, cond_f, precision=hi_prec)
    mixed_val = jnp.einsum('kvc,kvn->kcn', vec_bf, val_f, precision=hi_prec).astype(jnp.bfloat16).astype(jnp.float32)
    block_len = min(512, NPT)
    block_count = NPT // block_len

    def block_step(acc, block_id):
        first = (block_id * block_len).astype(jnp.int32)
        cond_blk = lax.dynamic_slice_in_dim(cond_f, first, block_len, 2)
        screen_blk = lax.dynamic_slice_in_dim(screened, first, block_len, 0).astype(jnp.float32)
        amp = jnp.einsum('kcm,kcn->mn', cond_blk, mixed_val, precision=hi_prec)
        kern = (screen_blk * amp * kernel_scale).astype(jnp.bfloat16).astype(jnp.float32)
        folded = jnp.einsum('mn,kvn->kvm', kern, val_f, precision=hi_prec)
        return (acc + jnp.einsum('kcm,kvm->kvc', cond_blk, folded, precision=hi_prec), None)
    direct_term, _ = lax.scan(block_step, jnp.zeros((K, NV, NC), jnp.float32), jnp.arange(block_count).astype(jnp.int32))
    energy_gap = cond_energy[:, None, :] - val_energy[:, :, None]
    result = energy_gap * vector.reshape(K, NV, NC) + 2.0 * exchange_term - direct_term
    return result.reshape(K, NV * NC)

def reference(start_vec, val_energy, cond_energy, val_orb, cond_orb, coulomb, screened):
    count_all = K * NV * NC
    current = start_vec / jnp.sqrt(jnp.sum(start_vec * start_vec) / count_all + 1e-06)
    previous = jnp.zeros_like(start_vec)
    beta_val = jnp.float32(0.0)
    alphas = []
    betas = []
    for turn_index in range(STEPS):
        resid_vec = hamiltonian(current, val_energy, cond_energy, val_orb, cond_orb, coulomb, screened)
        if turn_index > 0:
            resid_vec = resid_vec - beta_val * previous
        alpha_val = jnp.sum(current * resid_vec) / count_all
        resid_vec = resid_vec - alpha_val * current
        beta_val = jnp.sqrt(jnp.sum(resid_vec * resid_vec) / count_all + 1e-06)
        previous = current
        current = resid_vec / beta_val
        alphas.append(alpha_val)
        betas.append(beta_val)
    coeffs = jnp.stack(alphas + betas).astype(jnp.float32)
    return (current, coeffs)
```

```python
import math

import jax
import jax.numpy as jnp
from jax import lax
from jax.sharding import PartitionSpec as P

STEPS = 2
AXES = ("ka", "band")


def gather_all(block, devices):
    wide = jnp.broadcast_to(block[None], (devices,) + block.shape)
    return lax.all_to_all(wide, AXES, split_axis=0, concat_axis=0, tiled=True)


def scatter_sum(parts):
    return jnp.sum(lax.all_to_all(parts, AXES, split_axis=0, concat_axis=0, tiled=True), axis=0)


def per_device(start_vec, val_energy, cond_energy, val_orb, cond_orb, coulomb, screened):
    n_ka = lax.axis_size("ka")
    n_band = lax.axis_size("band")
    devices = n_ka * n_band
    ka, band = lax.axis_index("ka"), lax.axis_index("band")
    me = ka * n_band + band
    k_dev, pair_blk = start_vec.shape
    nv_blk = val_orb.shape[1]
    n_cond = cond_orb.shape[1]
    n_val = nv_blk * n_band
    npt_all = cond_orb.shape[2]
    k_points = k_dev * n_ka
    mu_blk, nu_blk = screened.shape
    own_pts = coulomb.shape[0]
    count_all = k_points * n_val * n_cond
    kernel_scale = 1.0 / (npt_all * math.sqrt(count_all))
    bf, f32 = jnp.bfloat16, jnp.float32

    start_all = gather_all(start_vec, devices)
    val_cut = lax.all_to_all(
        val_orb.reshape(k_dev, nv_blk, n_ka, nu_blk).transpose(2, 0, 1, 3),
        "ka", split_axis=0, concat_axis=0, tiled=True,
    ).reshape(k_points, nv_blk, nu_blk)
    val_pts = lax.all_gather(val_cut, "band", axis=1, tiled=True)
    cond_local = lax.dynamic_slice_in_dim(cond_orb, band * mu_blk, mu_blk, 2)
    cond_pts = lax.all_gather(cond_local, "ka", axis=0, tiled=True)
    cond_rows = cond_orb.reshape(k_dev, n_cond, n_ka, n_band, own_pts)
    cond_rows = lax.dynamic_index_in_dim(cond_rows, band, 3, keepdims=False)
    cond_own = lax.all_to_all(
        cond_rows.transpose(2, 0, 1, 3), "ka", split_axis=0, concat_axis=0, tiled=True
    ).reshape(k_points, n_cond, own_pts)
    val_own = lax.dynamic_slice_in_dim(val_pts, band * own_pts, own_pts, 2)

    energy_gap = (cond_energy[:, None, :] - val_energy[:, :, None]).reshape(k_dev, pair_blk)
    start_sq = jnp.sum(start_all * start_all)
    current = start_all / jnp.sqrt(start_sq / count_all + 1e-06)
    previous = jnp.zeros_like(current)
    beta_val = jnp.float32(0.0)
    alphas = []
    betas = []
    for turn_index in range(STEPS):
        full_vec = (
            current.astype(bf)
            .reshape(n_ka, n_band, k_dev, nv_blk, n_cond)
            .transpose(0, 2, 1, 3, 4)
            .reshape(k_points, n_val, n_cond)
        )
        mixed_f = jnp.einsum("kvc,kvn->kcn", full_vec, val_pts, preferred_element_type=f32)
        mixed_own = lax.dynamic_slice_in_dim(mixed_f, band * own_pts, own_pts, 2)
        density_own = jnp.sum(mixed_own * cond_own.astype(f32), axis=(0, 1))
        density = gather_all(density_own.astype(bf), devices).reshape(npt_all)
        mixed_val = mixed_f.astype(bf)
        amp = jnp.einsum("kcm,kcn->mn", cond_pts, mixed_val, preferred_element_type=f32)
        kern = (screened.astype(f32) * amp * kernel_scale).astype(bf)
        folded = jnp.einsum("mn,kvn->kvm", kern, val_pts, preferred_element_type=f32).astype(bf)
        direct_part = jnp.einsum("kcm,kvm->kvc", cond_pts, folded, preferred_element_type=f32)
        potential = kernel_scale * jnp.dot(coulomb, density, preferred_element_type=f32)
        weighted = (val_own.astype(f32) * potential).astype(bf)
        exchange = jnp.einsum("kvp,kcp->kvc", weighted, cond_own, preferred_element_type=f32)
        part = 2.0 * exchange - direct_part
        arranged = (
            part.reshape(n_ka, k_dev, n_band, nv_blk, n_cond)
            .transpose(0, 2, 1, 3, 4)
            .reshape(devices, k_dev, pair_blk)
        )
        inter_own = scatter_sum(arranged)
        current_own = lax.dynamic_index_in_dim(current, me, 0, keepdims=False)
        resid_vec = gather_all(energy_gap * current_own + inter_own, devices)
        resid_vec = resid_vec - beta_val * previous
        alpha_val = jnp.sum(current * resid_vec) / count_all
        resid_vec = resid_vec - alpha_val * current
        beta_val = jnp.sqrt(jnp.sum(resid_vec * resid_vec) / count_all + 1e-06)
        previous = current
        current = resid_vec / beta_val
        alphas.append(alpha_val)
        betas.append(beta_val)
    coeffs = jnp.stack(alphas + betas)
    return (lax.dynamic_index_in_dim(current, me, 0, keepdims=False), coeffs)


def solution(mesh):
    in_specs = (
        P("ka", "band"),
        P("ka", "band"),
        P("ka", None),
        P("ka", "band", None),
        P("ka", None, None),
        P(("ka", "band"), None),
        P("band", "ka"),
    )
    out_specs = (P("ka", "band"), P())
    return jax.shard_map(
        per_device, mesh=mesh, in_specs=in_specs, out_specs=out_specs, check_vma=False
    )
```

```python
import functools
import math

import jax
import jax.numpy as jnp
from jax import lax
from jax.experimental import pallas as pl
from jax.experimental.pallas import tpu as pltpu
from jax.sharding import PartitionSpec as P

STEPS = 2
AXES = ("ka", "band")
BF, F32 = jnp.bfloat16, jnp.float32
LANES = 128
HALF = 64
ROWS = 8
MIB = 1 << 20

VMEM = pl.BlockSpec(memory_space=pltpu.VMEM)
SMEM = pl.BlockSpec(memory_space=pltpu.SMEM)
ANY = pl.BlockSpec(memory_space=pl.ANY)


def gather_all(block, devices):
    wide = jnp.broadcast_to(block[None], (devices,) + block.shape)
    return exchange_all(wide)


def exchange_all(parts):
    return lax.all_to_all(parts, AXES, split_axis=0, concat_axis=0, tiled=True)


def dot_nt(lhs, rhs):
    return lax.dot_general(lhs, rhs, (((1,), (1,)), ((), ())), preferred_element_type=F32)


def dot_tn(lhs, rhs):
    return lax.dot_general(lhs, rhs, (((0,), (0,)), ((), ())), preferred_element_type=F32)


def pack_vector(block, k_dev):
    groups = (k_dev + 1) // 2
    block = jnp.pad(block, ((0, 2 * groups - k_dev), (0, 0)))
    block = block.reshape(groups, 2, ROWS, HALF).transpose(0, 2, 1, 3)
    return block.reshape(groups * ROWS, LANES)


def lane_half(tile, have, want):
    if have != want:
        tile = pltpu.roll(tile, HALF, axis=1)
    lane = lax.broadcasted_iota(jnp.int32, tile.shape, 1)
    keep = lane < HALF if want == 0 else lane >= HALF
    return jnp.where(keep, tile, 0.0)


def piece_copies(val_refs, column, width, dest, sems):
    copies = []
    for d, refs in enumerate(val_refs):
        row = 0
        for ref in refs:
            copies.append(
                pltpu.make_async_copy(
                    ref.at[:, pl.ds(column, width)],
                    dest.at[d, pl.ds(row, ref.shape[0]), :],
                    sems.at[len(copies)],
                )
            )
            row += ref.shape[0]
    return copies


def split_refs(refs, counts):
    out, at = [], 0
    for count in counts:
        out.append(refs[at : at + count])
        at += count
    return out


def density_kernel(first, cfg, *refs):
    n_band, k_dev, k_points, own, count_all, counts = cfg
    n_val = sum(counts)
    lead, refs = refs[: 1 if first else 2], refs[1 if first else 2 :]
    cond_ref, refs = refs[0], refs[1:]
    val_refs, refs = split_refs(refs[:n_val], counts), refs[n_val:]
    q_ref, qx_ref, rho_ref, coef_ref, xs, vown, sems = refs
    band = lax.axis_index("band")
    copies = piece_copies(val_refs, pl.multiple_of(band * own, LANES), own, vown, sems)
    for copy in copies:
        copy.start()
    if first:
        vec = lead[0][...]
        norm = jnp.sum(vec * vec) / count_all
        q_ref[...] = vec / jnp.sqrt(norm + 1e-06)
        coef_ref[0] = 0.0
        coef_ref[1] = 0.0
    else:
        vec, prev = lead[0][...], lead[1][...]
        alpha = jnp.sum(vec * prev) / count_all
        vec = vec - alpha * prev
        beta = jnp.sqrt(jnp.sum(vec * vec) / count_all + 1e-06)
        q_ref[...] = vec / beta
        coef_ref[0] = alpha
        coef_ref[1] = beta
    for d in range(n_band):
        for k in range(k_points):
            z, kl = divmod(k, k_dev)
            tile = q_ref[z * n_band + jnp.bitwise_xor(band, d), pl.ds(kl // 2 * ROWS, ROWS), :]
            xs[k // 2, pl.ds(d * 2 * ROWS + k % 2 * ROWS, ROWS), :] = lane_half(tile, kl % 2, k % 2)
    qx_ref[...] = xs[...].astype(BF)
    for copy in copies:
        copy.wait()
    rho = jnp.zeros((1, own), F32)
    for kp in range(k_points // 2):
        rows = vown[:, kp * 2 * ROWS : (kp + 1) * 2 * ROWS, :].reshape(n_band * 2 * ROWS, own)
        mixed = dot_tn(qx_ref[kp], rows)
        cond = cond_ref[kp * LANES : (kp + 1) * LANES, :].astype(F32)
        rho = rho + jnp.sum(mixed * cond, axis=0, keepdims=True)
    for r in range(own // LANES):
        part = rho[:, r * LANES : (r + 1) * LANES]
        rho_ref[:, r, :] = jnp.broadcast_to(part, (rho_ref.shape[0], LANES))


def direct_kernel(cfg, tile_m, tile_n, scale, *refs):
    n_band, k_points, counts = cfg
    n_val = sum(counts)
    qx_ref, cond_ref, scr_ref = refs[:3]
    val_refs, refs = split_refs(refs[3 : 3 + n_val], counts), refs[3 + n_val :]
    di_ref, vals, conds, scrs, mixed, kern, folded, val_sems, cond_sem, scr_sems = refs
    mu, nu = scr_ref.shape
    val_copies = piece_copies(val_refs, 0, nu, vals, val_sems)
    cond_copy = pltpu.make_async_copy(cond_ref, conds, cond_sem.at[0])
    scr_copies = [
        pltpu.make_async_copy(
            scr_ref.at[pl.ds(i * tile_m, tile_m), :], scrs.at[pl.ds(i * tile_m, tile_m), :], scr_sems.at[i]
        )
        for i in range(mu // tile_m)
    ]
    for copy in val_copies + [cond_copy] + scr_copies:
        copy.start()
    for copy in val_copies:
        copy.wait()
    pairs = k_points // 2
    for kp in range(pairs):
        rows = vals[:, kp * 2 * ROWS : (kp + 1) * 2 * ROWS, :].reshape(n_band * 2 * ROWS, nu)
        mixed[kp * LANES : (kp + 1) * LANES, :] = dot_tn(qx_ref[kp], rows).astype(BF)
    cond_copy.wait()
    all_vals = vals[...].reshape(-1, nu)
    for i in range(mu // tile_m):
        at_m = slice(i * tile_m, (i + 1) * tile_m)
        cond_t = conds[:, at_m].T
        scr_copies[i].wait()
        for j in range(nu // tile_n):
            at_n = slice(j * tile_n, (j + 1) * tile_n)
            amp = jnp.dot(cond_t, mixed[:, at_n], preferred_element_type=F32)
            kern[:, at_n] = (scrs[at_m, at_n].astype(F32) * amp * scale).astype(BF)
        folded[:, at_m] = dot_nt(all_vals, kern[...]).astype(BF)
    per_piece = pairs * 2 * ROWS
    for kp in range(pairs):
        rows = [folded[d * per_piece + kp * 2 * ROWS : d * per_piece + (kp + 1) * 2 * ROWS, :] for d in range(n_band)]
        di_ref[kp] = dot_nt(jnp.concatenate(rows, axis=0), conds[kp * LANES : (kp + 1) * LANES, :])


def exchange_kernel(cfg, chunk, scale, *refs):
    n_band, k_dev, k_points, own, counts = cfg
    n_val = sum(counts)
    rho_ref, di_ref, cond_ref, coul_ref = refs[:4]
    val_refs, refs = split_refs(refs[4 : 4 + n_val], counts), refs[4 + n_val :]
    msg_ref, coul, vown, part, msg, val_sems, coul_sems = refs
    band = lax.axis_index("band")
    npt = coul_ref.shape[1]
    coul_copies = [
        pltpu.make_async_copy(
            coul_ref.at[:, pl.ds(i * chunk, chunk)], coul.at[:, pl.ds(i * chunk, chunk)], coul_sems.at[i]
        )
        for i in range(npt // chunk)
    ]
    val_copies = piece_copies(val_refs, pl.multiple_of(band * own, LANES), own, vown, val_sems)
    for copy in coul_copies + val_copies:
        copy.start()
    acc = jnp.zeros((own, LANES), F32)
    per_dev = own // LANES
    for i in range(npt // chunk):
        coul_copies[i].wait()
        for j in range(i * chunk // LANES, (i + 1) * chunk // LANES):
            rho = rho_ref[j // per_dev, pl.ds(j % per_dev, 1), :].astype(BF).astype(F32)
            acc = acc + coul[:, j * LANES : (j + 1) * LANES].astype(F32) * rho
    potential = scale * jnp.sum(acc.T, axis=0, keepdims=True)
    for copy in val_copies:
        copy.wait()
    for kp in range(k_points // 2):
        rows = vown[:, kp * 2 * ROWS : (kp + 1) * 2 * ROWS, :].reshape(n_band * 2 * ROWS, own)
        weighted = (rows.astype(F32) * potential).astype(BF)
        ex = dot_nt(weighted, cond_ref[kp * LANES : (kp + 1) * LANES, :])
        part[kp] = 2.0 * ex - di_ref[kp]
    for d in range(n_band):
        for z in range(k_points // k_dev):
            for g in range((k_dev + 1) // 2):
                tile = None
                for kl in range(2 * g, min(2 * g + 2, k_dev)):
                    k = z * k_dev + kl
                    piece = part[k // 2, pl.ds(d * 2 * ROWS + k % 2 * ROWS, ROWS), :]
                    piece = lane_half(piece, k % 2, kl % 2)
                    tile = piece if tile is None else tile + piece
                msg[z * n_band + jnp.bitwise_xor(band, d), pl.ds(g * ROWS, ROWS), :] = tile
    msg_ref[...] = msg[...].astype(BF)


def owner_kernel(first, n_band, *refs):
    if first:
        recv_ref, gap_ref, q_ref, out_ref = refs
    else:
        recv_ref, gap_ref, q_ref, prev_ref, coef_ref, out_ref = refs
    me = lax.axis_index("ka") * n_band + lax.axis_index("band")
    total = jnp.sum(recv_ref[...].astype(F32), axis=0)
    total = total + gap_ref[...] * q_ref[me]
    if not first:
        total = total - coef_ref[1] * prev_ref[me]
    out_ref[...] = jnp.broadcast_to(total[None], out_ref.shape)


def finish_kernel(n_band, count_all, w_ref, q_ref, coef_ref, out_ref, coeffs_ref):
    me = lax.axis_index("ka") * n_band + lax.axis_index("band")
    vec, cur = w_ref[...], q_ref[...]
    alpha = jnp.sum(vec * cur) / count_all
    vec = vec - alpha * cur
    beta = jnp.sqrt(jnp.sum(vec * vec) / count_all + 1e-06)
    own = (w_ref[me] - alpha * q_ref[me]) / beta
    coeffs_ref[0] = coef_ref[0]
    coeffs_ref[1] = alpha
    coeffs_ref[2] = coef_ref[1]
    coeffs_ref[3] = beta
    for kl in range(out_ref.shape[0]):
        tile = own[kl // 2 * ROWS : (kl // 2 + 1) * ROWS, :]
        other = pltpu.roll(tile, HALF, axis=1)
        left, right = (tile, other) if kl % 2 == 0 else (other, tile)
        low = lax.broadcasted_iota(jnp.int32, (1, LANES), 1) < HALF
        for j in range(ROWS // 2):
            row = jnp.where(low, left[2 * j : 2 * j + 1], right[2 * j + 1 : 2 * j + 2])
            out_ref[pl.ds(kl, 1), pl.ds(j * LANES, LANES)] = row


def params(mib):
    return pltpu.CompilerParams(vmem_limit_bytes=mib * MIB)


def shape_of(dims, kind=F32):
    return jax.ShapeDtypeStruct(dims, kind)


def plane_pieces(own_piece, n_band):
    def move(block, d):
        return lax.ppermute(block, "band", [(i, i ^ d) for i in range(n_band)])

    half = own_piece.shape[0] // 2
    by_x, by_y = move(own_piece, 2), move(own_piece, 4)
    diag = [move(by_x[:half], 4), move(by_y[half:], 2)]
    pieces = [[own_piece], [move(own_piece, 1)], [by_x], [move(by_x, 1)], [by_y], [move(by_y, 1)]]
    return pieces + [diag, [move(part, 1) for part in diag]]


def kernel_path(start_vec, val_energy, cond_energy, val_orb, cond_orb, coulomb, screened):
    n_ka = lax.axis_size("ka")
    n_band = lax.axis_size("band")
    devices = n_ka * n_band
    band = lax.axis_index("band")
    k_dev = start_vec.shape[0]
    nv_blk = val_orb.shape[1]
    n_cond = cond_orb.shape[1]
    npt_all = cond_orb.shape[2]
    k_points = k_dev * n_ka
    pairs = k_points // 2
    mu_blk, nu_blk = screened.shape
    own = coulomb.shape[0]
    count_all = k_points * nv_blk * n_band * n_cond
    scale = 1.0 / (npt_all * math.sqrt(count_all))
    piece_rows = k_points * nv_blk

    cond_local = lax.dynamic_slice_in_dim(cond_orb, band * mu_blk, mu_blk, 2)
    cond_pts = lax.all_gather(
        cond_local.reshape(k_dev * n_cond, mu_blk), "ka", axis=0, tiled=True
    )
    val_cut = lax.all_to_all(
        val_orb.reshape(k_dev, nv_blk, n_ka, nu_blk).transpose(2, 0, 1, 3),
        "ka", split_axis=0, concat_axis=0, tiled=True,
    ).reshape(piece_rows, nu_blk)
    pieces = plane_pieces(val_cut, n_band)
    counts = tuple(len(piece) for piece in pieces)
    flat = [ref for piece in pieces for ref in piece]
    start_all = gather_all(pack_vector(start_vec, k_dev), devices)
    cond_cut = jnp.stack(
        [lax.dynamic_slice_in_dim(cond_orb, z * nu_blk + band * own, own, 2) for z in range(n_ka)]
    ).reshape(n_ka, k_dev * n_cond, own)
    cond_own = lax.all_to_all(
        cond_cut, "ka", split_axis=0, concat_axis=0, tiled=True
    ).reshape(k_points * n_cond, own)
    gap = (cond_energy[:, None, :] - val_energy[:, :, None]).reshape(k_dev, nv_blk * n_cond)
    gap = pack_vector(gap, k_dev)

    block = start_all.shape[1:]
    vec_shape = shape_of((devices,) + block)
    n_copies = len(flat)
    own_scratch = pltpu.VMEM((n_band, piece_rows, own), BF)
    vec, prev, coef = start_all, None, None
    for step in range(STEPS):
        first = step == 0
        lead = [vec] if first else [vec, prev]
        cur, qx, rho, coef = pl.pallas_call(
            functools.partial(density_kernel, first, (n_band, k_dev, k_points, own, count_all, counts)),
            out_shape=(
                vec_shape,
                shape_of((pairs, LANES, LANES), BF),
                shape_of((devices, own // LANES, LANES)),
                shape_of((2,)),
            ),
            in_specs=[VMEM] * len(lead) + [VMEM] + [ANY] * n_copies,
            out_specs=(VMEM, VMEM, VMEM, SMEM),
            scratch_shapes=[
                pltpu.VMEM((pairs, LANES, LANES), F32),
                own_scratch,
                pltpu.SemaphoreType.DMA((n_copies,)),
            ],
            compiler_params=params(16),
            name="density",
        )(*lead, cond_own, *flat)
        density = exchange_all(rho)
        tile_m, tile_n = 256, 512
        direct = pl.pallas_call(
            functools.partial(direct_kernel, (n_band, k_points, counts), tile_m, tile_n, scale),
            out_shape=shape_of((pairs, LANES, LANES)),
            in_specs=[VMEM] + [ANY] * (2 + n_copies),
            out_specs=VMEM,
            scratch_shapes=[
                pltpu.VMEM((n_band, piece_rows, nu_blk), BF),
                pltpu.VMEM((k_points * n_cond, mu_blk), BF),
                pltpu.VMEM((mu_blk, nu_blk), BF),
                pltpu.VMEM((k_points * n_cond, nu_blk), BF),
                pltpu.VMEM((tile_m, nu_blk), BF),
                pltpu.VMEM((n_band * piece_rows, mu_blk), BF),
                pltpu.SemaphoreType.DMA((n_copies,)),
                pltpu.SemaphoreType.DMA((1,)),
                pltpu.SemaphoreType.DMA((mu_blk // tile_m,)),
            ],
            compiler_params=params(40),
            cost_estimate=pl.CostEstimate(
                flops=4 * mu_blk * nu_blk * k_points * n_cond, bytes_accessed=9 * MIB, transcendentals=0
            ),
            name="direct",
        )(qx, cond_pts, screened, *flat)
        chunk = 1024
        message = pl.pallas_call(
            functools.partial(exchange_kernel, (n_band, k_dev, k_points, own, counts), chunk, scale),
            out_shape=shape_of((devices,) + block, BF),
            in_specs=[VMEM] * 3 + [ANY] * (1 + n_copies),
            out_specs=VMEM,
            scratch_shapes=[
                pltpu.VMEM((own, npt_all), BF),
                own_scratch,
                pltpu.VMEM((pairs, LANES, LANES), F32),
                pltpu.VMEM((devices,) + block, F32),
                pltpu.SemaphoreType.DMA((n_copies,)),
                pltpu.SemaphoreType.DMA((npt_all // chunk,)),
            ],
            compiler_params=params(24),
            name="exchange",
        )(density, direct, cond_own, coulomb, *flat)
        recv = exchange_all(message)
        extra = [] if first else [prev, coef]
        wide = pl.pallas_call(
            functools.partial(owner_kernel, first, n_band),
            out_shape=vec_shape,
            in_specs=[VMEM] * 3 + ([] if first else [VMEM, SMEM]),
            out_specs=VMEM,
            compiler_params=params(8),
            name="owner",
        )(recv, gap, cur, *extra)
        vec, prev = exchange_all(wide), cur
    return pl.pallas_call(
        functools.partial(finish_kernel, n_band, count_all),
        out_shape=(shape_of(start_vec.shape), shape_of((2 * STEPS,))),
        in_specs=[VMEM, VMEM, SMEM],
        out_specs=(VMEM, SMEM),
        compiler_params=params(8),
        name="finish",
    )(vec, prev, coef)


def array_path(start_vec, val_energy, cond_energy, val_orb, cond_orb, coulomb, screened):
    n_ka = lax.axis_size("ka")
    n_band = lax.axis_size("band")
    devices = n_ka * n_band
    ka, band = lax.axis_index("ka"), lax.axis_index("band")
    me = ka * n_band + band
    k_dev, pair_blk = start_vec.shape
    nv_blk = val_orb.shape[1]
    n_cond = cond_orb.shape[1]
    n_val = nv_blk * n_band
    npt_all = cond_orb.shape[2]
    k_points = k_dev * n_ka
    mu_blk, nu_blk = screened.shape
    own_pts = coulomb.shape[0]
    count_all = k_points * n_val * n_cond
    kernel_scale = 1.0 / (npt_all * math.sqrt(count_all))

    start_all = gather_all(start_vec, devices)
    val_cut = lax.all_to_all(
        val_orb.reshape(k_dev, nv_blk, n_ka, nu_blk).transpose(2, 0, 1, 3),
        "ka", split_axis=0, concat_axis=0, tiled=True,
    ).reshape(k_points, nv_blk, nu_blk)
    val_pts = lax.all_gather(val_cut, "band", axis=1, tiled=True)
    cond_local = lax.dynamic_slice_in_dim(cond_orb, band * mu_blk, mu_blk, 2)
    cond_pts = lax.all_gather(cond_local, "ka", axis=0, tiled=True)
    cond_rows = cond_orb.reshape(k_dev, n_cond, n_ka, n_band, own_pts)
    cond_rows = lax.dynamic_index_in_dim(cond_rows, band, 3, keepdims=False)
    cond_own = lax.all_to_all(
        cond_rows.transpose(2, 0, 1, 3), "ka", split_axis=0, concat_axis=0, tiled=True
    ).reshape(k_points, n_cond, own_pts)
    val_own = lax.dynamic_slice_in_dim(val_pts, band * own_pts, own_pts, 2)

    energy_gap = (cond_energy[:, None, :] - val_energy[:, :, None]).reshape(k_dev, pair_blk)
    start_sq = jnp.sum(start_all * start_all)
    current = start_all / jnp.sqrt(start_sq / count_all + 1e-06)
    previous = jnp.zeros_like(current)
    beta_val = jnp.float32(0.0)
    alphas = []
    betas = []
    for turn_index in range(STEPS):
        full_vec = (
            current.astype(BF)
            .reshape(n_ka, n_band, k_dev, nv_blk, n_cond)
            .transpose(0, 2, 1, 3, 4)
            .reshape(k_points, n_val, n_cond)
        )
        mixed_f = jnp.einsum("kvc,kvn->kcn", full_vec, val_pts, preferred_element_type=F32)
        mixed_own = lax.dynamic_slice_in_dim(mixed_f, band * own_pts, own_pts, 2)
        density_own = jnp.sum(mixed_own * cond_own.astype(F32), axis=(0, 1))
        density = gather_all(density_own.astype(BF), devices).reshape(npt_all)
        mixed_val = mixed_f.astype(BF)
        amp = jnp.einsum("kcm,kcn->mn", cond_pts, mixed_val, preferred_element_type=F32)
        kern = (screened.astype(F32) * amp * kernel_scale).astype(BF)
        folded = jnp.einsum("mn,kvn->kvm", kern, val_pts, preferred_element_type=F32).astype(BF)
        direct_part = jnp.einsum("kcm,kvm->kvc", cond_pts, folded, preferred_element_type=F32)
        potential = kernel_scale * jnp.dot(coulomb, density, preferred_element_type=F32)
        weighted = (val_own.astype(F32) * potential).astype(BF)
        exchange = jnp.einsum("kvp,kcp->kvc", weighted, cond_own, preferred_element_type=F32)
        part = 2.0 * exchange - direct_part
        arranged = (
            part.reshape(n_ka, k_dev, n_band, nv_blk, n_cond)
            .transpose(0, 2, 1, 3, 4)
            .reshape(devices, k_dev, pair_blk)
        )
        inter_own = jnp.sum(exchange_all(arranged), axis=0)
        current_own = lax.dynamic_index_in_dim(current, me, 0, keepdims=False)
        resid_vec = gather_all(energy_gap * current_own + inter_own, devices)
        resid_vec = resid_vec - beta_val * previous
        alpha_val = jnp.sum(current * resid_vec) / count_all
        resid_vec = resid_vec - alpha_val * current
        beta_val = jnp.sqrt(jnp.sum(resid_vec * resid_vec) / count_all + 1e-06)
        previous = current
        current = resid_vec / beta_val
        alphas.append(alpha_val)
        betas.append(beta_val)
    coeffs = jnp.stack(alphas + betas)
    return (lax.dynamic_index_in_dim(current, me, 0, keepdims=False), coeffs)


def per_device(*args):
    start_vec, _, _, val_orb, cond_orb, coulomb, screened = args
    n_ka, n_band = lax.axis_size("ka"), lax.axis_size("band")
    fits = (
        n_band == 8
        and val_orb.shape[1] == ROWS
        and cond_orb.shape[1] == HALF
        and start_vec.shape[0] * n_ka % 2 == 0
        and coulomb.shape[0] % LANES == 0
        and coulomb.shape[1] % 1024 == 0
        and screened.shape[0] % 256 == 0
        and screened.shape[1] % 512 == 0
        and screened.shape[0] * screened.shape[1] <= 2 * MIB
    )
    return (kernel_path if fits else array_path)(*args)


def solution(mesh):
    in_specs = (
        P("ka", "band"),
        P("ka", "band"),
        P("ka", None),
        P("ka", "band", None),
        P("ka", None, None),
        P(("ka", "band"), None),
        P("band", "ka"),
    )
    out_specs = (P("ka", "band"), P())
    return jax.shard_map(
        per_device, mesh=mesh, in_specs=in_specs, out_specs=out_specs, check_vma=False
    )
```

```python
import functools
import math

import jax
import jax.numpy as jnp
from jax import lax
from jax.experimental import pallas as pl
from jax.experimental.pallas import tpu as pltpu
from jax.sharding import PartitionSpec as P

STEPS = 2
AXES = ("ka", "band")
BF, F32 = jnp.bfloat16, jnp.float32
LANES = 128
HALF = 64
ROWS = 8
MIB = 1 << 20

VMEM = pl.BlockSpec(memory_space=pltpu.VMEM)
SMEM = pl.BlockSpec(memory_space=pltpu.SMEM)
ANY = pl.BlockSpec(memory_space=pl.ANY)


def gather_all(block, devices):
    wide = jnp.broadcast_to(block[None], (devices,) + block.shape)
    return exchange_all(wide)


def exchange_all(parts):
    return lax.all_to_all(parts, AXES, split_axis=0, concat_axis=0, tiled=True)


def dot_nt(lhs, rhs):
    return lax.dot_general(lhs, rhs, (((1,), (1,)), ((), ())), preferred_element_type=F32)


def dot_tn(lhs, rhs):
    return lax.dot_general(lhs, rhs, (((0,), (0,)), ((), ())), preferred_element_type=F32)


def pack_vector(block, k_dev):
    groups = (k_dev + 1) // 2
    block = jnp.pad(block, ((0, 2 * groups - k_dev), (0, 0)))
    block = block.reshape(groups, 2, ROWS, HALF).transpose(0, 2, 1, 3)
    return block.reshape(groups * ROWS, LANES)


def lane_half(tile, have, want):
    if have != want:
        tile = pltpu.roll(tile, HALF, axis=1)
    lane = lax.broadcasted_iota(jnp.int32, tile.shape, 1)
    keep = lane < HALF if want == 0 else lane >= HALF
    return jnp.where(keep, tile, 0.0)


def with_sums(block, sums):
    row = lax.broadcasted_iota(jnp.int32, block.shape, 0)
    lane = lax.broadcasted_iota(jnp.int32, block.shape, 1)
    free = row == block.shape[0] - ROWS
    for i, total in enumerate(sums):
        rest = jnp.full(block.shape, total, F32)
        for part in range(3):
            piece = rest.astype(BF).astype(F32)
            block = jnp.where(free & (lane == HALF + 3 * i + part), piece, block)
            rest = rest - piece
    return block


def read_sums(msgs_ref, count):
    rows = msgs_ref.shape[1]
    tile = jnp.sum(msgs_ref[...].astype(F32), axis=0)[rows - ROWS :, :]
    row = lax.broadcasted_iota(jnp.int32, tile.shape, 0)
    lane = lax.broadcasted_iota(jnp.int32, tile.shape, 1)
    out = []
    for i in range(count):
        mine = (row == 0) & (lane >= HALF + 3 * i) & (lane < HALF + 3 * i + 3)
        out.append(jnp.sum(jnp.where(mine, tile, 0.0)))
    return out


def block_copies(groups, width, dest, sems, column=0):
    copies = []
    for d, refs in enumerate(groups):
        row = 0
        for ref in refs:
            copies.append(
                pltpu.make_async_copy(
                    ref.at[:, pl.ds(column, width)],
                    dest.at[d, pl.ds(row, ref.shape[0]), :],
                    sems.at[len(copies)],
                )
            )
            row += ref.shape[0]
    return copies


def split_refs(refs, counts):
    out, at = [], 0
    for count in counts:
        out.append(refs[at : at + count])
        at += count
    return out


def start_all(copies):
    for copy in copies:
        copy.start()


def wait_all(copies):
    for copy in copies:
        copy.wait()


def device_at(n_band, j, d):
    ka = jnp.bitwise_xor(lax.axis_index("ka"), j)
    return ka * n_band + jnp.bitwise_xor(lax.axis_index("band"), d)


def pair_rows(ref, kp):
    part = ref[:, kp * 2 * ROWS : (kp + 1) * 2 * ROWS, :]
    return part.reshape(part.shape[0] * 2 * ROWS, part.shape[2])


def pack_kernel(start_ref, gap_ref, own_ref, msg_ref):
    own_ref[...] = jnp.zeros_like(own_ref)
    for kl in range(start_ref.shape[0]):
        for j in range(ROWS // 2):
            row = start_ref[pl.ds(kl, 1), pl.ds(j * LANES, LANES)]
            for v in range(2):
                at = pl.ds(kl // 2 * ROWS + 2 * j + v, 1)
                own_ref[at, :] = own_ref[at, :] + lane_half(row, v, kl % 2)
    own = own_ref[...]
    square = own * own
    block = with_sums(own, [jnp.sum(square), jnp.sum(gap_ref[...] * square)])
    msg_ref[...] = jnp.broadcast_to(block.astype(BF)[None], msg_ref.shape)


def density_kernel(cfg, *refs):
    n_ka, n_band, k_dev, own, counts = cfg
    n_val = sum(counts)
    k_points = n_ka * k_dev
    msgs_ref, cond_refs, refs = refs[0], refs[1 : 1 + n_ka], refs[1 + n_ka :]
    val_refs, refs = split_refs(refs[:n_val], counts), refs[n_val:]
    qx_ref, rho_ref, xs, conds, vown, cond_sems, val_sems = refs
    column = pl.multiple_of(lax.axis_index("band") * own, LANES)
    copies = block_copies([[ref] for ref in cond_refs], own, conds, cond_sems)
    copies += block_copies(val_refs, own, vown, val_sems, column)
    start_all(copies)
    for d in range(n_band):
        for k in range(k_points):
            j, kl = divmod(k, k_dev)
            tile = msgs_ref[device_at(n_band, j, d), :, :].astype(F32)
            tile = tile[kl // 2 * ROWS : (kl // 2 + 1) * ROWS, :]
            xs[k // 2, pl.ds(d * 2 * ROWS + k % 2 * ROWS, ROWS), :] = lane_half(tile, kl % 2, k % 2)
    qx_ref[...] = xs[...].astype(BF)
    wait_all(copies)
    cond_rows = conds[...].reshape(-1, own)
    rho = jnp.zeros((1, own), F32)
    for kp in range(k_points // 2):
        mixed = dot_tn(qx_ref[kp], pair_rows(vown, kp))
        cond = cond_rows[kp * LANES : (kp + 1) * LANES, :].astype(F32)
        rho = rho + jnp.sum(mixed * cond, axis=0, keepdims=True)
    for r in range(own // LANES):
        part = rho[:, r * LANES : (r + 1) * LANES]
        rho_ref[:, r, :] = jnp.broadcast_to(part, (rho_ref.shape[0], LANES))


def direct_kernel(first, cfg, tile, scale, *refs):
    n_ka, n_band, k_points, counts = cfg
    n_val = sum(counts)
    qx_ref, cond_ref, scr_ref = refs[:3]
    val_refs, refs = split_refs(refs[3 : 3 + n_val], counts), refs[3 + n_val :]
    if first:
        di_ref, cond_out, conds, refs = refs[0], refs[1], refs[2], refs[3:]
    else:
        di_ref, refs = refs[0], refs[1:]
    cond_t, vals, scrs, mixed, kern, folded, cond_sems, val_sems, scr_sems = refs
    mu, nu = scr_ref.shape
    pairs = k_points // 2
    val_copies = block_copies(val_refs, nu, vals, val_sems)
    if first:
        rows = cond_ref.shape[0] // n_ka
        cond_copies = [
            pltpu.make_async_copy(
                cond_ref.at[pl.ds(jnp.bitwise_xor(lax.axis_index("ka"), j) * rows, rows), :],
                conds.at[pl.ds(j * rows, rows), :],
                cond_sems.at[j],
            )
            for j in range(n_ka)
        ]
    else:
        cond_copies = [pltpu.make_async_copy(cond_ref, cond_t, cond_sems.at[0])]
    scr_copies = [
        pltpu.make_async_copy(
            scr_ref.at[:, pl.ds(j * tile, tile)], scrs.at[:, pl.ds(j * tile, tile)], scr_sems.at[j]
        )
        for j in range(nu // tile)
    ]
    start_all(val_copies + cond_copies + scr_copies)
    wait_all(val_copies)
    for kp in range(pairs):
        mixed[kp * LANES : (kp + 1) * LANES, :] = dot_tn(qx_ref[kp], pair_rows(vals, kp)).astype(BF)
    wait_all(cond_copies)
    if first:
        cond_t[...] = conds[...].T
        out_copy = pltpu.make_async_copy(cond_t, cond_out, cond_sems.at[0])
        out_copy.start()
    for j in range(nu // tile):
        at = slice(j * tile, (j + 1) * tile)
        scr_copies[j].wait()
        amp = jnp.dot(cond_t[...], mixed[:, at], preferred_element_type=F32)
        kern[:, at] = (scrs[:, at].astype(F32) * amp * scale).astype(BF)
    all_vals = vals[...].reshape(-1, nu)
    for i in range(mu // tile):
        at = slice(i * tile, (i + 1) * tile)
        folded[:, at] = dot_nt(all_vals, kern[at, :]).astype(BF)
    per_piece = pairs * 2 * ROWS
    for kp in range(pairs):
        rows = [
            folded[d * per_piece + kp * 2 * ROWS : d * per_piece + (kp + 1) * 2 * ROWS, :]
            for d in range(n_band)
        ]
        di_ref[kp] = jnp.dot(
            jnp.concatenate(rows, axis=0),
            cond_t[:, kp * LANES : (kp + 1) * LANES],
            preferred_element_type=F32,
        )
    if first:
        out_copy.wait()


def exchange_kernel(cfg, chunk, scale, *refs):
    n_ka, n_band, k_dev, own, counts = cfg
    n_val = sum(counts)
    k_points = n_ka * k_dev
    rho_ref, di_ref, coul_ref = refs[:3]
    cond_refs, refs = refs[3 : 3 + n_ka], refs[3 + n_ka :]
    val_refs, refs = split_refs(refs[:n_val], counts), refs[n_val:]
    msg_ref, coul, conds, vown, part, msg, coul_sems, cond_sems, val_sems = refs
    npt = coul_ref.shape[1]
    column = pl.multiple_of(lax.axis_index("band") * own, LANES)
    coul_copies = [
        pltpu.make_async_copy(
            coul_ref.at[:, pl.ds(i * chunk, chunk)], coul.at[:, pl.ds(i * chunk, chunk)], coul_sems.at[i]
        )
        for i in range(npt // chunk)
    ]
    copies = block_copies([[ref] for ref in cond_refs], own, conds, cond_sems)
    copies += block_copies(val_refs, own, vown, val_sems, column)
    start_all(coul_copies + copies)
    acc = jnp.zeros((own, LANES), F32)
    per_dev = own // LANES
    for i in range(npt // chunk):
        coul_copies[i].wait()
        for j in range(i * chunk // LANES, (i + 1) * chunk // LANES):
            rho = rho_ref[j // per_dev, pl.ds(j % per_dev, 1), :].astype(BF).astype(F32)
            acc = acc + coul[:, j * LANES : (j + 1) * LANES].astype(F32) * rho
    potential = scale * jnp.sum(acc.T, axis=0, keepdims=True)
    wait_all(copies)
    cond_rows = conds[...].reshape(-1, own)
    for kp in range(k_points // 2):
        weighted = (pair_rows(vown, kp).astype(F32) * potential).astype(BF)
        ex = dot_nt(weighted, cond_rows[kp * LANES : (kp + 1) * LANES, :])
        part[kp] = 2.0 * ex - di_ref[kp]
    for d in range(n_band):
        for j in range(n_ka):
            for g in range((k_dev + 1) // 2):
                tile = None
                for kl in range(2 * g, min(2 * g + 2, k_dev)):
                    k = j * k_dev + kl
                    piece = part[k // 2, pl.ds(d * 2 * ROWS + k % 2 * ROWS, ROWS), :]
                    piece = lane_half(piece, k % 2, kl % 2)
                    tile = piece if tile is None else tile + piece
                msg[device_at(n_band, j, d), pl.ds(g * ROWS, ROWS), :] = tile
    msg_ref[...] = msg[...].astype(BF)


def received(recv_ref):
    return jnp.sum(recv_ref[...].astype(F32), axis=0)


def shifted(count_all, shift, square, cross_sum, square_sum):
    alpha = shift * square + cross_sum / count_all
    d = alpha - shift
    mean_sq = (square_sum - 2.0 * d * cross_sum) / count_all + d * d * square
    mean_sq = jnp.maximum(mean_sq, 0.0)
    return alpha, d, mean_sq


def first_owner_kernel(count_all, recv_ref, msgs_ref, gap_ref, own_ref, state_ref, coef_ref, msg_ref):
    start_sq, gap_sq = read_sums(msgs_ref, 2)
    norm = start_sq / count_all
    inv = 1.0 / jnp.sqrt(norm + 1e-06)
    square = norm / (norm + 1e-06)
    shift = gap_sq / jnp.maximum(start_sq, 1e-30)
    cur = own_ref[...] * inv
    inter = received(recv_ref) * inv
    gap = gap_ref[...]
    resid = (gap - shift) * cur + inter
    state_ref[0] = cur
    state_ref[1] = resid
    state_ref[2] = inter
    coef_ref[0] = shift
    coef_ref[1] = square
    coef_ref[2] = gap_sq * inv * inv
    sums = [
        jnp.sum(cur * resid),
        jnp.sum(resid * resid),
        jnp.sum(gap * resid * resid),
        jnp.sum(gap * resid * cur),
    ]
    msg_ref[...] = jnp.broadcast_to(with_sums(resid, sums).astype(BF)[None], msg_ref.shape)


def second_owner_kernel(count_all, recv_ref, msgs_ref, gap_ref, state_ref, coef_ref, out_ref, coef_out, msg_ref):
    cross, total, gap_rr, gap_rq = read_sums(msgs_ref, 4)
    alpha, d, mean_sq = shifted(count_all, coef_ref[0], coef_ref[1], cross, total)
    beta = jnp.sqrt(mean_sq + 1e-06)
    square = mean_sq / (mean_sq + 1e-06)
    gap_qq = gap_rr - 2.0 * d * gap_rq + d * d * coef_ref[2]
    shift = gap_qq / (mean_sq + 1e-06) / count_all
    prev = state_ref[0]
    cur = (state_ref[1] - d * prev) / beta
    inter = (received(recv_ref) - d * state_ref[2]) / beta
    resid = (gap_ref[...] - shift) * cur + inter - beta * prev
    out_ref[0] = cur
    out_ref[1] = resid
    coef_out[0] = alpha
    coef_out[1] = beta
    coef_out[2] = shift
    coef_out[3] = square
    dims = msg_ref.shape[:1] + msg_ref.shape[2:]
    msg_ref[:, 0, :] = jnp.full(dims, jnp.sum(cur * resid), F32)
    msg_ref[:, 1, :] = jnp.full(dims, jnp.sum(resid * resid), F32)


def finish_kernel(count_all, msgs_ref, state_ref, coef_ref, out_ref, coeffs_ref):
    sums = jnp.sum(msgs_ref[...], axis=0)
    alpha, d, mean_sq = shifted(count_all, coef_ref[2], coef_ref[3], sums[0, 0], sums[1, 0])
    beta = jnp.sqrt(mean_sq + 1e-06)
    own = (state_ref[1] - d * state_ref[0]) / beta
    coeffs_ref[0] = coef_ref[0]
    coeffs_ref[1] = alpha
    coeffs_ref[2] = coef_ref[1]
    coeffs_ref[3] = beta
    for kl in range(out_ref.shape[0]):
        tile = own[kl // 2 * ROWS : (kl // 2 + 1) * ROWS, :]
        other = pltpu.roll(tile, HALF, axis=1)
        left, right = (tile, other) if kl % 2 == 0 else (other, tile)
        low = lax.broadcasted_iota(jnp.int32, (1, LANES), 1) < HALF
        for j in range(ROWS // 2):
            row = jnp.where(low, left[2 * j : 2 * j + 1], right[2 * j + 1 : 2 * j + 2])
            out_ref[pl.ds(kl, 1), pl.ds(j * LANES, LANES)] = row


def shape_of(dims, kind=F32):
    return jax.ShapeDtypeStruct(dims, kind)


def call(kernel, name, out_shape, in_specs, out_specs, scratch=(), flops=0, moved=0):
    return pl.pallas_call(
        kernel,
        out_shape=out_shape,
        in_specs=in_specs,
        out_specs=out_specs,
        scratch_shapes=list(scratch),
        compiler_params=pltpu.CompilerParams(vmem_limit_bytes=58 * MIB),
        cost_estimate=pl.CostEstimate(flops=flops, bytes_accessed=moved, transcendentals=0),
        name=name,
    )


def swap(block, axis, d):
    return lax.ppermute(block, axis, [(i, i ^ d) for i in range(lax.axis_size(axis))])


def plane_pieces(own_piece):
    def move(block, d):
        return swap(block, "band", d)

    half = own_piece.shape[0] // 2
    by_x, by_y = move(own_piece, 2), move(own_piece, 4)
    diag = [move(by_x[:half], 4), move(by_y[half:], 2)]
    pieces = [[own_piece], [move(own_piece, 1)], [by_x], [move(by_x, 1)], [by_y], [move(by_y, 1)]]
    return pieces + [diag, [move(part, 1) for part in diag]]


def kernel_path(start_vec, val_energy, cond_energy, val_orb, cond_orb, coulomb, screened):
    n_ka = lax.axis_size("ka")
    n_band = lax.axis_size("band")
    devices = n_ka * n_band
    ka, band = lax.axis_index("ka"), lax.axis_index("band")
    k_dev = start_vec.shape[0]
    nv_blk = val_orb.shape[1]
    n_cond = cond_orb.shape[1]
    npt_all = cond_orb.shape[2]
    k_points = k_dev * n_ka
    pairs = k_points // 2
    mu_blk, nu_blk = screened.shape
    own = coulomb.shape[0]
    count_all = k_points * nv_blk * n_band * n_cond
    scale = 1.0 / (npt_all * math.sqrt(count_all))
    piece_rows = k_points * nv_blk

    cond_local = lax.dynamic_slice_in_dim(cond_orb, band * mu_blk, mu_blk, 2)
    cond_pts = lax.all_gather(
        cond_local.reshape(k_dev * n_cond, mu_blk), "ka", axis=0, tiled=True
    )

    def val_to(j):
        part = lax.dynamic_slice_in_dim(val_orb, jnp.bitwise_xor(ka, j) * nu_blk, nu_blk, 2)
        return part.reshape(k_dev * nv_blk, nu_blk)

    def cond_to(j):
        at = jnp.bitwise_xor(ka, j) * nu_blk + band * own
        return lax.dynamic_slice_in_dim(cond_orb, at, own, 2).reshape(k_dev * n_cond, own)

    val_cut = jnp.concatenate(
        [val_to(0)] + [swap(val_to(j), "ka", j) for j in range(1, n_ka)], axis=0
    )
    cond_own = [cond_to(0)] + [swap(cond_to(j), "ka", j) for j in range(1, n_ka)]
    pieces = plane_pieces(val_cut)
    counts = tuple(len(piece) for piece in pieces)
    flat = [ref for piece in pieces for ref in piece]
    n_copies = len(flat)
    gap = (cond_energy[:, None, :] - val_energy[:, :, None]).reshape(k_dev, nv_blk * n_cond)
    gap = pack_vector(gap, k_dev)

    block = gap.shape
    msg_shape = shape_of((devices,) + block, BF)
    start_own, message = call(
        pack_kernel, "pack", (shape_of(block), msg_shape), [VMEM] * 2, (VMEM, VMEM)
    )(start_vec, gap)
    msgs = exchange_all(message)

    own_scratch = [
        pltpu.VMEM((n_ka, k_dev * n_cond, own), BF),
        pltpu.VMEM((n_band, piece_rows, own), BF),
    ]
    own_sems = [pltpu.SemaphoreType.DMA((n_ka,)), pltpu.SemaphoreType.DMA((n_copies,))]
    tile, chunk = 256, 1024
    cond_side, state, coef = cond_pts, None, None
    for step in range(STEPS):
        first = step == 0
        qx, rho = call(
            functools.partial(density_kernel, (n_ka, n_band, k_dev, own, counts)),
            "density",
            (shape_of((pairs, LANES, LANES), BF), shape_of((devices, own // LANES, LANES))),
            [VMEM] + [ANY] * (n_ka + n_copies),
            (VMEM, VMEM),
            [pltpu.VMEM((pairs, LANES, LANES), F32)] + own_scratch + own_sems,
        )(msgs, *cond_own, *flat)
        density = exchange_all(rho)
        cond_t_dims = (mu_blk, k_points * n_cond)
        out = call(
            functools.partial(direct_kernel, first, (n_ka, n_band, k_points, counts), tile, scale),
            "direct",
            (shape_of((pairs, LANES, LANES)),) + ((shape_of(cond_t_dims, BF),) if first else ()),
            [VMEM] + [ANY] * (2 + n_copies),
            (VMEM,) + ((ANY,) if first else ()),
            ([pltpu.VMEM((k_points * n_cond, mu_blk), BF)] if first else [])
            + [
                pltpu.VMEM(cond_t_dims, BF),
                pltpu.VMEM((n_band, piece_rows, nu_blk), BF),
                pltpu.VMEM((mu_blk, nu_blk), BF),
                pltpu.VMEM((k_points * n_cond, nu_blk), BF),
                pltpu.VMEM((mu_blk, nu_blk), BF),
                pltpu.VMEM((n_band * piece_rows, mu_blk), BF),
                pltpu.SemaphoreType.DMA((n_ka,)),
                pltpu.SemaphoreType.DMA((n_copies,)),
                pltpu.SemaphoreType.DMA((nu_blk // tile,)),
            ],
            4 * mu_blk * nu_blk * k_points * n_cond,
            9 * MIB,
        )(qx, cond_side, screened, *flat)
        direct = out[0]
        if first:
            cond_side = out[1]
        parts = call(
            functools.partial(exchange_kernel, (n_ka, n_band, k_dev, own, counts), chunk, scale),
            "exchange",
            msg_shape,
            [VMEM] * 2 + [ANY] * (1 + n_ka + n_copies),
            VMEM,
            [pltpu.VMEM((own, npt_all), BF)]
            + own_scratch
            + [
                pltpu.VMEM((pairs, LANES, LANES), F32),
                pltpu.VMEM((devices,) + block, F32),
                pltpu.SemaphoreType.DMA((npt_all // chunk,)),
            ]
            + own_sems,
        )(density, direct, coulomb, *cond_own, *flat)
        recv = exchange_all(parts)
        if first:
            state, coef, message = call(
                functools.partial(first_owner_kernel, count_all),
                "first_owner",
                (shape_of((3,) + block), shape_of((3,)), msg_shape),
                [VMEM] * 4,
                (VMEM, SMEM, VMEM),
            )(recv, msgs, gap, start_own)
        else:
            state, coef, message = call(
                functools.partial(second_owner_kernel, count_all),
                "second_owner",
                (shape_of((2,) + block), shape_of((4,)), shape_of((devices, 2, LANES))),
                [VMEM] * 4 + [SMEM],
                (VMEM, SMEM, VMEM),
            )(recv, msgs, gap, state, coef)
        msgs = exchange_all(message)
    return call(
        functools.partial(finish_kernel, count_all),
        "finish",
        (shape_of(start_vec.shape), shape_of((2 * STEPS,))),
        [VMEM] * 2 + [SMEM],
        (VMEM, SMEM),
    )(msgs, state, coef)


def array_path(start_vec, val_energy, cond_energy, val_orb, cond_orb, coulomb, screened):
    n_ka = lax.axis_size("ka")
    n_band = lax.axis_size("band")
    devices = n_ka * n_band
    ka, band = lax.axis_index("ka"), lax.axis_index("band")
    me = ka * n_band + band
    k_dev, pair_blk = start_vec.shape
    nv_blk = val_orb.shape[1]
    n_cond = cond_orb.shape[1]
    n_val = nv_blk * n_band
    npt_all = cond_orb.shape[2]
    k_points = k_dev * n_ka
    mu_blk, nu_blk = screened.shape
    own_pts = coulomb.shape[0]
    count_all = k_points * n_val * n_cond
    kernel_scale = 1.0 / (npt_all * math.sqrt(count_all))

    start_all = gather_all(start_vec, devices)
    val_cut = lax.all_to_all(
        val_orb.reshape(k_dev, nv_blk, n_ka, nu_blk).transpose(2, 0, 1, 3),
        "ka", split_axis=0, concat_axis=0, tiled=True,
    ).reshape(k_points, nv_blk, nu_blk)
    val_pts = lax.all_gather(val_cut, "band", axis=1, tiled=True)
    cond_local = lax.dynamic_slice_in_dim(cond_orb, band * mu_blk, mu_blk, 2)
    cond_pts = lax.all_gather(cond_local, "ka", axis=0, tiled=True)
    cond_rows = cond_orb.reshape(k_dev, n_cond, n_ka, n_band, own_pts)
    cond_rows = lax.dynamic_index_in_dim(cond_rows, band, 3, keepdims=False)
    cond_own = lax.all_to_all(
        cond_rows.transpose(2, 0, 1, 3), "ka", split_axis=0, concat_axis=0, tiled=True
    ).reshape(k_points, n_cond, own_pts)
    val_own = lax.dynamic_slice_in_dim(val_pts, band * own_pts, own_pts, 2)

    energy_gap = (cond_energy[:, None, :] - val_energy[:, :, None]).reshape(k_dev, pair_blk)
    start_sq = jnp.sum(start_all * start_all)
    current = start_all / jnp.sqrt(start_sq / count_all + 1e-06)
    previous = jnp.zeros_like(current)
    beta_val = jnp.float32(0.0)
    alphas = []
    betas = []
    for turn_index in range(STEPS):
        full_vec = (
            current.astype(BF)
            .reshape(n_ka, n_band, k_dev, nv_blk, n_cond)
            .transpose(0, 2, 1, 3, 4)
            .reshape(k_points, n_val, n_cond)
        )
        mixed_f = jnp.einsum("kvc,kvn->kcn", full_vec, val_pts, preferred_element_type=F32)
        mixed_own = lax.dynamic_slice_in_dim(mixed_f, band * own_pts, own_pts, 2)
        density_own = jnp.sum(mixed_own * cond_own.astype(F32), axis=(0, 1))
        density = gather_all(density_own.astype(BF), devices).reshape(npt_all)
        mixed_val = mixed_f.astype(BF)
        amp = jnp.einsum("kcm,kcn->mn", cond_pts, mixed_val, preferred_element_type=F32)
        kern = (screened.astype(F32) * amp * kernel_scale).astype(BF)
        folded = jnp.einsum("mn,kvn->kvm", kern, val_pts, preferred_element_type=F32).astype(BF)
        direct_part = jnp.einsum("kcm,kvm->kvc", cond_pts, folded, preferred_element_type=F32)
        potential = kernel_scale * jnp.dot(coulomb, density, preferred_element_type=F32)
        weighted = (val_own.astype(F32) * potential).astype(BF)
        exchange = jnp.einsum("kvp,kcp->kvc", weighted, cond_own, preferred_element_type=F32)
        part = 2.0 * exchange - direct_part
        arranged = (
            part.reshape(n_ka, k_dev, n_band, nv_blk, n_cond)
            .transpose(0, 2, 1, 3, 4)
            .reshape(devices, k_dev, pair_blk)
        )
        inter_own = jnp.sum(exchange_all(arranged), axis=0)
        current_own = lax.dynamic_index_in_dim(current, me, 0, keepdims=False)
        resid_vec = gather_all(energy_gap * current_own + inter_own, devices)
        resid_vec = resid_vec - beta_val * previous
        alpha_val = jnp.sum(current * resid_vec) / count_all
        resid_vec = resid_vec - alpha_val * current
        beta_val = jnp.sqrt(jnp.sum(resid_vec * resid_vec) / count_all + 1e-06)
        previous = current
        current = resid_vec / beta_val
        alphas.append(alpha_val)
        betas.append(beta_val)
    coeffs = jnp.stack(alphas + betas)
    return (lax.dynamic_index_in_dim(current, me, 0, keepdims=False), coeffs)


def per_device(*args):
    start_vec, _, _, val_orb, cond_orb, coulomb, screened = args
    n_ka, n_band = lax.axis_size("ka"), lax.axis_size("band")
    fits = (
        n_band == 8
        and n_ka & (n_ka - 1) == 0
        and start_vec.shape[0] % 2 == 1
        and val_orb.shape[1] == ROWS
        and cond_orb.shape[1] == HALF
        and start_vec.shape[0] * n_ka % 2 == 0
        and coulomb.shape[0] % LANES == 0
        and coulomb.shape[1] % 1024 == 0
        and screened.shape[0] % 256 == 0
        and screened.shape[1] % 512 == 0
        and screened.shape[0] * screened.shape[1] <= 2 * MIB
    )
    return (kernel_path if fits else array_path)(*args)


def solution(mesh):
    in_specs = (
        P("ka", "band"),
        P("ka", "band"),
        P("ka", None),
        P("ka", "band", None),
        P("ka", None, None),
        P(("ka", "band"), None),
        P("band", "ka"),
    )
    out_specs = (P("ka", "band"), P())
    return jax.shard_map(
        per_device, mesh=mesh, in_specs=in_specs, out_specs=out_specs, check_vma=False
    )
```

```python
import functools
import math

import jax
import jax.numpy as jnp
from jax import lax
from jax.experimental import pallas as pl
from jax.experimental.pallas import tpu as pltpu
from jax.sharding import PartitionSpec as P

STEPS = 2
AXES = ("ka", "band")
BF, F32 = jnp.bfloat16, jnp.float32
LANES = 128
HALF = 64
ROWS = 8
MIB = 1 << 20

VMEM = pl.BlockSpec(memory_space=pltpu.VMEM)
SMEM = pl.BlockSpec(memory_space=pltpu.SMEM)
ANY = pl.BlockSpec(memory_space=pl.ANY)


def gather_all(block, devices):
    wide = jnp.broadcast_to(block[None], (devices,) + block.shape)
    return exchange_all(wide)


def exchange_all(parts):
    return lax.all_to_all(parts, AXES, split_axis=0, concat_axis=0, tiled=True)


def dot_nt(lhs, rhs):
    return lax.dot_general(lhs, rhs, (((1,), (1,)), ((), ())), preferred_element_type=F32)


def dot_tn(lhs, rhs):
    return lax.dot_general(lhs, rhs, (((0,), (0,)), ((), ())), preferred_element_type=F32)


def pack_vector(block, k_dev):
    groups = (k_dev + 1) // 2
    block = jnp.pad(block, ((0, 2 * groups - k_dev), (0, 0)))
    block = block.reshape(groups, 2, ROWS, HALF).transpose(0, 2, 1, 3)
    return block.reshape(groups * ROWS, LANES)


def lane_half(tile, have, want):
    if have != want:
        tile = pltpu.roll(tile, HALF, axis=1)
    lane = lax.broadcasted_iota(jnp.int32, tile.shape, 1)
    keep = lane < HALF if want == 0 else lane >= HALF
    return jnp.where(keep, tile, 0.0)


def with_sums(block, sums):
    row = lax.broadcasted_iota(jnp.int32, block.shape, 0)
    lane = lax.broadcasted_iota(jnp.int32, block.shape, 1)
    free = row == block.shape[0] - ROWS
    for i, total in enumerate(sums):
        rest = jnp.full(block.shape, total, F32)
        for part in range(3):
            piece = rest.astype(BF).astype(F32)
            block = jnp.where(free & (lane == HALF + 3 * i + part), piece, block)
            rest = rest - piece
    return block


def read_sums(msgs_ref, count):
    rows = msgs_ref.shape[1]
    tile = jnp.sum(msgs_ref[...].astype(F32), axis=0)[rows - ROWS :, :]
    row = lax.broadcasted_iota(jnp.int32, tile.shape, 0)
    lane = lax.broadcasted_iota(jnp.int32, tile.shape, 1)
    out = []
    for i in range(count):
        mine = (row == 0) & (lane >= HALF + 3 * i) & (lane < HALF + 3 * i + 3)
        out.append(jnp.sum(jnp.where(mine, tile, 0.0)))
    return out


def block_copies(groups, width, dest, sems, column=0):
    copies = []
    for d, refs in enumerate(groups):
        row = 0
        for ref in refs:
            copies.append(
                pltpu.make_async_copy(
                    ref.at[:, pl.ds(column, width)],
                    dest.at[d, pl.ds(row, ref.shape[0]), :],
                    sems.at[len(copies)],
                )
            )
            row += ref.shape[0]
    return copies


def split_refs(refs, counts):
    out, at = [], 0
    for count in counts:
        out.append(refs[at : at + count])
        at += count
    return out


def start_all(copies):
    for copy in copies:
        copy.start()


def wait_all(copies):
    for copy in copies:
        copy.wait()


def device_at(n_band, j, d):
    ka = jnp.bitwise_xor(lax.axis_index("ka"), j)
    return ka * n_band + jnp.bitwise_xor(lax.axis_index("band"), d)


def pair_rows(ref, kp):
    part = ref[:, kp * 2 * ROWS : (kp + 1) * 2 * ROWS, :]
    return part.reshape(part.shape[0] * 2 * ROWS, part.shape[2])


def pack_kernel(start_ref, gap_ref, own_ref, msg_ref):
    own_ref[...] = jnp.zeros_like(own_ref)
    for kl in range(start_ref.shape[0]):
        for j in range(ROWS // 2):
            row = start_ref[pl.ds(kl, 1), pl.ds(j * LANES, LANES)]
            for v in range(2):
                at = pl.ds(kl // 2 * ROWS + 2 * j + v, 1)
                own_ref[at, :] = own_ref[at, :] + lane_half(row, v, kl % 2)
    own = own_ref[...]
    square = own * own
    block = with_sums(own, [jnp.sum(square), jnp.sum(gap_ref[...] * square)])
    msg_ref[...] = jnp.broadcast_to(block.astype(BF)[None], msg_ref.shape)


def cut_kernel(cond_ref, msgs_ref, *refs):
    outs, sems = refs[:-1], refs[-1]
    k_dev, n_cond, npt = cond_ref.shape
    own = outs[0].shape[1]
    nu = npt // len(outs)
    copies = []
    for j, out in enumerate(outs):
        at = jnp.bitwise_xor(lax.axis_index("ka"), j) * nu + lax.axis_index("band") * own
        for kl in range(k_dev):
            copies.append(
                pltpu.make_async_copy(
                    cond_ref.at[kl, :, pl.ds(pl.multiple_of(at, LANES), own)],
                    out.at[pl.ds(kl * n_cond, n_cond), :],
                    sems.at[len(copies)],
                )
            )
    start_all(copies)
    wait_all(copies)


def turn_kernel(tile, scr_ref, out_ref, scrs, turned, in_sems, out_sems):
    nu = scr_ref.shape[1]
    ins, outs = [], []
    for j in range(nu // tile):
        at = pl.ds(j * tile, tile)
        ins.append(pltpu.make_async_copy(scr_ref.at[:, at], scrs.at[:, at], in_sems.at[j]))
        outs.append(pltpu.make_async_copy(turned.at[at, :], out_ref.at[at, :], out_sems.at[j]))
    start_all(ins)
    for j in range(nu // tile):
        ins[j].wait()
        turned[j * tile : (j + 1) * tile, :] = scrs[:, j * tile : (j + 1) * tile].T
        outs[j].start()
    wait_all(outs)


def order_kernel(counts, *refs):
    n_val = sum(counts)
    val_refs, refs = split_refs(refs[:n_val], counts), refs[n_val:]
    rows_out, turned_out, own_out, vals, ordered, turned, val_sems, out_sems = refs
    own = own_out.shape[1]
    nu = ordered.shape[1]
    copies = block_copies(val_refs, nu, vals, val_sems)
    start_all(copies)
    wait_all(copies)
    group = vals.shape[0] * 2 * ROWS
    outs = []
    for kp in range(ordered.shape[0] // group):
        at = slice(kp * group, (kp + 1) * group)
        ordered[at, :] = pair_rows(vals, kp)
        turned[:, at] = ordered[at, :].T
    column = pl.multiple_of(lax.axis_index("band") * own, LANES)
    outs = [
        pltpu.make_async_copy(ordered, rows_out, out_sems.at[0]),
        pltpu.make_async_copy(turned, turned_out, out_sems.at[1]),
        pltpu.make_async_copy(ordered.at[:, pl.ds(column, own)], own_out, out_sems.at[2]),
    ]
    start_all(outs)
    wait_all(outs)


def density_kernel(cfg, *refs):
    n_ka, n_band, k_dev = cfg
    k_points = n_ka * k_dev
    msgs_ref, vown_ref, cond_refs, refs = refs[0], refs[1], refs[2 : 2 + n_ka], refs[2 + n_ka :]
    qx_ref, rho_ref, xs, conds, cond_sems = refs
    own = vown_ref.shape[1]
    copies = block_copies([[ref] for ref in cond_refs], own, conds, cond_sems)
    start_all(copies)
    xs[...] = jnp.zeros_like(xs)
    for d in range(n_band):
        for k in range(k_points):
            j, kl = divmod(k, k_dev)
            tile = msgs_ref[device_at(n_band, j, d), :, :].astype(F32)
            tile = tile[kl // 2 * ROWS : (kl // 2 + 1) * ROWS, :]
            base = k // 2 % 2 * LANES
            at = pl.ds(base + d * 2 * ROWS + k % 2 * ROWS, ROWS)
            xs[k // 4, at, pl.ds(base, LANES)] = lane_half(tile, kl % 2, k % 2)
    qx_ref[...] = xs[...].astype(BF)
    wait_all(copies)
    cond_rows = conds[...].reshape(-1, own)
    rho = jnp.zeros((1, own), F32)
    quad = 2 * LANES
    for kq in range(k_points // 4):
        at = slice(kq * quad, (kq + 1) * quad)
        mixed = dot_tn(qx_ref[kq], vown_ref[at, :])
        rho = rho + jnp.sum(mixed * cond_rows[at, :].astype(F32), axis=0, keepdims=True)
    for r in range(own // LANES):
        part = rho[:, r * LANES : (r + 1) * LANES]
        rho_ref[:, r, :] = jnp.broadcast_to(part, (rho_ref.shape[0], LANES))


def direct_kernel(n_ka, tile, scale, *refs):
    qx_ref, cond_ref, scr_ref, turned_ref, rows_ref, di_ref = refs[:6]
    qx, conds, scrs, turned, vals, mixed, kern, folded, qx_sem, cond_sems, row_sem, chunk_sems = refs[6:]
    nu, mu = scr_ref.shape
    quad = 2 * LANES
    part = cond_ref.shape[0] // n_ka
    qx_copy = pltpu.make_async_copy(qx_ref, qx, qx_sem.at[0])
    cond_copies = [
        pltpu.make_async_copy(
            cond_ref.at[pl.ds(jnp.bitwise_xor(lax.axis_index("ka"), j) * part, part), :],
            conds.at[pl.ds(j * part, part), :],
            cond_sems.at[j],
        )
        for j in range(n_ka)
    ]
    turned_copies, scr_copies = [], []
    for i in range(nu // tile):
        at = pl.ds(i * tile, tile)
        turned_copies.append(
            pltpu.make_async_copy(turned_ref.at[at, :], turned.at[at, :], chunk_sems.at[0, i])
        )
        scr_copies.append(
            pltpu.make_async_copy(scr_ref.at[at, :], scrs.at[at, :], chunk_sems.at[1, i])
        )
    row_copy = pltpu.make_async_copy(rows_ref, vals, row_sem.at[0])
    start_all([qx_copy, turned_copies[0]] + cond_copies + [scr_copies[0]])
    for i in range(1, nu // tile):
        start_all([turned_copies[i], scr_copies[i]])
    row_copy.start()
    qx_copy.wait()
    for i in range(nu // tile):
        at = slice(i * tile, (i + 1) * tile)
        turned_copies[i].wait()
        for kq in range(qx.shape[0]):
            cols = slice(kq * quad, (kq + 1) * quad)
            mixed[at, cols] = jnp.dot(
                turned[at, cols], qx[kq], preferred_element_type=F32
            ).astype(BF)
        if i == 0:
            wait_all(cond_copies)
        scr_copies[i].wait()
        amp = jnp.dot(mixed[at, :], conds[...], preferred_element_type=F32)
        kern[at, :] = (scrs[at, :].astype(F32) * amp * scale).astype(BF)
    row_copy.wait()
    for i in range(mu // quad):
        at = slice(i * quad, (i + 1) * quad)
        folded[:, at] = jnp.dot(vals[...], kern[:, at], preferred_element_type=F32).astype(BF)
    for kp in range(di_ref.shape[0]):
        at = slice(kp * LANES, (kp + 1) * LANES)
        di_ref[kp] = dot_nt(folded[at, :], conds[at, :])


def exchange_kernel(cfg, chunk, scale, *refs):
    n_ka, n_band, k_dev = cfg
    k_points = n_ka * k_dev
    rho_ref, di_ref, coul_ref, vown_ref = refs[:4]
    cond_refs, refs = refs[4 : 4 + n_ka], refs[4 + n_ka :]
    msg_ref, rhos, di, coul, conds, vown, part, msg, coul_sems, cond_sems, sems = refs
    own, npt = coul_ref.shape
    coul_copies = [
        pltpu.make_async_copy(
            coul_ref.at[:, pl.ds(i * chunk, chunk)], coul.at[:, pl.ds(i * chunk, chunk)], coul_sems.at[i]
        )
        for i in range(npt // chunk)
    ]
    rho_copy = pltpu.make_async_copy(rho_ref, rhos, sems.at[0])
    copies = block_copies([[ref] for ref in cond_refs], own, conds, cond_sems)
    copies.append(pltpu.make_async_copy(di_ref, di, sems.at[1]))
    copies.append(pltpu.make_async_copy(vown_ref, vown, sems.at[2]))
    start_all([rho_copy] + coul_copies + copies)
    rho_copy.wait()
    acc = jnp.zeros((own, LANES), F32)
    per_dev = own // LANES
    for i in range(npt // chunk):
        coul_copies[i].wait()
        for j in range(i * chunk // LANES, (i + 1) * chunk // LANES):
            rho = rhos[j // per_dev, pl.ds(j % per_dev, 1), :].astype(BF).astype(F32)
            acc = acc + coul[:, j * LANES : (j + 1) * LANES].astype(F32) * rho
    potential = scale * jnp.sum(acc.T, axis=0, keepdims=True)
    wait_all(copies)
    cond_rows = conds[...].reshape(-1, own)
    for kp in range(k_points // 2):
        at = slice(kp * LANES, (kp + 1) * LANES)
        weighted = (vown[at, :].astype(F32) * potential).astype(BF)
        part[kp] = 2.0 * dot_nt(weighted, cond_rows[at, :]) - di[kp]
    for d in range(n_band):
        for j in range(n_ka):
            for g in range((k_dev + 1) // 2):
                tile = None
                for kl in range(2 * g, min(2 * g + 2, k_dev)):
                    k = j * k_dev + kl
                    piece = part[k // 2, pl.ds(d * 2 * ROWS + k % 2 * ROWS, ROWS), :]
                    piece = lane_half(piece, k % 2, kl % 2)
                    tile = piece if tile is None else tile + piece
                msg[device_at(n_band, j, d), pl.ds(g * ROWS, ROWS), :] = tile
    msg_ref[...] = msg[...].astype(BF)


def received(recv_ref):
    return jnp.sum(recv_ref[...].astype(F32), axis=0)


def shifted(count_all, shift, square, cross_sum, square_sum):
    alpha = shift * square + cross_sum / count_all
    d = alpha - shift
    mean_sq = (square_sum - 2.0 * d * cross_sum) / count_all + d * d * square
    mean_sq = jnp.maximum(mean_sq, 0.0)
    return alpha, d, mean_sq


def first_owner_kernel(count_all, recv_ref, msgs_ref, gap_ref, own_ref, state_ref, coef_ref, msg_ref):
    start_sq, gap_sq = read_sums(msgs_ref, 2)
    norm = start_sq / count_all
    inv = 1.0 / jnp.sqrt(norm + 1e-06)
    square = norm / (norm + 1e-06)
    shift = gap_sq / jnp.maximum(start_sq, 1e-30)
    cur = own_ref[...] * inv
    inter = received(recv_ref) * inv
    gap = gap_ref[...]
    resid = (gap - shift) * cur + inter
    state_ref[0] = cur
    state_ref[1] = resid
    state_ref[2] = inter
    coef_ref[0] = shift
    coef_ref[1] = square
    coef_ref[2] = gap_sq * inv * inv
    sums = [
        jnp.sum(cur * resid),
        jnp.sum(resid * resid),
        jnp.sum(gap * resid * resid),
        jnp.sum(gap * resid * cur),
    ]
    msg_ref[...] = jnp.broadcast_to(with_sums(resid, sums).astype(BF)[None], msg_ref.shape)


def second_owner_kernel(count_all, recv_ref, msgs_ref, gap_ref, state_ref, coef_ref, out_ref, coef_out, msg_ref):
    cross, total, gap_rr, gap_rq = read_sums(msgs_ref, 4)
    alpha, d, mean_sq = shifted(count_all, coef_ref[0], coef_ref[1], cross, total)
    beta = jnp.sqrt(mean_sq + 1e-06)
    square = mean_sq / (mean_sq + 1e-06)
    gap_qq = gap_rr - 2.0 * d * gap_rq + d * d * coef_ref[2]
    shift = gap_qq / (mean_sq + 1e-06) / count_all
    prev = state_ref[0]
    cur = (state_ref[1] - d * prev) / beta
    inter = (received(recv_ref) - d * state_ref[2]) / beta
    resid = (gap_ref[...] - shift) * cur + inter - beta * prev
    out_ref[0] = cur
    out_ref[1] = resid
    coef_out[0] = alpha
    coef_out[1] = beta
    coef_out[2] = shift
    coef_out[3] = square
    dims = msg_ref.shape[:1] + msg_ref.shape[2:]
    msg_ref[:, 0, :] = jnp.full(dims, jnp.sum(cur * resid), F32)
    msg_ref[:, 1, :] = jnp.full(dims, jnp.sum(resid * resid), F32)


def finish_kernel(count_all, msgs_ref, state_ref, coef_ref, out_ref, coeffs_ref):
    sums = jnp.sum(msgs_ref[...], axis=0)
    alpha, d, mean_sq = shifted(count_all, coef_ref[2], coef_ref[3], sums[0, 0], sums[1, 0])
    beta = jnp.sqrt(mean_sq + 1e-06)
    own = (state_ref[1] - d * state_ref[0]) / beta
    coeffs_ref[0] = coef_ref[0]
    coeffs_ref[1] = alpha
    coeffs_ref[2] = coef_ref[1]
    coeffs_ref[3] = beta
    for kl in range(out_ref.shape[0]):
        tile = own[kl // 2 * ROWS : (kl // 2 + 1) * ROWS, :]
        other = pltpu.roll(tile, HALF, axis=1)
        left, right = (tile, other) if kl % 2 == 0 else (other, tile)
        low = lax.broadcasted_iota(jnp.int32, (1, LANES), 1) < HALF
        for j in range(ROWS // 2):
            row = jnp.where(low, left[2 * j : 2 * j + 1], right[2 * j + 1 : 2 * j + 2])
            out_ref[pl.ds(kl, 1), pl.ds(j * LANES, LANES)] = row


def shape_of(dims, kind=F32):
    return jax.ShapeDtypeStruct(dims, kind)


def call(kernel, name, out_shape, in_specs, out_specs, scratch=(), mib=58, flops=0, moved=0):
    return pl.pallas_call(
        kernel,
        out_shape=out_shape,
        in_specs=in_specs,
        out_specs=out_specs,
        scratch_shapes=list(scratch),
        compiler_params=pltpu.CompilerParams(vmem_limit_bytes=mib * MIB),
        cost_estimate=pl.CostEstimate(flops=flops, bytes_accessed=moved, transcendentals=0),
        name=name,
    )


def dma(*dims):
    return pltpu.SemaphoreType.DMA(dims)


def swap(block, axis, d):
    return lax.ppermute(block, axis, [(i, i ^ d) for i in range(lax.axis_size(axis))])


def plane_pieces(own_piece):
    def move(block, d):
        return swap(block, "band", d)

    half = own_piece.shape[0] // 2
    by_x, by_y = move(own_piece, 2), move(own_piece, 4)
    diag = [move(by_x[:half], 4), move(by_y[half:], 2)]
    pieces = [[own_piece], [move(own_piece, 1)], [by_x], [move(by_x, 1)], [by_y], [move(by_y, 1)]]
    return pieces + [diag, [move(part, 1) for part in diag]]


def kernel_path(start_vec, val_energy, cond_energy, val_orb, cond_orb, coulomb, screened):
    n_ka = lax.axis_size("ka")
    n_band = lax.axis_size("band")
    devices = n_ka * n_band
    ka, band = lax.axis_index("ka"), lax.axis_index("band")
    k_dev = start_vec.shape[0]
    nv_blk = val_orb.shape[1]
    n_cond = cond_orb.shape[1]
    npt_all = cond_orb.shape[2]
    k_points = k_dev * n_ka
    pairs = k_points // 2
    mu_blk, nu_blk = screened.shape
    own = coulomb.shape[0]
    count_all = k_points * nv_blk * n_band * n_cond
    scale = 1.0 / (npt_all * math.sqrt(count_all))
    piece_rows = k_points * nv_blk

    cond_local = lax.dynamic_slice_in_dim(cond_orb, band * mu_blk, mu_blk, 2)
    cond_pts = lax.all_gather(
        cond_local.reshape(k_dev * n_cond, mu_blk), "ka", axis=0, tiled=True
    )

    def val_to(j):
        part = lax.dynamic_slice_in_dim(val_orb, jnp.bitwise_xor(ka, j) * nu_blk, nu_blk, 2)
        return part.reshape(k_dev * nv_blk, nu_blk)

    val_cut = jnp.concatenate(
        [val_to(0)] + [swap(val_to(j), "ka", j) for j in range(1, n_ka)], axis=0
    )
    pieces = plane_pieces(val_cut)
    counts = tuple(len(piece) for piece in pieces)
    flat = [ref for piece in pieces for ref in piece]
    n_copies = len(flat)
    gap = (cond_energy[:, None, :] - val_energy[:, :, None]).reshape(k_dev, nv_blk * n_cond)
    gap = pack_vector(gap, k_dev)

    block = gap.shape
    msg_shape = shape_of((devices,) + block, BF)
    start_own, message = call(
        pack_kernel, "pack", (shape_of(block), msg_shape), [VMEM] * 2, (VMEM, VMEM), mib=8
    )(start_vec, gap)
    msgs = exchange_all(message)
    own_rows = k_dev * n_cond
    cuts = call(
        cut_kernel,
        "cut",
        (shape_of((own_rows, own), BF),) * n_ka,
        [ANY, ANY],
        (ANY,) * n_ka,
        [dma(n_ka * k_dev)],
        mib=8,
    )(cond_orb, msgs)
    cond_own = [cuts[0]] + [swap(cuts[j], "ka", j) for j in range(1, n_ka)]

    chunk, tile = 1024, 512
    rows_all, conds_all = k_points * nv_blk * n_band, k_points * n_cond
    scr_turned = call(
        functools.partial(turn_kernel, tile),
        "turn",
        shape_of((nu_blk, mu_blk), BF),
        [ANY],
        ANY,
        [pltpu.VMEM((mu_blk, nu_blk), BF), pltpu.VMEM((nu_blk, mu_blk), BF)]
        + [dma(nu_blk // tile)] * 2,
        moved=8 * MIB,
    )(screened)
    val_rows, val_turned, val_own = call(
        functools.partial(order_kernel, counts),
        "order",
        (
            shape_of((rows_all, nu_blk), BF),
            shape_of((nu_blk, rows_all), BF),
            shape_of((rows_all, own), BF),
        ),
        [ANY] * n_copies,
        (ANY, ANY, ANY),
        [
            pltpu.VMEM((n_band, piece_rows, nu_blk), BF),
            pltpu.VMEM((rows_all, nu_blk), BF),
            pltpu.VMEM((nu_blk, rows_all), BF),
            dma(n_copies),
            dma(3),
        ],
        moved=9 * MIB,
    )(*flat)

    cfg = (n_ka, n_band, k_dev)
    quads = k_points // 4
    state, coef = None, None
    for step in range(STEPS):
        first = step == 0
        qx, rho = call(
            functools.partial(density_kernel, cfg),
            "density",
            (
                shape_of((quads, 2 * LANES, 2 * LANES), BF),
                shape_of((devices, own // LANES, LANES)),
            ),
            [VMEM] * 2 + [ANY] * n_ka,
            (VMEM, VMEM),
            [
                pltpu.VMEM((quads, 2 * LANES, 2 * LANES), F32),
                pltpu.VMEM((n_ka, own_rows, own), BF),
                dma(n_ka),
            ],
            mib=8,
        )(msgs, val_own, *cond_own)
        density = exchange_all(rho)
        direct = call(
            functools.partial(direct_kernel, n_ka, tile, scale),
            "direct",
            shape_of((pairs, LANES, LANES)),
            [ANY] * 5,
            VMEM,
            [
                pltpu.VMEM((quads, 2 * LANES, 2 * LANES), BF),
                pltpu.VMEM((conds_all, mu_blk), BF),
                pltpu.VMEM((nu_blk, mu_blk), BF),
                pltpu.VMEM((nu_blk, rows_all), BF),
                pltpu.VMEM((rows_all, nu_blk), BF),
                pltpu.VMEM((nu_blk, conds_all), BF),
                pltpu.VMEM((nu_blk, mu_blk), BF),
                pltpu.VMEM((rows_all, mu_blk), BF),
                dma(1),
                dma(n_ka),
                dma(1),
                dma(2, nu_blk // tile),
            ],
            flops=4 * mu_blk * nu_blk * conds_all,
            moved=12 * MIB,
        )(qx, cond_pts, scr_turned, val_turned, val_rows)
        parts = call(
            functools.partial(exchange_kernel, cfg, chunk, scale),
            "exchange",
            msg_shape,
            [ANY] * (4 + n_ka),
            VMEM,
            [
                pltpu.VMEM((devices, own // LANES, LANES), F32),
                pltpu.VMEM((pairs, LANES, LANES), F32),
                pltpu.VMEM((own, npt_all), BF),
                pltpu.VMEM((n_ka, own_rows, own), BF),
                pltpu.VMEM((rows_all, own), BF),
                pltpu.VMEM((pairs, LANES, LANES), F32),
                pltpu.VMEM((devices,) + block, F32),
                dma(npt_all // chunk),
                dma(n_ka),
                dma(3),
            ],
        )(density, direct, coulomb, val_own, *cond_own)
        recv = exchange_all(parts)
        if first:
            state, coef, message = call(
                functools.partial(first_owner_kernel, count_all),
                "first_owner",
                (shape_of((3,) + block), shape_of((3,)), msg_shape),
                [VMEM] * 4,
                (VMEM, SMEM, VMEM),
                mib=8,
            )(recv, msgs, gap, start_own)
        else:
            state, coef, message = call(
                functools.partial(second_owner_kernel, count_all),
                "second_owner",
                (shape_of((2,) + block), shape_of((4,)), shape_of((devices, 2, LANES))),
                [VMEM] * 4 + [SMEM],
                (VMEM, SMEM, VMEM),
                mib=8,
            )(recv, msgs, gap, state, coef)
        msgs = exchange_all(message)
    return call(
        functools.partial(finish_kernel, count_all),
        "finish",
        (shape_of(start_vec.shape), shape_of((2 * STEPS,))),
        [VMEM] * 2 + [SMEM],
        (VMEM, SMEM),
        mib=8,
    )(msgs, state, coef)


def array_path(start_vec, val_energy, cond_energy, val_orb, cond_orb, coulomb, screened):
    n_ka = lax.axis_size("ka")
    n_band = lax.axis_size("band")
    devices = n_ka * n_band
    ka, band = lax.axis_index("ka"), lax.axis_index("band")
    me = ka * n_band + band
    k_dev, pair_blk = start_vec.shape
    nv_blk = val_orb.shape[1]
    n_cond = cond_orb.shape[1]
    n_val = nv_blk * n_band
    npt_all = cond_orb.shape[2]
    k_points = k_dev * n_ka
    mu_blk, nu_blk = screened.shape
    own_pts = coulomb.shape[0]
    count_all = k_points * n_val * n_cond
    kernel_scale = 1.0 / (npt_all * math.sqrt(count_all))

    start_all = gather_all(start_vec, devices)
    val_cut = lax.all_to_all(
        val_orb.reshape(k_dev, nv_blk, n_ka, nu_blk).transpose(2, 0, 1, 3),
        "ka", split_axis=0, concat_axis=0, tiled=True,
    ).reshape(k_points, nv_blk, nu_blk)
    val_pts = lax.all_gather(val_cut, "band", axis=1, tiled=True)
    cond_local = lax.dynamic_slice_in_dim(cond_orb, band * mu_blk, mu_blk, 2)
    cond_pts = lax.all_gather(cond_local, "ka", axis=0, tiled=True)
    cond_rows = cond_orb.reshape(k_dev, n_cond, n_ka, n_band, own_pts)
    cond_rows = lax.dynamic_index_in_dim(cond_rows, band, 3, keepdims=False)
    cond_own = lax.all_to_all(
        cond_rows.transpose(2, 0, 1, 3), "ka", split_axis=0, concat_axis=0, tiled=True
    ).reshape(k_points, n_cond, own_pts)
    val_own = lax.dynamic_slice_in_dim(val_pts, band * own_pts, own_pts, 2)

    energy_gap = (cond_energy[:, None, :] - val_energy[:, :, None]).reshape(k_dev, pair_blk)
    start_sq = jnp.sum(start_all * start_all)
    current = start_all / jnp.sqrt(start_sq / count_all + 1e-06)
    previous = jnp.zeros_like(current)
    beta_val = jnp.float32(0.0)
    alphas = []
    betas = []
    for turn_index in range(STEPS):
        full_vec = (
            current.astype(BF)
            .reshape(n_ka, n_band, k_dev, nv_blk, n_cond)
            .transpose(0, 2, 1, 3, 4)
            .reshape(k_points, n_val, n_cond)
        )
        mixed_f = jnp.einsum("kvc,kvn->kcn", full_vec, val_pts, preferred_element_type=F32)
        mixed_own = lax.dynamic_slice_in_dim(mixed_f, band * own_pts, own_pts, 2)
        density_own = jnp.sum(mixed_own * cond_own.astype(F32), axis=(0, 1))
        density = gather_all(density_own.astype(BF), devices).reshape(npt_all)
        mixed_val = mixed_f.astype(BF)
        amp = jnp.einsum("kcm,kcn->mn", cond_pts, mixed_val, preferred_element_type=F32)
        kern = (screened.astype(F32) * amp * kernel_scale).astype(BF)
        folded = jnp.einsum("mn,kvn->kvm", kern, val_pts, preferred_element_type=F32).astype(BF)
        direct_part = jnp.einsum("kcm,kvm->kvc", cond_pts, folded, preferred_element_type=F32)
        potential = kernel_scale * jnp.dot(coulomb, density, preferred_element_type=F32)
        weighted = (val_own.astype(F32) * potential).astype(BF)
        exchange = jnp.einsum("kvp,kcp->kvc", weighted, cond_own, preferred_element_type=F32)
        part = 2.0 * exchange - direct_part
        arranged = (
            part.reshape(n_ka, k_dev, n_band, nv_blk, n_cond)
            .transpose(0, 2, 1, 3, 4)
            .reshape(devices, k_dev, pair_blk)
        )
        inter_own = jnp.sum(exchange_all(arranged), axis=0)
        current_own = lax.dynamic_index_in_dim(current, me, 0, keepdims=False)
        resid_vec = gather_all(energy_gap * current_own + inter_own, devices)
        resid_vec = resid_vec - beta_val * previous
        alpha_val = jnp.sum(current * resid_vec) / count_all
        resid_vec = resid_vec - alpha_val * current
        beta_val = jnp.sqrt(jnp.sum(resid_vec * resid_vec) / count_all + 1e-06)
        previous = current
        current = resid_vec / beta_val
        alphas.append(alpha_val)
        betas.append(beta_val)
    coeffs = jnp.stack(alphas + betas)
    return (lax.dynamic_index_in_dim(current, me, 0, keepdims=False), coeffs)


def per_device(*args):
    start_vec, _, _, val_orb, cond_orb, coulomb, screened = args
    n_ka, n_band = lax.axis_size("ka"), lax.axis_size("band")
    fits = (
        n_band == 8
        and n_ka & (n_ka - 1) == 0
        and start_vec.shape[0] % 2 == 1
        and val_orb.shape[1] == ROWS
        and cond_orb.shape[1] == HALF
        and start_vec.shape[0] * n_ka % 4 == 0
        and coulomb.shape[0] % LANES == 0
        and coulomb.shape[1] % 1024 == 0
        and screened.shape[0] % 256 == 0
        and screened.shape[1] % 512 == 0
        and screened.shape[0] * screened.shape[1] <= 2 * MIB
    )
    return (kernel_path if fits else array_path)(*args)


def solution(mesh):
    in_specs = (
        P("ka", "band"),
        P("ka", "band"),
        P("ka", None),
        P("ka", "band", None),
        P("ka", None, None),
        P(("ka", "band"), None),
        P("band", "ka"),
    )
    out_specs = (P("ka", "band"), P())
    return jax.shard_map(
        per_device, mesh=mesh, in_specs=in_specs, out_specs=out_specs, check_vma=False
    )
```

```python
import functools
import math

import jax
import jax.numpy as jnp
from jax import lax
from jax.experimental import pallas as pl
from jax.experimental.pallas import tpu as pltpu
from jax.sharding import PartitionSpec as P

STEPS = 2
AXES = ("ka", "band")
BF, F32 = jnp.bfloat16, jnp.float32
LANES = 128
HALF = 64
ROWS = 8
MIB = 1 << 20

VMEM = pl.BlockSpec(memory_space=pltpu.VMEM)
SMEM = pl.BlockSpec(memory_space=pltpu.SMEM)
ANY = pl.BlockSpec(memory_space=pl.ANY)


def gather_all(block, devices):
    wide = jnp.broadcast_to(block[None], (devices,) + block.shape)
    return exchange_all(wide)


def exchange_all(parts):
    return lax.all_to_all(parts, AXES, split_axis=0, concat_axis=0, tiled=True)


def dot_nt(lhs, rhs):
    return lax.dot_general(lhs, rhs, (((1,), (1,)), ((), ())), preferred_element_type=F32)


def dot_tn(lhs, rhs):
    return lax.dot_general(lhs, rhs, (((0,), (0,)), ((), ())), preferred_element_type=F32)


def pack_vector(block, k_dev):
    groups = (k_dev + 1) // 2
    block = jnp.pad(block, ((0, 2 * groups - k_dev), (0, 0)))
    block = block.reshape(groups, 2, ROWS, HALF).transpose(0, 2, 1, 3)
    return block.reshape(groups * ROWS, LANES)


def lane_half(tile, have, want):
    if have != want:
        tile = pltpu.roll(tile, HALF, axis=1)
    lane = lax.broadcasted_iota(jnp.int32, tile.shape, 1)
    keep = lane < HALF if want == 0 else lane >= HALF
    return jnp.where(keep, tile, 0.0)


def with_sums(block, sums):
    row = lax.broadcasted_iota(jnp.int32, block.shape, 0)
    lane = lax.broadcasted_iota(jnp.int32, block.shape, 1)
    free = row == block.shape[0] - ROWS
    for i, total in enumerate(sums):
        rest = jnp.full(block.shape, total, F32)
        for part in range(3):
            piece = rest.astype(BF).astype(F32)
            block = jnp.where(free & (lane == HALF + 3 * i + part), piece, block)
            rest = rest - piece
    return block


def read_sums(msgs_ref, count):
    rows = msgs_ref.shape[1]
    tile = jnp.sum(msgs_ref[...].astype(F32), axis=0)[rows - ROWS :, :]
    row = lax.broadcasted_iota(jnp.int32, tile.shape, 0)
    lane = lax.broadcasted_iota(jnp.int32, tile.shape, 1)
    out = []
    for i in range(count):
        mine = (row == 0) & (lane >= HALF + 3 * i) & (lane < HALF + 3 * i + 3)
        out.append(jnp.sum(jnp.where(mine, tile, 0.0)))
    return out


def block_copies(groups, width, dest, sems, column=0):
    copies = []
    for d, refs in enumerate(groups):
        row = 0
        for ref in refs:
            copies.append(
                pltpu.make_async_copy(
                    ref.at[:, pl.ds(column, width)],
                    dest.at[d, pl.ds(row, ref.shape[0]), :],
                    sems.at[len(copies)],
                )
            )
            row += ref.shape[0]
    return copies


def split_refs(refs, counts):
    out, at = [], 0
    for count in counts:
        out.append(refs[at : at + count])
        at += count
    return out


def start_all(copies):
    for copy in copies:
        copy.start()


def wait_all(copies):
    for copy in copies:
        copy.wait()


def device_at(n_band, j, d):
    ka = jnp.bitwise_xor(lax.axis_index("ka"), j)
    return ka * n_band + jnp.bitwise_xor(lax.axis_index("band"), d)


def pair_rows(ref, kp):
    part = ref[:, kp * 2 * ROWS : (kp + 1) * 2 * ROWS, :]
    return part.reshape(part.shape[0] * 2 * ROWS, part.shape[2])


def pack_kernel(start_ref, gap_ref, own_ref, msg_ref):
    own_ref[...] = jnp.zeros_like(own_ref)
    for kl in range(start_ref.shape[0]):
        for j in range(ROWS // 2):
            row = start_ref[pl.ds(kl, 1), pl.ds(j * LANES, LANES)]
            for v in range(2):
                at = pl.ds(kl // 2 * ROWS + 2 * j + v, 1)
                own_ref[at, :] = own_ref[at, :] + lane_half(row, v, kl % 2)
    own = own_ref[...]
    square = own * own
    block = with_sums(own, [jnp.sum(square), jnp.sum(gap_ref[...] * square)])
    msg_ref[...] = jnp.broadcast_to(block.astype(BF)[None], msg_ref.shape)


def cut_kernel(cond_ref, after_ref, *refs):
    outs, sems = refs[:-1], refs[-1]
    k_dev, n_cond, npt = cond_ref.shape
    own = outs[0].shape[1]
    nu = npt // len(outs)
    copies = []
    for j, out in enumerate(outs):
        at = jnp.bitwise_xor(lax.axis_index("ka"), j) * nu + lax.axis_index("band") * own
        for kl in range(k_dev):
            copies.append(
                pltpu.make_async_copy(
                    cond_ref.at[kl, :, pl.ds(pl.multiple_of(at, LANES), own)],
                    out.at[pl.ds(kl * n_cond, n_cond), :],
                    sems.at[len(copies)],
                )
            )
    start_all(copies)
    wait_all(copies)


def turn_kernel(tile, scr_ref, out_ref, scrs, turned, in_sems, out_sems):
    nu = scr_ref.shape[1]
    ins, outs = [], []
    for j in range(nu // tile):
        at = pl.ds(j * tile, tile)
        ins.append(pltpu.make_async_copy(scr_ref.at[:, at], scrs.at[:, at], in_sems.at[j]))
        outs.append(pltpu.make_async_copy(turned.at[at, :], out_ref.at[at, :], out_sems.at[j]))
    start_all(ins)
    for j in range(nu // tile):
        ins[j].wait()
        turned[j * tile : (j + 1) * tile, :] = scrs[:, j * tile : (j + 1) * tile].T
        outs[j].start()
    wait_all(outs)


def order_kernel(counts, *refs):
    n_val = sum(counts)
    val_refs, refs = split_refs(refs[:n_val], counts), refs[n_val:]
    rows_out, turned_out, own_out, vals, ordered, turned, val_sems, out_sems = refs
    own = own_out.shape[1]
    nu = ordered.shape[1]
    copies = block_copies(val_refs, nu, vals, val_sems)
    start_all(copies)
    wait_all(copies)
    group = vals.shape[0] * 2 * ROWS
    column = pl.multiple_of(lax.axis_index("band") * own, LANES)
    outs = []
    for kp in range(ordered.shape[0] // group):
        at = slice(kp * group, (kp + 1) * group)
        ordered[at, :] = pair_rows(vals, kp)
        turned[:, at] = ordered[at, :].T
        at = pl.ds(kp * group, group)
        outs += [
            pltpu.make_async_copy(ordered.at[at, :], rows_out.at[at, :], out_sems.at[0, kp]),
            pltpu.make_async_copy(turned.at[:, at], turned_out.at[:, at], out_sems.at[1, kp]),
            pltpu.make_async_copy(
                ordered.at[at, pl.ds(column, own)], own_out.at[at, :], out_sems.at[2, kp]
            ),
        ]
        start_all(outs[-3:])
    wait_all(outs)


def density_kernel(cfg, *refs):
    n_ka, n_band, k_dev = cfg
    k_points = n_ka * k_dev
    msgs_ref, vown_ref, cond_refs, refs = refs[0], refs[1], refs[2 : 2 + n_ka], refs[2 + n_ka :]
    qx_ref, rho_ref, xs, conds, cond_sems = refs
    own = vown_ref.shape[1]
    copies = block_copies([[ref] for ref in cond_refs], own, conds, cond_sems)
    start_all(copies)
    xs[...] = jnp.zeros_like(xs)
    for d in range(n_band):
        for k in range(k_points):
            j, kl = divmod(k, k_dev)
            tile = msgs_ref[device_at(n_band, j, d), :, :].astype(F32)
            tile = tile[kl // 2 * ROWS : (kl // 2 + 1) * ROWS, :]
            base = k // 2 % 2 * LANES
            at = pl.ds(base + d * 2 * ROWS + k % 2 * ROWS, ROWS)
            xs[k // 4, at, pl.ds(base, LANES)] = lane_half(tile, kl % 2, k % 2)
    qx_ref[...] = xs[...].astype(BF)
    wait_all(copies)
    cond_rows = conds[...].reshape(-1, own)
    rho = jnp.zeros((1, own), F32)
    quad = 2 * LANES
    for kq in range(k_points // 4):
        at = slice(kq * quad, (kq + 1) * quad)
        mixed = dot_tn(qx_ref[kq], vown_ref[at, :])
        rho = rho + jnp.sum(mixed * cond_rows[at, :].astype(F32), axis=0, keepdims=True)
    for r in range(own // LANES):
        part = rho[:, r * LANES : (r + 1) * LANES]
        rho_ref[:, r, :] = jnp.broadcast_to(part, (rho_ref.shape[0], LANES))


def direct_kernel(n_ka, tile, scale, *refs):
    qx_ref, cond_ref, scr_ref, turned_ref, rows_ref, di_ref = refs[:6]
    qx, conds, scrs, turned, vals, mixed, kern, folded, qx_sem, cond_sems, row_sem, chunk_sems = refs[6:]
    nu, mu = scr_ref.shape
    quad = 2 * LANES
    part = cond_ref.shape[0] // n_ka
    qx_copy = pltpu.make_async_copy(qx_ref, qx, qx_sem.at[0])
    cond_copies = [
        pltpu.make_async_copy(
            cond_ref.at[pl.ds(jnp.bitwise_xor(lax.axis_index("ka"), j) * part, part), :],
            conds.at[pl.ds(j * part, part), :],
            cond_sems.at[j],
        )
        for j in range(n_ka)
    ]
    turned_copies, scr_copies = [], []
    for i in range(nu // tile):
        at = pl.ds(i * tile, tile)
        turned_copies.append(
            pltpu.make_async_copy(turned_ref.at[at, :], turned.at[at, :], chunk_sems.at[0, i])
        )
        scr_copies.append(
            pltpu.make_async_copy(scr_ref.at[at, :], scrs.at[at, :], chunk_sems.at[1, i])
        )
    row_copy = pltpu.make_async_copy(rows_ref, vals, row_sem.at[0])
    start_all([qx_copy, turned_copies[0]] + cond_copies + [scr_copies[0]])
    for i in range(1, nu // tile):
        start_all([turned_copies[i], scr_copies[i]])
    row_copy.start()
    qx_copy.wait()
    for i in range(nu // tile):
        at = slice(i * tile, (i + 1) * tile)
        turned_copies[i].wait()
        for kq in range(qx.shape[0]):
            cols = slice(kq * quad, (kq + 1) * quad)
            mixed[at, cols] = jnp.dot(
                turned[at, cols], qx[kq], preferred_element_type=F32
            ).astype(BF)
        if i == 0:
            wait_all(cond_copies)
        scr_copies[i].wait()
        amp = jnp.dot(mixed[at, :], conds[...], preferred_element_type=F32)
        kern[at, :] = (scrs[at, :].astype(F32) * amp * scale).astype(BF)
    row_copy.wait()
    for i in range(mu // quad):
        at = slice(i * quad, (i + 1) * quad)
        folded[:, at] = jnp.dot(vals[...], kern[:, at], preferred_element_type=F32).astype(BF)
    for kp in range(di_ref.shape[0]):
        at = slice(kp * LANES, (kp + 1) * LANES)
        di_ref[kp] = dot_nt(folded[at, :], conds[at, :])


def exchange_kernel(cfg, chunk, scale, *refs):
    n_ka, n_band, k_dev = cfg
    k_points = n_ka * k_dev
    rho_ref, di_ref, coul_ref, vown_ref = refs[:4]
    cond_refs, refs = refs[4 : 4 + n_ka], refs[4 + n_ka :]
    msg_ref, rhos, di, coul, conds, vown, part, msg, coul_sems, cond_sems, sems = refs
    own, npt = coul_ref.shape
    coul_copies = [
        pltpu.make_async_copy(
            coul_ref.at[:, pl.ds(i * chunk, chunk)], coul.at[:, pl.ds(i * chunk, chunk)], coul_sems.at[i]
        )
        for i in range(npt // chunk)
    ]
    rho_copy = pltpu.make_async_copy(rho_ref, rhos, sems.at[0])
    copies = block_copies([[ref] for ref in cond_refs], own, conds, cond_sems)
    copies.append(pltpu.make_async_copy(di_ref, di, sems.at[1]))
    copies.append(pltpu.make_async_copy(vown_ref, vown, sems.at[2]))
    start_all([rho_copy] + coul_copies + copies)
    rho_copy.wait()
    acc = jnp.zeros((own, LANES), F32)
    per_dev = own // LANES
    for i in range(npt // chunk):
        coul_copies[i].wait()
        for j in range(i * chunk // LANES, (i + 1) * chunk // LANES):
            rho = rhos[j // per_dev, pl.ds(j % per_dev, 1), :].astype(BF).astype(F32)
            acc = acc + coul[:, j * LANES : (j + 1) * LANES].astype(F32) * rho
    potential = scale * jnp.sum(acc.T, axis=0, keepdims=True)
    wait_all(copies)
    cond_rows = conds[...].reshape(-1, own)
    for kp in range(k_points // 2):
        at = slice(kp * LANES, (kp + 1) * LANES)
        weighted = (vown[at, :].astype(F32) * potential).astype(BF)
        part[kp] = 2.0 * dot_nt(weighted, cond_rows[at, :]) - di[kp]
    for d in range(n_band):
        for j in range(n_ka):
            for g in range((k_dev + 1) // 2):
                tile = None
                for kl in range(2 * g, min(2 * g + 2, k_dev)):
                    k = j * k_dev + kl
                    piece = part[k // 2, pl.ds(d * 2 * ROWS + k % 2 * ROWS, ROWS), :]
                    piece = lane_half(piece, k % 2, kl % 2)
                    tile = piece if tile is None else tile + piece
                to_ka = jnp.bitwise_xor(lax.axis_index("ka"), j)
                to_band = jnp.bitwise_xor(lax.axis_index("band"), d)
                msg[to_band, to_ka, pl.ds(g * ROWS, ROWS), :] = tile
    msg_ref[...] = msg[...].astype(BF)


def plane_sum_kernel(parts_ref, out_ref):
    out_ref[...] = jnp.sum(parts_ref[...].astype(F32), axis=0)


def received(recv_ref):
    return jnp.sum(recv_ref[...], axis=0)


def shifted(count_all, shift, square, cross_sum, square_sum):
    alpha = shift * square + cross_sum / count_all
    d = alpha - shift
    mean_sq = (square_sum - 2.0 * d * cross_sum) / count_all + d * d * square
    mean_sq = jnp.maximum(mean_sq, 0.0)
    return alpha, d, mean_sq


def first_owner_kernel(count_all, recv_ref, msgs_ref, gap_ref, own_ref, state_ref, coef_ref, msg_ref):
    start_sq, gap_sq = read_sums(msgs_ref, 2)
    norm = start_sq / count_all
    inv = 1.0 / jnp.sqrt(norm + 1e-06)
    square = norm / (norm + 1e-06)
    shift = gap_sq / jnp.maximum(start_sq, 1e-30)
    cur = own_ref[...] * inv
    inter = received(recv_ref) * inv
    gap = gap_ref[...]
    resid = (gap - shift) * cur + inter
    state_ref[0] = cur
    state_ref[1] = resid
    state_ref[2] = inter
    coef_ref[0] = shift
    coef_ref[1] = square
    coef_ref[2] = gap_sq * inv * inv
    sums = [
        jnp.sum(cur * resid),
        jnp.sum(resid * resid),
        jnp.sum(gap * resid * resid),
        jnp.sum(gap * resid * cur),
    ]
    msg_ref[...] = jnp.broadcast_to(with_sums(resid, sums).astype(BF)[None], msg_ref.shape)


def second_owner_kernel(count_all, recv_ref, msgs_ref, gap_ref, state_ref, coef_ref, out_ref, coef_out, msg_ref):
    cross, total, gap_rr, gap_rq = read_sums(msgs_ref, 4)
    alpha, d, mean_sq = shifted(count_all, coef_ref[0], coef_ref[1], cross, total)
    beta = jnp.sqrt(mean_sq + 1e-06)
    square = mean_sq / (mean_sq + 1e-06)
    gap_qq = gap_rr - 2.0 * d * gap_rq + d * d * coef_ref[2]
    shift = gap_qq / (mean_sq + 1e-06) / count_all
    prev = state_ref[0]
    cur = (state_ref[1] - d * prev) / beta
    inter = (received(recv_ref) - d * state_ref[2]) / beta
    resid = (gap_ref[...] - shift) * cur + inter - beta * prev
    out_ref[0] = cur
    out_ref[1] = resid
    coef_out[0] = alpha
    coef_out[1] = beta
    coef_out[2] = shift
    coef_out[3] = square
    dims = msg_ref.shape[:1] + msg_ref.shape[2:]
    msg_ref[:, 0, :] = jnp.full(dims, jnp.sum(cur * resid), F32)
    msg_ref[:, 1, :] = jnp.full(dims, jnp.sum(resid * resid), F32)


def finish_kernel(count_all, msgs_ref, state_ref, coef_ref, out_ref, coeffs_ref):
    sums = jnp.sum(msgs_ref[...], axis=0)
    alpha, d, mean_sq = shifted(count_all, coef_ref[2], coef_ref[3], sums[0, 0], sums[1, 0])
    beta = jnp.sqrt(mean_sq + 1e-06)
    own = (state_ref[1] - d * state_ref[0]) / beta
    coeffs_ref[0] = coef_ref[0]
    coeffs_ref[1] = alpha
    coeffs_ref[2] = coef_ref[1]
    coeffs_ref[3] = beta
    for kl in range(out_ref.shape[0]):
        tile = own[kl // 2 * ROWS : (kl // 2 + 1) * ROWS, :]
        other = pltpu.roll(tile, HALF, axis=1)
        left, right = (tile, other) if kl % 2 == 0 else (other, tile)
        low = lax.broadcasted_iota(jnp.int32, (1, LANES), 1) < HALF
        for j in range(ROWS // 2):
            row = jnp.where(low, left[2 * j : 2 * j + 1], right[2 * j + 1 : 2 * j + 2])
            out_ref[pl.ds(kl, 1), pl.ds(j * LANES, LANES)] = row


def shape_of(dims, kind=F32):
    return jax.ShapeDtypeStruct(dims, kind)


def call(kernel, name, out_shape, in_specs, out_specs, scratch=(), mib=58, flops=0, moved=0):
    return pl.pallas_call(
        kernel,
        out_shape=out_shape,
        in_specs=in_specs,
        out_specs=out_specs,
        scratch_shapes=list(scratch),
        compiler_params=pltpu.CompilerParams(vmem_limit_bytes=mib * MIB),
        cost_estimate=pl.CostEstimate(flops=flops, bytes_accessed=moved, transcendentals=0),
        name=name,
    )


def dma(*dims):
    return pltpu.SemaphoreType.DMA(dims)


def swap(block, axis, d):
    return lax.ppermute(block, axis, [(i, i ^ d) for i in range(lax.axis_size(axis))])


def plane_pieces(own_piece):
    def move(block, d):
        return swap(block, "band", d)

    half = own_piece.shape[0] // 2
    by_x, by_y = move(own_piece, 2), move(own_piece, 4)
    diag = [move(by_x[:half], 4), move(by_y[half:], 2)]
    pieces = [[own_piece], [move(own_piece, 1)], [by_x], [move(by_x, 1)], [by_y], [move(by_y, 1)]]
    return pieces + [diag, [move(part, 1) for part in diag]]


def kernel_path(start_vec, val_energy, cond_energy, val_orb, cond_orb, coulomb, screened):
    n_ka = lax.axis_size("ka")
    n_band = lax.axis_size("band")
    devices = n_ka * n_band
    ka, band = lax.axis_index("ka"), lax.axis_index("band")
    k_dev = start_vec.shape[0]
    nv_blk = val_orb.shape[1]
    n_cond = cond_orb.shape[1]
    npt_all = cond_orb.shape[2]
    k_points = k_dev * n_ka
    pairs = k_points // 2
    mu_blk, nu_blk = screened.shape
    own = coulomb.shape[0]
    count_all = k_points * nv_blk * n_band * n_cond
    scale = 1.0 / (npt_all * math.sqrt(count_all))
    piece_rows = k_points * nv_blk

    cond_local = lax.dynamic_slice_in_dim(cond_orb, band * mu_blk, mu_blk, 2)
    cond_pts = lax.all_gather(
        cond_local.reshape(k_dev * n_cond, mu_blk), "ka", axis=0, tiled=True
    )

    def val_to(j):
        part = lax.dynamic_slice_in_dim(val_orb, jnp.bitwise_xor(ka, j) * nu_blk, nu_blk, 2)
        return part.reshape(k_dev * nv_blk, nu_blk)

    val_cut = jnp.concatenate(
        [val_to(0)] + [swap(val_to(j), "ka", j) for j in range(1, n_ka)], axis=0
    )
    gap = (cond_energy[:, None, :] - val_energy[:, :, None]).reshape(k_dev, nv_blk * n_cond)
    gap = pack_vector(gap, k_dev)

    block = gap.shape
    msg_shape = shape_of((devices,) + block, BF)
    start_own, message = call(
        pack_kernel, "pack", (shape_of(block), msg_shape), [VMEM] * 2, (VMEM, VMEM), mib=8
    )(start_vec, gap)
    msgs = exchange_all(message)
    chunk, tile = 1024, 1024
    rows_all, conds_all = k_points * nv_blk * n_band, k_points * n_cond
    scr_turned = call(
        functools.partial(turn_kernel, tile // 2),
        "turn",
        shape_of((nu_blk, mu_blk), BF),
        [ANY],
        ANY,
        [pltpu.VMEM((mu_blk, nu_blk), BF), pltpu.VMEM((nu_blk, mu_blk), BF)]
        + [dma(2 * nu_blk // tile)] * 2,
        moved=8 * MIB,
    )(screened)
    val_cut, msgs, scr_turned = lax.optimization_barrier((val_cut, msgs, scr_turned))
    pieces = plane_pieces(val_cut)
    counts = tuple(len(piece) for piece in pieces)
    flat = [ref for piece in pieces for ref in piece]
    n_copies = len(flat)
    own_rows = k_dev * n_cond
    cuts = call(
        cut_kernel,
        "cut",
        (shape_of((own_rows, own), BF),) * n_ka,
        [ANY, ANY],
        (ANY,) * n_ka,
        [dma(n_ka * k_dev)],
        mib=8,
    )(cond_orb, val_cut)
    cond_own = [cuts[0]] + [swap(cuts[j], "ka", j) for j in range(1, n_ka)]

    val_rows, val_turned, val_own = call(
        functools.partial(order_kernel, counts),
        "order",
        (
            shape_of((rows_all, nu_blk), BF),
            shape_of((nu_blk, rows_all), BF),
            shape_of((rows_all, own), BF),
        ),
        [ANY] * n_copies,
        (ANY, ANY, ANY),
        [
            pltpu.VMEM((n_band, piece_rows, nu_blk), BF),
            pltpu.VMEM((rows_all, nu_blk), BF),
            pltpu.VMEM((nu_blk, rows_all), BF),
            dma(n_copies),
            dma(3, pairs),
        ],
        moved=9 * MIB,
    )(*flat)

    cfg = (n_ka, n_band, k_dev)
    quads = k_points // 4
    state, coef = None, None
    for step in range(STEPS):
        first = step == 0
        qx, rho = call(
            functools.partial(density_kernel, cfg),
            "density",
            (
                shape_of((quads, 2 * LANES, 2 * LANES), BF),
                shape_of((devices, own // LANES, LANES)),
            ),
            [VMEM] * 2 + [ANY] * n_ka,
            (VMEM, VMEM),
            [
                pltpu.VMEM((quads, 2 * LANES, 2 * LANES), F32),
                pltpu.VMEM((n_ka, own_rows, own), BF),
                dma(n_ka),
            ],
            mib=8,
        )(msgs, val_own, *cond_own)
        density = exchange_all(rho)
        direct = call(
            functools.partial(direct_kernel, n_ka, tile, scale),
            "direct",
            shape_of((pairs, LANES, LANES)),
            [ANY] * 5,
            VMEM,
            [
                pltpu.VMEM((quads, 2 * LANES, 2 * LANES), BF),
                pltpu.VMEM((conds_all, mu_blk), BF),
                pltpu.VMEM((nu_blk, mu_blk), BF),
                pltpu.VMEM((nu_blk, rows_all), BF),
                pltpu.VMEM((rows_all, nu_blk), BF),
                pltpu.VMEM((nu_blk, conds_all), BF),
                pltpu.VMEM((nu_blk, mu_blk), BF),
                pltpu.VMEM((rows_all, mu_blk), BF),
                dma(1),
                dma(n_ka),
                dma(1),
                dma(2, nu_blk // tile),
            ],
            flops=4 * mu_blk * nu_blk * conds_all,
            moved=12 * MIB,
        )(qx, cond_pts, scr_turned, val_turned, val_rows)
        parts = call(
            functools.partial(exchange_kernel, cfg, chunk, scale),
            "exchange",
            shape_of((n_band, n_ka) + block, BF),
            [ANY] * (4 + n_ka),
            VMEM,
            [
                pltpu.VMEM((devices, own // LANES, LANES), F32),
                pltpu.VMEM((pairs, LANES, LANES), F32),
                pltpu.VMEM((own, npt_all), BF),
                pltpu.VMEM((n_ka, own_rows, own), BF),
                pltpu.VMEM((rows_all, own), BF),
                pltpu.VMEM((pairs, LANES, LANES), F32),
                pltpu.VMEM((n_band, n_ka) + block, F32),
                dma(npt_all // chunk),
                dma(n_ka),
                dma(3),
            ],
        )(density, direct, coulomb, val_own, *cond_own)
        parts = lax.all_to_all(parts, "band", split_axis=0, concat_axis=0, tiled=True)
        plane = call(
            plane_sum_kernel, "plane_sum", shape_of((n_ka,) + block), [VMEM], VMEM, mib=8
        )(parts)
        recv = lax.all_to_all(plane, "ka", split_axis=0, concat_axis=0, tiled=True)
        if first:
            state, coef, message = call(
                functools.partial(first_owner_kernel, count_all),
                "first_owner",
                (shape_of((3,) + block), shape_of((3,)), msg_shape),
                [VMEM] * 4,
                (VMEM, SMEM, VMEM),
                mib=8,
            )(recv, msgs, gap, start_own)
        else:
            state, coef, message = call(
                functools.partial(second_owner_kernel, count_all),
                "second_owner",
                (shape_of((2,) + block), shape_of((4,)), shape_of((devices, 2, LANES))),
                [VMEM] * 4 + [SMEM],
                (VMEM, SMEM, VMEM),
                mib=8,
            )(recv, msgs, gap, state, coef)
        msgs = exchange_all(message)
    return call(
        functools.partial(finish_kernel, count_all),
        "finish",
        (shape_of(start_vec.shape), shape_of((2 * STEPS,))),
        [VMEM] * 2 + [SMEM],
        (VMEM, SMEM),
        mib=8,
    )(msgs, state, coef)


def array_path(start_vec, val_energy, cond_energy, val_orb, cond_orb, coulomb, screened):
    n_ka = lax.axis_size("ka")
    n_band = lax.axis_size("band")
    devices = n_ka * n_band
    ka, band = lax.axis_index("ka"), lax.axis_index("band")
    me = ka * n_band + band
    k_dev, pair_blk = start_vec.shape
    nv_blk = val_orb.shape[1]
    n_cond = cond_orb.shape[1]
    n_val = nv_blk * n_band
    npt_all = cond_orb.shape[2]
    k_points = k_dev * n_ka
    mu_blk, nu_blk = screened.shape
    own_pts = coulomb.shape[0]
    count_all = k_points * n_val * n_cond
    kernel_scale = 1.0 / (npt_all * math.sqrt(count_all))

    start_all = gather_all(start_vec, devices)
    val_cut = lax.all_to_all(
        val_orb.reshape(k_dev, nv_blk, n_ka, nu_blk).transpose(2, 0, 1, 3),
        "ka", split_axis=0, concat_axis=0, tiled=True,
    ).reshape(k_points, nv_blk, nu_blk)
    val_pts = lax.all_gather(val_cut, "band", axis=1, tiled=True)
    cond_local = lax.dynamic_slice_in_dim(cond_orb, band * mu_blk, mu_blk, 2)
    cond_pts = lax.all_gather(cond_local, "ka", axis=0, tiled=True)
    cond_rows = cond_orb.reshape(k_dev, n_cond, n_ka, n_band, own_pts)
    cond_rows = lax.dynamic_index_in_dim(cond_rows, band, 3, keepdims=False)
    cond_own = lax.all_to_all(
        cond_rows.transpose(2, 0, 1, 3), "ka", split_axis=0, concat_axis=0, tiled=True
    ).reshape(k_points, n_cond, own_pts)
    val_own = lax.dynamic_slice_in_dim(val_pts, band * own_pts, own_pts, 2)

    energy_gap = (cond_energy[:, None, :] - val_energy[:, :, None]).reshape(k_dev, pair_blk)
    start_sq = jnp.sum(start_all * start_all)
    current = start_all / jnp.sqrt(start_sq / count_all + 1e-06)
    previous = jnp.zeros_like(current)
    beta_val = jnp.float32(0.0)
    alphas = []
    betas = []
    for turn_index in range(STEPS):
        full_vec = (
            current.astype(BF)
            .reshape(n_ka, n_band, k_dev, nv_blk, n_cond)
            .transpose(0, 2, 1, 3, 4)
            .reshape(k_points, n_val, n_cond)
        )
        mixed_f = jnp.einsum("kvc,kvn->kcn", full_vec, val_pts, preferred_element_type=F32)
        mixed_own = lax.dynamic_slice_in_dim(mixed_f, band * own_pts, own_pts, 2)
        density_own = jnp.sum(mixed_own * cond_own.astype(F32), axis=(0, 1))
        density = gather_all(density_own.astype(BF), devices).reshape(npt_all)
        mixed_val = mixed_f.astype(BF)
        amp = jnp.einsum("kcm,kcn->mn", cond_pts, mixed_val, preferred_element_type=F32)
        kern = (screened.astype(F32) * amp * kernel_scale).astype(BF)
        folded = jnp.einsum("mn,kvn->kvm", kern, val_pts, preferred_element_type=F32).astype(BF)
        direct_part = jnp.einsum("kcm,kvm->kvc", cond_pts, folded, preferred_element_type=F32)
        potential = kernel_scale * jnp.dot(coulomb, density, preferred_element_type=F32)
        weighted = (val_own.astype(F32) * potential).astype(BF)
        exchange = jnp.einsum("kvp,kcp->kvc", weighted, cond_own, preferred_element_type=F32)
        part = 2.0 * exchange - direct_part
        arranged = (
            part.reshape(n_ka, k_dev, n_band, nv_blk, n_cond)
            .transpose(0, 2, 1, 3, 4)
            .reshape(devices, k_dev, pair_blk)
        )
        inter_own = jnp.sum(exchange_all(arranged), axis=0)
        current_own = lax.dynamic_index_in_dim(current, me, 0, keepdims=False)
        resid_vec = gather_all(energy_gap * current_own + inter_own, devices)
        resid_vec = resid_vec - beta_val * previous
        alpha_val = jnp.sum(current * resid_vec) / count_all
        resid_vec = resid_vec - alpha_val * current
        beta_val = jnp.sqrt(jnp.sum(resid_vec * resid_vec) / count_all + 1e-06)
        previous = current
        current = resid_vec / beta_val
        alphas.append(alpha_val)
        betas.append(beta_val)
    coeffs = jnp.stack(alphas + betas)
    return (lax.dynamic_index_in_dim(current, me, 0, keepdims=False), coeffs)


def per_device(*args):
    start_vec, _, _, val_orb, cond_orb, coulomb, screened = args
    n_ka, n_band = lax.axis_size("ka"), lax.axis_size("band")
    fits = (
        n_band == 8
        and n_ka & (n_ka - 1) == 0
        and start_vec.shape[0] % 2 == 1
        and val_orb.shape[1] == ROWS
        and cond_orb.shape[1] == HALF
        and start_vec.shape[0] * n_ka % 4 == 0
        and coulomb.shape[0] % LANES == 0
        and coulomb.shape[1] % 1024 == 0
        and screened.shape[0] % 256 == 0
        and screened.shape[1] % 1024 == 0
        and screened.shape[0] * screened.shape[1] <= 2 * MIB
    )
    return (kernel_path if fits else array_path)(*args)


def solution(mesh):
    in_specs = (
        P("ka", "band"),
        P("ka", "band"),
        P("ka", None),
        P("ka", "band", None),
        P("ka", None, None),
        P(("ka", "band"), None),
        P("band", "ka"),
    )
    out_specs = (P("ka", "band"), P())
    return jax.shard_map(
        per_device, mesh=mesh, in_specs=in_specs, out_specs=out_specs, check_vma=False
    )
```

```python
import functools
import math

import jax
import jax.numpy as jnp
from jax import lax
from jax.experimental import pallas as pl
from jax.experimental.pallas import tpu as pltpu
from jax.sharding import PartitionSpec as P

STEPS = 2
AXES = ("ka", "band")
BF, F32 = jnp.bfloat16, jnp.float32
LANES = 128
HALF = 64
ROWS = 8
MIB = 1 << 20

VMEM = pl.BlockSpec(memory_space=pltpu.VMEM)
SMEM = pl.BlockSpec(memory_space=pltpu.SMEM)
ANY = pl.BlockSpec(memory_space=pl.ANY)


def gather_all(block, devices):
    wide = jnp.broadcast_to(block[None], (devices,) + block.shape)
    return exchange_all(wide)


def exchange_all(parts):
    return lax.all_to_all(parts, AXES, split_axis=0, concat_axis=0, tiled=True)


def dot_nt(lhs, rhs):
    return lax.dot_general(lhs, rhs, (((1,), (1,)), ((), ())), preferred_element_type=F32)


def dot_tn(lhs, rhs):
    return lax.dot_general(lhs, rhs, (((0,), (0,)), ((), ())), preferred_element_type=F32)


def pack_vector(block, k_dev):
    groups = (k_dev + 1) // 2
    block = jnp.pad(block, ((0, 2 * groups - k_dev), (0, 0)))
    block = block.reshape(groups, 2, ROWS, HALF).transpose(0, 2, 1, 3)
    return block.reshape(groups * ROWS, LANES)


def lane_half(tile, have, want):
    if have != want:
        tile = pltpu.roll(tile, HALF, axis=1)
    lane = lax.broadcasted_iota(jnp.int32, tile.shape, 1)
    keep = lane < HALF if want == 0 else lane >= HALF
    return jnp.where(keep, tile, 0.0)


def with_sums(block, sums):
    row = lax.broadcasted_iota(jnp.int32, block.shape, 0)
    lane = lax.broadcasted_iota(jnp.int32, block.shape, 1)
    free = row == block.shape[0] - ROWS
    for i, total in enumerate(sums):
        rest = jnp.full(block.shape, total, F32)
        for part in range(3):
            piece = rest.astype(BF).astype(F32)
            block = jnp.where(free & (lane == HALF + 3 * i + part), piece, block)
            rest = rest - piece
    return block


def read_sums(msgs_ref, count):
    rows = msgs_ref.shape[1]
    tile = jnp.sum(msgs_ref[...].astype(F32), axis=0)[rows - ROWS :, :]
    row = lax.broadcasted_iota(jnp.int32, tile.shape, 0)
    lane = lax.broadcasted_iota(jnp.int32, tile.shape, 1)
    out = []
    for i in range(count):
        mine = (row == 0) & (lane >= HALF + 3 * i) & (lane < HALF + 3 * i + 3)
        out.append(jnp.sum(jnp.where(mine, tile, 0.0)))
    return out


def block_copies(groups, width, dest, sems, column=0):
    copies = []
    for d, refs in enumerate(groups):
        row = 0
        for ref in refs:
            copies.append(
                pltpu.make_async_copy(
                    ref.at[:, pl.ds(column, width)],
                    dest.at[d, pl.ds(row, ref.shape[0]), :],
                    sems.at[len(copies)],
                )
            )
            row += ref.shape[0]
    return copies


def split_refs(refs, counts):
    out, at = [], 0
    for count in counts:
        out.append(refs[at : at + count])
        at += count
    return out


def start_all(copies):
    for copy in copies:
        copy.start()


def wait_all(copies):
    for copy in copies:
        copy.wait()


def device_at(n_band, j, d):
    ka = jnp.bitwise_xor(lax.axis_index("ka"), j)
    return ka * n_band + jnp.bitwise_xor(lax.axis_index("band"), d)


def pair_rows(ref, kp):
    part = ref[:, kp * 2 * ROWS : (kp + 1) * 2 * ROWS, :]
    return part.reshape(part.shape[0] * 2 * ROWS, part.shape[2])


def pack_kernel(start_ref, gap_ref, own_ref, msg_ref):
    own_ref[...] = jnp.zeros_like(own_ref)
    for kl in range(start_ref.shape[0]):
        for j in range(ROWS // 2):
            row = start_ref[pl.ds(kl, 1), pl.ds(j * LANES, LANES)]
            for v in range(2):
                at = pl.ds(kl // 2 * ROWS + 2 * j + v, 1)
                own_ref[at, :] = own_ref[at, :] + lane_half(row, v, kl % 2)
    own = own_ref[...]
    square = own * own
    block = with_sums(own, [jnp.sum(square), jnp.sum(gap_ref[...] * square)])
    msg_ref[...] = jnp.broadcast_to(block.astype(BF)[None], msg_ref.shape)


def cut_kernel(cond_ref, *refs):
    outs, sems = refs[:-1], refs[-1]
    k_dev, n_cond, npt = cond_ref.shape
    own = outs[0].shape[1]
    nu = npt // len(outs)
    copies = []
    for j, out in enumerate(outs):
        at = jnp.bitwise_xor(lax.axis_index("ka"), j) * nu + lax.axis_index("band") * own
        for kl in range(k_dev):
            copies.append(
                pltpu.make_async_copy(
                    cond_ref.at[kl, :, pl.ds(pl.multiple_of(at, LANES), own)],
                    out.at[pl.ds(kl * n_cond, n_cond), :],
                    sems.at[len(copies)],
                )
            )
    start_all(copies)
    wait_all(copies)


def turn_kernel(tile, scr_ref, out_ref, scrs, turned, in_sems, out_sems):
    nu = scr_ref.shape[1]
    ins, outs = [], []
    for j in range(nu // tile):
        at = pl.ds(j * tile, tile)
        ins.append(pltpu.make_async_copy(scr_ref.at[:, at], scrs.at[:, at], in_sems.at[j]))
        outs.append(pltpu.make_async_copy(turned.at[at, :], out_ref.at[at, :], out_sems.at[j]))
    start_all(ins)
    for j in range(nu // tile):
        ins[j].wait()
        turned[j * tile : (j + 1) * tile, :] = scrs[:, j * tile : (j + 1) * tile].T
        outs[j].start()
    wait_all(outs)


def order_kernel(counts, *refs):
    n_val = sum(counts)
    val_refs, refs = split_refs(refs[:n_val], counts), refs[n_val:]
    rows_out, turned_out, own_out, vals, ordered, turned, val_sems, out_sems = refs
    own = own_out.shape[1]
    nu = ordered.shape[1]
    copies = block_copies(val_refs, nu, vals, val_sems)
    start_all(copies)
    wait_all(copies)
    group = vals.shape[0] * 2 * ROWS
    column = pl.multiple_of(lax.axis_index("band") * own, LANES)
    outs = []
    for kp in range(ordered.shape[0] // group):
        at = slice(kp * group, (kp + 1) * group)
        ordered[at, :] = pair_rows(vals, kp)
        turned[:, at] = ordered[at, :].T
        at = pl.ds(kp * group, group)
        outs += [
            pltpu.make_async_copy(ordered.at[at, :], rows_out.at[at, :], out_sems.at[0, kp]),
            pltpu.make_async_copy(turned.at[:, at], turned_out.at[:, at], out_sems.at[1, kp]),
            pltpu.make_async_copy(
                ordered.at[at, pl.ds(column, own)], own_out.at[at, :], out_sems.at[2, kp]
            ),
        ]
        start_all(outs[-3:])
    wait_all(outs)


def density_kernel(cfg, *refs):
    n_ka, n_band, k_dev = cfg
    k_points = n_ka * k_dev
    msgs_ref, vown_ref, cond_refs, refs = refs[0], refs[1], refs[2 : 2 + n_ka], refs[2 + n_ka :]
    qx_ref, rho_ref, xs, conds, cond_sems = refs
    own = vown_ref.shape[1]
    copies = block_copies([[ref] for ref in cond_refs], own, conds, cond_sems)
    start_all(copies)
    xs[...] = jnp.zeros_like(xs)
    for d in range(n_band):
        for k in range(k_points):
            j, kl = divmod(k, k_dev)
            tile = msgs_ref[device_at(n_band, j, d), :, :].astype(F32)
            tile = tile[kl // 2 * ROWS : (kl // 2 + 1) * ROWS, :]
            base = k // 2 % 2 * LANES
            at = pl.ds(base + d * 2 * ROWS + k % 2 * ROWS, ROWS)
            xs[k // 4, at, pl.ds(base, LANES)] = lane_half(tile, kl % 2, k % 2)
    qx_ref[...] = xs[...].astype(BF)
    wait_all(copies)
    cond_rows = conds[...].reshape(-1, own)
    rho = jnp.zeros((1, own), F32)
    quad = 2 * LANES
    for kq in range(k_points // 4):
        at = slice(kq * quad, (kq + 1) * quad)
        mixed = dot_tn(qx_ref[kq], vown_ref[at, :])
        rho = rho + jnp.sum(mixed * cond_rows[at, :].astype(F32), axis=0, keepdims=True)
    for r in range(own // LANES):
        part = rho[:, r * LANES : (r + 1) * LANES]
        rho_ref[:, r, :] = jnp.broadcast_to(part, (rho_ref.shape[0], LANES))


def direct_kernel(n_ka, halves, mixed_in, mixed_out, tile, scale, *refs):
    n_half = len(halves)
    lead_ref, scr_ref, rows_ref, refs = refs[0], refs[1], refs[2], refs[3:]
    if not mixed_in:
        qx_ref, refs = refs[0], refs[1:]
    cond_refs, di_ref, refs = refs[:n_half], refs[n_half], refs[n_half + 1 :]
    if mixed_out:
        mixed_ref, refs = refs[0], refs[1:]
    if not mixed_in:
        qx, turned, refs = refs[0], refs[1], refs[2:]
    conds, scrs, vals, mixed, kern, folded, qx_sem, cond_sems, row_sem, chunk_sems = refs
    nu = lead_ref.shape[0]
    half = cond_refs[0].shape[1]
    mu = half * n_half
    quad = 2 * LANES
    part = cond_refs[0].shape[0] // n_ka
    cond_copies = [
        pltpu.make_async_copy(
            ref.at[pl.ds(jnp.bitwise_xor(lax.axis_index("ka"), j) * part, part), :],
            conds.at[pl.ds(j * part, part), pl.ds(h * half, half)],
            cond_sems.at[h, j],
        )
        for h, ref in enumerate(cond_refs)
        for j in range(n_ka)
    ]
    lead = mixed if mixed_in else turned
    lead_copies, scr_copies = [], []
    for i in range(nu // tile):
        at = pl.ds(i * tile, tile)
        lead_copies.append(
            pltpu.make_async_copy(lead_ref.at[at, :], lead.at[at, :], chunk_sems.at[0, i])
        )
        scr_copies.append(
            pltpu.make_async_copy(
                scr_ref.at[at, pl.ds(halves[0] * half, mu)], scrs.at[at, :], chunk_sems.at[1, i]
            )
        )
    row_copy = pltpu.make_async_copy(rows_ref, vals, row_sem.at[0])
    if not mixed_in:
        qx_copy = pltpu.make_async_copy(qx_ref, qx, qx_sem.at[0])
        qx_copy.start()
    start_all([lead_copies[0]] + cond_copies + [scr_copies[0]])
    for i in range(1, nu // tile):
        start_all([lead_copies[i], scr_copies[i]])
    row_copy.start()
    if not mixed_in:
        qx_copy.wait()
    out_copies = []
    for i in range(nu // tile):
        rows = slice(i * tile, (i + 1) * tile)
        lead_copies[i].wait()
        if not mixed_in:
            for kq in range(qx.shape[0]):
                cols = slice(kq * quad, (kq + 1) * quad)
                mixed[rows, cols] = jnp.dot(
                    turned[rows, cols], qx[kq], preferred_element_type=F32
                ).astype(BF)
        if mixed_out:
            at = pl.ds(i * tile, tile)
            out_copies.append(
                pltpu.make_async_copy(mixed.at[at, :], mixed_ref.at[at, :], chunk_sems.at[2, i])
            )
            out_copies[-1].start()
        if i == 0:
            wait_all(cond_copies)
        scr_copies[i].wait()
        for m in range(mu // quad):
            cols = slice(m * quad, (m + 1) * quad)
            amp = jnp.dot(mixed[rows, :], conds[:, cols], preferred_element_type=F32)
            kern[rows, cols] = (scrs[rows, cols].astype(F32) * amp * scale).astype(BF)
    row_copy.wait()
    for m in range(mu // quad):
        cols = slice(m * quad, (m + 1) * quad)
        folded[:, cols] = jnp.dot(vals[...], kern[:, cols], preferred_element_type=F32).astype(BF)
    for kp in range(di_ref.shape[0]):
        at = slice(kp * LANES, (kp + 1) * LANES)
        di_ref[kp] = dot_nt(folded[at, :], conds[at, :])
    wait_all(out_copies)


def exchange_kernel(cfg, n_di, chunk, scale, *refs):
    n_ka, n_band, k_dev = cfg
    k_points = n_ka * k_dev
    rho_ref, coul_ref, vown_ref, refs = refs[0], refs[1], refs[2], refs[3:]
    di_refs, refs = refs[:n_di], refs[n_di:]
    cond_refs, refs = refs[:n_ka], refs[n_ka:]
    msg_ref, rhos, di, coul, conds, vown, part, msg, coul_sems, cond_sems, sems = refs
    own, npt = coul_ref.shape
    coul_copies = [
        pltpu.make_async_copy(
            coul_ref.at[:, pl.ds(i * chunk, chunk)], coul.at[:, pl.ds(i * chunk, chunk)], coul_sems.at[i]
        )
        for i in range(npt // chunk)
    ]
    rho_copy = pltpu.make_async_copy(rho_ref, rhos, sems.at[0])
    copies = block_copies([[ref] for ref in cond_refs], own, conds, cond_sems)
    copies.append(pltpu.make_async_copy(vown_ref, vown, sems.at[1]))
    for i, ref in enumerate(di_refs):
        copies.append(pltpu.make_async_copy(ref, di.at[i], sems.at[2 + i]))
    start_all([rho_copy] + coul_copies + copies)
    rho_copy.wait()
    acc = jnp.zeros((own, LANES), F32)
    per_dev = own // LANES
    for i in range(npt // chunk):
        coul_copies[i].wait()
        for j in range(i * chunk // LANES, (i + 1) * chunk // LANES):
            rho = rhos[j // per_dev, pl.ds(j % per_dev, 1), :].astype(BF).astype(F32)
            acc = acc + coul[:, j * LANES : (j + 1) * LANES].astype(F32) * rho
    potential = scale * jnp.sum(acc.T, axis=0, keepdims=True)
    wait_all(copies)
    cond_rows = conds[...].reshape(-1, own)
    for kp in range(k_points // 2):
        at = slice(kp * LANES, (kp + 1) * LANES)
        weighted = (vown[at, :].astype(F32) * potential).astype(BF)
        term = 2.0 * dot_nt(weighted, cond_rows[at, :])
        for i in range(n_di):
            term = term - di[i, kp]
        part[kp] = term
    for d in range(n_band):
        for j in range(n_ka):
            for g in range((k_dev + 1) // 2):
                tile = None
                for kl in range(2 * g, min(2 * g + 2, k_dev)):
                    k = j * k_dev + kl
                    piece = part[k // 2, pl.ds(d * 2 * ROWS + k % 2 * ROWS, ROWS), :]
                    piece = lane_half(piece, k % 2, kl % 2)
                    tile = piece if tile is None else tile + piece
                msg[device_at(n_band, j, d), pl.ds(g * ROWS, ROWS), :] = tile
    msg_ref[...] = msg[...].astype(BF)


def received(recv_ref):
    return jnp.sum(recv_ref[...].astype(F32), axis=0)


def shifted(count_all, shift, square, cross_sum, square_sum):
    alpha = shift * square + cross_sum / count_all
    d = alpha - shift
    mean_sq = (square_sum - 2.0 * d * cross_sum) / count_all + d * d * square
    mean_sq = jnp.maximum(mean_sq, 0.0)
    return alpha, d, mean_sq


def first_owner_kernel(count_all, recv_ref, msgs_ref, gap_ref, own_ref, state_ref, coef_ref, msg_ref):
    start_sq, gap_sq = read_sums(msgs_ref, 2)
    norm = start_sq / count_all
    inv = 1.0 / jnp.sqrt(norm + 1e-06)
    square = norm / (norm + 1e-06)
    shift = gap_sq / jnp.maximum(start_sq, 1e-30)
    cur = own_ref[...] * inv
    inter = received(recv_ref) * inv
    gap = gap_ref[...]
    resid = (gap - shift) * cur + inter
    state_ref[0] = cur
    state_ref[1] = resid
    state_ref[2] = inter
    coef_ref[0] = shift
    coef_ref[1] = square
    coef_ref[2] = gap_sq * inv * inv
    sums = [
        jnp.sum(cur * resid),
        jnp.sum(resid * resid),
        jnp.sum(gap * resid * resid),
        jnp.sum(gap * resid * cur),
    ]
    msg_ref[...] = jnp.broadcast_to(with_sums(resid, sums).astype(BF)[None], msg_ref.shape)


def second_owner_kernel(count_all, recv_ref, msgs_ref, gap_ref, state_ref, coef_ref, out_ref, coef_out, msg_ref):
    cross, total, gap_rr, gap_rq = read_sums(msgs_ref, 4)
    alpha, d, mean_sq = shifted(count_all, coef_ref[0], coef_ref[1], cross, total)
    beta = jnp.sqrt(mean_sq + 1e-06)
    square = mean_sq / (mean_sq + 1e-06)
    gap_qq = gap_rr - 2.0 * d * gap_rq + d * d * coef_ref[2]
    shift = gap_qq / (mean_sq + 1e-06) / count_all
    prev = state_ref[0]
    cur = (state_ref[1] - d * prev) / beta
    inter = (received(recv_ref) - d * state_ref[2]) / beta
    resid = (gap_ref[...] - shift) * cur + inter - beta * prev
    out_ref[0] = cur
    out_ref[1] = resid
    coef_out[0] = alpha
    coef_out[1] = beta
    coef_out[2] = shift
    coef_out[3] = square
    dims = msg_ref.shape[:1] + msg_ref.shape[2:]
    msg_ref[:, 0, :] = jnp.full(dims, jnp.sum(cur * resid), F32)
    msg_ref[:, 1, :] = jnp.full(dims, jnp.sum(resid * resid), F32)


def finish_kernel(count_all, msgs_ref, state_ref, coef_ref, out_ref, coeffs_ref):
    sums = jnp.sum(msgs_ref[...], axis=0)
    alpha, d, mean_sq = shifted(count_all, coef_ref[2], coef_ref[3], sums[0, 0], sums[1, 0])
    beta = jnp.sqrt(mean_sq + 1e-06)
    own = (state_ref[1] - d * state_ref[0]) / beta
    coeffs_ref[0] = coef_ref[0]
    coeffs_ref[1] = alpha
    coeffs_ref[2] = coef_ref[1]
    coeffs_ref[3] = beta
    for kl in range(out_ref.shape[0]):
        tile = own[kl // 2 * ROWS : (kl // 2 + 1) * ROWS, :]
        other = pltpu.roll(tile, HALF, axis=1)
        left, right = (tile, other) if kl % 2 == 0 else (other, tile)
        low = lax.broadcasted_iota(jnp.int32, (1, LANES), 1) < HALF
        for j in range(ROWS // 2):
            row = jnp.where(low, left[2 * j : 2 * j + 1], right[2 * j + 1 : 2 * j + 2])
            out_ref[pl.ds(kl, 1), pl.ds(j * LANES, LANES)] = row


def shape_of(dims, kind=F32):
    return jax.ShapeDtypeStruct(dims, kind)


def call(kernel, name, out_shape, in_specs, out_specs, scratch=(), mib=58, flops=0, moved=0):
    return pl.pallas_call(
        kernel,
        out_shape=out_shape,
        in_specs=in_specs,
        out_specs=out_specs,
        scratch_shapes=list(scratch),
        compiler_params=pltpu.CompilerParams(vmem_limit_bytes=mib * MIB),
        cost_estimate=pl.CostEstimate(flops=flops, bytes_accessed=moved, transcendentals=0),
        name=name,
    )


def dma(*dims):
    return pltpu.SemaphoreType.DMA(dims)


def swap(block, axis, d):
    return lax.ppermute(block, axis, [(i, i ^ d) for i in range(lax.axis_size(axis))])


def plane_pieces(own_piece, others):
    def move(block, d):
        return swap(block, "band", d)

    half = own_piece.shape[0] // 2
    core, by_x, by_y = move(own_piece, 1), move(own_piece, 2), move(own_piece, 4)
    by_x, by_y, others = lax.optimization_barrier((by_x, by_y, others))
    diag = [move(by_x[:half], 4), move(by_y[half:], 2)]
    pieces = [[own_piece], [core], [by_x], [move(by_x, 1)], [by_y], [move(by_y, 1)]]
    return pieces + [diag, [move(part, 1) for part in diag]], others


def kernel_path(start_vec, val_energy, cond_energy, val_orb, cond_orb, coulomb, screened):
    n_ka = lax.axis_size("ka")
    n_band = lax.axis_size("band")
    devices = n_ka * n_band
    ka, band = lax.axis_index("ka"), lax.axis_index("band")
    k_dev = start_vec.shape[0]
    nv_blk = val_orb.shape[1]
    n_cond = cond_orb.shape[1]
    npt_all = cond_orb.shape[2]
    k_points = k_dev * n_ka
    pairs = k_points // 2
    mu_blk, nu_blk = screened.shape
    own = coulomb.shape[0]
    count_all = k_points * nv_blk * n_band * n_cond
    scale = 1.0 / (npt_all * math.sqrt(count_all))
    piece_rows = k_points * nv_blk

    def val_to(j):
        part = lax.dynamic_slice_in_dim(val_orb, jnp.bitwise_xor(ka, j) * nu_blk, nu_blk, 2)
        return part.reshape(k_dev * nv_blk, nu_blk)

    val_parts = [val_to(0)] + [swap(val_to(j), "ka", j) for j in range(1, n_ka)]
    base, val_parts = lax.optimization_barrier((band * mu_blk, val_parts))
    val_cut = jnp.concatenate(val_parts, axis=0)
    half = mu_blk // 2
    cond_pts = []
    for h in range(2):
        cut = lax.dynamic_slice_in_dim(cond_orb, base + h * half, half, 2)
        cond_pts.append(
            lax.all_gather(cut.reshape(k_dev * n_cond, half), "ka", axis=0, tiled=True)
        )
    gap = (cond_energy[:, None, :] - val_energy[:, :, None]).reshape(k_dev, nv_blk * n_cond)
    gap = pack_vector(gap, k_dev)

    block = gap.shape
    msg_shape = shape_of((devices,) + block, BF)
    start_own, message = call(
        pack_kernel, "pack", (shape_of(block), msg_shape), [VMEM] * 2, (VMEM, VMEM), mib=8
    )(start_vec, gap)
    msgs = exchange_all(message)
    chunk, tile = 1024, 1024
    rows_all, conds_all = k_points * nv_blk * n_band, k_points * n_cond
    scr_turned = call(
        functools.partial(turn_kernel, tile // 2),
        "turn",
        shape_of((nu_blk, mu_blk), BF),
        [ANY],
        ANY,
        [pltpu.VMEM((mu_blk, nu_blk), BF), pltpu.VMEM((nu_blk, mu_blk), BF)]
        + [dma(2 * nu_blk // tile)] * 2,
        moved=8 * MIB,
    )(screened)
    own_rows = k_dev * n_cond
    cuts = call(
        cut_kernel,
        "cut",
        (shape_of((own_rows, own), BF),) * n_ka,
        [ANY],
        (ANY,) * n_ka,
        [dma(n_ka * k_dev)],
        mib=8,
    )(cond_orb)
    cond_own = [cuts[0]] + [swap(cuts[j], "ka", j) for j in range(1, n_ka)]
    pieces, (msgs, cond_own, scr_turned) = plane_pieces(val_cut, (msgs, cond_own, scr_turned))
    counts = tuple(len(piece) for piece in pieces)
    flat = [ref for piece in pieces for ref in piece]
    n_copies = len(flat)

    val_rows, val_turned, val_own = call(
        functools.partial(order_kernel, counts),
        "order",
        (
            shape_of((rows_all, nu_blk), BF),
            shape_of((nu_blk, rows_all), BF),
            shape_of((rows_all, own), BF),
        ),
        [ANY] * n_copies,
        (ANY, ANY, ANY),
        [
            pltpu.VMEM((n_band, piece_rows, nu_blk), BF),
            pltpu.VMEM((rows_all, nu_blk), BF),
            pltpu.VMEM((nu_blk, rows_all), BF),
            dma(n_copies),
            dma(3, pairs),
        ],
        moved=9 * MIB,
    )(*flat)

    cfg = (n_ka, n_band, k_dev)
    quads = k_points // 4
    state, coef = None, None
    for step in range(STEPS):
        first = step == 0
        qx, rho = call(
            functools.partial(density_kernel, cfg),
            "density",
            (
                shape_of((quads, 2 * LANES, 2 * LANES), BF),
                shape_of((devices, own // LANES, LANES)),
            ),
            [VMEM] * 2 + [ANY] * n_ka,
            (VMEM, VMEM),
            [
                pltpu.VMEM((quads, 2 * LANES, 2 * LANES), F32),
                pltpu.VMEM((n_ka, own_rows, own), BF),
                dma(n_ka),
            ],
            mib=8,
        )(msgs, val_own, *cond_own)
        density = exchange_all(rho)
        direct, mixed = [], None
        for halves in ((0,), (1,)) if first else ((0, 1),):
            mixed_in, mixed_out = mixed is not None, first and mixed is None
            mu = half * len(halves)
            out = call(
                functools.partial(direct_kernel, n_ka, halves, mixed_in, mixed_out, tile, scale),
                "direct",
                (shape_of((pairs, LANES, LANES)),)
                + ((shape_of((nu_blk, conds_all), BF),) if mixed_out else ()),
                [ANY] * (3 + (not mixed_in) + len(halves)),
                (VMEM,) + ((ANY,) if mixed_out else ()),
                (
                    []
                    if mixed_in
                    else [
                        pltpu.VMEM((quads, 2 * LANES, 2 * LANES), BF),
                        pltpu.VMEM((nu_blk, rows_all), BF),
                    ]
                )
                + [
                    pltpu.VMEM((conds_all, mu), BF),
                    pltpu.VMEM((nu_blk, mu), BF),
                    pltpu.VMEM((rows_all, nu_blk), BF),
                    pltpu.VMEM((nu_blk, conds_all), BF),
                    pltpu.VMEM((nu_blk, mu), BF),
                    pltpu.VMEM((rows_all, mu), BF),
                    dma(1),
                    dma(len(halves), n_ka),
                    dma(1),
                    dma(3, nu_blk // tile),
                ],
                flops=4 * mu * nu_blk * conds_all,
                moved=12 * MIB,
            )(
                mixed if mixed_in else val_turned,
                scr_turned,
                val_rows,
                *([] if mixed_in else [qx]),
                *[cond_pts[h] for h in halves],
            )
            direct.append(out[0])
            if mixed_out:
                mixed = out[1]
        parts = call(
            functools.partial(exchange_kernel, cfg, len(direct), chunk, scale),
            "exchange",
            msg_shape,
            [ANY] * (3 + len(direct) + n_ka),
            VMEM,
            [
                pltpu.VMEM((devices, own // LANES, LANES), F32),
                pltpu.VMEM((len(direct), pairs, LANES, LANES), F32),
                pltpu.VMEM((own, npt_all), BF),
                pltpu.VMEM((n_ka, own_rows, own), BF),
                pltpu.VMEM((rows_all, own), BF),
                pltpu.VMEM((pairs, LANES, LANES), F32),
                pltpu.VMEM((devices,) + block, F32),
                dma(npt_all // chunk),
                dma(n_ka),
                dma(2 + len(direct)),
            ],
        )(density, coulomb, val_own, *direct, *cond_own)
        recv = exchange_all(parts)
        if first:
            state, coef, message = call(
                functools.partial(first_owner_kernel, count_all),
                "first_owner",
                (shape_of((3,) + block), shape_of((3,)), msg_shape),
                [VMEM] * 4,
                (VMEM, SMEM, VMEM),
                mib=8,
            )(recv, msgs, gap, start_own)
        else:
            state, coef, message = call(
                functools.partial(second_owner_kernel, count_all),
                "second_owner",
                (shape_of((2,) + block), shape_of((4,)), shape_of((devices, 2, LANES))),
                [VMEM] * 4 + [SMEM],
                (VMEM, SMEM, VMEM),
                mib=8,
            )(recv, msgs, gap, state, coef)
        msgs = exchange_all(message)
    return call(
        functools.partial(finish_kernel, count_all),
        "finish",
        (shape_of(start_vec.shape), shape_of((2 * STEPS,))),
        [VMEM] * 2 + [SMEM],
        (VMEM, SMEM),
        mib=8,
    )(msgs, state, coef)


def array_path(start_vec, val_energy, cond_energy, val_orb, cond_orb, coulomb, screened):
    n_ka = lax.axis_size("ka")
    n_band = lax.axis_size("band")
    devices = n_ka * n_band
    ka, band = lax.axis_index("ka"), lax.axis_index("band")
    me = ka * n_band + band
    k_dev, pair_blk = start_vec.shape
    nv_blk = val_orb.shape[1]
    n_cond = cond_orb.shape[1]
    n_val = nv_blk * n_band
    npt_all = cond_orb.shape[2]
    k_points = k_dev * n_ka
    mu_blk, nu_blk = screened.shape
    own_pts = coulomb.shape[0]
    count_all = k_points * n_val * n_cond
    kernel_scale = 1.0 / (npt_all * math.sqrt(count_all))

    start_all = gather_all(start_vec, devices)
    val_cut = lax.all_to_all(
        val_orb.reshape(k_dev, nv_blk, n_ka, nu_blk).transpose(2, 0, 1, 3),
        "ka", split_axis=0, concat_axis=0, tiled=True,
    ).reshape(k_points, nv_blk, nu_blk)
    val_pts = lax.all_gather(val_cut, "band", axis=1, tiled=True)
    cond_local = lax.dynamic_slice_in_dim(cond_orb, band * mu_blk, mu_blk, 2)
    cond_pts = lax.all_gather(cond_local, "ka", axis=0, tiled=True)
    cond_rows = cond_orb.reshape(k_dev, n_cond, n_ka, n_band, own_pts)
    cond_rows = lax.dynamic_index_in_dim(cond_rows, band, 3, keepdims=False)
    cond_own = lax.all_to_all(
        cond_rows.transpose(2, 0, 1, 3), "ka", split_axis=0, concat_axis=0, tiled=True
    ).reshape(k_points, n_cond, own_pts)
    val_own = lax.dynamic_slice_in_dim(val_pts, band * own_pts, own_pts, 2)

    energy_gap = (cond_energy[:, None, :] - val_energy[:, :, None]).reshape(k_dev, pair_blk)
    start_sq = jnp.sum(start_all * start_all)
    current = start_all / jnp.sqrt(start_sq / count_all + 1e-06)
    previous = jnp.zeros_like(current)
    beta_val = jnp.float32(0.0)
    alphas = []
    betas = []
    for turn_index in range(STEPS):
        full_vec = (
            current.astype(BF)
            .reshape(n_ka, n_band, k_dev, nv_blk, n_cond)
            .transpose(0, 2, 1, 3, 4)
            .reshape(k_points, n_val, n_cond)
        )
        mixed_f = jnp.einsum("kvc,kvn->kcn", full_vec, val_pts, preferred_element_type=F32)
        mixed_own = lax.dynamic_slice_in_dim(mixed_f, band * own_pts, own_pts, 2)
        density_own = jnp.sum(mixed_own * cond_own.astype(F32), axis=(0, 1))
        density = gather_all(density_own.astype(BF), devices).reshape(npt_all)
        mixed_val = mixed_f.astype(BF)
        amp = jnp.einsum("kcm,kcn->mn", cond_pts, mixed_val, preferred_element_type=F32)
        kern = (screened.astype(F32) * amp * kernel_scale).astype(BF)
        folded = jnp.einsum("mn,kvn->kvm", kern, val_pts, preferred_element_type=F32).astype(BF)
        direct_part = jnp.einsum("kcm,kvm->kvc", cond_pts, folded, preferred_element_type=F32)
        potential = kernel_scale * jnp.dot(coulomb, density, preferred_element_type=F32)
        weighted = (val_own.astype(F32) * potential).astype(BF)
        exchange = jnp.einsum("kvp,kcp->kvc", weighted, cond_own, preferred_element_type=F32)
        part = 2.0 * exchange - direct_part
        arranged = (
            part.reshape(n_ka, k_dev, n_band, nv_blk, n_cond)
            .transpose(0, 2, 1, 3, 4)
            .reshape(devices, k_dev, pair_blk)
        )
        inter_own = jnp.sum(exchange_all(arranged), axis=0)
        current_own = lax.dynamic_index_in_dim(current, me, 0, keepdims=False)
        resid_vec = gather_all(energy_gap * current_own + inter_own, devices)
        resid_vec = resid_vec - beta_val * previous
        alpha_val = jnp.sum(current * resid_vec) / count_all
        resid_vec = resid_vec - alpha_val * current
        beta_val = jnp.sqrt(jnp.sum(resid_vec * resid_vec) / count_all + 1e-06)
        previous = current
        current = resid_vec / beta_val
        alphas.append(alpha_val)
        betas.append(beta_val)
    coeffs = jnp.stack(alphas + betas)
    return (lax.dynamic_index_in_dim(current, me, 0, keepdims=False), coeffs)


def per_device(*args):
    start_vec, _, _, val_orb, cond_orb, coulomb, screened = args
    n_ka, n_band = lax.axis_size("ka"), lax.axis_size("band")
    fits = (
        n_band == 8
        and n_ka & (n_ka - 1) == 0
        and start_vec.shape[0] % 2 == 1
        and val_orb.shape[1] == ROWS
        and cond_orb.shape[1] == HALF
        and start_vec.shape[0] * n_ka % 4 == 0
        and coulomb.shape[0] % LANES == 0
        and coulomb.shape[1] % 1024 == 0
        and screened.shape[0] % 512 == 0
        and screened.shape[1] % 1024 == 0
        and screened.shape[0] * screened.shape[1] <= 2 * MIB
    )
    return (kernel_path if fits else array_path)(*args)


def solution(mesh):
    in_specs = (
        P("ka", "band"),
        P("ka", "band"),
        P("ka", None),
        P("ka", "band", None),
        P("ka", None, None),
        P(("ka", "band"), None),
        P("band", "ka"),
    )
    out_specs = (P("ka", "band"), P())
    return jax.shard_map(
        per_device, mesh=mesh, in_specs=in_specs, out_specs=out_specs, check_vma=False
    )
```

```python
import functools
import math

import jax
import jax.numpy as jnp
from jax import lax
from jax.experimental import pallas as pl
from jax.experimental.pallas import tpu as pltpu
from jax.sharding import PartitionSpec as P

STEPS = 2
AXES = ("ka", "band")
BF, F32 = jnp.bfloat16, jnp.float32
LANES = 128
HALF = 64
ROWS = 8
MIB = 1 << 20

VMEM = pl.BlockSpec(memory_space=pltpu.VMEM)
SMEM = pl.BlockSpec(memory_space=pltpu.SMEM)
ANY = pl.BlockSpec(memory_space=pl.ANY)


def gather_all(block, devices):
    wide = jnp.broadcast_to(block[None], (devices,) + block.shape)
    return exchange_all(wide)


def exchange_all(parts):
    return lax.all_to_all(parts, AXES, split_axis=0, concat_axis=0, tiled=True)


def dot_nt(lhs, rhs):
    return lax.dot_general(lhs, rhs, (((1,), (1,)), ((), ())), preferred_element_type=F32)


def dot_tn(lhs, rhs):
    return lax.dot_general(lhs, rhs, (((0,), (0,)), ((), ())), preferred_element_type=F32)


def pack_vector(block, k_dev):
    groups = (k_dev + 1) // 2
    block = jnp.pad(block, ((0, 2 * groups - k_dev), (0, 0)))
    block = block.reshape(groups, 2, ROWS, HALF).transpose(0, 2, 1, 3)
    return block.reshape(groups * ROWS, LANES)


def lane_half(tile, have, want):
    if have != want:
        tile = pltpu.roll(tile, HALF, axis=1)
    lane = lax.broadcasted_iota(jnp.int32, tile.shape, 1)
    keep = lane < HALF if want == 0 else lane >= HALF
    return jnp.where(keep, tile, 0.0)


def with_sums(block, sums):
    row = lax.broadcasted_iota(jnp.int32, block.shape, 0)
    lane = lax.broadcasted_iota(jnp.int32, block.shape, 1)
    free = row == block.shape[0] - ROWS
    for i, total in enumerate(sums):
        rest = jnp.full(block.shape, total, F32)
        for part in range(3):
            piece = rest.astype(BF).astype(F32)
            block = jnp.where(free & (lane == HALF + 3 * i + part), piece, block)
            rest = rest - piece
    return block


def read_sums(msgs_ref, count):
    rows = msgs_ref.shape[1]
    tile = jnp.sum(msgs_ref[...].astype(F32), axis=0)[rows - ROWS :, :]
    row = lax.broadcasted_iota(jnp.int32, tile.shape, 0)
    lane = lax.broadcasted_iota(jnp.int32, tile.shape, 1)
    out = []
    for i in range(count):
        mine = (row == 0) & (lane >= HALF + 3 * i) & (lane < HALF + 3 * i + 3)
        out.append(jnp.sum(jnp.where(mine, tile, 0.0)))
    return out


def block_copies(groups, width, dest, sems, column=0):
    copies = []
    for d, refs in enumerate(groups):
        row = 0
        for ref in refs:
            copies.append(
                pltpu.make_async_copy(
                    ref.at[:, pl.ds(column, width)],
                    dest.at[d, pl.ds(row, ref.shape[0]), :],
                    sems.at[len(copies)],
                )
            )
            row += ref.shape[0]
    return copies


def split_refs(refs, counts):
    out, at = [], 0
    for count in counts:
        out.append(refs[at : at + count])
        at += count
    return out


def start_all(copies):
    for copy in copies:
        copy.start()


def wait_all(copies):
    for copy in copies:
        copy.wait()


def device_at(n_band, j, d):
    ka = jnp.bitwise_xor(lax.axis_index("ka"), j)
    return ka * n_band + jnp.bitwise_xor(lax.axis_index("band"), d)


def pair_rows(ref, kp):
    part = ref[:, kp * 2 * ROWS : (kp + 1) * 2 * ROWS, :]
    return part.reshape(part.shape[0] * 2 * ROWS, part.shape[2])


def pack_kernel(start_ref, gap_ref, own_ref, msg_ref):
    own_ref[...] = jnp.zeros_like(own_ref)
    for kl in range(start_ref.shape[0]):
        for j in range(ROWS // 2):
            row = start_ref[pl.ds(kl, 1), pl.ds(j * LANES, LANES)]
            for v in range(2):
                at = pl.ds(kl // 2 * ROWS + 2 * j + v, 1)
                own_ref[at, :] = own_ref[at, :] + lane_half(row, v, kl % 2)
    own = own_ref[...]
    square = own * own
    block = with_sums(own, [jnp.sum(square), jnp.sum(gap_ref[...] * square)])
    msg_ref[...] = jnp.broadcast_to(block.astype(BF)[None], msg_ref.shape)


def cut_kernel(cond_ref, *refs):
    outs, sems = refs[:-1], refs[-1]
    k_dev, n_cond, npt = cond_ref.shape
    own = outs[0].shape[1]
    nu = npt // len(outs)
    copies = []
    for j, out in enumerate(outs):
        at = jnp.bitwise_xor(lax.axis_index("ka"), j) * nu + lax.axis_index("band") * own
        for kl in range(k_dev):
            copies.append(
                pltpu.make_async_copy(
                    cond_ref.at[kl, :, pl.ds(pl.multiple_of(at, LANES), own)],
                    out.at[pl.ds(kl * n_cond, n_cond), :],
                    sems.at[len(copies)],
                )
            )
    start_all(copies)
    wait_all(copies)


def turn_kernel(tile, scr_ref, out_ref, scrs, turned, in_sems, out_sems):
    nu = scr_ref.shape[1]
    ins, outs = [], []
    for j in range(nu // tile):
        at = pl.ds(j * tile, tile)
        ins.append(pltpu.make_async_copy(scr_ref.at[:, at], scrs.at[:, at], in_sems.at[j]))
        outs.append(pltpu.make_async_copy(turned.at[at, :], out_ref.at[at, :], out_sems.at[j]))
    start_all(ins)
    for j in range(nu // tile):
        ins[j].wait()
        turned[j * tile : (j + 1) * tile, :] = scrs[:, j * tile : (j + 1) * tile].T
        outs[j].start()
    wait_all(outs)


def order_kernel(counts, *refs):
    n_val = sum(counts)
    val_refs, refs = split_refs(refs[:n_val], counts), refs[n_val:]
    rows_out, turned_out, own_out, vals, ordered, turned, val_sems, out_sems = refs
    own = own_out.shape[1]
    nu = ordered.shape[1]
    copies = block_copies(val_refs, nu, vals, val_sems)
    start_all(copies)
    wait_all(copies)
    group = vals.shape[0] * 2 * ROWS
    column = pl.multiple_of(lax.axis_index("band") * own, LANES)
    outs = []
    for kp in range(ordered.shape[0] // group):
        at = slice(kp * group, (kp + 1) * group)
        ordered[at, :] = pair_rows(vals, kp)
        turned[:, at] = ordered[at, :].T
        at = pl.ds(kp * group, group)
        outs += [
            pltpu.make_async_copy(ordered.at[at, :], rows_out.at[at, :], out_sems.at[0, kp]),
            pltpu.make_async_copy(turned.at[:, at], turned_out.at[:, at], out_sems.at[1, kp]),
            pltpu.make_async_copy(
                ordered.at[at, pl.ds(column, own)], own_out.at[at, :], out_sems.at[2, kp]
            ),
        ]
        start_all(outs[-3:])
    wait_all(outs)


def density_kernel(cfg, *refs):
    n_ka, n_band, k_dev = cfg
    k_points = n_ka * k_dev
    msgs_ref, vown_ref, cond_refs, refs = refs[0], refs[1], refs[2 : 2 + n_ka], refs[2 + n_ka :]
    qx_ref, rho_ref, xs, conds, cond_sems = refs
    own = vown_ref.shape[1]
    copies = block_copies([[ref] for ref in cond_refs], own, conds, cond_sems)
    start_all(copies)
    xs[...] = jnp.zeros_like(xs)
    for d in range(n_band):
        for k in range(k_points):
            j, kl = divmod(k, k_dev)
            tile = msgs_ref[device_at(n_band, j, d), :, :].astype(F32)
            tile = tile[kl // 2 * ROWS : (kl // 2 + 1) * ROWS, :]
            base = k // 2 % 2 * LANES
            at = pl.ds(base + d * 2 * ROWS + k % 2 * ROWS, ROWS)
            xs[k // 4, at, pl.ds(base, LANES)] = lane_half(tile, kl % 2, k % 2)
    qx_ref[...] = xs[...].astype(BF)
    wait_all(copies)
    cond_rows = conds[...].reshape(-1, own)
    rho = jnp.zeros((1, own), F32)
    quad = 2 * LANES
    for kq in range(k_points // 4):
        at = slice(kq * quad, (kq + 1) * quad)
        mixed = dot_tn(qx_ref[kq], vown_ref[at, :])
        rho = rho + jnp.sum(mixed * cond_rows[at, :].astype(F32), axis=0, keepdims=True)
    for r in range(own // LANES):
        part = rho[:, r * LANES : (r + 1) * LANES]
        rho_ref[:, r, :] = jnp.broadcast_to(part, (rho_ref.shape[0], LANES))


def line_blocks(n_ka):
    return [(way, hop) for way in (-1, 1) for hop in range(1, n_ka)]


def direct_kernel(n_ka, tile, scale, *refs):
    turned_ref, scr_ref, rows_ref, qx_ref, refs = refs[0], refs[1], refs[2], refs[3], refs[4:]
    hops = [(0, 0)] + line_blocks(n_ka)
    cond_refs, refs = split_refs(refs, [2] * len(hops)), refs[2 * len(hops) :]
    di_ref, qx, turned, conds, scrs, vals, mixed, kern, folded = refs[:9]
    qx_sem, cond_sems, row_sem, chunk_sems = refs[9:]
    nu, mu = scr_ref.shape
    part, half = cond_refs[0][0].shape
    quad = 2 * LANES
    ka = lax.axis_index("ka")

    def each_block(act):
        for i, (way, hop) in enumerate(hops):
            origin = ka + way * hop

            def act_on(i=i, origin=origin):
                row = pl.multiple_of(jnp.bitwise_xor(ka, origin) * part, part)
                for h, ref in enumerate(cond_refs[i]):
                    dest = conds.at[pl.ds(row, part), pl.ds(h * half, half)]
                    act(pltpu.make_async_copy(ref, dest, cond_sems.at[i, h]))

            if hop == 0:
                act_on()
            else:
                pl.when((origin >= 0) & (origin < n_ka))(act_on)

    qx_copy = pltpu.make_async_copy(qx_ref, qx, qx_sem.at[0])
    turned_copies, scr_copies = [], []
    for i in range(nu // tile):
        at = pl.ds(i * tile, tile)
        turned_copies.append(
            pltpu.make_async_copy(turned_ref.at[at, :], turned.at[at, :], chunk_sems.at[0, i])
        )
        scr_copies.append(
            pltpu.make_async_copy(scr_ref.at[at, :], scrs.at[at, :], chunk_sems.at[1, i])
        )
    row_copy = pltpu.make_async_copy(rows_ref, vals, row_sem.at[0])
    start_all([qx_copy, turned_copies[0]])
    each_block(lambda copy: copy.start())
    scr_copies[0].start()
    for i in range(1, nu // tile):
        start_all([turned_copies[i], scr_copies[i]])
    row_copy.start()
    qx_copy.wait()
    for i in range(nu // tile):
        rows = slice(i * tile, (i + 1) * tile)
        turned_copies[i].wait()
        for kq in range(qx.shape[0]):
            cols = slice(kq * quad, (kq + 1) * quad)
            mixed[rows, cols] = jnp.dot(
                turned[rows, cols], qx[kq], preferred_element_type=F32
            ).astype(BF)
        if i == 0:
            each_block(lambda copy: copy.wait())
        scr_copies[i].wait()
        for m in range(mu // quad):
            cols = slice(m * quad, (m + 1) * quad)
            amp = jnp.dot(mixed[rows, :], conds[:, cols], preferred_element_type=F32)
            kern[rows, cols] = (scrs[rows, cols].astype(F32) * amp * scale).astype(BF)
    row_copy.wait()
    for m in range(mu // quad):
        cols = slice(m * quad, (m + 1) * quad)
        folded[:, cols] = jnp.dot(vals[...], kern[:, cols], preferred_element_type=F32).astype(BF)
    for kp in range(di_ref.shape[0]):
        at = slice(kp * LANES, (kp + 1) * LANES)
        di_ref[kp] = dot_nt(folded[at, :], conds[at, :])


def exchange_kernel(cfg, chunk, scale, *refs):
    n_ka, n_band, k_dev = cfg
    k_points = n_ka * k_dev
    rho_ref, di_ref, coul_ref, vown_ref, refs = refs[0], refs[1], refs[2], refs[3], refs[4:]
    cond_refs, refs = refs[:n_ka], refs[n_ka:]
    msg_ref, rhos, di, coul, conds, vown, part, msg, coul_sems, cond_sems, sems = refs
    own, npt = coul_ref.shape
    coul_copies = [
        pltpu.make_async_copy(
            coul_ref.at[:, pl.ds(i * chunk, chunk)], coul.at[:, pl.ds(i * chunk, chunk)], coul_sems.at[i]
        )
        for i in range(npt // chunk)
    ]
    rho_copy = pltpu.make_async_copy(rho_ref, rhos, sems.at[0])
    copies = block_copies([[ref] for ref in cond_refs], own, conds, cond_sems)
    copies.append(pltpu.make_async_copy(vown_ref, vown, sems.at[1]))
    copies.append(pltpu.make_async_copy(di_ref, di, sems.at[2]))
    start_all([rho_copy] + coul_copies + copies)
    rho_copy.wait()
    acc = jnp.zeros((own, LANES), F32)
    per_dev = own // LANES
    for i in range(npt // chunk):
        coul_copies[i].wait()
        for j in range(i * chunk // LANES, (i + 1) * chunk // LANES):
            rho = rhos[j // per_dev, pl.ds(j % per_dev, 1), :].astype(BF).astype(F32)
            acc = acc + coul[:, j * LANES : (j + 1) * LANES].astype(F32) * rho
    potential = scale * jnp.sum(acc.T, axis=0, keepdims=True)
    wait_all(copies)
    cond_rows = conds[...].reshape(-1, own)
    for kp in range(k_points // 2):
        at = slice(kp * LANES, (kp + 1) * LANES)
        weighted = (vown[at, :].astype(F32) * potential).astype(BF)
        part[kp] = 2.0 * dot_nt(weighted, cond_rows[at, :]) - di[kp]
    for d in range(n_band):
        for j in range(n_ka):
            for g in range((k_dev + 1) // 2):
                tile = None
                for kl in range(2 * g, min(2 * g + 2, k_dev)):
                    k = j * k_dev + kl
                    piece = part[k // 2, pl.ds(d * 2 * ROWS + k % 2 * ROWS, ROWS), :]
                    piece = lane_half(piece, k % 2, kl % 2)
                    tile = piece if tile is None else tile + piece
                msg[device_at(n_band, j, d), pl.ds(g * ROWS, ROWS), :] = tile
    msg_ref[...] = msg[...].astype(BF)


def received(recv_ref):
    return jnp.sum(recv_ref[...].astype(F32), axis=0)


def shifted(count_all, shift, square, cross_sum, square_sum):
    alpha = shift * square + cross_sum / count_all
    d = alpha - shift
    mean_sq = (square_sum - 2.0 * d * cross_sum) / count_all + d * d * square
    mean_sq = jnp.maximum(mean_sq, 0.0)
    return alpha, d, mean_sq


def first_owner_kernel(count_all, recv_ref, msgs_ref, gap_ref, own_ref, state_ref, coef_ref, msg_ref):
    start_sq, gap_sq = read_sums(msgs_ref, 2)
    norm = start_sq / count_all
    inv = 1.0 / jnp.sqrt(norm + 1e-06)
    square = norm / (norm + 1e-06)
    shift = gap_sq / jnp.maximum(start_sq, 1e-30)
    cur = own_ref[...] * inv
    inter = received(recv_ref) * inv
    gap = gap_ref[...]
    resid = (gap - shift) * cur + inter
    state_ref[0] = cur
    state_ref[1] = resid
    state_ref[2] = inter
    coef_ref[0] = shift
    coef_ref[1] = square
    coef_ref[2] = gap_sq * inv * inv
    sums = [
        jnp.sum(cur * resid),
        jnp.sum(resid * resid),
        jnp.sum(gap * resid * resid),
        jnp.sum(gap * resid * cur),
    ]
    msg_ref[...] = jnp.broadcast_to(with_sums(resid, sums).astype(BF)[None], msg_ref.shape)


def second_owner_kernel(count_all, recv_ref, msgs_ref, gap_ref, state_ref, coef_ref, out_ref, coef_out, msg_ref):
    cross, total, gap_rr, gap_rq = read_sums(msgs_ref, 4)
    alpha, d, mean_sq = shifted(count_all, coef_ref[0], coef_ref[1], cross, total)
    beta = jnp.sqrt(mean_sq + 1e-06)
    square = mean_sq / (mean_sq + 1e-06)
    gap_qq = gap_rr - 2.0 * d * gap_rq + d * d * coef_ref[2]
    shift = gap_qq / (mean_sq + 1e-06) / count_all
    prev = state_ref[0]
    cur = (state_ref[1] - d * prev) / beta
    inter = (received(recv_ref) - d * state_ref[2]) / beta
    resid = (gap_ref[...] - shift) * cur + inter - beta * prev
    out_ref[0] = cur
    out_ref[1] = resid
    coef_out[0] = alpha
    coef_out[1] = beta
    coef_out[2] = shift
    coef_out[3] = square
    dims = msg_ref.shape[:1] + msg_ref.shape[2:]
    msg_ref[:, 0, :] = jnp.full(dims, jnp.sum(cur * resid), F32)
    msg_ref[:, 1, :] = jnp.full(dims, jnp.sum(resid * resid), F32)


def finish_kernel(count_all, msgs_ref, state_ref, coef_ref, out_ref, coeffs_ref):
    sums = jnp.sum(msgs_ref[...], axis=0)
    alpha, d, mean_sq = shifted(count_all, coef_ref[2], coef_ref[3], sums[0, 0], sums[1, 0])
    beta = jnp.sqrt(mean_sq + 1e-06)
    own = (state_ref[1] - d * state_ref[0]) / beta
    coeffs_ref[0] = coef_ref[0]
    coeffs_ref[1] = alpha
    coeffs_ref[2] = coef_ref[1]
    coeffs_ref[3] = beta
    for kl in range(out_ref.shape[0]):
        tile = own[kl // 2 * ROWS : (kl // 2 + 1) * ROWS, :]
        other = pltpu.roll(tile, HALF, axis=1)
        left, right = (tile, other) if kl % 2 == 0 else (other, tile)
        low = lax.broadcasted_iota(jnp.int32, (1, LANES), 1) < HALF
        for j in range(ROWS // 2):
            row = jnp.where(low, left[2 * j : 2 * j + 1], right[2 * j + 1 : 2 * j + 2])
            out_ref[pl.ds(kl, 1), pl.ds(j * LANES, LANES)] = row


def shape_of(dims, kind=F32):
    return jax.ShapeDtypeStruct(dims, kind)


def call(kernel, name, out_shape, in_specs, out_specs, scratch=(), mib=58, flops=0, moved=0):
    return pl.pallas_call(
        kernel,
        out_shape=out_shape,
        in_specs=in_specs,
        out_specs=out_specs,
        scratch_shapes=list(scratch),
        compiler_params=pltpu.CompilerParams(vmem_limit_bytes=mib * MIB),
        cost_estimate=pl.CostEstimate(flops=flops, bytes_accessed=moved, transcendentals=0),
        name=name,
    )


def dma(*dims):
    return pltpu.SemaphoreType.DMA(dims)


def swap(block, axis, d):
    return lax.ppermute(block, axis, [(i, i ^ d) for i in range(lax.axis_size(axis))])


def line_gather(block, axis):
    n = lax.axis_size(axis)
    out = [block]
    for way in (-1, 1):
        moving = block
        for hop in range(1, n):
            pairs = [(i, i - way) for i in range(n) if 0 <= i + way * (hop - 1) < n and 0 <= i - way < n]
            moving = lax.ppermute(moving, axis, pairs)
            out.append(moving)
    return out


def plane_pieces(own_piece, others):
    def move(block, d):
        return swap(block, "band", d)

    half = own_piece.shape[0] // 2
    core, by_x, by_y = move(own_piece, 1), move(own_piece, 2), move(own_piece, 4)
    by_x, by_y, others = lax.optimization_barrier((by_x, by_y, others))
    diag = [move(by_x[:half], 4), move(by_y[half:], 2)]
    pieces = [[own_piece], [core], [by_x], [move(by_x, 1)], [by_y], [move(by_y, 1)]]
    return pieces + [diag, [move(part, 1) for part in diag]], others


def kernel_path(start_vec, val_energy, cond_energy, val_orb, cond_orb, coulomb, screened):
    n_ka = lax.axis_size("ka")
    n_band = lax.axis_size("band")
    devices = n_ka * n_band
    ka, band = lax.axis_index("ka"), lax.axis_index("band")
    k_dev = start_vec.shape[0]
    nv_blk = val_orb.shape[1]
    n_cond = cond_orb.shape[1]
    npt_all = cond_orb.shape[2]
    k_points = k_dev * n_ka
    pairs = k_points // 2
    mu_blk, nu_blk = screened.shape
    own = coulomb.shape[0]
    count_all = k_points * nv_blk * n_band * n_cond
    scale = 1.0 / (npt_all * math.sqrt(count_all))
    piece_rows = k_points * nv_blk

    def val_to(j):
        part = lax.dynamic_slice_in_dim(val_orb, jnp.bitwise_xor(ka, j) * nu_blk, nu_blk, 2)
        return part.reshape(k_dev * nv_blk, nu_blk)

    val_parts = [val_to(0)] + [swap(val_to(j), "ka", j) for j in range(1, n_ka)]
    val_cut = jnp.concatenate(val_parts, axis=0)
    half = mu_blk // 2
    cond_halves = []
    for h in range(2):
        cut = lax.dynamic_slice_in_dim(cond_orb, band * mu_blk + h * half, half, 2)
        cond_halves.append(line_gather(cut.reshape(k_dev * n_cond, half), "ka"))
    cond_pts = [ref for pair in zip(*cond_halves) for ref in pair]
    gap = (cond_energy[:, None, :] - val_energy[:, :, None]).reshape(k_dev, nv_blk * n_cond)
    gap = pack_vector(gap, k_dev)

    block = gap.shape
    msg_shape = shape_of((devices,) + block, BF)
    start_own, message = call(
        pack_kernel, "pack", (shape_of(block), msg_shape), [VMEM] * 2, (VMEM, VMEM), mib=8
    )(start_vec, gap)
    msgs = exchange_all(message)
    chunk, tile = 1024, 1024
    rows_all, conds_all = k_points * nv_blk * n_band, k_points * n_cond
    scr_turned = call(
        functools.partial(turn_kernel, tile // 2),
        "turn",
        shape_of((nu_blk, mu_blk), BF),
        [ANY],
        ANY,
        [pltpu.VMEM((mu_blk, nu_blk), BF), pltpu.VMEM((nu_blk, mu_blk), BF)]
        + [dma(2 * nu_blk // tile)] * 2,
        moved=8 * MIB,
    )(screened)
    own_rows = k_dev * n_cond
    cuts = call(
        cut_kernel,
        "cut",
        (shape_of((own_rows, own), BF),) * n_ka,
        [ANY],
        (ANY,) * n_ka,
        [dma(n_ka * k_dev)],
    )(cond_orb)
    cond_own = [cuts[0]] + [swap(cuts[j], "ka", j) for j in range(1, n_ka)]
    pieces, (msgs, cond_own, scr_turned) = plane_pieces(val_cut, (msgs, cond_own, scr_turned))
    counts = tuple(len(piece) for piece in pieces)
    flat = [ref for piece in pieces for ref in piece]
    n_copies = len(flat)

    val_rows, val_turned, val_own = call(
        functools.partial(order_kernel, counts),
        "order",
        (
            shape_of((rows_all, nu_blk), BF),
            shape_of((nu_blk, rows_all), BF),
            shape_of((rows_all, own), BF),
        ),
        [ANY] * n_copies,
        (ANY, ANY, ANY),
        [
            pltpu.VMEM((n_band, piece_rows, nu_blk), BF),
            pltpu.VMEM((rows_all, nu_blk), BF),
            pltpu.VMEM((nu_blk, rows_all), BF),
            dma(n_copies),
            dma(3, pairs),
        ],
        moved=9 * MIB,
    )(*flat)

    cfg = (n_ka, n_band, k_dev)
    quads = k_points // 4
    state, coef = None, None
    for step in range(STEPS):
        first = step == 0
        qx, rho = call(
            functools.partial(density_kernel, cfg),
            "density",
            (
                shape_of((quads, 2 * LANES, 2 * LANES), BF),
                shape_of((devices, own // LANES, LANES)),
            ),
            [VMEM] * 2 + [ANY] * n_ka,
            (VMEM, VMEM),
            [
                pltpu.VMEM((quads, 2 * LANES, 2 * LANES), F32),
                pltpu.VMEM((n_ka, own_rows, own), BF),
                dma(n_ka),
            ],
            mib=8,
        )(msgs, val_own, *cond_own)
        density = exchange_all(rho)
        direct = call(
            functools.partial(direct_kernel, n_ka, tile, scale),
            "direct",
            shape_of((pairs, LANES, LANES)),
            [ANY] * (4 + len(cond_pts)),
            VMEM,
            [
                pltpu.VMEM((quads, 2 * LANES, 2 * LANES), BF),
                pltpu.VMEM((nu_blk, rows_all), BF),
                pltpu.VMEM((conds_all, mu_blk), BF),
                pltpu.VMEM((nu_blk, mu_blk), BF),
                pltpu.VMEM((rows_all, nu_blk), BF),
                pltpu.VMEM((nu_blk, conds_all), BF),
                pltpu.VMEM((nu_blk, mu_blk), BF),
                pltpu.VMEM((rows_all, mu_blk), BF),
                dma(1),
                dma(len(cond_pts) // 2, 2),
                dma(1),
                dma(2, nu_blk // tile),
            ],
            flops=4 * mu_blk * nu_blk * conds_all,
            moved=12 * MIB,
        )(val_turned, scr_turned, val_rows, qx, *cond_pts)
        parts = call(
            functools.partial(exchange_kernel, cfg, chunk, scale),
            "exchange",
            msg_shape,
            [ANY] * (4 + n_ka),
            VMEM,
            [
                pltpu.VMEM((devices, own // LANES, LANES), F32),
                pltpu.VMEM((pairs, LANES, LANES), F32),
                pltpu.VMEM((own, npt_all), BF),
                pltpu.VMEM((n_ka, own_rows, own), BF),
                pltpu.VMEM((rows_all, own), BF),
                pltpu.VMEM((pairs, LANES, LANES), F32),
                pltpu.VMEM((devices,) + block, F32),
                dma(npt_all // chunk),
                dma(n_ka),
                dma(3),
            ],
        )(density, direct, coulomb, val_own, *cond_own)
        recv = exchange_all(parts)
        if first:
            state, coef, message = call(
                functools.partial(first_owner_kernel, count_all),
                "first_owner",
                (shape_of((3,) + block), shape_of((3,)), msg_shape),
                [VMEM] * 4,
                (VMEM, SMEM, VMEM),
                mib=8,
            )(recv, msgs, gap, start_own)
        else:
            state, coef, message = call(
                functools.partial(second_owner_kernel, count_all),
                "second_owner",
                (shape_of((2,) + block), shape_of((4,)), shape_of((devices, 2, LANES))),
                [VMEM] * 4 + [SMEM],
                (VMEM, SMEM, VMEM),
                mib=8,
            )(recv, msgs, gap, state, coef)
        msgs = exchange_all(message)
    return call(
        functools.partial(finish_kernel, count_all),
        "finish",
        (shape_of(start_vec.shape), shape_of((2 * STEPS,))),
        [VMEM] * 2 + [SMEM],
        (VMEM, SMEM),
        mib=8,
    )(msgs, state, coef)


def array_path(start_vec, val_energy, cond_energy, val_orb, cond_orb, coulomb, screened):
    n_ka = lax.axis_size("ka")
    n_band = lax.axis_size("band")
    devices = n_ka * n_band
    ka, band = lax.axis_index("ka"), lax.axis_index("band")
    me = ka * n_band + band
    k_dev, pair_blk = start_vec.shape
    nv_blk = val_orb.shape[1]
    n_cond = cond_orb.shape[1]
    n_val = nv_blk * n_band
    npt_all = cond_orb.shape[2]
    k_points = k_dev * n_ka
    mu_blk, nu_blk = screened.shape
    own_pts = coulomb.shape[0]
    count_all = k_points * n_val * n_cond
    kernel_scale = 1.0 / (npt_all * math.sqrt(count_all))

    start_all = gather_all(start_vec, devices)
    val_cut = lax.all_to_all(
        val_orb.reshape(k_dev, nv_blk, n_ka, nu_blk).transpose(2, 0, 1, 3),
        "ka", split_axis=0, concat_axis=0, tiled=True,
    ).reshape(k_points, nv_blk, nu_blk)
    val_pts = lax.all_gather(val_cut, "band", axis=1, tiled=True)
    cond_local = lax.dynamic_slice_in_dim(cond_orb, band * mu_blk, mu_blk, 2)
    cond_pts = lax.all_gather(cond_local, "ka", axis=0, tiled=True)
    cond_rows = cond_orb.reshape(k_dev, n_cond, n_ka, n_band, own_pts)
    cond_rows = lax.dynamic_index_in_dim(cond_rows, band, 3, keepdims=False)
    cond_own = lax.all_to_all(
        cond_rows.transpose(2, 0, 1, 3), "ka", split_axis=0, concat_axis=0, tiled=True
    ).reshape(k_points, n_cond, own_pts)
    val_own = lax.dynamic_slice_in_dim(val_pts, band * own_pts, own_pts, 2)

    energy_gap = (cond_energy[:, None, :] - val_energy[:, :, None]).reshape(k_dev, pair_blk)
    start_sq = jnp.sum(start_all * start_all)
    current = start_all / jnp.sqrt(start_sq / count_all + 1e-06)
    previous = jnp.zeros_like(current)
    beta_val = jnp.float32(0.0)
    alphas = []
    betas = []
    for turn_index in range(STEPS):
        full_vec = (
            current.astype(BF)
            .reshape(n_ka, n_band, k_dev, nv_blk, n_cond)
            .transpose(0, 2, 1, 3, 4)
            .reshape(k_points, n_val, n_cond)
        )
        mixed_f = jnp.einsum("kvc,kvn->kcn", full_vec, val_pts, preferred_element_type=F32)
        mixed_own = lax.dynamic_slice_in_dim(mixed_f, band * own_pts, own_pts, 2)
        density_own = jnp.sum(mixed_own * cond_own.astype(F32), axis=(0, 1))
        density = gather_all(density_own.astype(BF), devices).reshape(npt_all)
        mixed_val = mixed_f.astype(BF)
        amp = jnp.einsum("kcm,kcn->mn", cond_pts, mixed_val, preferred_element_type=F32)
        kern = (screened.astype(F32) * amp * kernel_scale).astype(BF)
        folded = jnp.einsum("mn,kvn->kvm", kern, val_pts, preferred_element_type=F32).astype(BF)
        direct_part = jnp.einsum("kcm,kvm->kvc", cond_pts, folded, preferred_element_type=F32)
        potential = kernel_scale * jnp.dot(coulomb, density, preferred_element_type=F32)
        weighted = (val_own.astype(F32) * potential).astype(BF)
        exchange = jnp.einsum("kvp,kcp->kvc", weighted, cond_own, preferred_element_type=F32)
        part = 2.0 * exchange - direct_part
        arranged = (
            part.reshape(n_ka, k_dev, n_band, nv_blk, n_cond)
            .transpose(0, 2, 1, 3, 4)
            .reshape(devices, k_dev, pair_blk)
        )
        inter_own = jnp.sum(exchange_all(arranged), axis=0)
        current_own = lax.dynamic_index_in_dim(current, me, 0, keepdims=False)
        resid_vec = gather_all(energy_gap * current_own + inter_own, devices)
        resid_vec = resid_vec - beta_val * previous
        alpha_val = jnp.sum(current * resid_vec) / count_all
        resid_vec = resid_vec - alpha_val * current
        beta_val = jnp.sqrt(jnp.sum(resid_vec * resid_vec) / count_all + 1e-06)
        previous = current
        current = resid_vec / beta_val
        alphas.append(alpha_val)
        betas.append(beta_val)
    coeffs = jnp.stack(alphas + betas)
    return (lax.dynamic_index_in_dim(current, me, 0, keepdims=False), coeffs)


def per_device(*args):
    start_vec, _, _, val_orb, cond_orb, coulomb, screened = args
    n_ka, n_band = lax.axis_size("ka"), lax.axis_size("band")
    fits = (
        n_band == 8
        and n_ka & (n_ka - 1) == 0
        and start_vec.shape[0] % 2 == 1
        and val_orb.shape[1] == ROWS
        and cond_orb.shape[1] == HALF
        and start_vec.shape[0] * n_ka % 4 == 0
        and coulomb.shape[0] % LANES == 0
        and coulomb.shape[1] % 1024 == 0
        and screened.shape[0] % 512 == 0
        and screened.shape[1] % 1024 == 0
        and screened.shape[0] * screened.shape[1] <= 2 * MIB
    )
    return (kernel_path if fits else array_path)(*args)


def solution(mesh):
    in_specs = (
        P("ka", "band"),
        P("ka", "band"),
        P("ka", None),
        P("ka", "band", None),
        P("ka", None, None),
        P(("ka", "band"), None),
        P("band", "ka"),
    )
    out_specs = (P("ka", "band"), P())
    return jax.shard_map(
        per_device, mesh=mesh, in_specs=in_specs, out_specs=out_specs, check_vma=False
    )
```

```python
import functools
import math

import jax
import jax.numpy as jnp
from jax import lax
from jax.experimental import pallas as pl
from jax.experimental.pallas import tpu as pltpu
from jax.sharding import PartitionSpec as P

STEPS = 2
AXES = ("ka", "band")
BF, F32 = jnp.bfloat16, jnp.float32
LANES = 128
HALF = 64
ROWS = 8
MIB = 1 << 20

VMEM = pl.BlockSpec(memory_space=pltpu.VMEM)
SMEM = pl.BlockSpec(memory_space=pltpu.SMEM)
ANY = pl.BlockSpec(memory_space=pl.ANY)


def gather_all(block, devices):
    wide = jnp.broadcast_to(block[None], (devices,) + block.shape)
    return exchange_all(wide)


def exchange_all(parts):
    return lax.all_to_all(parts, AXES, split_axis=0, concat_axis=0, tiled=True)


def dot_nt(lhs, rhs):
    return lax.dot_general(lhs, rhs, (((1,), (1,)), ((), ())), preferred_element_type=F32)


def dot_tn(lhs, rhs):
    return lax.dot_general(lhs, rhs, (((0,), (0,)), ((), ())), preferred_element_type=F32)


def pack_vector(block, k_dev):
    groups = (k_dev + 1) // 2
    block = jnp.pad(block, ((0, 2 * groups - k_dev), (0, 0)))
    block = block.reshape(groups, 2, ROWS, HALF).transpose(0, 2, 1, 3)
    return block.reshape(groups * ROWS, LANES)


def lane_half(tile, have, want):
    if have != want:
        tile = pltpu.roll(tile, HALF, axis=1)
    lane = lax.broadcasted_iota(jnp.int32, tile.shape, 1)
    keep = lane < HALF if want == 0 else lane >= HALF
    return jnp.where(keep, tile, 0.0)


def with_sums(block, sums):
    row = lax.broadcasted_iota(jnp.int32, block.shape, 0)
    lane = lax.broadcasted_iota(jnp.int32, block.shape, 1)
    free = row == block.shape[0] - ROWS
    for i, total in enumerate(sums):
        rest = jnp.full(block.shape, total, F32)
        for part in range(3):
            piece = rest.astype(BF).astype(F32)
            block = jnp.where(free & (lane == HALF + 3 * i + part), piece, block)
            rest = rest - piece
    return block


def read_sums(msgs_ref, count):
    rows = msgs_ref.shape[1]
    tile = jnp.sum(msgs_ref[...].astype(F32), axis=0)[rows - ROWS :, :]
    row = lax.broadcasted_iota(jnp.int32, tile.shape, 0)
    lane = lax.broadcasted_iota(jnp.int32, tile.shape, 1)
    out = []
    for i in range(count):
        mine = (row == 0) & (lane >= HALF + 3 * i) & (lane < HALF + 3 * i + 3)
        out.append(jnp.sum(jnp.where(mine, tile, 0.0)))
    return out


def block_copies(groups, width, dest, sems, column=0):
    copies = []
    for d, refs in enumerate(groups):
        row = 0
        for ref in refs:
            copies.append(
                pltpu.make_async_copy(
                    ref.at[:, pl.ds(column, width)],
                    dest.at[d, pl.ds(row, ref.shape[0]), :],
                    sems.at[len(copies)],
                )
            )
            row += ref.shape[0]
    return copies


def split_refs(refs, counts):
    out, at = [], 0
    for count in counts:
        out.append(refs[at : at + count])
        at += count
    return out


def start_all(copies):
    for copy in copies:
        copy.start()


def wait_all(copies):
    for copy in copies:
        copy.wait()


def device_at(n_band, j, d):
    ka = jnp.bitwise_xor(lax.axis_index("ka"), j)
    return ka * n_band + jnp.bitwise_xor(lax.axis_index("band"), d)


def own_copies(ref, dest, sems):
    return [
        pltpu.make_async_copy(
            ref.at[jnp.bitwise_xor(lax.axis_index("ka"), j)], dest.at[j], sems.at[j]
        )
        for j in range(dest.shape[0])
    ]


def pair_rows(ref, kp):
    part = ref[:, kp * 2 * ROWS : (kp + 1) * 2 * ROWS, :]
    return part.reshape(part.shape[0] * 2 * ROWS, part.shape[2])


def pack_kernel(start_ref, gap_ref, own_ref, msg_ref):
    own_ref[...] = jnp.zeros_like(own_ref)
    for kl in range(start_ref.shape[0]):
        for j in range(ROWS // 2):
            row = start_ref[pl.ds(kl, 1), pl.ds(j * LANES, LANES)]
            for v in range(2):
                at = pl.ds(kl // 2 * ROWS + 2 * j + v, 1)
                own_ref[at, :] = own_ref[at, :] + lane_half(row, v, kl % 2)
    own = own_ref[...]
    square = own * own
    block = with_sums(own, [jnp.sum(square), jnp.sum(gap_ref[...] * square)])
    msg_ref[...] = block.astype(BF)


def cut_kernel(cond_ref, out_ref, sems):
    n_ka, _, own = out_ref.shape
    k_dev, n_cond, npt = cond_ref.shape
    copies = []
    for z in range(n_ka):
        at = z * (npt // n_ka) + lax.axis_index("band") * own
        for kl in range(k_dev):
            copies.append(
                pltpu.make_async_copy(
                    cond_ref.at[kl, :, pl.ds(pl.multiple_of(at, LANES), own)],
                    out_ref.at[z, pl.ds(kl * n_cond, n_cond), :],
                    sems.at[len(copies)],
                )
            )
    start_all(copies)
    wait_all(copies)


def turn_kernel(tile, scr_ref, out_ref, scrs, turned, in_sems, out_sems):
    nu = scr_ref.shape[1]
    ins, outs = [], []
    for j in range(nu // tile):
        at = pl.ds(j * tile, tile)
        ins.append(pltpu.make_async_copy(scr_ref.at[:, at], scrs.at[:, at], in_sems.at[j]))
        outs.append(pltpu.make_async_copy(turned.at[at, :], out_ref.at[at, :], out_sems.at[j]))
    start_all(ins)
    for j in range(nu // tile):
        ins[j].wait()
        turned[j * tile : (j + 1) * tile, :] = scrs[:, j * tile : (j + 1) * tile].T
        outs[j].start()
    wait_all(outs)


def order_kernel(counts, n_ka, *refs):
    n_val = sum(counts)
    val_refs, refs = split_refs(refs[:n_val], counts), refs[n_val:]
    rows_out, turned_out, own_out, msgs_out, vals, heads, ordered, turned, val_sems, out_sems = refs
    own = own_out.shape[1]
    nu = ordered.shape[1]
    copies = block_copies(val_refs, nu, vals, val_sems.at[0])
    head_copies = block_copies(val_refs, LANES, heads, val_sems.at[1], nu)
    start_all(copies + head_copies)
    wait_all(copies)
    n_band, group = vals.shape[0], vals.shape[0] * 2 * ROWS
    column = pl.multiple_of(lax.axis_index("band") * own, LANES)
    outs = []
    for kp in range(ordered.shape[0] // group):
        at = slice(kp * group, (kp + 1) * group)
        ordered[at, :] = pair_rows(vals, kp)
        turned[:, at] = ordered[at, :].T
        at = pl.ds(kp * group, group)
        outs += [
            pltpu.make_async_copy(ordered.at[at, :], rows_out.at[at, :], out_sems.at[0, kp]),
            pltpu.make_async_copy(turned.at[:, at], turned_out.at[:, at], out_sems.at[1, kp]),
            pltpu.make_async_copy(
                ordered.at[at, pl.ds(column, own)], own_out.at[at, :], out_sems.at[2, kp]
            ),
        ]
        start_all(outs[-3:])
    wait_all(head_copies)
    rows = msgs_out.shape[1]
    step = heads.shape[1] // n_ka
    for d in range(n_band):
        head = heads[d].astype(F32)
        for j in range(n_ka):
            msgs_out[device_at(n_band, j, d)] = head[j * step : j * step + rows, :].astype(BF)
    wait_all(outs)


def density_kernel(cfg, *refs):
    n_ka, n_band, k_dev = cfg
    k_points = n_ka * k_dev
    msgs_ref, vown_ref, cond_ref, qx_ref, rho_ref, xs, conds, cond_sems = refs
    own = vown_ref.shape[1]
    copies = own_copies(cond_ref, conds, cond_sems)
    start_all(copies)
    xs[...] = jnp.zeros_like(xs)
    for d in range(n_band):
        for k in range(k_points):
            j, kl = divmod(k, k_dev)
            tile = msgs_ref[device_at(n_band, j, d), :, :].astype(F32)
            tile = tile[kl // 2 * ROWS : (kl // 2 + 1) * ROWS, :]
            base = k // 2 % 2 * LANES
            at = pl.ds(base + d * 2 * ROWS + k % 2 * ROWS, ROWS)
            xs[k // 4, at, pl.ds(base, LANES)] = lane_half(tile, kl % 2, k % 2)
    qx_ref[...] = xs[...].astype(BF)
    wait_all(copies)
    cond_rows = conds[...].reshape(-1, own)
    rho = jnp.zeros((1, own), F32)
    quad = 2 * LANES
    for kq in range(k_points // 4):
        at = slice(kq * quad, (kq + 1) * quad)
        mixed = dot_tn(qx_ref[kq], vown_ref[at, :])
        rho = rho + jnp.sum(mixed * cond_rows[at, :].astype(F32), axis=0, keepdims=True)
    for r in range(own // LANES):
        part = rho[:, r * LANES : (r + 1) * LANES]
        rho_ref[:, r, :] = jnp.broadcast_to(part, (rho_ref.shape[0], LANES))


def direct_kernel(n_ka, tile, scale, *refs):
    turned_ref, scr_ref, rows_ref, qx_ref, refs = refs[0], refs[1], refs[2], refs[3], refs[4:]
    cond_refs, refs = refs[:n_ka], refs[n_ka:]
    di_ref, qx, turned, conds, scrs, vals, mixed, kern, folded = refs[:9]
    qx_sem, cond_sems, row_sem, chunk_sems = refs[9:]
    nu, mu = scr_ref.shape
    quad = 2 * LANES
    qx_copy = pltpu.make_async_copy(qx_ref, qx, qx_sem.at[0])
    cond_copies = block_copies([[ref] for ref in cond_refs], mu, conds, cond_sems)
    turned_copies, scr_copies = [], []
    for i in range(nu // tile):
        at = pl.ds(i * tile, tile)
        turned_copies.append(
            pltpu.make_async_copy(turned_ref.at[at, :], turned.at[at, :], chunk_sems.at[0, i])
        )
        scr_copies.append(
            pltpu.make_async_copy(scr_ref.at[at, :], scrs.at[at, :], chunk_sems.at[1, i])
        )
    row_copy = pltpu.make_async_copy(rows_ref, vals, row_sem.at[0])
    start_all([qx_copy, turned_copies[0]] + cond_copies + [scr_copies[0]])
    for i in range(1, nu // tile):
        start_all([turned_copies[i], scr_copies[i]])
    row_copy.start()
    qx_copy.wait()
    for i in range(nu // tile):
        rows = slice(i * tile, (i + 1) * tile)
        turned_copies[i].wait()
        for kq in range(qx.shape[0]):
            cols = slice(kq * quad, (kq + 1) * quad)
            mixed[rows, cols] = jnp.dot(
                turned[rows, cols], qx[kq], preferred_element_type=F32
            ).astype(BF)
        if i == 0:
            wait_all(cond_copies)
            cond_rows = conds[...].reshape(-1, mu)
        scr_copies[i].wait()
        amp = jnp.dot(mixed[rows, :], cond_rows, preferred_element_type=F32)
        kern[rows, :] = (scrs[rows, :].astype(F32) * amp * scale).astype(BF)
    row_copy.wait()
    for m in range(mu // quad):
        cols = slice(m * quad, (m + 1) * quad)
        folded[:, cols] = jnp.dot(vals[...], kern[:, cols], preferred_element_type=F32).astype(BF)
    for kp in range(di_ref.shape[0]):
        at = slice(kp * LANES, (kp + 1) * LANES)
        di_ref[kp] = dot_nt(folded[at, :], cond_rows[at, :])


def exchange_kernel(cfg, chunk, scale, *refs):
    n_ka, n_band, k_dev = cfg
    k_points = n_ka * k_dev
    rho_ref, di_ref, coul_ref, vown_ref, cond_ref, refs = refs[:5] + (refs[5:],)
    msg_ref, rhos, di, coul, conds, vown, part, msg, coul_sems, cond_sems, sems = refs
    own, npt = coul_ref.shape
    coul_copies = [
        pltpu.make_async_copy(
            coul_ref.at[:, pl.ds(i * chunk, chunk)], coul.at[:, pl.ds(i * chunk, chunk)], coul_sems.at[i]
        )
        for i in range(npt // chunk)
    ]
    rho_copy = pltpu.make_async_copy(rho_ref, rhos, sems.at[0])
    copies = own_copies(cond_ref, conds, cond_sems)
    copies.append(pltpu.make_async_copy(vown_ref, vown, sems.at[1]))
    copies.append(pltpu.make_async_copy(di_ref, di, sems.at[2]))
    start_all([rho_copy] + coul_copies + copies)
    rho_copy.wait()
    acc = jnp.zeros((own, LANES), F32)
    per_dev = own // LANES
    for i in range(npt // chunk):
        coul_copies[i].wait()
        for j in range(i * chunk // LANES, (i + 1) * chunk // LANES):
            rho = rhos[j // per_dev, pl.ds(j % per_dev, 1), :].astype(BF).astype(F32)
            acc = acc + coul[:, j * LANES : (j + 1) * LANES].astype(F32) * rho
    potential = scale * jnp.sum(acc.T, axis=0, keepdims=True)
    wait_all(copies)
    cond_rows = conds[...].reshape(-1, own)
    for kp in range(k_points // 2):
        at = slice(kp * LANES, (kp + 1) * LANES)
        weighted = (vown[at, :].astype(F32) * potential).astype(BF)
        part[kp] = 2.0 * dot_nt(weighted, cond_rows[at, :]) - di[kp]
    for d in range(n_band):
        for j in range(n_ka):
            for g in range((k_dev + 1) // 2):
                tile = None
                for kl in range(2 * g, min(2 * g + 2, k_dev)):
                    k = j * k_dev + kl
                    piece = part[k // 2, pl.ds(d * 2 * ROWS + k % 2 * ROWS, ROWS), :]
                    piece = lane_half(piece, k % 2, kl % 2)
                    tile = piece if tile is None else tile + piece
                msg[device_at(n_band, j, d), pl.ds(g * ROWS, ROWS), :] = tile
    msg_ref[...] = msg[...].astype(BF)


def received(recv_ref):
    return jnp.sum(recv_ref[...].astype(F32), axis=0)


def shifted(count_all, shift, square, cross_sum, square_sum):
    alpha = shift * square + cross_sum / count_all
    d = alpha - shift
    mean_sq = (square_sum - 2.0 * d * cross_sum) / count_all + d * d * square
    mean_sq = jnp.maximum(mean_sq, 0.0)
    return alpha, d, mean_sq


def first_owner_kernel(count_all, recv_ref, msgs_ref, gap_ref, own_ref, state_ref, coef_ref, msg_ref):
    start_sq, gap_sq = read_sums(msgs_ref, 2)
    norm = start_sq / count_all
    inv = 1.0 / jnp.sqrt(norm + 1e-06)
    square = norm / (norm + 1e-06)
    shift = gap_sq / jnp.maximum(start_sq, 1e-30)
    cur = own_ref[...] * inv
    inter = received(recv_ref) * inv
    gap = gap_ref[...]
    resid = (gap - shift) * cur + inter
    state_ref[0] = cur
    state_ref[1] = resid
    state_ref[2] = inter
    coef_ref[0] = shift
    coef_ref[1] = square
    coef_ref[2] = gap_sq * inv * inv
    sums = [
        jnp.sum(cur * resid),
        jnp.sum(resid * resid),
        jnp.sum(gap * resid * resid),
        jnp.sum(gap * resid * cur),
    ]
    msg_ref[...] = jnp.broadcast_to(with_sums(resid, sums).astype(BF)[None], msg_ref.shape)


def second_owner_kernel(count_all, recv_ref, msgs_ref, gap_ref, state_ref, coef_ref, out_ref, coef_out, msg_ref):
    cross, total, gap_rr, gap_rq = read_sums(msgs_ref, 4)
    alpha, d, mean_sq = shifted(count_all, coef_ref[0], coef_ref[1], cross, total)
    beta = jnp.sqrt(mean_sq + 1e-06)
    square = mean_sq / (mean_sq + 1e-06)
    gap_qq = gap_rr - 2.0 * d * gap_rq + d * d * coef_ref[2]
    shift = gap_qq / (mean_sq + 1e-06) / count_all
    prev = state_ref[0]
    cur = (state_ref[1] - d * prev) / beta
    inter = (received(recv_ref) - d * state_ref[2]) / beta
    resid = (gap_ref[...] - shift) * cur + inter - beta * prev
    out_ref[0] = cur
    out_ref[1] = resid
    coef_out[0] = alpha
    coef_out[1] = beta
    coef_out[2] = shift
    coef_out[3] = square
    dims = msg_ref.shape[:1] + msg_ref.shape[2:]
    msg_ref[:, 0, :] = jnp.full(dims, jnp.sum(cur * resid), F32)
    msg_ref[:, 1, :] = jnp.full(dims, jnp.sum(resid * resid), F32)


def finish_kernel(count_all, msgs_ref, state_ref, coef_ref, out_ref, coeffs_ref):
    sums = jnp.sum(msgs_ref[...], axis=0)
    alpha, d, mean_sq = shifted(count_all, coef_ref[2], coef_ref[3], sums[0, 0], sums[1, 0])
    beta = jnp.sqrt(mean_sq + 1e-06)
    own = (state_ref[1] - d * state_ref[0]) / beta
    coeffs_ref[0] = coef_ref[0]
    coeffs_ref[1] = alpha
    coeffs_ref[2] = coef_ref[1]
    coeffs_ref[3] = beta
    for kl in range(out_ref.shape[0]):
        tile = own[kl // 2 * ROWS : (kl // 2 + 1) * ROWS, :]
        other = pltpu.roll(tile, HALF, axis=1)
        left, right = (tile, other) if kl % 2 == 0 else (other, tile)
        low = lax.broadcasted_iota(jnp.int32, (1, LANES), 1) < HALF
        for j in range(ROWS // 2):
            row = jnp.where(low, left[2 * j : 2 * j + 1], right[2 * j + 1 : 2 * j + 2])
            out_ref[pl.ds(kl, 1), pl.ds(j * LANES, LANES)] = row


def shape_of(dims, kind=F32):
    return jax.ShapeDtypeStruct(dims, kind)


def call(kernel, name, out_shape, in_specs, out_specs, scratch=(), mib=58, flops=0, moved=0):
    return pl.pallas_call(
        kernel,
        out_shape=out_shape,
        in_specs=in_specs,
        out_specs=out_specs,
        scratch_shapes=list(scratch),
        compiler_params=pltpu.CompilerParams(vmem_limit_bytes=mib * MIB),
        cost_estimate=pl.CostEstimate(flops=flops, bytes_accessed=moved, transcendentals=0),
        name=name,
    )


def dma(*dims):
    return pltpu.SemaphoreType.DMA(dims)


def swap(block, axis, d):
    return lax.ppermute(block, axis, [(i, i ^ d) for i in range(lax.axis_size(axis))])


def plane_pieces(own_piece, others):
    def move(block, d):
        return swap(block, "band", d)

    half = own_piece.shape[0] // 2
    core, by_x, by_y = move(own_piece, 1), move(own_piece, 2), move(own_piece, 4)
    by_x, by_y, others = lax.optimization_barrier((by_x, by_y, others))
    diag = [move(by_x[:half], 4), move(by_y[half:], 2)]
    pieces = [[own_piece], [core], [by_x], [move(by_x, 1)], [by_y], [move(by_y, 1)]]
    return pieces + [diag, [move(part, 1) for part in diag]], others


def kernel_path(start_vec, val_energy, cond_energy, val_orb, cond_orb, coulomb, screened):
    n_ka = lax.axis_size("ka")
    n_band = lax.axis_size("band")
    devices = n_ka * n_band
    ka, band = lax.axis_index("ka"), lax.axis_index("band")
    k_dev = start_vec.shape[0]
    nv_blk = val_orb.shape[1]
    n_cond = cond_orb.shape[1]
    npt_all = cond_orb.shape[2]
    k_points = k_dev * n_ka
    pairs = k_points // 2
    mu_blk, nu_blk = screened.shape
    own = coulomb.shape[0]
    count_all = k_points * nv_blk * n_band * n_cond
    scale = 1.0 / (npt_all * math.sqrt(count_all))
    piece_rows = k_points * nv_blk

    gap = (cond_energy[:, None, :] - val_energy[:, :, None]).reshape(k_dev, nv_blk * n_cond)
    gap = pack_vector(gap, k_dev)
    block = gap.shape
    msg_shape = shape_of((devices,) + block, BF)
    start_own, message = call(
        pack_kernel, "pack", (shape_of(block), shape_of(block, BF)), [VMEM] * 2, (VMEM, VMEM), mib=8
    )(start_vec, gap)

    head = jnp.pad(message, ((0, k_dev * nv_blk - block[0]), (0, 0)))

    def val_to(j):
        part = lax.dynamic_slice_in_dim(val_orb, jnp.bitwise_xor(ka, j) * nu_blk, nu_blk, 2)
        return jnp.concatenate([part.reshape(k_dev * nv_blk, nu_blk), head], axis=1)

    val_cut = jnp.concatenate(
        [val_to(0)] + [swap(val_to(j), "ka", j) for j in range(1, n_ka)], axis=0
    )
    cond_local = lax.dynamic_slice_in_dim(cond_orb, band * mu_blk, mu_blk, 2)
    cond_local = cond_local.reshape(k_dev * n_cond, mu_blk)
    cond_pts = [cond_local] + [swap(cond_local, "ka", j) for j in range(1, n_ka)]
    own_rows = k_dev * n_cond
    cuts = call(
        cut_kernel,
        "cut",
        shape_of((n_ka, own_rows, own), BF),
        [ANY],
        VMEM,
        [dma(n_ka * k_dev)],
    )(cond_orb)
    cond_own = lax.all_to_all(cuts, "ka", split_axis=0, concat_axis=0, tiled=True)

    chunk, tile = 1024, 1024
    rows_all, conds_all = k_points * nv_blk * n_band, k_points * n_cond
    scr_turned = call(
        functools.partial(turn_kernel, tile // 2),
        "turn",
        shape_of((nu_blk, mu_blk), BF),
        [ANY],
        ANY,
        [pltpu.VMEM((mu_blk, nu_blk), BF), pltpu.VMEM((nu_blk, mu_blk), BF)]
        + [dma(2 * nu_blk // tile)] * 2,
        moved=8 * MIB,
    )(screened)
    pieces, (scr_turned, cond_pts[1 : n_ka - 1]) = plane_pieces(
        val_cut, (scr_turned, cond_pts[1 : n_ka - 1])
    )
    counts = tuple(len(piece) for piece in pieces)
    flat = [ref for piece in pieces for ref in piece]
    n_copies = len(flat)
    val_rows, val_turned, val_own, msgs = call(
        functools.partial(order_kernel, counts, n_ka),
        "order",
        (
            shape_of((rows_all, nu_blk), BF),
            shape_of((nu_blk, rows_all), BF),
            shape_of((rows_all, own), BF),
            msg_shape,
        ),
        [ANY] * n_copies,
        (ANY, ANY, ANY, VMEM),
        [
            pltpu.VMEM((n_band, piece_rows, nu_blk), BF),
            pltpu.VMEM((n_band, piece_rows, LANES), BF),
            pltpu.VMEM((rows_all, nu_blk), BF),
            pltpu.VMEM((nu_blk, rows_all), BF),
            dma(2, n_copies),
            dma(3, pairs),
        ],
        moved=9 * MIB,
    )(*flat)

    cfg = (n_ka, n_band, k_dev)
    quads = k_points // 4
    state, coef = None, None
    for step in range(STEPS):
        first = step == 0
        qx, rho = call(
            functools.partial(density_kernel, cfg),
            "density",
            (
                shape_of((quads, 2 * LANES, 2 * LANES), BF),
                shape_of((devices, own // LANES, LANES)),
            ),
            [VMEM] * 2 + [ANY],
            (VMEM, VMEM),
            [
                pltpu.VMEM((quads, 2 * LANES, 2 * LANES), F32),
                pltpu.VMEM((n_ka, own_rows, own), BF),
                dma(n_ka),
            ],
            mib=8,
        )(msgs, val_own, cond_own)
        density = exchange_all(rho)
        direct = call(
            functools.partial(direct_kernel, n_ka, tile, scale),
            "direct",
            shape_of((pairs, LANES, LANES)),
            [ANY] * (4 + len(cond_pts)),
            VMEM,
            [
                pltpu.VMEM((quads, 2 * LANES, 2 * LANES), BF),
                pltpu.VMEM((nu_blk, rows_all), BF),
                pltpu.VMEM((n_ka, own_rows, mu_blk), BF),
                pltpu.VMEM((nu_blk, mu_blk), BF),
                pltpu.VMEM((rows_all, nu_blk), BF),
                pltpu.VMEM((nu_blk, conds_all), BF),
                pltpu.VMEM((nu_blk, mu_blk), BF),
                pltpu.VMEM((rows_all, mu_blk), BF),
                dma(1),
                dma(n_ka),
                dma(1),
                dma(2, nu_blk // tile),
            ],
            flops=4 * mu_blk * nu_blk * conds_all,
            moved=12 * MIB,
        )(val_turned, scr_turned, val_rows, qx, *cond_pts)
        parts = call(
            functools.partial(exchange_kernel, cfg, chunk, scale),
            "exchange",
            msg_shape,
            [ANY] * 5,
            VMEM,
            [
                pltpu.VMEM((devices, own // LANES, LANES), F32),
                pltpu.VMEM((pairs, LANES, LANES), F32),
                pltpu.VMEM((own, npt_all), BF),
                pltpu.VMEM((n_ka, own_rows, own), BF),
                pltpu.VMEM((rows_all, own), BF),
                pltpu.VMEM((pairs, LANES, LANES), F32),
                pltpu.VMEM((devices,) + block, F32),
                dma(npt_all // chunk),
                dma(n_ka),
                dma(3),
            ],
        )(density, direct, coulomb, val_own, cond_own)
        recv = exchange_all(parts)
        if first:
            state, coef, message = call(
                functools.partial(first_owner_kernel, count_all),
                "first_owner",
                (shape_of((3,) + block), shape_of((3,)), msg_shape),
                [VMEM] * 4,
                (VMEM, SMEM, VMEM),
                mib=8,
            )(recv, msgs, gap, start_own)
        else:
            state, coef, message = call(
                functools.partial(second_owner_kernel, count_all),
                "second_owner",
                (shape_of((2,) + block), shape_of((4,)), shape_of((devices, 2, LANES))),
                [VMEM] * 4 + [SMEM],
                (VMEM, SMEM, VMEM),
                mib=8,
            )(recv, msgs, gap, state, coef)
        msgs = exchange_all(message)
    return call(
        functools.partial(finish_kernel, count_all),
        "finish",
        (shape_of(start_vec.shape), shape_of((2 * STEPS,))),
        [VMEM] * 2 + [SMEM],
        (VMEM, SMEM),
        mib=8,
    )(msgs, state, coef)


def array_path(start_vec, val_energy, cond_energy, val_orb, cond_orb, coulomb, screened):
    n_ka = lax.axis_size("ka")
    n_band = lax.axis_size("band")
    devices = n_ka * n_band
    ka, band = lax.axis_index("ka"), lax.axis_index("band")
    me = ka * n_band + band
    k_dev, pair_blk = start_vec.shape
    nv_blk = val_orb.shape[1]
    n_cond = cond_orb.shape[1]
    n_val = nv_blk * n_band
    npt_all = cond_orb.shape[2]
    k_points = k_dev * n_ka
    mu_blk, nu_blk = screened.shape
    own_pts = coulomb.shape[0]
    count_all = k_points * n_val * n_cond
    kernel_scale = 1.0 / (npt_all * math.sqrt(count_all))

    start_all = gather_all(start_vec, devices)
    val_cut = lax.all_to_all(
        val_orb.reshape(k_dev, nv_blk, n_ka, nu_blk).transpose(2, 0, 1, 3),
        "ka", split_axis=0, concat_axis=0, tiled=True,
    ).reshape(k_points, nv_blk, nu_blk)
    val_pts = lax.all_gather(val_cut, "band", axis=1, tiled=True)
    cond_local = lax.dynamic_slice_in_dim(cond_orb, band * mu_blk, mu_blk, 2)
    cond_pts = lax.all_gather(cond_local, "ka", axis=0, tiled=True)
    cond_rows = cond_orb.reshape(k_dev, n_cond, n_ka, n_band, own_pts)
    cond_rows = lax.dynamic_index_in_dim(cond_rows, band, 3, keepdims=False)
    cond_own = lax.all_to_all(
        cond_rows.transpose(2, 0, 1, 3), "ka", split_axis=0, concat_axis=0, tiled=True
    ).reshape(k_points, n_cond, own_pts)
    val_own = lax.dynamic_slice_in_dim(val_pts, band * own_pts, own_pts, 2)

    energy_gap = (cond_energy[:, None, :] - val_energy[:, :, None]).reshape(k_dev, pair_blk)
    start_sq = jnp.sum(start_all * start_all)
    current = start_all / jnp.sqrt(start_sq / count_all + 1e-06)
    previous = jnp.zeros_like(current)
    beta_val = jnp.float32(0.0)
    alphas = []
    betas = []
    for turn_index in range(STEPS):
        full_vec = (
            current.astype(BF)
            .reshape(n_ka, n_band, k_dev, nv_blk, n_cond)
            .transpose(0, 2, 1, 3, 4)
            .reshape(k_points, n_val, n_cond)
        )
        mixed_f = jnp.einsum("kvc,kvn->kcn", full_vec, val_pts, preferred_element_type=F32)
        mixed_own = lax.dynamic_slice_in_dim(mixed_f, band * own_pts, own_pts, 2)
        density_own = jnp.sum(mixed_own * cond_own.astype(F32), axis=(0, 1))
        density = gather_all(density_own.astype(BF), devices).reshape(npt_all)
        mixed_val = mixed_f.astype(BF)
        amp = jnp.einsum("kcm,kcn->mn", cond_pts, mixed_val, preferred_element_type=F32)
        kern = (screened.astype(F32) * amp * kernel_scale).astype(BF)
        folded = jnp.einsum("mn,kvn->kvm", kern, val_pts, preferred_element_type=F32).astype(BF)
        direct_part = jnp.einsum("kcm,kvm->kvc", cond_pts, folded, preferred_element_type=F32)
        potential = kernel_scale * jnp.dot(coulomb, density, preferred_element_type=F32)
        weighted = (val_own.astype(F32) * potential).astype(BF)
        exchange = jnp.einsum("kvp,kcp->kvc", weighted, cond_own, preferred_element_type=F32)
        part = 2.0 * exchange - direct_part
        arranged = (
            part.reshape(n_ka, k_dev, n_band, nv_blk, n_cond)
            .transpose(0, 2, 1, 3, 4)
            .reshape(devices, k_dev, pair_blk)
        )
        inter_own = jnp.sum(exchange_all(arranged), axis=0)
        current_own = lax.dynamic_index_in_dim(current, me, 0, keepdims=False)
        resid_vec = gather_all(energy_gap * current_own + inter_own, devices)
        resid_vec = resid_vec - beta_val * previous
        alpha_val = jnp.sum(current * resid_vec) / count_all
        resid_vec = resid_vec - alpha_val * current
        beta_val = jnp.sqrt(jnp.sum(resid_vec * resid_vec) / count_all + 1e-06)
        previous = current
        current = resid_vec / beta_val
        alphas.append(alpha_val)
        betas.append(beta_val)
    coeffs = jnp.stack(alphas + betas)
    return (lax.dynamic_index_in_dim(current, me, 0, keepdims=False), coeffs)


def per_device(*args):
    start_vec, _, _, val_orb, cond_orb, coulomb, screened = args
    n_ka, n_band = lax.axis_size("ka"), lax.axis_size("band")
    fits = (
        n_band == 8
        and n_ka & (n_ka - 1) == 0
        and start_vec.shape[0] % 2 == 1
        and val_orb.shape[1] == ROWS
        and cond_orb.shape[1] == HALF
        and start_vec.shape[0] * n_ka % 4 == 0
        and coulomb.shape[0] % LANES == 0
        and coulomb.shape[1] % 1024 == 0
        and screened.shape[0] % 512 == 0
        and screened.shape[1] % 1024 == 0
        and screened.shape[0] * screened.shape[1] <= 2 * MIB
    )
    return (kernel_path if fits else array_path)(*args)


def solution(mesh):
    in_specs = (
        P("ka", "band"),
        P("ka", "band"),
        P("ka", None),
        P("ka", "band", None),
        P("ka", None, None),
        P(("ka", "band"), None),
        P("band", "ka"),
    )
    out_specs = (P("ka", "band"), P())
    return jax.shard_map(
        per_device, mesh=mesh, in_specs=in_specs, out_specs=out_specs, check_vma=False
    )
```

```python
import functools
import math

import jax
import jax.numpy as jnp
from jax import lax
from jax.experimental import pallas as pl
from jax.experimental.pallas import tpu as pltpu
from jax.sharding import PartitionSpec as P

STEPS = 2
AXES = ("ka", "band")
BF, F32 = jnp.bfloat16, jnp.float32
LANES = 128
HALF = 64
ROWS = 8
MIB = 1 << 20

VMEM = pl.BlockSpec(memory_space=pltpu.VMEM)
SMEM = pl.BlockSpec(memory_space=pltpu.SMEM)
ANY = pl.BlockSpec(memory_space=pl.ANY)


def gather_all(block, devices):
    wide = jnp.broadcast_to(block[None], (devices,) + block.shape)
    return exchange_all(wide)


def exchange_all(parts):
    return lax.all_to_all(parts, AXES, split_axis=0, concat_axis=0, tiled=True)


def dot_nt(lhs, rhs):
    return lax.dot_general(lhs, rhs, (((1,), (1,)), ((), ())), preferred_element_type=F32)


def dot_tn(lhs, rhs):
    return lax.dot_general(lhs, rhs, (((0,), (0,)), ((), ())), preferred_element_type=F32)


def lane_half(tile, have, want):
    if have != want:
        tile = pltpu.roll(tile, HALF, axis=1)
    lane = lax.broadcasted_iota(jnp.int32, tile.shape, 1)
    keep = lane < HALF if want == 0 else lane >= HALF
    return jnp.where(keep, tile, 0.0)


def with_sums(block, sums):
    row = lax.broadcasted_iota(jnp.int32, block.shape, 0)
    lane = lax.broadcasted_iota(jnp.int32, block.shape, 1)
    free = row == block.shape[0] - ROWS
    for i, total in enumerate(sums):
        rest = jnp.full(block.shape, total, F32)
        for part in range(3):
            piece = rest.astype(BF).astype(F32)
            block = jnp.where(free & (lane == HALF + 3 * i + part), piece, block)
            rest = rest - piece
    return block


def read_sums(msgs_ref, count):
    rows = msgs_ref.shape[1]
    tile = jnp.sum(msgs_ref[...].astype(F32), axis=0)[rows - ROWS :, :]
    row = lax.broadcasted_iota(jnp.int32, tile.shape, 0)
    lane = lax.broadcasted_iota(jnp.int32, tile.shape, 1)
    out = []
    for i in range(count):
        mine = (row == 0) & (lane >= HALF + 3 * i) & (lane < HALF + 3 * i + 3)
        out.append(jnp.sum(jnp.where(mine, tile, 0.0)))
    return out


def block_copies(groups, width, dest, sems, column=0):
    copies = []
    for d, refs in enumerate(groups):
        row = 0
        for ref in refs:
            copies.append(
                pltpu.make_async_copy(
                    ref.at[:, pl.ds(column, width)],
                    dest.at[d, pl.ds(row, ref.shape[0]), :],
                    sems.at[len(copies)],
                )
            )
            row += ref.shape[0]
    return copies


def split_refs(refs, counts):
    out, at = [], 0
    for count in counts:
        out.append(refs[at : at + count])
        at += count
    return out


def start_all(copies):
    for copy in copies:
        copy.start()


def wait_all(copies):
    for copy in copies:
        copy.wait()


def device_at(n_band, j, d):
    ka = jnp.bitwise_xor(lax.axis_index("ka"), j)
    return ka * n_band + jnp.bitwise_xor(lax.axis_index("band"), d)


def own_copies(ref, dest, sems):
    return [
        pltpu.make_async_copy(
            ref.at[jnp.bitwise_xor(lax.axis_index("ka"), j)], dest.at[j], sems.at[j]
        )
        for j in range(dest.shape[0])
    ]


def pair_rows(ref, kp):
    part = ref[:, kp * 2 * ROWS : (kp + 1) * 2 * ROWS, :]
    return part.reshape(part.shape[0] * 2 * ROWS, part.shape[2])


def pack_kernel(start_ref, cond_ref, val_ref, own_ref, gap_ref, msg_ref):
    own_ref[...] = jnp.zeros_like(own_ref)
    gap_ref[...] = jnp.zeros_like(gap_ref)
    cond = jnp.concatenate([cond_ref[...], cond_ref[...]], axis=1)
    for kl in range(start_ref.shape[0]):
        half = kl % 2
        for v in range(ROWS):
            at = pl.ds(kl // 2 * ROWS + v, 1)
            row = start_ref[pl.ds(kl, 1), pl.ds(v // 2 * LANES, LANES)]
            own_ref[at, :] = own_ref[at, :] + lane_half(row, v % 2, half)
            gap = cond[kl : kl + 1, :] - val_ref[kl, v]
            gap_ref[at, :] = gap_ref[at, :] + lane_half(gap, half, half)
    own = own_ref[...]
    square = own * own
    block = with_sums(own, [jnp.sum(square), jnp.sum(gap_ref[...] * square)])
    msg_ref[...] = block.astype(BF)


def cut_kernel(cond_ref, out_ref, sems):
    n_ka, _, own = out_ref.shape
    k_dev, n_cond, npt = cond_ref.shape
    copies = []
    for z in range(n_ka):
        at = z * (npt // n_ka) + lax.axis_index("band") * own
        for kl in range(k_dev):
            copies.append(
                pltpu.make_async_copy(
                    cond_ref.at[kl, :, pl.ds(pl.multiple_of(at, LANES), own)],
                    out_ref.at[z, pl.ds(kl * n_cond, n_cond), :],
                    sems.at[len(copies)],
                )
            )
    start_all(copies)
    wait_all(copies)


def turn_kernel(tile, scr_ref, out_ref, scrs, turned, in_sems, out_sems):
    nu = scr_ref.shape[1]
    ins, outs = [], []
    for j in range(nu // tile):
        at = pl.ds(j * tile, tile)
        ins.append(pltpu.make_async_copy(scr_ref.at[:, at], scrs.at[:, at], in_sems.at[j]))
        outs.append(pltpu.make_async_copy(turned.at[at, :], out_ref.at[at, :], out_sems.at[j]))
    start_all(ins)
    for j in range(nu // tile):
        ins[j].wait()
        turned[j * tile : (j + 1) * tile, :] = scrs[:, j * tile : (j + 1) * tile].T
        outs[j].start()
    wait_all(outs)


def order_kernel(counts, n_ka, *refs):
    n_val = sum(counts)
    val_refs, refs = split_refs(refs[:n_val], counts), refs[n_val:]
    rows_out, turned_out, own_out, msgs_out, vals, heads, ordered, turned, val_sems, out_sems = refs
    own = own_out.shape[1]
    nu = ordered.shape[1]
    copies = block_copies(val_refs, nu, vals, val_sems.at[0])
    head_copies = block_copies(val_refs, LANES, heads, val_sems.at[1], nu)
    start_all(copies + head_copies)
    wait_all(copies)
    n_band, group = vals.shape[0], vals.shape[0] * 2 * ROWS
    column = pl.multiple_of(lax.axis_index("band") * own, LANES)
    outs = []
    for kp in range(ordered.shape[0] // group):
        at = slice(kp * group, (kp + 1) * group)
        ordered[at, :] = pair_rows(vals, kp)
        turned[:, at] = ordered[at, :].T
        at = pl.ds(kp * group, group)
        outs += [
            pltpu.make_async_copy(ordered.at[at, :], rows_out.at[at, :], out_sems.at[0, kp]),
            pltpu.make_async_copy(turned.at[:, at], turned_out.at[:, at], out_sems.at[1, kp]),
            pltpu.make_async_copy(
                ordered.at[at, pl.ds(column, own)], own_out.at[at, :], out_sems.at[2, kp]
            ),
        ]
        start_all(outs[-3:])
    wait_all(head_copies)
    rows = msgs_out.shape[1]
    step = heads.shape[1] // n_ka
    for d in range(n_band):
        head = heads[d].astype(F32)
        for j in range(n_ka):
            msgs_out[device_at(n_band, j, d)] = head[j * step : j * step + rows, :].astype(BF)
    wait_all(outs)


def density_kernel(cfg, *refs):
    n_ka, n_band, k_dev = cfg
    k_points = n_ka * k_dev
    msgs_ref, vown_ref, cond_ref, qx_ref, rho_ref = refs[:5]
    xs, msgs, vown, conds, cond_sems, sems = refs[5:]
    own = vown_ref.shape[1]
    msg_copy = pltpu.make_async_copy(msgs_ref, msgs, sems.at[0])
    copies = own_copies(cond_ref, conds, cond_sems)
    copies.append(pltpu.make_async_copy(vown_ref, vown, sems.at[1]))
    start_all([msg_copy] + copies)
    xs[...] = jnp.zeros_like(xs)
    msg_copy.wait()
    for d in range(n_band):
        for k in range(k_points):
            j, kl = divmod(k, k_dev)
            tile = msgs[device_at(n_band, j, d), :, :].astype(F32)
            tile = tile[kl // 2 * ROWS : (kl // 2 + 1) * ROWS, :]
            base = k // 2 % 2 * LANES
            at = pl.ds(base + d * 2 * ROWS + k % 2 * ROWS, ROWS)
            xs[k // 4, at, pl.ds(base, LANES)] = lane_half(tile, kl % 2, k % 2)
    qx_ref[...] = xs[...].astype(BF)
    wait_all(copies)
    cond_rows = conds[...].reshape(-1, own)
    rho = jnp.zeros((1, own), F32)
    quad = 2 * LANES
    for kq in range(k_points // 4):
        at = slice(kq * quad, (kq + 1) * quad)
        mixed = dot_tn(qx_ref[kq], vown[at, :])
        rho = rho + jnp.sum(mixed * cond_rows[at, :].astype(F32), axis=0, keepdims=True)
    for r in range(own // LANES):
        part = rho[:, r * LANES : (r + 1) * LANES]
        rho_ref[:, r, :] = jnp.broadcast_to(part, (rho_ref.shape[0], LANES))


def direct_kernel(n_ka, tile, scale, *refs):
    turned_ref, scr_ref, rows_ref, qx_ref, refs = refs[0], refs[1], refs[2], refs[3], refs[4:]
    cond_refs, refs = refs[:n_ka], refs[n_ka:]
    di_ref, qx, turned, conds, scrs, vals, mixed, kern, folded = refs[:9]
    qx_sem, cond_sems, row_sem, chunk_sems = refs[9:]
    nu, mu = scr_ref.shape
    quad = 2 * LANES
    qx_copy = pltpu.make_async_copy(qx_ref, qx, qx_sem.at[0])
    cond_copies = block_copies([[ref] for ref in cond_refs], mu, conds, cond_sems)
    turned_copies, scr_copies = [], []
    for i in range(nu // tile):
        at = pl.ds(i * tile, tile)
        turned_copies.append(
            pltpu.make_async_copy(turned_ref.at[at, :], turned.at[at, :], chunk_sems.at[0, i])
        )
        scr_copies.append(
            pltpu.make_async_copy(scr_ref.at[at, :], scrs.at[at, :], chunk_sems.at[1, i])
        )
    row_copy = pltpu.make_async_copy(rows_ref, vals, row_sem.at[0])
    start_all([qx_copy, turned_copies[0]] + cond_copies + [scr_copies[0]])
    for i in range(1, nu // tile):
        start_all([turned_copies[i], scr_copies[i]])
    row_copy.start()
    qx_copy.wait()
    for i in range(nu // tile):
        rows = slice(i * tile, (i + 1) * tile)
        turned_copies[i].wait()
        for kq in range(qx.shape[0]):
            cols = slice(kq * quad, (kq + 1) * quad)
            mixed[rows, cols] = jnp.dot(
                turned[rows, cols], qx[kq], preferred_element_type=F32
            ).astype(BF)
        if i == 0:
            wait_all(cond_copies)
            cond_rows = conds[...].reshape(-1, mu)
        scr_copies[i].wait()
        amp = jnp.dot(mixed[rows, :], cond_rows, preferred_element_type=F32)
        kern[rows, :] = (scrs[rows, :].astype(F32) * amp * scale).astype(BF)
    row_copy.wait()
    folded[...] = jnp.dot(vals[...], kern[...], preferred_element_type=F32).astype(BF)
    for kp in range(di_ref.shape[0]):
        at = slice(kp * LANES, (kp + 1) * LANES)
        di_ref[kp] = dot_nt(folded[at, :], cond_rows[at, :])


def exchange_kernel(cfg, chunk, scale, *refs):
    n_ka, n_band, k_dev = cfg
    k_points = n_ka * k_dev
    rho_ref, di_ref, coul_ref, vown_ref, cond_ref, refs = refs[:5] + (refs[5:],)
    msg_ref, rhos, di, coul, conds, vown, part, msg, coul_sems, cond_sems, sems = refs
    own, npt = coul_ref.shape
    coul_copies = [
        pltpu.make_async_copy(
            coul_ref.at[:, pl.ds(i * chunk, chunk)], coul.at[:, pl.ds(i * chunk, chunk)], coul_sems.at[i]
        )
        for i in range(npt // chunk)
    ]
    rho_copy = pltpu.make_async_copy(rho_ref, rhos, sems.at[0])
    copies = own_copies(cond_ref, conds, cond_sems)
    copies.append(pltpu.make_async_copy(vown_ref, vown, sems.at[1]))
    copies.append(pltpu.make_async_copy(di_ref, di, sems.at[2]))
    start_all([rho_copy] + coul_copies + copies)
    rho_copy.wait()
    acc = jnp.zeros((own, LANES), F32)
    per_dev = own // LANES
    for i in range(npt // chunk):
        coul_copies[i].wait()
        for j in range(i * chunk // LANES, (i + 1) * chunk // LANES):
            rho = rhos[j // per_dev, pl.ds(j % per_dev, 1), :].astype(BF).astype(F32)
            acc = acc + coul[:, j * LANES : (j + 1) * LANES].astype(F32) * rho
    potential = scale * jnp.sum(acc.T, axis=0, keepdims=True)
    wait_all(copies)
    cond_rows = conds[...].reshape(-1, own)
    for kp in range(k_points // 2):
        at = slice(kp * LANES, (kp + 1) * LANES)
        weighted = (vown[at, :].astype(F32) * potential).astype(BF)
        part[kp] = 2.0 * dot_nt(weighted, cond_rows[at, :]) - di[kp]
    for d in range(n_band):
        for j in range(n_ka):
            for g in range((k_dev + 1) // 2):
                tile = None
                for kl in range(2 * g, min(2 * g + 2, k_dev)):
                    k = j * k_dev + kl
                    piece = part[k // 2, pl.ds(d * 2 * ROWS + k % 2 * ROWS, ROWS), :]
                    piece = lane_half(piece, k % 2, kl % 2)
                    tile = piece if tile is None else tile + piece
                msg[device_at(n_band, j, d), pl.ds(g * ROWS, ROWS), :] = tile
    msg_ref[...] = msg[...].astype(BF)


def received(recv_ref):
    return jnp.sum(recv_ref[...].astype(F32), axis=0)


def shifted(count_all, shift, square, cross_sum, square_sum):
    alpha = shift * square + cross_sum / count_all
    d = alpha - shift
    mean_sq = (square_sum - 2.0 * d * cross_sum) / count_all + d * d * square
    mean_sq = jnp.maximum(mean_sq, 0.0)
    return alpha, d, mean_sq


def first_owner_kernel(count_all, recv_ref, msgs_ref, gap_ref, own_ref, state_ref, coef_ref, msg_ref):
    start_sq, gap_sq = read_sums(msgs_ref, 2)
    norm = start_sq / count_all
    inv = 1.0 / jnp.sqrt(norm + 1e-06)
    square = norm / (norm + 1e-06)
    shift = gap_sq / jnp.maximum(start_sq, 1e-30)
    cur = own_ref[...] * inv
    inter = received(recv_ref) * inv
    gap = gap_ref[...]
    resid = (gap - shift) * cur + inter
    state_ref[0] = cur
    state_ref[1] = resid
    state_ref[2] = inter
    coef_ref[0] = shift
    coef_ref[1] = square
    coef_ref[2] = gap_sq * inv * inv
    sums = [
        jnp.sum(cur * resid),
        jnp.sum(resid * resid),
        jnp.sum(gap * resid * resid),
        jnp.sum(gap * resid * cur),
    ]
    msg_ref[...] = jnp.broadcast_to(with_sums(resid, sums).astype(BF)[None], msg_ref.shape)


def second_owner_kernel(count_all, recv_ref, msgs_ref, gap_ref, state_ref, coef_ref, out_ref, coef_out, msg_ref):
    cross, total, gap_rr, gap_rq = read_sums(msgs_ref, 4)
    alpha, d, mean_sq = shifted(count_all, coef_ref[0], coef_ref[1], cross, total)
    beta = jnp.sqrt(mean_sq + 1e-06)
    square = mean_sq / (mean_sq + 1e-06)
    gap_qq = gap_rr - 2.0 * d * gap_rq + d * d * coef_ref[2]
    shift = gap_qq / (mean_sq + 1e-06) / count_all
    prev = state_ref[0]
    cur = (state_ref[1] - d * prev) / beta
    inter = (received(recv_ref) - d * state_ref[2]) / beta
    resid = (gap_ref[...] - shift) * cur + inter - beta * prev
    out_ref[0] = cur
    out_ref[1] = resid
    coef_out[0] = alpha
    coef_out[1] = beta
    coef_out[2] = shift
    coef_out[3] = square
    dims = msg_ref.shape[:1] + msg_ref.shape[2:]
    msg_ref[:, 0, :] = jnp.full(dims, jnp.sum(cur * resid), F32)
    msg_ref[:, 1, :] = jnp.full(dims, jnp.sum(resid * resid), F32)


def finish_kernel(count_all, msgs_ref, state_ref, coef_ref, out_ref, coeffs_ref):
    sums = jnp.sum(msgs_ref[...], axis=0)
    alpha, d, mean_sq = shifted(count_all, coef_ref[2], coef_ref[3], sums[0, 0], sums[1, 0])
    beta = jnp.sqrt(mean_sq + 1e-06)
    own = (state_ref[1] - d * state_ref[0]) / beta
    coeffs_ref[0] = coef_ref[0]
    coeffs_ref[1] = alpha
    coeffs_ref[2] = coef_ref[1]
    coeffs_ref[3] = beta
    for kl in range(out_ref.shape[0]):
        tile = own[kl // 2 * ROWS : (kl // 2 + 1) * ROWS, :]
        other = pltpu.roll(tile, HALF, axis=1)
        left, right = (tile, other) if kl % 2 == 0 else (other, tile)
        low = lax.broadcasted_iota(jnp.int32, (1, LANES), 1) < HALF
        for j in range(ROWS // 2):
            row = jnp.where(low, left[2 * j : 2 * j + 1], right[2 * j + 1 : 2 * j + 2])
            out_ref[pl.ds(kl, 1), pl.ds(j * LANES, LANES)] = row


def shape_of(dims, kind=F32):
    return jax.ShapeDtypeStruct(dims, kind)


def call(kernel, name, out_shape, in_specs, out_specs, scratch=(), mib=58, flops=0, moved=0):
    return pl.pallas_call(
        kernel,
        out_shape=out_shape,
        in_specs=in_specs,
        out_specs=out_specs,
        scratch_shapes=list(scratch),
        compiler_params=pltpu.CompilerParams(vmem_limit_bytes=mib * MIB),
        cost_estimate=pl.CostEstimate(flops=flops, bytes_accessed=moved, transcendentals=0),
        name=name,
    )


def dma(*dims):
    return pltpu.SemaphoreType.DMA(dims)


def swap(block, axis, d):
    return lax.ppermute(block, axis, [(i, i ^ d) for i in range(lax.axis_size(axis))])


def plane_pieces(own_piece, others):
    def move(block, d):
        return swap(block, "band", d)

    half = own_piece.shape[0] // 2
    core, by_x, by_y = move(own_piece, 1), move(own_piece, 2), move(own_piece, 4)
    by_x, by_y, others = lax.optimization_barrier((by_x, by_y, others))
    diag = [move(by_x[:half], 4), move(by_y[half:], 2)]
    pieces = [[own_piece], [core], [by_x], [move(by_x, 1)], [by_y], [move(by_y, 1)]]
    return pieces + [diag, [move(part, 1) for part in diag]], others


def kernel_path(start_vec, val_energy, cond_energy, val_orb, cond_orb, coulomb, screened):
    n_ka = lax.axis_size("ka")
    n_band = lax.axis_size("band")
    devices = n_ka * n_band
    ka, band = lax.axis_index("ka"), lax.axis_index("band")
    k_dev = start_vec.shape[0]
    nv_blk = val_orb.shape[1]
    n_cond = cond_orb.shape[1]
    npt_all = cond_orb.shape[2]
    k_points = k_dev * n_ka
    pairs = k_points // 2
    mu_blk, nu_blk = screened.shape
    own = coulomb.shape[0]
    count_all = k_points * nv_blk * n_band * n_cond
    scale = 1.0 / (npt_all * math.sqrt(count_all))
    piece_rows = k_points * nv_blk

    block = ((k_dev + 1) // 2 * ROWS, LANES)
    msg_shape = shape_of((devices,) + block, BF)
    start_own, gap, message = call(
        pack_kernel,
        "pack",
        (shape_of(block), shape_of(block), shape_of(block, BF)),
        [VMEM, VMEM, SMEM],
        (VMEM, VMEM, VMEM),
        mib=8,
    )(start_vec, cond_energy, val_energy)

    head = jnp.pad(message, ((0, k_dev * nv_blk - block[0]), (0, 0)))

    def val_to(j):
        part = lax.dynamic_slice_in_dim(val_orb, jnp.bitwise_xor(ka, j) * nu_blk, nu_blk, 2)
        return jnp.concatenate([part.reshape(k_dev * nv_blk, nu_blk), head], axis=1)

    val_cut = jnp.concatenate(
        [val_to(0)] + [swap(val_to(j), "ka", j) for j in range(1, n_ka)], axis=0
    )
    cond_local = lax.dynamic_slice_in_dim(cond_orb, band * mu_blk, mu_blk, 2)
    cond_local = cond_local.reshape(k_dev * n_cond, mu_blk)
    cond_pts = [cond_local] + [swap(cond_local, "ka", j) for j in range(1, n_ka)]
    own_rows = k_dev * n_cond
    cuts = call(
        cut_kernel,
        "cut",
        shape_of((n_ka, own_rows, own), BF),
        [ANY],
        VMEM,
        [dma(n_ka * k_dev)],
    )(cond_orb)
    cond_own = lax.all_to_all(cuts, "ka", split_axis=0, concat_axis=0, tiled=True)

    chunk, tile = 1024, 1024
    rows_all, conds_all = k_points * nv_blk * n_band, k_points * n_cond
    scr_turned = call(
        functools.partial(turn_kernel, tile // 2),
        "turn",
        shape_of((nu_blk, mu_blk), BF),
        [ANY],
        ANY,
        [pltpu.VMEM((mu_blk, nu_blk), BF), pltpu.VMEM((nu_blk, mu_blk), BF)]
        + [dma(2 * nu_blk // tile)] * 2,
        moved=8 * MIB,
    )(screened)
    pieces, scr_turned = plane_pieces(val_cut, scr_turned)
    pieces, cond_pts[1 : n_ka - 1] = lax.optimization_barrier(
        (pieces, cond_pts[1 : n_ka - 1])
    )
    counts = tuple(len(piece) for piece in pieces)
    flat = [ref for piece in pieces for ref in piece]
    n_copies = len(flat)
    val_rows, val_turned, val_own, msgs = call(
        functools.partial(order_kernel, counts, n_ka),
        "order",
        (
            shape_of((rows_all, nu_blk), BF),
            shape_of((nu_blk, rows_all), BF),
            shape_of((rows_all, own), BF),
            msg_shape,
        ),
        [ANY] * n_copies,
        (ANY, ANY, ANY, VMEM),
        [
            pltpu.VMEM((n_band, piece_rows, nu_blk), BF),
            pltpu.VMEM((n_band, piece_rows, LANES), BF),
            pltpu.VMEM((rows_all, nu_blk), BF),
            pltpu.VMEM((nu_blk, rows_all), BF),
            dma(2, n_copies),
            dma(3, pairs),
        ],
        moved=9 * MIB,
    )(*flat)

    cfg = (n_ka, n_band, k_dev)
    quads = k_points // 4
    state, coef = None, None
    for step in range(STEPS):
        first = step == 0
        qx, rho = call(
            functools.partial(density_kernel, cfg),
            "density",
            (
                shape_of((quads, 2 * LANES, 2 * LANES), BF),
                shape_of((devices, own // LANES, LANES)),
            ),
            [ANY] * 3,
            (VMEM, VMEM),
            [
                pltpu.VMEM((quads, 2 * LANES, 2 * LANES), F32),
                pltpu.VMEM((devices,) + block, BF),
                pltpu.VMEM((rows_all, own), BF),
                pltpu.VMEM((n_ka, own_rows, own), BF),
                dma(n_ka),
                dma(2),
            ],
        )(msgs, val_own, cond_own)
        density = exchange_all(rho)
        direct = call(
            functools.partial(direct_kernel, n_ka, tile, scale),
            "direct",
            shape_of((pairs, LANES, LANES)),
            [ANY] * (4 + len(cond_pts)),
            VMEM,
            [
                pltpu.VMEM((quads, 2 * LANES, 2 * LANES), BF),
                pltpu.VMEM((nu_blk, rows_all), BF),
                pltpu.VMEM((n_ka, own_rows, mu_blk), BF),
                pltpu.VMEM((nu_blk, mu_blk), BF),
                pltpu.VMEM((rows_all, nu_blk), BF),
                pltpu.VMEM((nu_blk, conds_all), BF),
                pltpu.VMEM((nu_blk, mu_blk), BF),
                pltpu.VMEM((rows_all, mu_blk), BF),
                dma(1),
                dma(n_ka),
                dma(1),
                dma(2, nu_blk // tile),
            ],
            flops=4 * mu_blk * nu_blk * conds_all,
            moved=12 * MIB,
        )(val_turned, scr_turned, val_rows, qx, *cond_pts)
        parts = call(
            functools.partial(exchange_kernel, cfg, chunk, scale),
            "exchange",
            msg_shape,
            [ANY] * 5,
            VMEM,
            [
                pltpu.VMEM((devices, own // LANES, LANES), F32),
                pltpu.VMEM((pairs, LANES, LANES), F32),
                pltpu.VMEM((own, npt_all), BF),
                pltpu.VMEM((n_ka, own_rows, own), BF),
                pltpu.VMEM((rows_all, own), BF),
                pltpu.VMEM((pairs, LANES, LANES), F32),
                pltpu.VMEM((devices,) + block, F32),
                dma(npt_all // chunk),
                dma(n_ka),
                dma(3),
            ],
        )(density, direct, coulomb, val_own, cond_own)
        recv = exchange_all(parts)
        if first:
            state, coef, message = call(
                functools.partial(first_owner_kernel, count_all),
                "first_owner",
                (shape_of((3,) + block), shape_of((3,)), msg_shape),
                [VMEM] * 4,
                (VMEM, SMEM, VMEM),
                mib=8,
            )(recv, msgs, gap, start_own)
        else:
            state, coef, message = call(
                functools.partial(second_owner_kernel, count_all),
                "second_owner",
                (shape_of((2,) + block), shape_of((4,)), shape_of((devices, 2, LANES))),
                [VMEM] * 4 + [SMEM],
                (VMEM, SMEM, VMEM),
                mib=8,
            )(recv, msgs, gap, state, coef)
        msgs = exchange_all(message)
    return call(
        functools.partial(finish_kernel, count_all),
        "finish",
        (shape_of(start_vec.shape), shape_of((2 * STEPS,))),
        [VMEM] * 2 + [SMEM],
        (VMEM, SMEM),
        mib=8,
    )(msgs, state, coef)


def array_path(start_vec, val_energy, cond_energy, val_orb, cond_orb, coulomb, screened):
    n_ka = lax.axis_size("ka")
    n_band = lax.axis_size("band")
    devices = n_ka * n_band
    ka, band = lax.axis_index("ka"), lax.axis_index("band")
    me = ka * n_band + band
    k_dev, pair_blk = start_vec.shape
    nv_blk = val_orb.shape[1]
    n_cond = cond_orb.shape[1]
    n_val = nv_blk * n_band
    npt_all = cond_orb.shape[2]
    k_points = k_dev * n_ka
    mu_blk, nu_blk = screened.shape
    own_pts = coulomb.shape[0]
    count_all = k_points * n_val * n_cond
    kernel_scale = 1.0 / (npt_all * math.sqrt(count_all))

    start_all = gather_all(start_vec, devices)
    val_cut = lax.all_to_all(
        val_orb.reshape(k_dev, nv_blk, n_ka, nu_blk).transpose(2, 0, 1, 3),
        "ka", split_axis=0, concat_axis=0, tiled=True,
    ).reshape(k_points, nv_blk, nu_blk)
    val_pts = lax.all_gather(val_cut, "band", axis=1, tiled=True)
    cond_local = lax.dynamic_slice_in_dim(cond_orb, band * mu_blk, mu_blk, 2)
    cond_pts = lax.all_gather(cond_local, "ka", axis=0, tiled=True)
    cond_rows = cond_orb.reshape(k_dev, n_cond, n_ka, n_band, own_pts)
    cond_rows = lax.dynamic_index_in_dim(cond_rows, band, 3, keepdims=False)
    cond_own = lax.all_to_all(
        cond_rows.transpose(2, 0, 1, 3), "ka", split_axis=0, concat_axis=0, tiled=True
    ).reshape(k_points, n_cond, own_pts)
    val_own = lax.dynamic_slice_in_dim(val_pts, band * own_pts, own_pts, 2)

    energy_gap = (cond_energy[:, None, :] - val_energy[:, :, None]).reshape(k_dev, pair_blk)
    start_sq = jnp.sum(start_all * start_all)
    current = start_all / jnp.sqrt(start_sq / count_all + 1e-06)
    previous = jnp.zeros_like(current)
    beta_val = jnp.float32(0.0)
    alphas = []
    betas = []
    for turn_index in range(STEPS):
        full_vec = (
            current.astype(BF)
            .reshape(n_ka, n_band, k_dev, nv_blk, n_cond)
            .transpose(0, 2, 1, 3, 4)
            .reshape(k_points, n_val, n_cond)
        )
        mixed_f = jnp.einsum("kvc,kvn->kcn", full_vec, val_pts, preferred_element_type=F32)
        mixed_own = lax.dynamic_slice_in_dim(mixed_f, band * own_pts, own_pts, 2)
        density_own = jnp.sum(mixed_own * cond_own.astype(F32), axis=(0, 1))
        density = gather_all(density_own.astype(BF), devices).reshape(npt_all)
        mixed_val = mixed_f.astype(BF)
        amp = jnp.einsum("kcm,kcn->mn", cond_pts, mixed_val, preferred_element_type=F32)
        kern = (screened.astype(F32) * amp * kernel_scale).astype(BF)
        folded = jnp.einsum("mn,kvn->kvm", kern, val_pts, preferred_element_type=F32).astype(BF)
        direct_part = jnp.einsum("kcm,kvm->kvc", cond_pts, folded, preferred_element_type=F32)
        potential = kernel_scale * jnp.dot(coulomb, density, preferred_element_type=F32)
        weighted = (val_own.astype(F32) * potential).astype(BF)
        exchange = jnp.einsum("kvp,kcp->kvc", weighted, cond_own, preferred_element_type=F32)
        part = 2.0 * exchange - direct_part
        arranged = (
            part.reshape(n_ka, k_dev, n_band, nv_blk, n_cond)
            .transpose(0, 2, 1, 3, 4)
            .reshape(devices, k_dev, pair_blk)
        )
        inter_own = jnp.sum(exchange_all(arranged), axis=0)
        current_own = lax.dynamic_index_in_dim(current, me, 0, keepdims=False)
        resid_vec = gather_all(energy_gap * current_own + inter_own, devices)
        resid_vec = resid_vec - beta_val * previous
        alpha_val = jnp.sum(current * resid_vec) / count_all
        resid_vec = resid_vec - alpha_val * current
        beta_val = jnp.sqrt(jnp.sum(resid_vec * resid_vec) / count_all + 1e-06)
        previous = current
        current = resid_vec / beta_val
        alphas.append(alpha_val)
        betas.append(beta_val)
    coeffs = jnp.stack(alphas + betas)
    return (lax.dynamic_index_in_dim(current, me, 0, keepdims=False), coeffs)


def per_device(*args):
    start_vec, _, _, val_orb, cond_orb, coulomb, screened = args
    n_ka, n_band = lax.axis_size("ka"), lax.axis_size("band")
    fits = (
        n_band == 8
        and n_ka & (n_ka - 1) == 0
        and start_vec.shape[0] % 2 == 1
        and val_orb.shape[1] == ROWS
        and cond_orb.shape[1] == HALF
        and start_vec.shape[0] * n_ka % 4 == 0
        and coulomb.shape[0] % LANES == 0
        and coulomb.shape[1] % 1024 == 0
        and screened.shape[0] % 512 == 0
        and screened.shape[1] % 1024 == 0
        and screened.shape[0] * screened.shape[1] <= 2 * MIB
    )
    return (kernel_path if fits else array_path)(*args)


def solution(mesh):
    in_specs = (
        P("ka", "band"),
        P("ka", "band"),
        P("ka", None),
        P("ka", "band", None),
        P("ka", None, None),
        P(("ka", "band"), None),
        P("band", "ka"),
    )
    out_specs = (P("ka", "band"), P())
    return jax.shard_map(
        per_device, mesh=mesh, in_specs=in_specs, out_specs=out_specs, check_vma=False
    )
```

```python
import functools
import math

import jax
import jax.numpy as jnp
from jax import lax
from jax.experimental import pallas as pl
from jax.experimental.pallas import tpu as pltpu
from jax.sharding import PartitionSpec as P

STEPS = 2
AXES = ("ka", "band")
BF, F32 = jnp.bfloat16, jnp.float32
LANES = 128
HALF = 64
ROWS = 8
MIB = 1 << 20

VMEM = pl.BlockSpec(memory_space=pltpu.VMEM)
SMEM = pl.BlockSpec(memory_space=pltpu.SMEM)
ANY = pl.BlockSpec(memory_space=pl.ANY)


def gather_all(block, devices):
    wide = jnp.broadcast_to(block[None], (devices,) + block.shape)
    return exchange_all(wide)


def exchange_all(parts):
    return lax.all_to_all(parts, AXES, split_axis=0, concat_axis=0, tiled=True)


def dot_nt(lhs, rhs):
    return lax.dot_general(lhs, rhs, (((1,), (1,)), ((), ())), preferred_element_type=F32)


def dot_tn(lhs, rhs):
    return lax.dot_general(lhs, rhs, (((0,), (0,)), ((), ())), preferred_element_type=F32)


def lane_half(tile, have, want):
    if have != want:
        tile = pltpu.roll(tile, HALF, axis=1)
    lane = lax.broadcasted_iota(jnp.int32, tile.shape, 1)
    keep = lane < HALF if want == 0 else lane >= HALF
    return jnp.where(keep, tile, 0.0)


def with_sums(block, sums):
    row = lax.broadcasted_iota(jnp.int32, block.shape, 0)
    lane = lax.broadcasted_iota(jnp.int32, block.shape, 1)
    free = row == block.shape[0] - ROWS
    for i, total in enumerate(sums):
        rest = jnp.full(block.shape, total, F32)
        for part in range(3):
            piece = rest.astype(BF).astype(F32)
            block = jnp.where(free & (lane == HALF + 3 * i + part), piece, block)
            rest = rest - piece
    return block


def read_sums(msgs_ref, count):
    rows = msgs_ref.shape[1]
    tile = jnp.sum(msgs_ref[...].astype(F32), axis=0)[rows - ROWS :, :]
    row = lax.broadcasted_iota(jnp.int32, tile.shape, 0)
    lane = lax.broadcasted_iota(jnp.int32, tile.shape, 1)
    out = []
    for i in range(count):
        mine = (row == 0) & (lane >= HALF + 3 * i) & (lane < HALF + 3 * i + 3)
        out.append(jnp.sum(jnp.where(mine, tile, 0.0)))
    return out


def piece_copies(refs, parts, column, width, dest, sems):
    copies = []
    for d, piece in enumerate(parts):
        row = 0
        for ref, start, rows in piece:
            copies.append(
                pltpu.make_async_copy(
                    refs[ref].at[pl.ds(start, rows), pl.ds(column, width)],
                    dest.at[d, pl.ds(row, rows), :],
                    sems.at[len(copies)],
                )
            )
            row += rows
    return copies


def start_all(copies):
    for copy in copies:
        copy.start()


def wait_all(copies):
    for copy in copies:
        copy.wait()


def device_at(n_band, j, d):
    ka = jnp.bitwise_xor(lax.axis_index("ka"), j)
    return ka * n_band + jnp.bitwise_xor(lax.axis_index("band"), d)


def own_copies(ref, dest, sems):
    return [
        pltpu.make_async_copy(
            ref.at[jnp.bitwise_xor(lax.axis_index("ka"), j)], dest.at[j], sems.at[j]
        )
        for j in range(dest.shape[0])
    ]


def pair_rows(ref, kp):
    part = ref[:, kp * 2 * ROWS : (kp + 1) * 2 * ROWS, :]
    return part.reshape(part.shape[0] * 2 * ROWS, part.shape[2])


def pack_kernel(start_in, cond_in, val_in, own_ref, gap_ref, msg_ref, start_ref, cond_ref, val_ref, sems):
    ins = ((start_in, start_ref), (cond_in, cond_ref), (val_in, val_ref))
    copies = [pltpu.make_async_copy(ref, to, sems.at[i]) for i, (ref, to) in enumerate(ins)]
    start_all(copies)
    wait_all(copies)
    own_ref[...] = jnp.zeros_like(own_ref)
    gap_ref[...] = jnp.zeros_like(gap_ref)
    cond = jnp.concatenate([cond_ref[...], cond_ref[...]], axis=1)
    for kl in range(start_ref.shape[0]):
        half = kl % 2
        for v in range(ROWS):
            at = pl.ds(kl // 2 * ROWS + v, 1)
            row = start_ref[pl.ds(kl, 1), pl.ds(v // 2 * LANES, LANES)]
            own_ref[at, :] = own_ref[at, :] + lane_half(row, v % 2, half)
            gap = cond[kl : kl + 1, :] - val_ref[kl, v]
            gap_ref[at, :] = gap_ref[at, :] + lane_half(gap, half, half)
    own = own_ref[...]
    square = own * own
    block = with_sums(own, [jnp.sum(square), jnp.sum(gap_ref[...] * square)])
    msg_ref[...] = block.astype(BF)


def cut_kernel(cond_ref, out_ref, sems):
    n_ka, _, own = out_ref.shape
    k_dev, n_cond, npt = cond_ref.shape
    copies = []
    for z in range(n_ka):
        at = z * (npt // n_ka) + lax.axis_index("band") * own
        for kl in range(k_dev):
            copies.append(
                pltpu.make_async_copy(
                    cond_ref.at[kl, :, pl.ds(pl.multiple_of(at, LANES), own)],
                    out_ref.at[z, pl.ds(kl * n_cond, n_cond), :],
                    sems.at[len(copies)],
                )
            )
    start_all(copies)
    wait_all(copies)


def turn_kernel(tile, scr_ref, out_ref, scrs, turned, in_sems, out_sems):
    nu = scr_ref.shape[1]
    ins, outs = [], []
    for j in range(nu // tile):
        at = pl.ds(j * tile, tile)
        ins.append(pltpu.make_async_copy(scr_ref.at[:, at], scrs.at[:, at], in_sems.at[j]))
        outs.append(pltpu.make_async_copy(turned.at[at, :], out_ref.at[at, :], out_sems.at[j]))
    start_all(ins)
    for j in range(nu // tile):
        ins[j].wait()
        turned[j * tile : (j + 1) * tile, :] = scrs[:, j * tile : (j + 1) * tile].T
        outs[j].start()
    wait_all(outs)


def order_kernel(parts, n_ka, *refs):
    val_refs, refs = refs[:-10], refs[-10:]
    rows_out, turned_out, own_out, msgs_out, vals, heads, ordered, turned, val_sems, out_sems = refs
    own = own_out.shape[1]
    nu = ordered.shape[1]
    copies = piece_copies(val_refs, parts, 0, nu, vals, val_sems.at[0])
    head_copies = piece_copies(val_refs, parts, nu, LANES, heads, val_sems.at[1])
    start_all(copies + head_copies)
    wait_all(copies)
    n_band, group = vals.shape[0], vals.shape[0] * 2 * ROWS
    column = pl.multiple_of(lax.axis_index("band") * own, LANES)
    outs = []
    for kp in range(ordered.shape[0] // group):
        at = slice(kp * group, (kp + 1) * group)
        ordered[at, :] = pair_rows(vals, kp)
        turned[:, at] = ordered[at, :].T
        at = pl.ds(kp * group, group)
        outs += [
            pltpu.make_async_copy(ordered.at[at, :], rows_out.at[at, :], out_sems.at[0, kp]),
            pltpu.make_async_copy(turned.at[:, at], turned_out.at[:, at], out_sems.at[1, kp]),
            pltpu.make_async_copy(
                ordered.at[at, pl.ds(column, own)], own_out.at[at, :], out_sems.at[2, kp]
            ),
        ]
        start_all(outs[-3:])
    wait_all(head_copies)
    rows = msgs_out.shape[1]
    step = heads.shape[1] // n_ka
    for d in range(n_band):
        head = heads[d].astype(F32)
        for j in range(n_ka):
            msgs_out[device_at(n_band, j, d)] = head[j * step : j * step + rows, :].astype(BF)
    wait_all(outs)


def density_kernel(cfg, *refs):
    n_ka, n_band, k_dev = cfg
    k_points = n_ka * k_dev
    msgs_ref, vown_ref, cond_ref, qx_ref, rho_ref = refs[:5]
    xs, msgs, vown, conds, cond_sems, sems = refs[5:]
    own = vown_ref.shape[1]
    msg_copy = pltpu.make_async_copy(msgs_ref, msgs, sems.at[0])
    copies = own_copies(cond_ref, conds, cond_sems)
    copies.append(pltpu.make_async_copy(vown_ref, vown, sems.at[1]))
    start_all([msg_copy] + copies)
    xs[...] = jnp.zeros_like(xs)
    msg_copy.wait()
    for d in range(n_band):
        for k in range(k_points):
            j, kl = divmod(k, k_dev)
            tile = msgs[device_at(n_band, j, d), :, :].astype(F32)
            tile = tile[kl // 2 * ROWS : (kl // 2 + 1) * ROWS, :]
            base = k // 2 % 2 * LANES
            at = pl.ds(base + d * 2 * ROWS + k % 2 * ROWS, ROWS)
            xs[k // 4, at, pl.ds(base, LANES)] = lane_half(tile, kl % 2, k % 2)
    qx_ref[...] = xs[...].astype(BF)
    wait_all(copies)
    cond_rows = conds[...].reshape(-1, own)
    rho = jnp.zeros((1, own), F32)
    quad = 2 * LANES
    for kq in range(k_points // 4):
        at = slice(kq * quad, (kq + 1) * quad)
        mixed = dot_tn(qx_ref[kq], vown[at, :])
        rho = rho + jnp.sum(mixed * cond_rows[at, :].astype(F32), axis=0, keepdims=True)
    for r in range(own // LANES):
        part = rho[:, r * LANES : (r + 1) * LANES]
        rho_ref[:, r, :] = jnp.broadcast_to(part, (rho_ref.shape[0], LANES))


def direct_kernel(n_ka, tile, scale, *refs):
    turned_ref, scr_ref, rows_ref, qx_ref, refs = refs[0], refs[1], refs[2], refs[3], refs[4:]
    hops = [(0, 0)] + [(way, hop) for way in (-1, 1) for hop in range(1, n_ka)]
    cond_refs, refs = refs[: len(hops)], refs[len(hops) :]
    di_ref, qx, turned, conds, scrs, vals, mixed, kern, folded = refs[:9]
    qx_sem, cond_sems, row_sem, chunk_sems = refs[9:]
    nu, mu = scr_ref.shape
    quad = 2 * LANES
    qx_copy = pltpu.make_async_copy(qx_ref, qx, qx_sem.at[0])
    ka = lax.axis_index("ka")

    def each_cond(act):
        for i, (way, hop) in enumerate(hops):
            origin = ka + way * hop
            pl.when((origin >= 0) & (origin < n_ka))(
                lambda i=i, origin=origin: act(
                    pltpu.make_async_copy(
                        cond_refs[i], conds.at[jnp.bitwise_xor(ka, origin)], cond_sems.at[i]
                    )
                )
            )

    turned_copies, scr_copies = [], []
    for i in range(nu // tile):
        at = pl.ds(i * tile, tile)
        turned_copies.append(
            pltpu.make_async_copy(turned_ref.at[at, :], turned.at[at, :], chunk_sems.at[0, i])
        )
        scr_copies.append(
            pltpu.make_async_copy(scr_ref.at[at, :], scrs.at[at, :], chunk_sems.at[1, i])
        )
    row_copy = pltpu.make_async_copy(rows_ref, vals, row_sem.at[0])
    start_all([qx_copy, turned_copies[0]])
    each_cond(lambda copy: copy.start())
    scr_copies[0].start()
    for i in range(1, nu // tile):
        start_all([turned_copies[i], scr_copies[i]])
    row_copy.start()
    qx_copy.wait()
    for i in range(nu // tile):
        rows = slice(i * tile, (i + 1) * tile)
        turned_copies[i].wait()
        for kq in range(qx.shape[0]):
            cols = slice(kq * quad, (kq + 1) * quad)
            mixed[rows, cols] = jnp.dot(
                turned[rows, cols], qx[kq], preferred_element_type=F32
            ).astype(BF)
        if i == 0:
            each_cond(lambda copy: copy.wait())
            cond_rows = conds[...].reshape(-1, mu)
        scr_copies[i].wait()
        amp = jnp.dot(mixed[rows, :], cond_rows, preferred_element_type=F32)
        kern[rows, :] = (scrs[rows, :].astype(F32) * amp * scale).astype(BF)
    row_copy.wait()
    folded[...] = jnp.dot(vals[...], kern[...], preferred_element_type=F32).astype(BF)
    for kp in range(di_ref.shape[0]):
        at = slice(kp * LANES, (kp + 1) * LANES)
        di_ref[kp] = dot_nt(folded[at, :], cond_rows[at, :])


def exchange_kernel(cfg, chunk, scale, *refs):
    n_ka, n_band, k_dev = cfg
    k_points = n_ka * k_dev
    rho_ref, di_ref, coul_ref, vown_ref, cond_ref, refs = refs[:5] + (refs[5:],)
    msg_ref, rhos, di, coul, conds, vown, part, msg, coul_sems, cond_sems, sems = refs
    own, npt = coul_ref.shape
    coul_copies = [
        pltpu.make_async_copy(
            coul_ref.at[:, pl.ds(i * chunk, chunk)], coul.at[:, pl.ds(i * chunk, chunk)], coul_sems.at[i]
        )
        for i in range(npt // chunk)
    ]
    rho_copy = pltpu.make_async_copy(rho_ref, rhos, sems.at[0])
    copies = own_copies(cond_ref, conds, cond_sems)
    copies.append(pltpu.make_async_copy(vown_ref, vown, sems.at[1]))
    copies.append(pltpu.make_async_copy(di_ref, di, sems.at[2]))
    start_all([rho_copy] + coul_copies + copies)
    rho_copy.wait()
    acc = jnp.zeros((own, LANES), F32)
    per_dev = own // LANES
    for i in range(npt // chunk):
        coul_copies[i].wait()
        for j in range(i * chunk // LANES, (i + 1) * chunk // LANES):
            rho = rhos[j // per_dev, pl.ds(j % per_dev, 1), :].astype(BF).astype(F32)
            acc = acc + coul[:, j * LANES : (j + 1) * LANES].astype(F32) * rho
    potential = scale * jnp.sum(acc.T, axis=0, keepdims=True)
    wait_all(copies)
    cond_rows = conds[...].reshape(-1, own)
    for kp in range(k_points // 2):
        at = slice(kp * LANES, (kp + 1) * LANES)
        weighted = (vown[at, :].astype(F32) * potential).astype(BF)
        part[kp] = 2.0 * dot_nt(weighted, cond_rows[at, :]) - di[kp]
    for d in range(n_band):
        for j in range(n_ka):
            for g in range((k_dev + 1) // 2):
                tile = None
                for kl in range(2 * g, min(2 * g + 2, k_dev)):
                    k = j * k_dev + kl
                    piece = part[k // 2, pl.ds(d * 2 * ROWS + k % 2 * ROWS, ROWS), :]
                    piece = lane_half(piece, k % 2, kl % 2)
                    tile = piece if tile is None else tile + piece
                msg[device_at(n_band, j, d), pl.ds(g * ROWS, ROWS), :] = tile
    msg_ref[...] = msg[...].astype(BF)


def received(recv_ref):
    return jnp.sum(recv_ref[...].astype(F32), axis=0)


def shifted(count_all, shift, square, cross_sum, square_sum):
    alpha = shift * square + cross_sum / count_all
    d = alpha - shift
    mean_sq = (square_sum - 2.0 * d * cross_sum) / count_all + d * d * square
    mean_sq = jnp.maximum(mean_sq, 0.0)
    return alpha, d, mean_sq


def first_owner_kernel(count_all, recv_ref, msgs_ref, gap_ref, own_ref, state_ref, coef_ref, msg_ref):
    start_sq, gap_sq = read_sums(msgs_ref, 2)
    norm = start_sq / count_all
    inv = 1.0 / jnp.sqrt(norm + 1e-06)
    square = norm / (norm + 1e-06)
    shift = gap_sq / jnp.maximum(start_sq, 1e-30)
    cur = own_ref[...] * inv
    inter = received(recv_ref) * inv
    gap = gap_ref[...]
    resid = (gap - shift) * cur + inter
    state_ref[0] = cur
    state_ref[1] = resid
    state_ref[2] = inter
    coef_ref[0] = shift
    coef_ref[1] = square
    coef_ref[2] = gap_sq * inv * inv
    sums = [
        jnp.sum(cur * resid),
        jnp.sum(resid * resid),
        jnp.sum(gap * resid * resid),
        jnp.sum(gap * resid * cur),
    ]
    msg_ref[...] = jnp.broadcast_to(with_sums(resid, sums).astype(BF)[None], msg_ref.shape)


def second_owner_kernel(count_all, recv_ref, msgs_ref, gap_ref, state_ref, coef_ref, out_ref, coef_out, msg_ref):
    cross, total, gap_rr, gap_rq = read_sums(msgs_ref, 4)
    alpha, d, mean_sq = shifted(count_all, coef_ref[0], coef_ref[1], cross, total)
    beta = jnp.sqrt(mean_sq + 1e-06)
    square = mean_sq / (mean_sq + 1e-06)
    gap_qq = gap_rr - 2.0 * d * gap_rq + d * d * coef_ref[2]
    shift = gap_qq / (mean_sq + 1e-06) / count_all
    prev = state_ref[0]
    cur = (state_ref[1] - d * prev) / beta
    inter = (received(recv_ref) - d * state_ref[2]) / beta
    resid = (gap_ref[...] - shift) * cur + inter - beta * prev
    out_ref[0] = cur
    out_ref[1] = resid
    coef_out[0] = alpha
    coef_out[1] = beta
    coef_out[2] = shift
    coef_out[3] = square
    dims = msg_ref.shape[:1] + msg_ref.shape[2:]
    msg_ref[:, 0, :] = jnp.full(dims, jnp.sum(cur * resid), F32)
    msg_ref[:, 1, :] = jnp.full(dims, jnp.sum(resid * resid), F32)


def finish_kernel(count_all, msgs_ref, state_ref, coef_ref, out_ref, coeffs_ref):
    sums = jnp.sum(msgs_ref[...], axis=0)
    alpha, d, mean_sq = shifted(count_all, coef_ref[2], coef_ref[3], sums[0, 0], sums[1, 0])
    beta = jnp.sqrt(mean_sq + 1e-06)
    own = (state_ref[1] - d * state_ref[0]) / beta
    coeffs_ref[0] = coef_ref[0]
    coeffs_ref[1] = alpha
    coeffs_ref[2] = coef_ref[1]
    coeffs_ref[3] = beta
    for kl in range(out_ref.shape[0]):
        tile = own[kl // 2 * ROWS : (kl // 2 + 1) * ROWS, :]
        other = pltpu.roll(tile, HALF, axis=1)
        left, right = (tile, other) if kl % 2 == 0 else (other, tile)
        low = lax.broadcasted_iota(jnp.int32, (1, LANES), 1) < HALF
        for j in range(ROWS // 2):
            row = jnp.where(low, left[2 * j : 2 * j + 1], right[2 * j + 1 : 2 * j + 2])
            out_ref[pl.ds(kl, 1), pl.ds(j * LANES, LANES)] = row


def shape_of(dims, kind=F32):
    return jax.ShapeDtypeStruct(dims, kind)


def call(kernel, name, out_shape, in_specs, out_specs, scratch=(), mib=58, flops=0, moved=0):
    return pl.pallas_call(
        kernel,
        out_shape=out_shape,
        in_specs=in_specs,
        out_specs=out_specs,
        scratch_shapes=list(scratch),
        compiler_params=pltpu.CompilerParams(vmem_limit_bytes=mib * MIB),
        cost_estimate=pl.CostEstimate(flops=flops, bytes_accessed=moved, transcendentals=0),
        name=name,
    )


def dma(*dims):
    return pltpu.SemaphoreType.DMA(dims)


def swap(block, axis, d):
    return lax.ppermute(block, axis, [(i, i ^ d) for i in range(lax.axis_size(axis))])


def line_gather(block, axis):
    n = lax.axis_size(axis)
    flows = []
    for way in (-1, 1):
        moving, flow = block, []
        for hop in range(1, n):
            senders = [i for i in range(n) if 0 <= i + way * (hop - 1) < n and 0 <= i - way < n]
            moving = lax.ppermute(moving, axis, [(i, i - way) for i in senders])
            flow.append(moving)
        flows.append(flow)
    return flows


def plane_pieces(own_piece, others):
    def move(block, d):
        return swap(block, "band", d)

    rows = own_piece.shape[0]
    half = rows // 2
    by_x, by_y = move(own_piece, 2), move(own_piece, 4)
    by_x, by_y, others = lax.optimization_barrier((by_x, by_y, others))
    diag = [move(by_x[:half], 4), move(by_y[half:], 2)]
    near = move(jnp.concatenate([own_piece, by_x, by_y], axis=0), 1)
    far = move(jnp.concatenate(diag, axis=0), 1)
    arrays = [own_piece, by_x, by_y, diag[0], diag[1], near, far]
    parts = (
        ((0, 0, rows),),
        ((5, 0, rows),),
        ((1, 0, rows),),
        ((5, rows, rows),),
        ((2, 0, rows),),
        ((5, 2 * rows, rows),),
        ((3, 0, half), (4, 0, half)),
        ((6, 0, rows),),
    )
    return arrays, parts, others


def kernel_path(start_vec, val_energy, cond_energy, val_orb, cond_orb, coulomb, screened):
    n_ka = lax.axis_size("ka")
    n_band = lax.axis_size("band")
    devices = n_ka * n_band
    ka, band = lax.axis_index("ka"), lax.axis_index("band")
    k_dev = start_vec.shape[0]
    nv_blk = val_orb.shape[1]
    n_cond = cond_orb.shape[1]
    npt_all = cond_orb.shape[2]
    k_points = k_dev * n_ka
    pairs = k_points // 2
    mu_blk, nu_blk = screened.shape
    own = coulomb.shape[0]
    count_all = k_points * nv_blk * n_band * n_cond
    scale = 1.0 / (npt_all * math.sqrt(count_all))
    piece_rows = k_points * nv_blk

    block = ((k_dev + 1) // 2 * ROWS, LANES)
    msg_shape = shape_of((devices,) + block, BF)
    start_own, gap, message = call(
        pack_kernel,
        "pack",
        (shape_of(block), shape_of(block), shape_of(block, BF)),
        [ANY] * 3,
        (VMEM, VMEM, VMEM),
        [
            pltpu.VMEM(start_vec.shape, F32),
            pltpu.VMEM(cond_energy.shape, F32),
            pltpu.SMEM(val_energy.shape, F32),
            dma(3),
        ],
    )(start_vec, cond_energy, val_energy)

    head = jnp.pad(message, ((0, k_dev * nv_blk - block[0]), (0, 0)))

    def val_to(j):
        part = lax.dynamic_slice_in_dim(val_orb, jnp.bitwise_xor(ka, j) * nu_blk, nu_blk, 2)
        return jnp.concatenate([part.reshape(k_dev * nv_blk, nu_blk), head], axis=1)

    val_cut = jnp.concatenate(
        [val_to(0)] + [swap(val_to(j), "ka", j) for j in range(1, n_ka)], axis=0
    )
    cond_local = lax.dynamic_slice_in_dim(cond_orb, band * mu_blk, mu_blk, 2)
    cond_local = cond_local.reshape(k_dev * n_cond, mu_blk)
    below, above = line_gather(cond_local, "ka")
    own_rows = k_dev * n_cond
    cuts = call(
        cut_kernel,
        "cut",
        shape_of((n_ka, own_rows, own), BF),
        [ANY],
        VMEM,
        [dma(n_ka * k_dev)],
    )(cond_orb)
    cond_own = lax.all_to_all(cuts, "ka", split_axis=0, concat_axis=0, tiled=True)

    chunk, tile = 1024, 1024
    rows_all, conds_all = k_points * nv_blk * n_band, k_points * n_cond
    scr_turned = call(
        functools.partial(turn_kernel, tile // 2),
        "turn",
        shape_of((nu_blk, mu_blk), BF),
        [ANY],
        ANY,
        [pltpu.VMEM((mu_blk, nu_blk), BF), pltpu.VMEM((nu_blk, mu_blk), BF)]
        + [dma(2 * nu_blk // tile)] * 2,
        moved=8 * MIB,
    )(screened)
    pieces, parts, (scr_turned, below[0], above[0]) = plane_pieces(
        val_cut, (scr_turned, below[0], above[0])
    )
    pieces, below[1:-1], above[1:-1] = lax.optimization_barrier((pieces, below[1:-1], above[1:-1]))
    cond_pts = [cond_local] + below + above
    val_rows, val_turned, val_own, msgs = call(
        functools.partial(order_kernel, parts, n_ka),
        "order",
        (
            shape_of((rows_all, nu_blk), BF),
            shape_of((nu_blk, rows_all), BF),
            shape_of((rows_all, own), BF),
            msg_shape,
        ),
        [ANY] * len(pieces),
        (ANY, ANY, ANY, VMEM),
        [
            pltpu.VMEM((n_band, piece_rows, nu_blk), BF),
            pltpu.VMEM((n_band, piece_rows, LANES), BF),
            pltpu.VMEM((rows_all, nu_blk), BF),
            pltpu.VMEM((nu_blk, rows_all), BF),
            dma(2, sum(len(piece) for piece in parts)),
            dma(3, pairs),
        ],
        moved=9 * MIB,
    )(*pieces)

    cfg = (n_ka, n_band, k_dev)
    quads = k_points // 4
    state, coef = None, None
    for step in range(STEPS):
        first = step == 0
        qx, rho = call(
            functools.partial(density_kernel, cfg),
            "density",
            (
                shape_of((quads, 2 * LANES, 2 * LANES), BF),
                shape_of((devices, own // LANES, LANES)),
            ),
            [ANY] * 3,
            (VMEM, VMEM),
            [
                pltpu.VMEM((quads, 2 * LANES, 2 * LANES), F32),
                pltpu.VMEM((devices,) + block, BF),
                pltpu.VMEM((rows_all, own), BF),
                pltpu.VMEM((n_ka, own_rows, own), BF),
                dma(n_ka),
                dma(2),
            ],
        )(msgs, val_own, cond_own)
        density = exchange_all(rho)
        direct = call(
            functools.partial(direct_kernel, n_ka, tile, scale),
            "direct",
            shape_of((pairs, LANES, LANES)),
            [ANY] * (4 + len(cond_pts)),
            VMEM,
            [
                pltpu.VMEM((quads, 2 * LANES, 2 * LANES), BF),
                pltpu.VMEM((nu_blk, rows_all), BF),
                pltpu.VMEM((n_ka, own_rows, mu_blk), BF),
                pltpu.VMEM((nu_blk, mu_blk), BF),
                pltpu.VMEM((rows_all, nu_blk), BF),
                pltpu.VMEM((nu_blk, conds_all), BF),
                pltpu.VMEM((nu_blk, mu_blk), BF),
                pltpu.VMEM((rows_all, mu_blk), BF),
                dma(1),
                dma(len(cond_pts)),
                dma(1),
                dma(2, nu_blk // tile),
            ],
            flops=4 * mu_blk * nu_blk * conds_all,
            moved=12 * MIB,
        )(val_turned, scr_turned, val_rows, qx, *cond_pts)
        summed = call(
            functools.partial(exchange_kernel, cfg, chunk, scale),
            "exchange",
            msg_shape,
            [ANY] * 5,
            VMEM,
            [
                pltpu.VMEM((devices, own // LANES, LANES), F32),
                pltpu.VMEM((pairs, LANES, LANES), F32),
                pltpu.VMEM((own, npt_all), BF),
                pltpu.VMEM((n_ka, own_rows, own), BF),
                pltpu.VMEM((rows_all, own), BF),
                pltpu.VMEM((pairs, LANES, LANES), F32),
                pltpu.VMEM((devices,) + block, F32),
                dma(npt_all // chunk),
                dma(n_ka),
                dma(3),
            ],
        )(density, direct, coulomb, val_own, cond_own)
        recv = exchange_all(summed)
        if first:
            state, coef, message = call(
                functools.partial(first_owner_kernel, count_all),
                "first_owner",
                (shape_of((3,) + block), shape_of((3,)), msg_shape),
                [VMEM] * 4,
                (VMEM, SMEM, VMEM),
                mib=8,
            )(recv, msgs, gap, start_own)
        else:
            state, coef, message = call(
                functools.partial(second_owner_kernel, count_all),
                "second_owner",
                (shape_of((2,) + block), shape_of((4,)), shape_of((devices, 2, LANES))),
                [VMEM] * 4 + [SMEM],
                (VMEM, SMEM, VMEM),
                mib=8,
            )(recv, msgs, gap, state, coef)
        msgs = exchange_all(message)
    return call(
        functools.partial(finish_kernel, count_all),
        "finish",
        (shape_of(start_vec.shape), shape_of((2 * STEPS,))),
        [VMEM] * 2 + [SMEM],
        (VMEM, SMEM),
        mib=8,
    )(msgs, state, coef)


def array_path(start_vec, val_energy, cond_energy, val_orb, cond_orb, coulomb, screened):
    n_ka = lax.axis_size("ka")
    n_band = lax.axis_size("band")
    devices = n_ka * n_band
    ka, band = lax.axis_index("ka"), lax.axis_index("band")
    me = ka * n_band + band
    k_dev, pair_blk = start_vec.shape
    nv_blk = val_orb.shape[1]
    n_cond = cond_orb.shape[1]
    n_val = nv_blk * n_band
    npt_all = cond_orb.shape[2]
    k_points = k_dev * n_ka
    mu_blk, nu_blk = screened.shape
    own_pts = coulomb.shape[0]
    count_all = k_points * n_val * n_cond
    kernel_scale = 1.0 / (npt_all * math.sqrt(count_all))

    start_all = gather_all(start_vec, devices)
    val_cut = lax.all_to_all(
        val_orb.reshape(k_dev, nv_blk, n_ka, nu_blk).transpose(2, 0, 1, 3),
        "ka", split_axis=0, concat_axis=0, tiled=True,
    ).reshape(k_points, nv_blk, nu_blk)
    val_pts = lax.all_gather(val_cut, "band", axis=1, tiled=True)
    cond_local = lax.dynamic_slice_in_dim(cond_orb, band * mu_blk, mu_blk, 2)
    cond_pts = lax.all_gather(cond_local, "ka", axis=0, tiled=True)
    cond_rows = cond_orb.reshape(k_dev, n_cond, n_ka, n_band, own_pts)
    cond_rows = lax.dynamic_index_in_dim(cond_rows, band, 3, keepdims=False)
    cond_own = lax.all_to_all(
        cond_rows.transpose(2, 0, 1, 3), "ka", split_axis=0, concat_axis=0, tiled=True
    ).reshape(k_points, n_cond, own_pts)
    val_own = lax.dynamic_slice_in_dim(val_pts, band * own_pts, own_pts, 2)

    energy_gap = (cond_energy[:, None, :] - val_energy[:, :, None]).reshape(k_dev, pair_blk)
    start_sq = jnp.sum(start_all * start_all)
    current = start_all / jnp.sqrt(start_sq / count_all + 1e-06)
    previous = jnp.zeros_like(current)
    beta_val = jnp.float32(0.0)
    alphas = []
    betas = []
    for turn_index in range(STEPS):
        full_vec = (
            current.astype(BF)
            .reshape(n_ka, n_band, k_dev, nv_blk, n_cond)
            .transpose(0, 2, 1, 3, 4)
            .reshape(k_points, n_val, n_cond)
        )
        mixed_f = jnp.einsum("kvc,kvn->kcn", full_vec, val_pts, preferred_element_type=F32)
        mixed_own = lax.dynamic_slice_in_dim(mixed_f, band * own_pts, own_pts, 2)
        density_own = jnp.sum(mixed_own * cond_own.astype(F32), axis=(0, 1))
        density = gather_all(density_own.astype(BF), devices).reshape(npt_all)
        mixed_val = mixed_f.astype(BF)
        amp = jnp.einsum("kcm,kcn->mn", cond_pts, mixed_val, preferred_element_type=F32)
        kern = (screened.astype(F32) * amp * kernel_scale).astype(BF)
        folded = jnp.einsum("mn,kvn->kvm", kern, val_pts, preferred_element_type=F32).astype(BF)
        direct_part = jnp.einsum("kcm,kvm->kvc", cond_pts, folded, preferred_element_type=F32)
        potential = kernel_scale * jnp.dot(coulomb, density, preferred_element_type=F32)
        weighted = (val_own.astype(F32) * potential).astype(BF)
        exchange = jnp.einsum("kvp,kcp->kvc", weighted, cond_own, preferred_element_type=F32)
        part = 2.0 * exchange - direct_part
        arranged = (
            part.reshape(n_ka, k_dev, n_band, nv_blk, n_cond)
            .transpose(0, 2, 1, 3, 4)
            .reshape(devices, k_dev, pair_blk)
        )
        inter_own = jnp.sum(exchange_all(arranged), axis=0)
        current_own = lax.dynamic_index_in_dim(current, me, 0, keepdims=False)
        resid_vec = gather_all(energy_gap * current_own + inter_own, devices)
        resid_vec = resid_vec - beta_val * previous
        alpha_val = jnp.sum(current * resid_vec) / count_all
        resid_vec = resid_vec - alpha_val * current
        beta_val = jnp.sqrt(jnp.sum(resid_vec * resid_vec) / count_all + 1e-06)
        previous = current
        current = resid_vec / beta_val
        alphas.append(alpha_val)
        betas.append(beta_val)
    coeffs = jnp.stack(alphas + betas)
    return (lax.dynamic_index_in_dim(current, me, 0, keepdims=False), coeffs)


def per_device(*args):
    start_vec, _, _, val_orb, cond_orb, coulomb, screened = args
    n_ka, n_band = lax.axis_size("ka"), lax.axis_size("band")
    fits = (
        n_band == 8
        and n_ka & (n_ka - 1) == 0
        and start_vec.shape[0] % 2 == 1
        and val_orb.shape[1] == ROWS
        and cond_orb.shape[1] == HALF
        and start_vec.shape[0] * n_ka % 4 == 0
        and coulomb.shape[0] % LANES == 0
        and coulomb.shape[1] % 1024 == 0
        and screened.shape[0] % 512 == 0
        and screened.shape[1] % 1024 == 0
        and screened.shape[0] * screened.shape[1] <= 2 * MIB
    )
    return (kernel_path if fits else array_path)(*args)


def solution(mesh):
    in_specs = (
        P("ka", "band"),
        P("ka", "band"),
        P("ka", None),
        P("ka", "band", None),
        P("ka", None, None),
        P(("ka", "band"), None),
        P("band", "ka"),
    )
    out_specs = (P("ka", "band"), P())
    return jax.shard_map(
        per_device, mesh=mesh, in_specs=in_specs, out_specs=out_specs, check_vma=False
    )
```

```python
import functools
import math

import jax
import jax.numpy as jnp
from jax import lax
from jax.experimental import pallas as pl
from jax.experimental.pallas import tpu as pltpu
from jax.sharding import PartitionSpec as P

STEPS = 2
AXES = ("ka", "band")
BF, F32 = jnp.bfloat16, jnp.float32
LANES = 128
HALF = 64
ROWS = 8
MIB = 1 << 20

VMEM = pl.BlockSpec(memory_space=pltpu.VMEM)
SMEM = pl.BlockSpec(memory_space=pltpu.SMEM)
ANY = pl.BlockSpec(memory_space=pl.ANY)


def gather_all(block, devices):
    wide = jnp.broadcast_to(block[None], (devices,) + block.shape)
    return exchange_all(wide)


def exchange_all(parts):
    return lax.all_to_all(parts, AXES, split_axis=0, concat_axis=0, tiled=True)


def dot_nt(lhs, rhs):
    return lax.dot_general(lhs, rhs, (((1,), (1,)), ((), ())), preferred_element_type=F32)


def dot_tn(lhs, rhs):
    return lax.dot_general(lhs, rhs, (((0,), (0,)), ((), ())), preferred_element_type=F32)


def lane_half(tile, have, want):
    if have != want:
        tile = pltpu.roll(tile, HALF, axis=1)
    lane = lax.broadcasted_iota(jnp.int32, tile.shape, 1)
    keep = lane < HALF if want == 0 else lane >= HALF
    return jnp.where(keep, tile, 0.0)


def with_sums(block, sums):
    row = lax.broadcasted_iota(jnp.int32, block.shape, 0)
    lane = lax.broadcasted_iota(jnp.int32, block.shape, 1)
    free = row == block.shape[0] - ROWS
    for i, total in enumerate(sums):
        rest = jnp.full(block.shape, total, F32)
        for part in range(3):
            piece = rest.astype(BF).astype(F32)
            block = jnp.where(free & (lane == HALF + 3 * i + part), piece, block)
            rest = rest - piece
    return block


def read_sums(msgs_ref, count):
    rows = msgs_ref.shape[1]
    tile = jnp.sum(msgs_ref[...].astype(F32), axis=0)[rows - ROWS :, :]
    row = lax.broadcasted_iota(jnp.int32, tile.shape, 0)
    lane = lax.broadcasted_iota(jnp.int32, tile.shape, 1)
    out = []
    for i in range(count):
        mine = (row == 0) & (lane >= HALF + 3 * i) & (lane < HALF + 3 * i + 3)
        out.append(jnp.sum(jnp.where(mine, tile, 0.0)))
    return out


def piece_copies(refs, parts, column, width, dest, sems):
    copies = []
    for d, piece in enumerate(parts):
        row = 0
        for ref, start, rows in piece:
            copies.append(
                pltpu.make_async_copy(
                    refs[ref].at[pl.ds(start, rows), pl.ds(column, width)],
                    dest.at[d, pl.ds(row, rows), :],
                    sems.at[len(copies)],
                )
            )
            row += rows
    return copies


def start_all(copies):
    for copy in copies:
        copy.start()


def wait_all(copies):
    for copy in copies:
        copy.wait()


def device_at(n_band, j, d):
    ka = jnp.bitwise_xor(lax.axis_index("ka"), j)
    return ka * n_band + jnp.bitwise_xor(lax.axis_index("band"), d)


def own_copies(ref, dest, sems):
    return [
        pltpu.make_async_copy(
            ref.at[jnp.bitwise_xor(lax.axis_index("ka"), j)], dest.at[j], sems.at[j]
        )
        for j in range(dest.shape[0])
    ]


def pair_rows(ref, kp):
    part = ref[:, kp * 2 * ROWS : (kp + 1) * 2 * ROWS, :]
    return part.reshape(part.shape[0] * 2 * ROWS, part.shape[2])


def pack_kernel(start_in, cond_in, val_in, own_ref, gap_ref, msg_ref, start_ref, cond_ref, val_ref, sems):
    ins = ((start_in, start_ref), (cond_in, cond_ref), (val_in, val_ref))
    copies = [pltpu.make_async_copy(ref, to, sems.at[i]) for i, (ref, to) in enumerate(ins)]
    start_all(copies)
    wait_all(copies)
    own_ref[...] = jnp.zeros_like(own_ref)
    gap_ref[...] = jnp.zeros_like(gap_ref)
    cond = jnp.concatenate([cond_ref[...], cond_ref[...]], axis=1)
    for kl in range(start_ref.shape[0]):
        half = kl % 2
        for v in range(ROWS):
            at = pl.ds(kl // 2 * ROWS + v, 1)
            row = start_ref[pl.ds(kl, 1), pl.ds(v // 2 * LANES, LANES)]
            own_ref[at, :] = own_ref[at, :] + lane_half(row, v % 2, half)
            gap = cond[kl : kl + 1, :] - val_ref[kl, v]
            gap_ref[at, :] = gap_ref[at, :] + lane_half(gap, half, half)
    own = own_ref[...]
    square = own * own
    block = with_sums(own, [jnp.sum(square), jnp.sum(gap_ref[...] * square)])
    msg_ref[...] = block.astype(BF)


def cut_kernel(cond_ref, out_ref, sems):
    n_ka, _, own = out_ref.shape
    k_dev, n_cond, npt = cond_ref.shape
    copies = []
    for z in range(n_ka):
        at = z * (npt // n_ka) + lax.axis_index("band") * own
        for kl in range(k_dev):
            copies.append(
                pltpu.make_async_copy(
                    cond_ref.at[kl, :, pl.ds(pl.multiple_of(at, LANES), own)],
                    out_ref.at[z, pl.ds(kl * n_cond, n_cond), :],
                    sems.at[len(copies)],
                )
            )
    start_all(copies)
    wait_all(copies)


def turn_kernel(tile, scr_ref, out_ref, scrs, turned, in_sems, out_sems):
    nu = scr_ref.shape[1]
    ins, outs = [], []
    for j in range(nu // tile):
        at = pl.ds(j * tile, tile)
        ins.append(pltpu.make_async_copy(scr_ref.at[:, at], scrs.at[:, at], in_sems.at[j]))
        outs.append(pltpu.make_async_copy(turned.at[at, :], out_ref.at[at, :], out_sems.at[j]))
    start_all(ins)
    for j in range(nu // tile):
        ins[j].wait()
        turned[j * tile : (j + 1) * tile, :] = scrs[:, j * tile : (j + 1) * tile].T
        outs[j].start()
    wait_all(outs)


def order_kernel(parts, n_ka, *refs):
    val_refs, refs = refs[:-10], refs[-10:]
    rows_out, turned_out, own_out, msgs_out, vals, heads, ordered, turned, val_sems, out_sems = refs
    own = own_out.shape[1]
    nu = ordered.shape[1]
    copies = piece_copies(val_refs, parts, 0, nu, vals, val_sems.at[0])
    head_copies = piece_copies(val_refs, parts, nu, LANES, heads, val_sems.at[1])
    start_all(copies + head_copies)
    wait_all(copies)
    n_band, group = vals.shape[0], vals.shape[0] * 2 * ROWS
    column = pl.multiple_of(lax.axis_index("band") * own, LANES)
    outs = []
    for kp in range(ordered.shape[0] // group):
        at = slice(kp * group, (kp + 1) * group)
        ordered[at, :] = pair_rows(vals, kp)
        turned[:, at] = ordered[at, :].T
        at = pl.ds(kp * group, group)
        outs += [
            pltpu.make_async_copy(ordered.at[at, :], rows_out.at[at, :], out_sems.at[0, kp]),
            pltpu.make_async_copy(turned.at[:, at], turned_out.at[:, at], out_sems.at[1, kp]),
            pltpu.make_async_copy(
                ordered.at[at, pl.ds(column, own)], own_out.at[at, :], out_sems.at[2, kp]
            ),
        ]
        start_all(outs[-3:])
    wait_all(head_copies)
    rows = msgs_out.shape[1]
    step = heads.shape[1] // n_ka
    for d in range(n_band):
        head = heads[d].astype(F32)
        for j in range(n_ka):
            msgs_out[device_at(n_band, j, d)] = head[j * step : j * step + rows, :].astype(BF)
    wait_all(outs)


def density_kernel(cfg, *refs):
    n_ka, n_band, k_dev = cfg
    k_points = n_ka * k_dev
    msgs_ref, vown_ref, cond_ref, qx_ref, rho_ref = refs[:5]
    xs, msgs, vown, conds, cond_sems, sems = refs[5:]
    own = vown_ref.shape[1]
    msg_copy = pltpu.make_async_copy(msgs_ref, msgs, sems.at[0])
    copies = own_copies(cond_ref, conds, cond_sems)
    copies.append(pltpu.make_async_copy(vown_ref, vown, sems.at[1]))
    start_all([msg_copy] + copies)
    xs[...] = jnp.zeros_like(xs)
    msg_copy.wait()
    for d in range(n_band):
        for k in range(k_points):
            j, kl = divmod(k, k_dev)
            tile = msgs[device_at(n_band, j, d), :, :].astype(F32)
            tile = tile[kl // 2 * ROWS : (kl // 2 + 1) * ROWS, :]
            base = k // 2 % 2 * LANES
            at = pl.ds(base + d * 2 * ROWS + k % 2 * ROWS, ROWS)
            xs[k // 4, at, pl.ds(base, LANES)] = lane_half(tile, kl % 2, k % 2)
    qx_ref[...] = xs[...].astype(BF)
    wait_all(copies)
    cond_rows = conds[...].reshape(-1, own)
    rho = jnp.zeros((1, own), F32)
    quad = 2 * LANES
    for kq in range(k_points // 4):
        at = slice(kq * quad, (kq + 1) * quad)
        mixed = dot_tn(qx_ref[kq], vown[at, :])
        rho = rho + jnp.sum(mixed * cond_rows[at, :].astype(F32), axis=0, keepdims=True)
    for r in range(own // LANES):
        part = rho[:, r * LANES : (r + 1) * LANES]
        rho_ref[:, r, :] = jnp.broadcast_to(part, (rho_ref.shape[0], LANES))


def direct_kernel(n_ka, tile, scale, *refs):
    turned_ref, scr_ref, rows_ref, qx_ref, refs = refs[0], refs[1], refs[2], refs[3], refs[4:]
    hops = [(0, 0)] + [(way, hop) for way in (-1, 1) for hop in range(1, n_ka)]
    cond_refs, refs = refs[: len(hops)], refs[len(hops) :]
    di_ref, qx, turned, conds, scrs, vals, mixed, kern, folded = refs[:9]
    qx_sem, cond_sems, row_sem, chunk_sems = refs[9:]
    nu, mu = scr_ref.shape
    quad = 2 * LANES
    qx_copy = pltpu.make_async_copy(qx_ref, qx, qx_sem.at[0])
    ka = lax.axis_index("ka")

    def each_cond(act):
        for i, (way, hop) in enumerate(hops):
            origin = ka + way * hop
            pl.when((origin >= 0) & (origin < n_ka))(
                lambda i=i, origin=origin: act(
                    pltpu.make_async_copy(
                        cond_refs[i], conds.at[jnp.bitwise_xor(ka, origin)], cond_sems.at[i]
                    )
                )
            )

    turned_copies, scr_copies = [], []
    for i in range(nu // tile):
        at = pl.ds(i * tile, tile)
        turned_copies.append(
            pltpu.make_async_copy(turned_ref.at[at, :], turned.at[at, :], chunk_sems.at[0, i])
        )
        scr_copies.append(
            pltpu.make_async_copy(scr_ref.at[at, :], scrs.at[at, :], chunk_sems.at[1, i])
        )
    row_copy = pltpu.make_async_copy(rows_ref, vals, row_sem.at[0])
    start_all([qx_copy, turned_copies[0]])
    each_cond(lambda copy: copy.start())
    scr_copies[0].start()
    for i in range(1, nu // tile):
        start_all([turned_copies[i], scr_copies[i]])
    row_copy.start()
    qx_copy.wait()
    for i in range(nu // tile):
        rows = slice(i * tile, (i + 1) * tile)
        turned_copies[i].wait()
        for kq in range(qx.shape[0]):
            cols = slice(kq * quad, (kq + 1) * quad)
            mixed[rows, cols] = jnp.dot(
                turned[rows, cols], qx[kq], preferred_element_type=F32
            ).astype(BF)
        if i == 0:
            each_cond(lambda copy: copy.wait())
            cond_rows = conds[...].reshape(-1, mu)
        scr_copies[i].wait()
        amp = jnp.dot(mixed[rows, :], cond_rows, preferred_element_type=F32)
        kern[rows, :] = (scrs[rows, :].astype(F32) * amp * scale).astype(BF)
    row_copy.wait()
    folded[...] = jnp.dot(vals[...], kern[...], preferred_element_type=F32).astype(BF)
    for kp in range(di_ref.shape[0]):
        at = slice(kp * LANES, (kp + 1) * LANES)
        di_ref[kp] = dot_nt(folded[at, :], cond_rows[at, :])


def exchange_kernel(cfg, chunk, scale, *refs):
    n_ka, n_band, k_dev = cfg
    k_points = n_ka * k_dev
    rho_ref, di_ref, coul_ref, vown_ref, cond_ref, refs = refs[:5] + (refs[5:],)
    msg_ref, rhos, di, coul, conds, vown, part, msg, coul_sems, cond_sems, sems = refs
    own, npt = coul_ref.shape
    coul_copies = [
        pltpu.make_async_copy(
            coul_ref.at[:, pl.ds(i * chunk, chunk)], coul.at[:, pl.ds(i * chunk, chunk)], coul_sems.at[i]
        )
        for i in range(npt // chunk)
    ]
    rho_copy = pltpu.make_async_copy(rho_ref, rhos, sems.at[0])
    copies = own_copies(cond_ref, conds, cond_sems)
    copies.append(pltpu.make_async_copy(vown_ref, vown, sems.at[1]))
    copies.append(pltpu.make_async_copy(di_ref, di, sems.at[2]))
    start_all([rho_copy] + coul_copies + copies)
    rho_copy.wait()
    acc = jnp.zeros((own, LANES), F32)
    per_dev = own // LANES
    for i in range(npt // chunk):
        coul_copies[i].wait()
        for j in range(i * chunk // LANES, (i + 1) * chunk // LANES):
            rho = rhos[j // per_dev, pl.ds(j % per_dev, 1), :].astype(BF).astype(F32)
            acc = acc + coul[:, j * LANES : (j + 1) * LANES].astype(F32) * rho
    potential = scale * jnp.sum(acc.T, axis=0, keepdims=True)
    wait_all(copies)
    cond_rows = conds[...].reshape(-1, own)
    for kp in range(k_points // 2):
        at = slice(kp * LANES, (kp + 1) * LANES)
        weighted = (vown[at, :].astype(F32) * potential).astype(BF)
        part[kp] = 2.0 * dot_nt(weighted, cond_rows[at, :]) - di[kp]
    for d in range(n_band):
        for j in range(n_ka):
            for g in range((k_dev + 1) // 2):
                tile = None
                for kl in range(2 * g, min(2 * g + 2, k_dev)):
                    k = j * k_dev + kl
                    piece = part[k // 2, pl.ds(d * 2 * ROWS + k % 2 * ROWS, ROWS), :]
                    piece = lane_half(piece, k % 2, kl % 2)
                    tile = piece if tile is None else tile + piece
                msg[device_at(n_band, j, d), pl.ds(g * ROWS, ROWS), :] = tile
    msg_ref[...] = msg[...].astype(BF)


def received(recv_ref):
    return jnp.sum(recv_ref[...].astype(F32), axis=0)


def shifted(count_all, shift, square, cross_sum, square_sum):
    alpha = shift * square + cross_sum / count_all
    d = alpha - shift
    mean_sq = (square_sum - 2.0 * d * cross_sum) / count_all + d * d * square
    mean_sq = jnp.maximum(mean_sq, 0.0)
    return alpha, d, mean_sq


def first_owner_kernel(count_all, recv_ref, msgs_ref, gap_ref, own_ref, state_ref, coef_ref, msg_ref):
    start_sq, gap_sq = read_sums(msgs_ref, 2)
    norm = start_sq / count_all
    inv = 1.0 / jnp.sqrt(norm + 1e-06)
    square = norm / (norm + 1e-06)
    shift = gap_sq / jnp.maximum(start_sq, 1e-30)
    cur = own_ref[...] * inv
    inter = received(recv_ref) * inv
    gap = gap_ref[...]
    resid = (gap - shift) * cur + inter
    state_ref[0] = cur
    state_ref[1] = resid
    state_ref[2] = inter
    coef_ref[0] = shift
    coef_ref[1] = square
    coef_ref[2] = gap_sq * inv * inv
    sums = [
        jnp.sum(cur * resid),
        jnp.sum(resid * resid),
        jnp.sum(gap * resid * resid),
        jnp.sum(gap * resid * cur),
    ]
    msg_ref[...] = jnp.broadcast_to(with_sums(resid, sums).astype(BF)[None], msg_ref.shape)


def second_owner_kernel(count_all, recv_ref, msgs_ref, gap_ref, state_ref, coef_ref, out_ref, coef_out, msg_ref):
    cross, total, gap_rr, gap_rq = read_sums(msgs_ref, 4)
    alpha, d, mean_sq = shifted(count_all, coef_ref[0], coef_ref[1], cross, total)
    beta = jnp.sqrt(mean_sq + 1e-06)
    square = mean_sq / (mean_sq + 1e-06)
    gap_qq = gap_rr - 2.0 * d * gap_rq + d * d * coef_ref[2]
    shift = gap_qq / (mean_sq + 1e-06) / count_all
    prev = state_ref[0]
    cur = (state_ref[1] - d * prev) / beta
    inter = (received(recv_ref) - d * state_ref[2]) / beta
    resid = (gap_ref[...] - shift) * cur + inter - beta * prev
    out_ref[0] = cur
    out_ref[1] = resid
    coef_out[0] = alpha
    coef_out[1] = beta
    coef_out[2] = shift
    coef_out[3] = square
    dims = msg_ref.shape[:1] + msg_ref.shape[2:]
    msg_ref[:, 0, :] = jnp.full(dims, jnp.sum(cur * resid), F32)
    msg_ref[:, 1, :] = jnp.full(dims, jnp.sum(resid * resid), F32)


def finish_kernel(count_all, msgs_ref, state_ref, coef_ref, out_ref, coeffs_ref):
    sums = jnp.sum(msgs_ref[...], axis=0)
    alpha, d, mean_sq = shifted(count_all, coef_ref[2], coef_ref[3], sums[0, 0], sums[1, 0])
    beta = jnp.sqrt(mean_sq + 1e-06)
    own = (state_ref[1] - d * state_ref[0]) / beta
    coeffs_ref[0] = coef_ref[0]
    coeffs_ref[1] = alpha
    coeffs_ref[2] = coef_ref[1]
    coeffs_ref[3] = beta
    for kl in range(out_ref.shape[0]):
        tile = own[kl // 2 * ROWS : (kl // 2 + 1) * ROWS, :]
        other = pltpu.roll(tile, HALF, axis=1)
        left, right = (tile, other) if kl % 2 == 0 else (other, tile)
        low = lax.broadcasted_iota(jnp.int32, (1, LANES), 1) < HALF
        for j in range(ROWS // 2):
            row = jnp.where(low, left[2 * j : 2 * j + 1], right[2 * j + 1 : 2 * j + 2])
            out_ref[pl.ds(kl, 1), pl.ds(j * LANES, LANES)] = row


def shape_of(dims, kind=F32):
    return jax.ShapeDtypeStruct(dims, kind)


def call(kernel, name, out_shape, in_specs, out_specs, scratch=(), mib=58, flops=0, moved=0):
    return pl.pallas_call(
        kernel,
        out_shape=out_shape,
        in_specs=in_specs,
        out_specs=out_specs,
        scratch_shapes=list(scratch),
        compiler_params=pltpu.CompilerParams(vmem_limit_bytes=mib * MIB),
        cost_estimate=pl.CostEstimate(flops=flops, bytes_accessed=moved, transcendentals=0),
        name=name,
    )


def dma(*dims):
    return pltpu.SemaphoreType.DMA(dims)


def swap(block, axis, d):
    return lax.ppermute(block, axis, [(i, i ^ d) for i in range(lax.axis_size(axis))])


def line_gather(block, axis):
    n = lax.axis_size(axis)
    flows = []
    for way in (-1, 1):
        moving, flow = block, []
        for hop in range(1, n):
            senders = [i for i in range(n) if 0 <= i + way * (hop - 1) < n and 0 <= i - way < n]
            moving = lax.ppermute(moving, axis, [(i, i - way) for i in senders])
            flow.append(moving)
        flows.append(flow)
    return flows


def plane_pieces(own_piece, others):
    def move(block, d):
        return swap(block, "band", d)

    rows = own_piece.shape[0]
    half = rows // 2
    by_x, by_y, core = move(own_piece, 2), move(own_piece, 4), move(own_piece, 1)
    by_x, by_y, core, others = lax.optimization_barrier((by_x, by_y, core, others))
    diag = [move(by_x[:half], 4), move(by_y[half:], 2)]
    near_x, near_y = move(by_x, 1), move(by_y, 1)
    far = move(jnp.concatenate(diag, axis=0), 1)
    arrays = [own_piece, core, by_x, near_x, by_y, near_y, diag[0], diag[1], far]
    parts = tuple(((i, 0, rows),) for i in range(6))
    parts += (((6, 0, half), (7, 0, half)), ((8, 0, rows),))
    return arrays, parts, others


def kernel_path(start_vec, val_energy, cond_energy, val_orb, cond_orb, coulomb, screened):
    n_ka = lax.axis_size("ka")
    n_band = lax.axis_size("band")
    devices = n_ka * n_band
    ka, band = lax.axis_index("ka"), lax.axis_index("band")
    k_dev = start_vec.shape[0]
    nv_blk = val_orb.shape[1]
    n_cond = cond_orb.shape[1]
    npt_all = cond_orb.shape[2]
    k_points = k_dev * n_ka
    pairs = k_points // 2
    mu_blk, nu_blk = screened.shape
    own = coulomb.shape[0]
    count_all = k_points * nv_blk * n_band * n_cond
    scale = 1.0 / (npt_all * math.sqrt(count_all))
    piece_rows = k_points * nv_blk

    block = ((k_dev + 1) // 2 * ROWS, LANES)
    msg_shape = shape_of((devices,) + block, BF)
    start_own, gap, message = call(
        pack_kernel,
        "pack",
        (shape_of(block), shape_of(block), shape_of(block, BF)),
        [ANY] * 3,
        (VMEM, VMEM, VMEM),
        [
            pltpu.VMEM(start_vec.shape, F32),
            pltpu.VMEM(cond_energy.shape, F32),
            pltpu.SMEM(val_energy.shape, F32),
            dma(3),
        ],
    )(start_vec, cond_energy, val_energy)

    head = jnp.pad(message, ((0, k_dev * nv_blk - block[0]), (0, 0)))

    def val_to(j):
        part = lax.dynamic_slice_in_dim(val_orb, jnp.bitwise_xor(ka, j) * nu_blk, nu_blk, 2)
        return jnp.concatenate([part.reshape(k_dev * nv_blk, nu_blk), head], axis=1)

    val_cut = jnp.concatenate(
        [val_to(0)] + [swap(val_to(j), "ka", j) for j in range(1, n_ka)], axis=0
    )
    cond_local = lax.dynamic_slice_in_dim(cond_orb, band * mu_blk, mu_blk, 2)
    cond_local = cond_local.reshape(k_dev * n_cond, mu_blk)
    below, above = line_gather(cond_local, "ka")
    own_rows = k_dev * n_cond
    cuts = call(
        cut_kernel,
        "cut",
        shape_of((n_ka, own_rows, own), BF),
        [ANY],
        VMEM,
        [dma(n_ka * k_dev)],
    )(cond_orb)
    cond_own = lax.all_to_all(cuts, "ka", split_axis=0, concat_axis=0, tiled=True)

    chunk, tile = 1024, 1024
    rows_all, conds_all = k_points * nv_blk * n_band, k_points * n_cond
    scr_turned = call(
        functools.partial(turn_kernel, tile // 2),
        "turn",
        shape_of((nu_blk, mu_blk), BF),
        [ANY],
        ANY,
        [pltpu.VMEM((mu_blk, nu_blk), BF), pltpu.VMEM((nu_blk, mu_blk), BF)]
        + [dma(2 * nu_blk // tile)] * 2,
        moved=8 * MIB,
    )(screened)
    pieces, parts, (scr_turned, cond_own, below[0], above[0]) = plane_pieces(
        val_cut, (scr_turned, cond_own, below[0], above[0])
    )
    val_rows, val_turned, val_own, msgs = call(
        functools.partial(order_kernel, parts, n_ka),
        "order",
        (
            shape_of((rows_all, nu_blk), BF),
            shape_of((nu_blk, rows_all), BF),
            shape_of((rows_all, own), BF),
            msg_shape,
        ),
        [ANY] * len(pieces),
        (ANY, ANY, ANY, VMEM),
        [
            pltpu.VMEM((n_band, piece_rows, nu_blk), BF),
            pltpu.VMEM((n_band, piece_rows, LANES), BF),
            pltpu.VMEM((rows_all, nu_blk), BF),
            pltpu.VMEM((nu_blk, rows_all), BF),
            dma(2, sum(len(piece) for piece in parts)),
            dma(3, pairs),
        ],
        moved=9 * MIB,
    )(*pieces)

    msgs, below[1:-1], above[1:-1] = lax.optimization_barrier((msgs, below[1:-1], above[1:-1]))
    cond_pts = [cond_local] + below + above
    cfg = (n_ka, n_band, k_dev)
    quads = k_points // 4
    state, coef = None, None
    for step in range(STEPS):
        first = step == 0
        qx, rho = call(
            functools.partial(density_kernel, cfg),
            "density",
            (
                shape_of((quads, 2 * LANES, 2 * LANES), BF),
                shape_of((devices, own // LANES, LANES)),
            ),
            [ANY] * 3,
            (VMEM, VMEM),
            [
                pltpu.VMEM((quads, 2 * LANES, 2 * LANES), F32),
                pltpu.VMEM((devices,) + block, BF),
                pltpu.VMEM((rows_all, own), BF),
                pltpu.VMEM((n_ka, own_rows, own), BF),
                dma(n_ka),
                dma(2),
            ],
        )(msgs, val_own, cond_own)
        density = exchange_all(rho)
        direct = call(
            functools.partial(direct_kernel, n_ka, tile, scale),
            "direct",
            shape_of((pairs, LANES, LANES)),
            [ANY] * (4 + len(cond_pts)),
            VMEM,
            [
                pltpu.VMEM((quads, 2 * LANES, 2 * LANES), BF),
                pltpu.VMEM((nu_blk, rows_all), BF),
                pltpu.VMEM((n_ka, own_rows, mu_blk), BF),
                pltpu.VMEM((nu_blk, mu_blk), BF),
                pltpu.VMEM((rows_all, nu_blk), BF),
                pltpu.VMEM((nu_blk, conds_all), BF),
                pltpu.VMEM((nu_blk, mu_blk), BF),
                pltpu.VMEM((rows_all, mu_blk), BF),
                dma(1),
                dma(len(cond_pts)),
                dma(1),
                dma(2, nu_blk // tile),
            ],
            flops=4 * mu_blk * nu_blk * conds_all,
            moved=12 * MIB,
        )(val_turned, scr_turned, val_rows, qx, *cond_pts)
        summed = call(
            functools.partial(exchange_kernel, cfg, chunk, scale),
            "exchange",
            msg_shape,
            [ANY] * 5,
            VMEM,
            [
                pltpu.VMEM((devices, own // LANES, LANES), F32),
                pltpu.VMEM((pairs, LANES, LANES), F32),
                pltpu.VMEM((own, npt_all), BF),
                pltpu.VMEM((n_ka, own_rows, own), BF),
                pltpu.VMEM((rows_all, own), BF),
                pltpu.VMEM((pairs, LANES, LANES), F32),
                pltpu.VMEM((devices,) + block, F32),
                dma(npt_all // chunk),
                dma(n_ka),
                dma(3),
            ],
        )(density, direct, coulomb, val_own, cond_own)
        recv = exchange_all(summed)
        if first:
            state, coef, message = call(
                functools.partial(first_owner_kernel, count_all),
                "first_owner",
                (shape_of((3,) + block), shape_of((3,)), msg_shape),
                [VMEM] * 4,
                (VMEM, SMEM, VMEM),
                mib=8,
            )(recv, msgs, gap, start_own)
        else:
            state, coef, message = call(
                functools.partial(second_owner_kernel, count_all),
                "second_owner",
                (shape_of((2,) + block), shape_of((4,)), shape_of((devices, 2, LANES))),
                [VMEM] * 4 + [SMEM],
                (VMEM, SMEM, VMEM),
                mib=8,
            )(recv, msgs, gap, state, coef)
        msgs = exchange_all(message)
    return call(
        functools.partial(finish_kernel, count_all),
        "finish",
        (shape_of(start_vec.shape), shape_of((2 * STEPS,))),
        [VMEM] * 2 + [SMEM],
        (VMEM, SMEM),
        mib=8,
    )(msgs, state, coef)


def array_path(start_vec, val_energy, cond_energy, val_orb, cond_orb, coulomb, screened):
    n_ka = lax.axis_size("ka")
    n_band = lax.axis_size("band")
    devices = n_ka * n_band
    ka, band = lax.axis_index("ka"), lax.axis_index("band")
    me = ka * n_band + band
    k_dev, pair_blk = start_vec.shape
    nv_blk = val_orb.shape[1]
    n_cond = cond_orb.shape[1]
    n_val = nv_blk * n_band
    npt_all = cond_orb.shape[2]
    k_points = k_dev * n_ka
    mu_blk, nu_blk = screened.shape
    own_pts = coulomb.shape[0]
    count_all = k_points * n_val * n_cond
    kernel_scale = 1.0 / (npt_all * math.sqrt(count_all))

    start_all = gather_all(start_vec, devices)
    val_cut = lax.all_to_all(
        val_orb.reshape(k_dev, nv_blk, n_ka, nu_blk).transpose(2, 0, 1, 3),
        "ka", split_axis=0, concat_axis=0, tiled=True,
    ).reshape(k_points, nv_blk, nu_blk)
    val_pts = lax.all_gather(val_cut, "band", axis=1, tiled=True)
    cond_local = lax.dynamic_slice_in_dim(cond_orb, band * mu_blk, mu_blk, 2)
    cond_pts = lax.all_gather(cond_local, "ka", axis=0, tiled=True)
    cond_rows = cond_orb.reshape(k_dev, n_cond, n_ka, n_band, own_pts)
    cond_rows = lax.dynamic_index_in_dim(cond_rows, band, 3, keepdims=False)
    cond_own = lax.all_to_all(
        cond_rows.transpose(2, 0, 1, 3), "ka", split_axis=0, concat_axis=0, tiled=True
    ).reshape(k_points, n_cond, own_pts)
    val_own = lax.dynamic_slice_in_dim(val_pts, band * own_pts, own_pts, 2)

    energy_gap = (cond_energy[:, None, :] - val_energy[:, :, None]).reshape(k_dev, pair_blk)
    start_sq = jnp.sum(start_all * start_all)
    current = start_all / jnp.sqrt(start_sq / count_all + 1e-06)
    previous = jnp.zeros_like(current)
    beta_val = jnp.float32(0.0)
    alphas = []
    betas = []
    for turn_index in range(STEPS):
        full_vec = (
            current.astype(BF)
            .reshape(n_ka, n_band, k_dev, nv_blk, n_cond)
            .transpose(0, 2, 1, 3, 4)
            .reshape(k_points, n_val, n_cond)
        )
        mixed_f = jnp.einsum("kvc,kvn->kcn", full_vec, val_pts, preferred_element_type=F32)
        mixed_own = lax.dynamic_slice_in_dim(mixed_f, band * own_pts, own_pts, 2)
        density_own = jnp.sum(mixed_own * cond_own.astype(F32), axis=(0, 1))
        density = gather_all(density_own.astype(BF), devices).reshape(npt_all)
        mixed_val = mixed_f.astype(BF)
        amp = jnp.einsum("kcm,kcn->mn", cond_pts, mixed_val, preferred_element_type=F32)
        kern = (screened.astype(F32) * amp * kernel_scale).astype(BF)
        folded = jnp.einsum("mn,kvn->kvm", kern, val_pts, preferred_element_type=F32).astype(BF)
        direct_part = jnp.einsum("kcm,kvm->kvc", cond_pts, folded, preferred_element_type=F32)
        potential = kernel_scale * jnp.dot(coulomb, density, preferred_element_type=F32)
        weighted = (val_own.astype(F32) * potential).astype(BF)
        exchange = jnp.einsum("kvp,kcp->kvc", weighted, cond_own, preferred_element_type=F32)
        part = 2.0 * exchange - direct_part
        arranged = (
            part.reshape(n_ka, k_dev, n_band, nv_blk, n_cond)
            .transpose(0, 2, 1, 3, 4)
            .reshape(devices, k_dev, pair_blk)
        )
        inter_own = jnp.sum(exchange_all(arranged), axis=0)
        current_own = lax.dynamic_index_in_dim(current, me, 0, keepdims=False)
        resid_vec = gather_all(energy_gap * current_own + inter_own, devices)
        resid_vec = resid_vec - beta_val * previous
        alpha_val = jnp.sum(current * resid_vec) / count_all
        resid_vec = resid_vec - alpha_val * current
        beta_val = jnp.sqrt(jnp.sum(resid_vec * resid_vec) / count_all + 1e-06)
        previous = current
        current = resid_vec / beta_val
        alphas.append(alpha_val)
        betas.append(beta_val)
    coeffs = jnp.stack(alphas + betas)
    return (lax.dynamic_index_in_dim(current, me, 0, keepdims=False), coeffs)


def per_device(*args):
    start_vec, _, _, val_orb, cond_orb, coulomb, screened = args
    n_ka, n_band = lax.axis_size("ka"), lax.axis_size("band")
    fits = (
        n_band == 8
        and n_ka & (n_ka - 1) == 0
        and start_vec.shape[0] % 2 == 1
        and val_orb.shape[1] == ROWS
        and cond_orb.shape[1] == HALF
        and start_vec.shape[0] * n_ka % 4 == 0
        and coulomb.shape[0] % LANES == 0
        and coulomb.shape[1] % 1024 == 0
        and screened.shape[0] % 512 == 0
        and screened.shape[1] % 1024 == 0
        and screened.shape[0] * screened.shape[1] <= 2 * MIB
    )
    return (kernel_path if fits else array_path)(*args)


def solution(mesh):
    in_specs = (
        P("ka", "band"),
        P("ka", "band"),
        P("ka", None),
        P("ka", "band", None),
        P("ka", None, None),
        P(("ka", "band"), None),
        P("band", "ka"),
    )
    out_specs = (P("ka", "band"), P())
    return jax.shard_map(
        per_device, mesh=mesh, in_specs=in_specs, out_specs=out_specs, check_vma=False
    )
```

```python
import functools
import math

import jax
import jax.numpy as jnp
from jax import lax
from jax.experimental import pallas as pl
from jax.experimental.pallas import tpu as pltpu
from jax.sharding import PartitionSpec as P

STEPS = 2
AXES = ("ka", "band")
BF, F32 = jnp.bfloat16, jnp.float32
LANES = 128
HALF = 64
ROWS = 8
MIB = 1 << 20

VMEM = pl.BlockSpec(memory_space=pltpu.VMEM)
SMEM = pl.BlockSpec(memory_space=pltpu.SMEM)
ANY = pl.BlockSpec(memory_space=pl.ANY)


def gather_all(block, devices):
    wide = jnp.broadcast_to(block[None], (devices,) + block.shape)
    return exchange_all(wide)


def exchange_all(parts):
    return lax.all_to_all(parts, AXES, split_axis=0, concat_axis=0, tiled=True)


def dot_nt(lhs, rhs):
    return lax.dot_general(lhs, rhs, (((1,), (1,)), ((), ())), preferred_element_type=F32)


def dot_tn(lhs, rhs):
    return lax.dot_general(lhs, rhs, (((0,), (0,)), ((), ())), preferred_element_type=F32)


def lane_half(tile, have, want):
    if have != want:
        tile = pltpu.roll(tile, HALF, axis=1)
    lane = lax.broadcasted_iota(jnp.int32, tile.shape, 1)
    keep = lane < HALF if want == 0 else lane >= HALF
    return jnp.where(keep, tile, 0.0)


def with_sums(block, sums):
    row = lax.broadcasted_iota(jnp.int32, block.shape, 0)
    lane = lax.broadcasted_iota(jnp.int32, block.shape, 1)
    free = row == block.shape[0] - ROWS
    for i, total in enumerate(sums):
        rest = jnp.full(block.shape, total, F32)
        for part in range(3):
            piece = rest.astype(BF).astype(F32)
            block = jnp.where(free & (lane == HALF + 3 * i + part), piece, block)
            rest = rest - piece
    return block


def read_sums(msgs_ref, count):
    rows = msgs_ref.shape[1]
    tile = jnp.sum(msgs_ref[...].astype(F32), axis=0)[rows - ROWS :, :]
    row = lax.broadcasted_iota(jnp.int32, tile.shape, 0)
    lane = lax.broadcasted_iota(jnp.int32, tile.shape, 1)
    out = []
    for i in range(count):
        mine = (row == 0) & (lane >= HALF + 3 * i) & (lane < HALF + 3 * i + 3)
        out.append(jnp.sum(jnp.where(mine, tile, 0.0)))
    return out


def piece_copies(refs, parts, column, width, dest, sems):
    copies = []
    for d, piece in enumerate(parts):
        row = 0
        for ref, start, rows in piece:
            copies.append(
                pltpu.make_async_copy(
                    refs[ref].at[pl.ds(start, rows), pl.ds(column, width)],
                    dest.at[d, pl.ds(row, rows), :],
                    sems.at[len(copies)],
                )
            )
            row += rows
    return copies


def start_all(copies):
    for copy in copies:
        copy.start()


def wait_all(copies):
    for copy in copies:
        copy.wait()


def device_at(n_band, j, d):
    ka = jnp.bitwise_xor(lax.axis_index("ka"), j)
    return ka * n_band + jnp.bitwise_xor(lax.axis_index("band"), d)


def pair_rows(ref, kp):
    part = ref[:, kp * 2 * ROWS : (kp + 1) * 2 * ROWS, :]
    return part.reshape(part.shape[0] * 2 * ROWS, part.shape[2])


def pack_kernel(n_ka, nu, *refs):
    start_in, cond_in, val_in, val_ref, orb_ref = refs[:5]
    own_ref, gap_ref, outs, refs = refs[5], refs[6], refs[7 : 7 + n_ka], refs[7 + n_ka :]
    start_ref, cond_ref, energy_ref, cuts, sems, cut_sems = refs
    own = cuts.shape[-1]
    ins = ((start_in, start_ref), (cond_in, cond_ref), (val_in, energy_ref))
    small = [pltpu.make_async_copy(ref, to, sems.at[i]) for i, (ref, to) in enumerate(ins)]
    k_dev = val_ref.shape[0]
    val_copies, cut_copies = [], []
    for j in range(n_ka):
        at = pl.multiple_of(jnp.bitwise_xor(lax.axis_index("ka"), j) * nu, nu)
        point = pl.multiple_of(at + lax.axis_index("band") * own, LANES)
        val_copies.append(
            pltpu.make_async_copy(
                val_ref.at[:, :, pl.ds(at, nu)], outs[j].at[:, :, pl.ds(0, nu)], cut_sems.at[0, j]
            )
        )
        cut_copies.append(
            pltpu.make_async_copy(
                orb_ref.at[:, :, pl.ds(point, own)], cuts.at[j], cut_sems.at[1, j]
            )
        )
    start_all(small + cut_copies + val_copies)
    wait_all(small)
    own_ref[...] = jnp.zeros_like(own_ref)
    gap_ref[...] = jnp.zeros_like(gap_ref)
    cond = jnp.concatenate([cond_ref[...], cond_ref[...]], axis=1)
    for kl in range(k_dev):
        half = kl % 2
        for v in range(ROWS):
            at = pl.ds(kl // 2 * ROWS + v, 1)
            row = start_ref[pl.ds(kl, 1), pl.ds(v // 2 * LANES, LANES)]
            own_ref[at, :] = own_ref[at, :] + lane_half(row, v % 2, half)
            gap = cond[kl : kl + 1, :] - energy_ref[kl, v]
            gap_ref[at, :] = gap_ref[at, :] + lane_half(gap, half, half)
    mine = own_ref[...]
    square = mine * mine
    block = with_sums(mine, [jnp.sum(square), jnp.sum(gap_ref[...] * square)])
    for j in range(n_ka):
        for g in range(k_dev):
            head = jnp.zeros((ROWS, LANES), F32)
            if (g + 1) * ROWS <= block.shape[0]:
                head = block[g * ROWS : (g + 1) * ROWS, :]
            outs[j][g, :, nu : nu + LANES] = head.astype(BF)
        cut_copies[j].wait()
        for kl in range(k_dev):
            cut = cuts[j, kl].astype(F32)
            wide = [cut[q * ROWS : (q + 1) * ROWS, :] for q in range(cut.shape[0] // ROWS)]
            outs[j][kl, :, nu + LANES :] = jnp.concatenate(wide, axis=1).astype(BF)
    wait_all(val_copies)


def turn_kernel(tile, scr_ref, out_ref, scrs, turned, in_sems, out_sems):
    nu = scr_ref.shape[1]
    ins, outs = [], []
    for j in range(nu // tile):
        at = pl.ds(j * tile, tile)
        ins.append(pltpu.make_async_copy(scr_ref.at[:, at], scrs.at[:, at], in_sems.at[j]))
        outs.append(pltpu.make_async_copy(turned.at[at, :], out_ref.at[at, :], out_sems.at[j]))
    start_all(ins)
    for j in range(nu // tile):
        ins[j].wait()
        turned[j * tile : (j + 1) * tile, :] = scrs[:, j * tile : (j + 1) * tile].T
        outs[j].start()
    wait_all(outs)


def order_kernel(parts, n_ka, *refs):
    got_refs, val_refs, refs = refs[:n_ka], refs[n_ka:-13], refs[-13:]
    rows_out, turned_out, own_out, cond_out, msgs_out = refs[:5]
    vals, heads, ordered, turned, cuts, val_sems, out_sems, cut_sems = refs[5:]
    own = own_out.shape[1]
    nu = ordered.shape[1]
    copies = piece_copies(val_refs, parts, 0, nu, vals, val_sems.at[0])
    head_copies = piece_copies(val_refs, parts, nu, LANES, heads, val_sems.at[1])
    cut_copies = [
        pltpu.make_async_copy(
            ref.at[:, :, pl.ds(nu + LANES, cuts.shape[-1])], cuts.at[j], cut_sems.at[j]
        )
        for j, ref in enumerate(got_refs)
    ]
    start_all(copies + head_copies + cut_copies)
    wait_all(cut_copies)
    k_dev, points = cuts.shape[1], cuts.shape[-1] // own
    for j in range(n_ka):
        for kl in range(k_dev):
            cut = cuts[j, kl].astype(F32)
            tall = [cut[:, q * own : (q + 1) * own] for q in range(points)]
            at = (j * k_dev + kl) * points * ROWS
            cond_out[at : at + points * ROWS, :] = jnp.concatenate(tall, axis=0).astype(BF)
    wait_all(copies)
    n_band, group = vals.shape[0], vals.shape[0] * 2 * ROWS
    column = pl.multiple_of(lax.axis_index("band") * own, LANES)
    outs = []
    for kp in range(ordered.shape[0] // group):
        at = slice(kp * group, (kp + 1) * group)
        ordered[at, :] = pair_rows(vals, kp)
        turned[:, at] = ordered[at, :].T
        at = pl.ds(kp * group, group)
        outs += [
            pltpu.make_async_copy(ordered.at[at, :], rows_out.at[at, :], out_sems.at[0, kp]),
            pltpu.make_async_copy(turned.at[:, at], turned_out.at[:, at], out_sems.at[1, kp]),
            pltpu.make_async_copy(
                ordered.at[at, pl.ds(column, own)], own_out.at[at, :], out_sems.at[2, kp]
            ),
        ]
        start_all(outs[-3:])
    wait_all(head_copies)
    rows = msgs_out.shape[1]
    step = heads.shape[1] // n_ka
    for d in range(n_band):
        head = heads[d].astype(F32)
        for j in range(n_ka):
            msgs_out[device_at(n_band, j, d)] = head[j * step : j * step + rows, :].astype(BF)
    wait_all(outs)


def density_kernel(cfg, *refs):
    n_ka, n_band, k_dev = cfg
    k_points = n_ka * k_dev
    msgs_ref, vown_ref, cond_ref, qx_ref, rho_ref, xs, msgs, vown, conds, sems = refs
    own = vown_ref.shape[1]
    msg_copy = pltpu.make_async_copy(msgs_ref, msgs, sems.at[0])
    copies = [
        pltpu.make_async_copy(vown_ref, vown, sems.at[1]),
        pltpu.make_async_copy(cond_ref, conds, sems.at[2]),
    ]
    start_all([msg_copy] + copies)
    xs[...] = jnp.zeros_like(xs)
    msg_copy.wait()
    for d in range(n_band):
        for k in range(k_points):
            j, kl = divmod(k, k_dev)
            tile = msgs[device_at(n_band, j, d), :, :].astype(F32)
            tile = tile[kl // 2 * ROWS : (kl // 2 + 1) * ROWS, :]
            base = k // 2 % 2 * LANES
            at = pl.ds(base + d * 2 * ROWS + k % 2 * ROWS, ROWS)
            xs[k // 4, at, pl.ds(base, LANES)] = lane_half(tile, kl % 2, k % 2)
    qx_ref[...] = xs[...].astype(BF)
    wait_all(copies)
    rho = jnp.zeros((1, own), F32)
    quad = 2 * LANES
    for kq in range(k_points // 4):
        at = slice(kq * quad, (kq + 1) * quad)
        mixed = dot_tn(qx_ref[kq], vown[at, :])
        rho = rho + jnp.sum(mixed * conds[at, :].astype(F32), axis=0, keepdims=True)
    for r in range(own // LANES):
        part = rho[:, r * LANES : (r + 1) * LANES]
        rho_ref[:, r, :] = jnp.broadcast_to(part, (rho_ref.shape[0], LANES))


def direct_kernel(n_ka, tile, scale, *refs):
    turned_ref, scr_ref, rows_ref, qx_ref, refs = refs[0], refs[1], refs[2], refs[3], refs[4:]
    hops = [(0, 0)] + [(way, hop) for way in (-1, 1) for hop in range(1, n_ka)]
    cond_refs, refs = refs[: len(hops)], refs[len(hops) :]
    di_ref, qx, turned, conds, scrs, vals, mixed, kern, folded = refs[:9]
    qx_sem, cond_sems, row_sem, chunk_sems = refs[9:]
    nu, mu = scr_ref.shape
    quad = 2 * LANES
    qx_copy = pltpu.make_async_copy(qx_ref, qx, qx_sem.at[0])
    ka = lax.axis_index("ka")

    def each_cond(act):
        for i, (way, hop) in enumerate(hops):
            origin = ka + way * hop
            pl.when((origin >= 0) & (origin < n_ka))(
                lambda i=i, origin=origin: act(
                    pltpu.make_async_copy(
                        cond_refs[i], conds.at[jnp.bitwise_xor(ka, origin)], cond_sems.at[i]
                    )
                )
            )

    turned_copies, scr_copies = [], []
    for i in range(nu // tile):
        at = pl.ds(i * tile, tile)
        turned_copies.append(
            pltpu.make_async_copy(turned_ref.at[at, :], turned.at[at, :], chunk_sems.at[0, i])
        )
        scr_copies.append(
            pltpu.make_async_copy(scr_ref.at[at, :], scrs.at[at, :], chunk_sems.at[1, i])
        )
    row_copy = pltpu.make_async_copy(rows_ref, vals, row_sem.at[0])
    start_all([qx_copy, turned_copies[0]])
    each_cond(lambda copy: copy.start())
    qx_copy.wait()
    for i in range(nu // tile):
        rows = slice(i * tile, (i + 1) * tile)
        turned_copies[i].wait()
        scr_copies[i].start()
        for kq in range(qx.shape[0]):
            cols = slice(kq * quad, (kq + 1) * quad)
            mixed[rows, cols] = jnp.dot(
                turned[rows, cols], qx[kq], preferred_element_type=F32
            ).astype(BF)
        if i == 0:
            each_cond(lambda copy: copy.wait())
            cond_rows = conds[...].reshape(-1, mu)
        start_all(turned_copies[i + 1 : i + 2] or [row_copy])
        scr_copies[i].wait()
        amp = jnp.dot(mixed[rows, :], cond_rows, preferred_element_type=F32)
        kern[rows, :] = (scrs[rows, :].astype(F32) * amp * scale).astype(BF)
    row_copy.wait()
    folded[...] = jnp.dot(vals[...], kern[...], preferred_element_type=F32).astype(BF)
    for kp in range(di_ref.shape[0]):
        at = slice(kp * LANES, (kp + 1) * LANES)
        di_ref[kp] = dot_nt(folded[at, :], cond_rows[at, :])


def exchange_kernel(cfg, chunk, scale, *refs):
    n_ka, n_band, k_dev = cfg
    k_points = n_ka * k_dev
    rho_ref, di_ref, coul_ref, vown_ref, cond_ref, msg_ref = refs[:6]
    rhos, di, coul, conds, vown, part, msg, coul_sems, sems = refs[6:]
    own, npt = coul_ref.shape
    coul_copies = [
        pltpu.make_async_copy(
            coul_ref.at[:, pl.ds(i * chunk, chunk)], coul.at[:, pl.ds(i * chunk, chunk)], coul_sems.at[i]
        )
        for i in range(npt // chunk)
    ]
    rho_copy = pltpu.make_async_copy(rho_ref, rhos, sems.at[0])
    copies = [
        pltpu.make_async_copy(vown_ref, vown, sems.at[1]),
        pltpu.make_async_copy(di_ref, di, sems.at[2]),
        pltpu.make_async_copy(cond_ref, conds, sems.at[3]),
    ]
    ahead = 2
    start_all([rho_copy] + coul_copies[:ahead])
    rho_copy.wait()
    acc = jnp.zeros((own, LANES), F32)
    per_dev = own // LANES
    for i in range(npt // chunk):
        coul_copies[i].wait()
        start_all(coul_copies[i + ahead : i + ahead + 1])
        if i + ahead == npt // chunk:
            start_all(copies)
        for j in range(i * chunk // LANES, (i + 1) * chunk // LANES):
            rho = rhos[j // per_dev, pl.ds(j % per_dev, 1), :].astype(BF).astype(F32)
            acc = acc + coul[:, j * LANES : (j + 1) * LANES].astype(F32) * rho
    potential = scale * jnp.sum(acc.T, axis=0, keepdims=True)
    wait_all(copies)
    for kp in range(k_points // 2):
        at = slice(kp * LANES, (kp + 1) * LANES)
        weighted = (vown[at, :].astype(F32) * potential).astype(BF)
        part[kp] = 2.0 * dot_nt(weighted, conds[at, :]) - di[kp]
    for d in range(n_band):
        for j in range(n_ka):
            for g in range((k_dev + 1) // 2):
                tile = None
                for kl in range(2 * g, min(2 * g + 2, k_dev)):
                    k = j * k_dev + kl
                    piece = part[k // 2, pl.ds(d * 2 * ROWS + k % 2 * ROWS, ROWS), :]
                    piece = lane_half(piece, k % 2, kl % 2)
                    tile = piece if tile is None else tile + piece
                msg[device_at(n_band, j, d), pl.ds(g * ROWS, ROWS), :] = tile
    msg_ref[...] = msg[...].astype(BF)


def received(recv_ref):
    return jnp.sum(recv_ref[...].astype(F32), axis=0)


def shifted(count_all, shift, square, cross_sum, square_sum):
    alpha = shift * square + cross_sum / count_all
    d = alpha - shift
    mean_sq = (square_sum - 2.0 * d * cross_sum) / count_all + d * d * square
    mean_sq = jnp.maximum(mean_sq, 0.0)
    return alpha, d, mean_sq


def first_owner_kernel(count_all, recv_ref, msgs_ref, gap_ref, own_ref, state_ref, coef_ref, msg_ref):
    start_sq, gap_sq = read_sums(msgs_ref, 2)
    norm = start_sq / count_all
    inv = 1.0 / jnp.sqrt(norm + 1e-06)
    square = norm / (norm + 1e-06)
    shift = gap_sq / jnp.maximum(start_sq, 1e-30)
    cur = own_ref[...] * inv
    inter = received(recv_ref) * inv
    gap = gap_ref[...]
    resid = (gap - shift) * cur + inter
    state_ref[0] = cur
    state_ref[1] = resid
    state_ref[2] = inter
    coef_ref[0] = shift
    coef_ref[1] = square
    coef_ref[2] = gap_sq * inv * inv
    sums = [
        jnp.sum(cur * resid),
        jnp.sum(resid * resid),
        jnp.sum(gap * resid * resid),
        jnp.sum(gap * resid * cur),
    ]
    msg_ref[...] = jnp.broadcast_to(with_sums(resid, sums).astype(BF)[None], msg_ref.shape)


def second_owner_kernel(count_all, recv_ref, msgs_ref, gap_ref, state_ref, coef_ref, out_ref, coef_out, msg_ref):
    cross, total, gap_rr, gap_rq = read_sums(msgs_ref, 4)
    alpha, d, mean_sq = shifted(count_all, coef_ref[0], coef_ref[1], cross, total)
    beta = jnp.sqrt(mean_sq + 1e-06)
    square = mean_sq / (mean_sq + 1e-06)
    gap_qq = gap_rr - 2.0 * d * gap_rq + d * d * coef_ref[2]
    shift = gap_qq / (mean_sq + 1e-06) / count_all
    prev = state_ref[0]
    cur = (state_ref[1] - d * prev) / beta
    inter = (received(recv_ref) - d * state_ref[2]) / beta
    resid = (gap_ref[...] - shift) * cur + inter - beta * prev
    out_ref[0] = cur
    out_ref[1] = resid
    coef_out[0] = alpha
    coef_out[1] = beta
    coef_out[2] = shift
    coef_out[3] = square
    dims = msg_ref.shape[:1] + msg_ref.shape[2:]
    msg_ref[:, 0, :] = jnp.full(dims, jnp.sum(cur * resid), F32)
    msg_ref[:, 1, :] = jnp.full(dims, jnp.sum(resid * resid), F32)


def finish_kernel(count_all, msgs_ref, state_ref, coef_ref, out_ref, coeffs_ref):
    sums = jnp.sum(msgs_ref[...], axis=0)
    alpha, d, mean_sq = shifted(count_all, coef_ref[2], coef_ref[3], sums[0, 0], sums[1, 0])
    beta = jnp.sqrt(mean_sq + 1e-06)
    own = (state_ref[1] - d * state_ref[0]) / beta
    coeffs_ref[0] = coef_ref[0]
    coeffs_ref[1] = alpha
    coeffs_ref[2] = coef_ref[1]
    coeffs_ref[3] = beta
    for kl in range(out_ref.shape[0]):
        tile = own[kl // 2 * ROWS : (kl // 2 + 1) * ROWS, :]
        other = pltpu.roll(tile, HALF, axis=1)
        left, right = (tile, other) if kl % 2 == 0 else (other, tile)
        low = lax.broadcasted_iota(jnp.int32, (1, LANES), 1) < HALF
        for j in range(ROWS // 2):
            row = jnp.where(low, left[2 * j : 2 * j + 1], right[2 * j + 1 : 2 * j + 2])
            out_ref[pl.ds(kl, 1), pl.ds(j * LANES, LANES)] = row


def shape_of(dims, kind=F32):
    return jax.ShapeDtypeStruct(dims, kind)


def call(kernel, name, out_shape, in_specs, out_specs, scratch=(), mib=58, flops=0, moved=0):
    return pl.pallas_call(
        kernel,
        out_shape=out_shape,
        in_specs=in_specs,
        out_specs=out_specs,
        scratch_shapes=list(scratch),
        compiler_params=pltpu.CompilerParams(vmem_limit_bytes=mib * MIB),
        cost_estimate=pl.CostEstimate(flops=flops, bytes_accessed=moved, transcendentals=0),
        name=name,
    )


def dma(*dims):
    return pltpu.SemaphoreType.DMA(dims)


def swap(block, axis, d):
    return lax.ppermute(block, axis, [(i, i ^ d) for i in range(lax.axis_size(axis))])


def line_gather(block, axis):
    n = lax.axis_size(axis)
    flows = []
    for way in (-1, 1):
        moving, flow = block, []
        for hop in range(1, n):
            senders = [i for i in range(n) if 0 <= i + way * (hop - 1) < n and 0 <= i - way < n]
            moving = lax.ppermute(moving, axis, [(i, i - way) for i in senders])
            flow.append(moving)
        flows.append(flow)
    return flows


def plane_pieces(own_piece, others, later):
    def move(block, d):
        return swap(block, "band", d)

    rows = own_piece.shape[0]
    half = rows // 2
    by_x, by_y, core = move(own_piece, 2), move(own_piece, 4), move(own_piece, 1)
    by_x, by_y, core, others = lax.optimization_barrier((by_x, by_y, core, others))
    diag = [move(by_x[:half], 4), move(by_y[half:], 2)]
    near_x, near_y = move(by_x, 1), move(by_y, 1)
    diag, later = lax.optimization_barrier((diag, later))
    far = move(jnp.concatenate(diag, axis=0), 1)
    arrays = [own_piece, core, by_x, near_x, by_y, near_y, diag[0], diag[1], far]
    parts = tuple(((i, 0, rows),) for i in range(6))
    parts += (((6, 0, half), (7, 0, half)), ((8, 0, rows),))
    return arrays, parts, others, later


def kernel_path(start_vec, val_energy, cond_energy, val_orb, cond_orb, coulomb, screened):
    n_ka = lax.axis_size("ka")
    n_band = lax.axis_size("band")
    devices = n_ka * n_band
    ka, band = lax.axis_index("ka"), lax.axis_index("band")
    k_dev = start_vec.shape[0]
    nv_blk = val_orb.shape[1]
    n_cond = cond_orb.shape[1]
    npt_all = cond_orb.shape[2]
    k_points = k_dev * n_ka
    pairs = k_points // 2
    mu_blk, nu_blk = screened.shape
    own = coulomb.shape[0]
    count_all = k_points * nv_blk * n_band * n_cond
    scale = 1.0 / (npt_all * math.sqrt(count_all))
    piece_rows = k_points * nv_blk

    block = ((k_dev + 1) // 2 * ROWS, LANES)
    msg_shape = shape_of((devices,) + block, BF)
    wide = nu_blk + LANES
    cut_lanes = n_cond // ROWS * own
    start_own, gap, *payloads = call(
        functools.partial(pack_kernel, n_ka, nu_blk),
        "pack",
        (shape_of(block), shape_of(block))
        + (shape_of((k_dev, nv_blk, wide + cut_lanes), BF),) * n_ka,
        [ANY] * 5,
        (VMEM,) * (2 + n_ka),
        [
            pltpu.VMEM(start_vec.shape, F32),
            pltpu.VMEM(cond_energy.shape, F32),
            pltpu.SMEM(val_energy.shape, F32),
            pltpu.VMEM((n_ka, k_dev, n_cond, own), BF),
            dma(3),
            dma(2, n_ka),
        ],
    )(start_vec, cond_energy, val_energy, val_orb, cond_orb)
    base, payloads = lax.optimization_barrier((band * mu_blk, payloads))
    got = [payloads[0]] + [swap(payloads[j], "ka", j) for j in range(1, n_ka)]
    val_cut = jnp.concatenate([part[:, :, :wide] for part in got], axis=0)
    val_cut = val_cut.reshape(piece_rows, wide)
    cond_local = lax.dynamic_slice_in_dim(cond_orb, base, mu_blk, 2)
    cond_local = cond_local.reshape(k_dev * n_cond, mu_blk)
    below, above = line_gather(cond_local, "ka")

    chunk, tile = 1024, 1024
    rows_all, conds_all = k_points * nv_blk * n_band, k_points * n_cond
    scr_turned = call(
        functools.partial(turn_kernel, tile // 2),
        "turn",
        shape_of((nu_blk, mu_blk), BF),
        [ANY],
        ANY,
        [pltpu.VMEM((mu_blk, nu_blk), BF), pltpu.VMEM((nu_blk, mu_blk), BF)]
        + [dma(2 * nu_blk // tile)] * 2,
        moved=8 * MIB,
    )(screened)
    pieces, parts, others, later = plane_pieces(
        val_cut, (scr_turned, below[0], above[0]), (below[1:-1], above[1:-1])
    )
    scr_turned, below[0], above[0] = others
    below[1:-1], above[1:-1] = later
    val_rows, val_turned, val_own, cond_own, msgs = call(
        functools.partial(order_kernel, parts, n_ka),
        "order",
        (
            shape_of((rows_all, nu_blk), BF),
            shape_of((nu_blk, rows_all), BF),
            shape_of((rows_all, own), BF),
            shape_of((conds_all, own), BF),
            msg_shape,
        ),
        [ANY] * (n_ka + len(pieces)),
        (ANY, ANY, ANY, VMEM, VMEM),
        [
            pltpu.VMEM((n_band, piece_rows, nu_blk), BF),
            pltpu.VMEM((n_band, piece_rows, LANES), BF),
            pltpu.VMEM((rows_all, nu_blk), BF),
            pltpu.VMEM((nu_blk, rows_all), BF),
            pltpu.VMEM((n_ka, k_dev, nv_blk, cut_lanes), BF),
            dma(2, sum(len(piece) for piece in parts)),
            dma(3, pairs),
            dma(n_ka),
        ],
        moved=9 * MIB,
    )(*got, *pieces)

    cond_pts = [cond_local] + below + above
    cfg = (n_ka, n_band, k_dev)
    quads = k_points // 4
    state, coef = None, None
    for step in range(STEPS):
        first = step == 0
        qx, rho = call(
            functools.partial(density_kernel, cfg),
            "density",
            (
                shape_of((quads, 2 * LANES, 2 * LANES), BF),
                shape_of((devices, own // LANES, LANES)),
            ),
            [ANY] * 3,
            (VMEM, VMEM),
            [
                pltpu.VMEM((quads, 2 * LANES, 2 * LANES), F32),
                pltpu.VMEM((devices,) + block, BF),
                pltpu.VMEM((rows_all, own), BF),
                pltpu.VMEM((conds_all, own), BF),
                dma(3),
            ],
        )(msgs, val_own, cond_own)
        density = exchange_all(rho)
        direct = call(
            functools.partial(direct_kernel, n_ka, tile, scale),
            "direct",
            shape_of((pairs, LANES, LANES)),
            [ANY] * (4 + len(cond_pts)),
            VMEM,
            [
                pltpu.VMEM((quads, 2 * LANES, 2 * LANES), BF),
                pltpu.VMEM((nu_blk, rows_all), BF),
                pltpu.VMEM((n_ka, k_dev * n_cond, mu_blk), BF),
                pltpu.VMEM((nu_blk, mu_blk), BF),
                pltpu.VMEM((rows_all, nu_blk), BF),
                pltpu.VMEM((nu_blk, conds_all), BF),
                pltpu.VMEM((nu_blk, mu_blk), BF),
                pltpu.VMEM((rows_all, mu_blk), BF),
                dma(1),
                dma(len(cond_pts)),
                dma(1),
                dma(2, nu_blk // tile),
            ],
            flops=4 * mu_blk * nu_blk * conds_all,
            moved=12 * MIB,
        )(val_turned, scr_turned, val_rows, qx, *cond_pts)
        summed = call(
            functools.partial(exchange_kernel, cfg, chunk, scale),
            "exchange",
            msg_shape,
            [ANY] * 5,
            VMEM,
            [
                pltpu.VMEM((devices, own // LANES, LANES), F32),
                pltpu.VMEM((pairs, LANES, LANES), F32),
                pltpu.VMEM((own, npt_all), BF),
                pltpu.VMEM((conds_all, own), BF),
                pltpu.VMEM((rows_all, own), BF),
                pltpu.VMEM((pairs, LANES, LANES), F32),
                pltpu.VMEM((devices,) + block, F32),
                dma(npt_all // chunk),
                dma(4),
            ],
        )(density, direct, coulomb, val_own, cond_own)
        recv = exchange_all(summed)
        if first:
            state, coef, message = call(
                functools.partial(first_owner_kernel, count_all),
                "first_owner",
                (shape_of((3,) + block), shape_of((3,)), msg_shape),
                [VMEM] * 4,
                (VMEM, SMEM, VMEM),
                mib=8,
            )(recv, msgs, gap, start_own)
        else:
            state, coef, message = call(
                functools.partial(second_owner_kernel, count_all),
                "second_owner",
                (shape_of((2,) + block), shape_of((4,)), shape_of((devices, 2, LANES))),
                [VMEM] * 4 + [SMEM],
                (VMEM, SMEM, VMEM),
                mib=8,
            )(recv, msgs, gap, state, coef)
        msgs = exchange_all(message)
    return call(
        functools.partial(finish_kernel, count_all),
        "finish",
        (shape_of(start_vec.shape), shape_of((2 * STEPS,))),
        [VMEM] * 2 + [SMEM],
        (VMEM, SMEM),
        mib=8,
    )(msgs, state, coef)


def array_path(start_vec, val_energy, cond_energy, val_orb, cond_orb, coulomb, screened):
    n_ka = lax.axis_size("ka")
    n_band = lax.axis_size("band")
    devices = n_ka * n_band
    ka, band = lax.axis_index("ka"), lax.axis_index("band")
    me = ka * n_band + band
    k_dev, pair_blk = start_vec.shape
    nv_blk = val_orb.shape[1]
    n_cond = cond_orb.shape[1]
    n_val = nv_blk * n_band
    npt_all = cond_orb.shape[2]
    k_points = k_dev * n_ka
    mu_blk, nu_blk = screened.shape
    own_pts = coulomb.shape[0]
    count_all = k_points * n_val * n_cond
    kernel_scale = 1.0 / (npt_all * math.sqrt(count_all))

    start_all = gather_all(start_vec, devices)
    val_cut = lax.all_to_all(
        val_orb.reshape(k_dev, nv_blk, n_ka, nu_blk).transpose(2, 0, 1, 3),
        "ka", split_axis=0, concat_axis=0, tiled=True,
    ).reshape(k_points, nv_blk, nu_blk)
    val_pts = lax.all_gather(val_cut, "band", axis=1, tiled=True)
    cond_local = lax.dynamic_slice_in_dim(cond_orb, band * mu_blk, mu_blk, 2)
    cond_pts = lax.all_gather(cond_local, "ka", axis=0, tiled=True)
    cond_rows = cond_orb.reshape(k_dev, n_cond, n_ka, n_band, own_pts)
    cond_rows = lax.dynamic_index_in_dim(cond_rows, band, 3, keepdims=False)
    cond_own = lax.all_to_all(
        cond_rows.transpose(2, 0, 1, 3), "ka", split_axis=0, concat_axis=0, tiled=True
    ).reshape(k_points, n_cond, own_pts)
    val_own = lax.dynamic_slice_in_dim(val_pts, band * own_pts, own_pts, 2)

    energy_gap = (cond_energy[:, None, :] - val_energy[:, :, None]).reshape(k_dev, pair_blk)
    start_sq = jnp.sum(start_all * start_all)
    current = start_all / jnp.sqrt(start_sq / count_all + 1e-06)
    previous = jnp.zeros_like(current)
    beta_val = jnp.float32(0.0)
    alphas = []
    betas = []
    for turn_index in range(STEPS):
        full_vec = (
            current.astype(BF)
            .reshape(n_ka, n_band, k_dev, nv_blk, n_cond)
            .transpose(0, 2, 1, 3, 4)
            .reshape(k_points, n_val, n_cond)
        )
        mixed_f = jnp.einsum("kvc,kvn->kcn", full_vec, val_pts, preferred_element_type=F32)
        mixed_own = lax.dynamic_slice_in_dim(mixed_f, band * own_pts, own_pts, 2)
        density_own = jnp.sum(mixed_own * cond_own.astype(F32), axis=(0, 1))
        density = gather_all(density_own.astype(BF), devices).reshape(npt_all)
        mixed_val = mixed_f.astype(BF)
        amp = jnp.einsum("kcm,kcn->mn", cond_pts, mixed_val, preferred_element_type=F32)
        kern = (screened.astype(F32) * amp * kernel_scale).astype(BF)
        folded = jnp.einsum("mn,kvn->kvm", kern, val_pts, preferred_element_type=F32).astype(BF)
        direct_part = jnp.einsum("kcm,kvm->kvc", cond_pts, folded, preferred_element_type=F32)
        potential = kernel_scale * jnp.dot(coulomb, density, preferred_element_type=F32)
        weighted = (val_own.astype(F32) * potential).astype(BF)
        exchange = jnp.einsum("kvp,kcp->kvc", weighted, cond_own, preferred_element_type=F32)
        part = 2.0 * exchange - direct_part
        arranged = (
            part.reshape(n_ka, k_dev, n_band, nv_blk, n_cond)
            .transpose(0, 2, 1, 3, 4)
            .reshape(devices, k_dev, pair_blk)
        )
        inter_own = jnp.sum(exchange_all(arranged), axis=0)
        current_own = lax.dynamic_index_in_dim(current, me, 0, keepdims=False)
        resid_vec = gather_all(energy_gap * current_own + inter_own, devices)
        resid_vec = resid_vec - beta_val * previous
        alpha_val = jnp.sum(current * resid_vec) / count_all
        resid_vec = resid_vec - alpha_val * current
        beta_val = jnp.sqrt(jnp.sum(resid_vec * resid_vec) / count_all + 1e-06)
        previous = current
        current = resid_vec / beta_val
        alphas.append(alpha_val)
        betas.append(beta_val)
    coeffs = jnp.stack(alphas + betas)
    return (lax.dynamic_index_in_dim(current, me, 0, keepdims=False), coeffs)


def per_device(*args):
    start_vec, _, _, val_orb, cond_orb, coulomb, screened = args
    n_ka, n_band = lax.axis_size("ka"), lax.axis_size("band")
    fits = (
        n_band == 8
        and n_ka & (n_ka - 1) == 0
        and start_vec.shape[0] % 2 == 1
        and val_orb.shape[1] == ROWS
        and cond_orb.shape[1] == HALF
        and start_vec.shape[0] * n_ka % 4 == 0
        and coulomb.shape[0] % LANES == 0
        and coulomb.shape[1] % 1024 == 0
        and screened.shape[0] % 512 == 0
        and screened.shape[1] % 1024 == 0
        and screened.shape[0] * screened.shape[1] <= 2 * MIB
    )
    return (kernel_path if fits else array_path)(*args)


def solution(mesh):
    in_specs = (
        P("ka", "band"),
        P("ka", "band"),
        P("ka", None),
        P("ka", "band", None),
        P("ka", None, None),
        P(("ka", "band"), None),
        P("band", "ka"),
    )
    out_specs = (P("ka", "band"), P())
    return jax.shard_map(
        per_device, mesh=mesh, in_specs=in_specs, out_specs=out_specs, check_vma=False
    )
```

```python
import functools
import math

import jax
import jax.numpy as jnp
from jax import lax
from jax.experimental import pallas as pl
from jax.experimental.pallas import tpu as pltpu
from jax.sharding import PartitionSpec as P

STEPS = 2
AXES = ("ka", "band")
BF, F32 = jnp.bfloat16, jnp.float32
LANES = 128
HALF = 64
ROWS = 8
MIB = 1 << 20

VMEM = pl.BlockSpec(memory_space=pltpu.VMEM)
SMEM = pl.BlockSpec(memory_space=pltpu.SMEM)
ANY = pl.BlockSpec(memory_space=pl.ANY)


def gather_all(block, devices):
    wide = jnp.broadcast_to(block[None], (devices,) + block.shape)
    return exchange_all(wide)


def exchange_all(parts):
    return lax.all_to_all(parts, AXES, split_axis=0, concat_axis=0, tiled=True)


def dot_nt(lhs, rhs):
    return lax.dot_general(lhs, rhs, (((1,), (1,)), ((), ())), preferred_element_type=F32)


def dot_tn(lhs, rhs):
    return lax.dot_general(lhs, rhs, (((0,), (0,)), ((), ())), preferred_element_type=F32)


def lane_half(tile, have, want):
    if have != want:
        tile = pltpu.roll(tile, HALF, axis=1)
    lane = lax.broadcasted_iota(jnp.int32, tile.shape, 1)
    keep = lane < HALF if want == 0 else lane >= HALF
    return jnp.where(keep, tile, 0.0)


def with_sums(block, sums):
    row = lax.broadcasted_iota(jnp.int32, block.shape, 0)
    lane = lax.broadcasted_iota(jnp.int32, block.shape, 1)
    free = row == block.shape[0] - ROWS
    for i, total in enumerate(sums):
        rest = jnp.full(block.shape, total, F32)
        for part in range(3):
            piece = rest.astype(BF).astype(F32)
            block = jnp.where(free & (lane == HALF + 3 * i + part), piece, block)
            rest = rest - piece
    return block


def read_sums(msgs_ref, count):
    rows = msgs_ref.shape[1]
    tile = jnp.sum(msgs_ref[...].astype(F32), axis=0)[rows - ROWS :, :]
    row = lax.broadcasted_iota(jnp.int32, tile.shape, 0)
    lane = lax.broadcasted_iota(jnp.int32, tile.shape, 1)
    out = []
    for i in range(count):
        mine = (row == 0) & (lane >= HALF + 3 * i) & (lane < HALF + 3 * i + 3)
        out.append(jnp.sum(jnp.where(mine, tile, 0.0)))
    return out


def piece_copies(refs, parts, column, width, dest, sems):
    copies = []
    for d, piece in enumerate(parts):
        row = 0
        for ref, start, rows in piece:
            copies.append(
                pltpu.make_async_copy(
                    refs[ref].at[pl.ds(start, rows), pl.ds(column, width)],
                    dest.at[d, pl.ds(row, rows), :],
                    sems.at[len(copies)],
                )
            )
            row += rows
    return copies


def start_all(copies):
    for copy in copies:
        copy.start()


def wait_all(copies):
    for copy in copies:
        copy.wait()


def device_at(n_band, j, d):
    ka = jnp.bitwise_xor(lax.axis_index("ka"), j)
    return ka * n_band + jnp.bitwise_xor(lax.axis_index("band"), d)


def pair_rows(ref, kp):
    part = ref[:, kp * 2 * ROWS : (kp + 1) * 2 * ROWS, :]
    return part.reshape(part.shape[0] * 2 * ROWS, part.shape[2])


def pack_kernel(n_ka, nu, *refs):
    start_in, cond_in, val_in, val_ref, orb_ref = refs[:5]
    own_ref, gap_ref, outs, refs = refs[5], refs[6], refs[7 : 7 + n_ka], refs[7 + n_ka :]
    start_ref, cond_ref, energy_ref, cuts, sems, cut_sems = refs
    own = cuts.shape[-1]
    ins = ((start_in, start_ref), (cond_in, cond_ref), (val_in, energy_ref))
    small = [pltpu.make_async_copy(ref, to, sems.at[i]) for i, (ref, to) in enumerate(ins)]
    k_dev = val_ref.shape[0]
    val_copies, cut_copies = [], []
    for j in range(n_ka):
        at = pl.multiple_of(jnp.bitwise_xor(lax.axis_index("ka"), j) * nu, nu)
        point = pl.multiple_of(at + lax.axis_index("band") * own, LANES)
        val_copies.append(
            pltpu.make_async_copy(
                val_ref.at[:, :, pl.ds(at, nu)], outs[j].at[:, :, pl.ds(0, nu)], cut_sems.at[0, j]
            )
        )
        cut_copies.append(
            pltpu.make_async_copy(
                orb_ref.at[:, :, pl.ds(point, own)], cuts.at[j], cut_sems.at[1, j]
            )
        )
    start_all(small + cut_copies + val_copies)
    wait_all(small)
    own_ref[...] = jnp.zeros_like(own_ref)
    gap_ref[...] = jnp.zeros_like(gap_ref)
    cond = jnp.concatenate([cond_ref[...], cond_ref[...]], axis=1)
    for kl in range(k_dev):
        half = kl % 2
        for v in range(ROWS):
            at = pl.ds(kl // 2 * ROWS + v, 1)
            row = start_ref[pl.ds(kl, 1), pl.ds(v // 2 * LANES, LANES)]
            own_ref[at, :] = own_ref[at, :] + lane_half(row, v % 2, half)
            gap = cond[kl : kl + 1, :] - energy_ref[kl, v]
            gap_ref[at, :] = gap_ref[at, :] + lane_half(gap, half, half)
    mine = own_ref[...]
    square = mine * mine
    block = with_sums(mine, [jnp.sum(square), jnp.sum(gap_ref[...] * square)])
    for j in range(n_ka):
        for g in range(k_dev):
            head = jnp.zeros((ROWS, LANES), F32)
            if (g + 1) * ROWS <= block.shape[0]:
                head = block[g * ROWS : (g + 1) * ROWS, :]
            outs[j][g, :, nu : nu + LANES] = head.astype(BF)
        cut_copies[j].wait()
        for kl in range(k_dev):
            cut = cuts[j, kl].astype(F32)
            wide = [cut[q * ROWS : (q + 1) * ROWS, :] for q in range(cut.shape[0] // ROWS)]
            outs[j][kl, :, nu + LANES :] = jnp.concatenate(wide, axis=1).astype(BF)
    wait_all(val_copies)


def turn_kernel(tile, scr_ref, out_ref, scrs, turned, in_sems, out_sems):
    nu = scr_ref.shape[1]
    ins, outs = [], []
    for j in range(nu // tile):
        at = pl.ds(j * tile, tile)
        ins.append(pltpu.make_async_copy(scr_ref.at[:, at], scrs.at[:, at], in_sems.at[j]))
        outs.append(pltpu.make_async_copy(turned.at[at, :], out_ref.at[at, :], out_sems.at[j]))
    start_all(ins)
    for j in range(nu // tile):
        ins[j].wait()
        turned[j * tile : (j + 1) * tile, :] = scrs[:, j * tile : (j + 1) * tile].T
        outs[j].start()
    wait_all(outs)


def order_kernel(parts, n_ka, *refs):
    got_refs, val_refs, refs = refs[:n_ka], refs[n_ka:-13], refs[-13:]
    rows_out, turned_out, own_out, cond_out, msgs_out = refs[:5]
    vals, heads, ordered, turned, cuts, val_sems, out_sems, cut_sems = refs[5:]
    own = own_out.shape[1]
    nu = ordered.shape[1]
    copies = piece_copies(val_refs, parts, 0, nu, vals, val_sems.at[0])
    head_copies = piece_copies(val_refs, parts, nu, LANES, heads, val_sems.at[1])
    cut_copies = [
        pltpu.make_async_copy(
            ref.at[:, :, pl.ds(nu + LANES, cuts.shape[-1])], cuts.at[j], cut_sems.at[j]
        )
        for j, ref in enumerate(got_refs)
    ]
    start_all(copies + head_copies + cut_copies)
    wait_all(cut_copies)
    k_dev, points = cuts.shape[1], cuts.shape[-1] // own
    for j in range(n_ka):
        for kl in range(k_dev):
            cut = cuts[j, kl].astype(F32)
            tall = [cut[:, q * own : (q + 1) * own] for q in range(points)]
            at = (j * k_dev + kl) * points * ROWS
            cond_out[at : at + points * ROWS, :] = jnp.concatenate(tall, axis=0).astype(BF)
    wait_all(copies)
    n_band, group = vals.shape[0], vals.shape[0] * 2 * ROWS
    column = pl.multiple_of(lax.axis_index("band") * own, LANES)
    outs = []
    for kp in range(ordered.shape[0] // group):
        at = slice(kp * group, (kp + 1) * group)
        ordered[at, :] = pair_rows(vals, kp)
        turned[:, at] = ordered[at, :].T
        at = pl.ds(kp * group, group)
        outs += [
            pltpu.make_async_copy(ordered.at[at, :], rows_out.at[at, :], out_sems.at[0, kp]),
            pltpu.make_async_copy(turned.at[:, at], turned_out.at[:, at], out_sems.at[1, kp]),
            pltpu.make_async_copy(
                ordered.at[at, pl.ds(column, own)], own_out.at[at, :], out_sems.at[2, kp]
            ),
        ]
        start_all(outs[-3:])
    wait_all(head_copies)
    rows = msgs_out.shape[1]
    step = heads.shape[1] // n_ka
    for d in range(n_band):
        head = heads[d].astype(F32)
        for j in range(n_ka):
            msgs_out[device_at(n_band, j, d)] = head[j * step : j * step + rows, :].astype(BF)
    wait_all(outs)


def density_kernel(cfg, *refs):
    n_ka, n_band, k_dev = cfg
    k_points = n_ka * k_dev
    msgs_ref, vown_ref, cond_ref, qx_ref, rho_ref, xs, msgs, vown, conds, sems = refs
    own = vown_ref.shape[1]
    msg_copy = pltpu.make_async_copy(msgs_ref, msgs, sems.at[0])
    copies = [
        pltpu.make_async_copy(vown_ref, vown, sems.at[1]),
        pltpu.make_async_copy(cond_ref, conds, sems.at[2]),
    ]
    start_all([msg_copy] + copies)
    xs[...] = jnp.zeros_like(xs)
    msg_copy.wait()
    for d in range(n_band):
        for k in range(k_points):
            j, kl = divmod(k, k_dev)
            tile = msgs[device_at(n_band, j, d), :, :].astype(F32)
            tile = tile[kl // 2 * ROWS : (kl // 2 + 1) * ROWS, :]
            base = k // 2 % 2 * LANES
            at = pl.ds(base + d * 2 * ROWS + k % 2 * ROWS, ROWS)
            xs[k // 4, at, pl.ds(base, LANES)] = lane_half(tile, kl % 2, k % 2)
    qx_ref[...] = xs[...].astype(BF)
    wait_all(copies)
    rho = jnp.zeros((1, own), F32)
    quad = 2 * LANES
    for kq in range(k_points // 4):
        at = slice(kq * quad, (kq + 1) * quad)
        mixed = dot_tn(qx_ref[kq], vown[at, :])
        rho = rho + jnp.sum(mixed * conds[at, :].astype(F32), axis=0, keepdims=True)
    for r in range(own // LANES):
        part = rho[:, r * LANES : (r + 1) * LANES]
        rho_ref[:, r, :] = jnp.broadcast_to(part, (rho_ref.shape[0], LANES))


def direct_kernel(n_ka, tile, scale, *refs):
    turned_ref, scr_ref, rows_ref, qx_ref, refs = refs[0], refs[1], refs[2], refs[3], refs[4:]
    hops = [(0, 0)] + [(way, hop) for way in (-1, 1) for hop in range(1, n_ka)]
    cond_refs, refs = refs[: len(hops)], refs[len(hops) :]
    di_ref, qx, turned, conds, scrs, vals, mixed, kern, folded = refs[:9]
    qx_sem, cond_sems, row_sem, chunk_sems = refs[9:]
    nu, mu = scr_ref.shape
    quad = 2 * LANES
    qx_copy = pltpu.make_async_copy(qx_ref, qx, qx_sem.at[0])
    ka = lax.axis_index("ka")

    def each_cond(act):
        for i, (way, hop) in enumerate(hops):
            origin = ka + way * hop
            pl.when((origin >= 0) & (origin < n_ka))(
                lambda i=i, origin=origin: act(
                    pltpu.make_async_copy(
                        cond_refs[i], conds.at[jnp.bitwise_xor(ka, origin)], cond_sems.at[i]
                    )
                )
            )

    turned_copies, scr_copies = [], []
    for i in range(nu // tile):
        at = pl.ds(i * tile, tile)
        turned_copies.append(
            pltpu.make_async_copy(turned_ref.at[at, :], turned.at[at, :], chunk_sems.at[0, i])
        )
        scr_copies.append(
            pltpu.make_async_copy(scr_ref.at[at, :], scrs.at[at, :], chunk_sems.at[1, i])
        )
    row_copy = pltpu.make_async_copy(rows_ref, vals, row_sem.at[0])
    start_all([qx_copy, turned_copies[0]])
    each_cond(lambda copy: copy.start())
    scr_copies[0].start()
    for i in range(1, nu // tile):
        start_all([turned_copies[i], scr_copies[i]])
    row_copy.start()
    qx_copy.wait()
    for i in range(nu // tile):
        rows = slice(i * tile, (i + 1) * tile)
        turned_copies[i].wait()
        for kq in range(qx.shape[0]):
            cols = slice(kq * quad, (kq + 1) * quad)
            mixed[rows, cols] = jnp.dot(
                turned[rows, cols], qx[kq], preferred_element_type=F32
            ).astype(BF)
        if i == 0:
            each_cond(lambda copy: copy.wait())
            cond_rows = conds[...].reshape(-1, mu)
        scr_copies[i].wait()
        amp = jnp.dot(mixed[rows, :], cond_rows, preferred_element_type=F32)
        kern[rows, :] = (scrs[rows, :].astype(F32) * amp * scale).astype(BF)
    row_copy.wait()
    folded[...] = jnp.dot(vals[...], kern[...], preferred_element_type=F32).astype(BF)
    for kp in range(di_ref.shape[0]):
        at = slice(kp * LANES, (kp + 1) * LANES)
        di_ref[kp] = dot_nt(folded[at, :], cond_rows[at, :])


def exchange_kernel(cfg, chunk, scale, *refs):
    n_ka, n_band, k_dev = cfg
    k_points = n_ka * k_dev
    rho_ref, di_ref, coul_ref, vown_ref, cond_ref, msg_ref = refs[:6]
    rhos, di, coul, conds, vown, part, msg, coul_sems, sems = refs[6:]
    own, npt = coul_ref.shape
    coul_copies = [
        pltpu.make_async_copy(
            coul_ref.at[:, pl.ds(i * chunk, chunk)], coul.at[:, pl.ds(i * chunk, chunk)], coul_sems.at[i]
        )
        for i in range(npt // chunk)
    ]
    rho_copy = pltpu.make_async_copy(rho_ref, rhos, sems.at[0])
    copies = [
        pltpu.make_async_copy(vown_ref, vown, sems.at[1]),
        pltpu.make_async_copy(di_ref, di, sems.at[2]),
        pltpu.make_async_copy(cond_ref, conds, sems.at[3]),
    ]
    start_all([rho_copy] + coul_copies + copies)
    rho_copy.wait()
    acc = jnp.zeros((own, LANES), F32)
    per_dev = own // LANES
    for i in range(npt // chunk):
        coul_copies[i].wait()
        for j in range(i * chunk // LANES, (i + 1) * chunk // LANES):
            rho = rhos[j // per_dev, pl.ds(j % per_dev, 1), :].astype(BF).astype(F32)
            acc = acc + coul[:, j * LANES : (j + 1) * LANES].astype(F32) * rho
    potential = scale * jnp.sum(acc.T, axis=0, keepdims=True)
    wait_all(copies)
    for kp in range(k_points // 2):
        at = slice(kp * LANES, (kp + 1) * LANES)
        weighted = (vown[at, :].astype(F32) * potential).astype(BF)
        part[kp] = 2.0 * dot_nt(weighted, conds[at, :]) - di[kp]
    for d in range(n_band):
        for j in range(n_ka):
            for g in range((k_dev + 1) // 2):
                tile = None
                for kl in range(2 * g, min(2 * g + 2, k_dev)):
                    k = j * k_dev + kl
                    piece = part[k // 2, pl.ds(d * 2 * ROWS + k % 2 * ROWS, ROWS), :]
                    piece = lane_half(piece, k % 2, kl % 2)
                    tile = piece if tile is None else tile + piece
                msg[device_at(n_band, j, d), pl.ds(g * ROWS, ROWS), :] = tile
    msg_ref[...] = msg[...].astype(BF)


def received(recv_ref):
    return jnp.sum(recv_ref[...].astype(F32), axis=0)


def shifted(count_all, shift, square, cross_sum, square_sum):
    alpha = shift * square + cross_sum / count_all
    d = alpha - shift
    mean_sq = (square_sum - 2.0 * d * cross_sum) / count_all + d * d * square
    mean_sq = jnp.maximum(mean_sq, 0.0)
    return alpha, d, mean_sq


def first_owner_kernel(count_all, recv_ref, msgs_ref, gap_ref, own_ref, state_ref, coef_ref, msg_ref):
    start_sq, gap_sq = read_sums(msgs_ref, 2)
    norm = start_sq / count_all
    inv = 1.0 / jnp.sqrt(norm + 1e-06)
    square = norm / (norm + 1e-06)
    shift = gap_sq / jnp.maximum(start_sq, 1e-30)
    cur = own_ref[...] * inv
    inter = received(recv_ref) * inv
    gap = gap_ref[...]
    resid = (gap - shift) * cur + inter
    state_ref[0] = cur
    state_ref[1] = resid
    state_ref[2] = inter
    coef_ref[0] = shift
    coef_ref[1] = square
    coef_ref[2] = gap_sq * inv * inv
    sums = [
        jnp.sum(cur * resid),
        jnp.sum(resid * resid),
        jnp.sum(gap * resid * resid),
        jnp.sum(gap * resid * cur),
    ]
    msg_ref[...] = jnp.broadcast_to(with_sums(resid, sums).astype(BF)[None], msg_ref.shape)


def second_owner_kernel(count_all, recv_ref, msgs_ref, gap_ref, state_ref, coef_ref, out_ref, coef_out, msg_ref):
    cross, total, gap_rr, gap_rq = read_sums(msgs_ref, 4)
    alpha, d, mean_sq = shifted(count_all, coef_ref[0], coef_ref[1], cross, total)
    beta = jnp.sqrt(mean_sq + 1e-06)
    square = mean_sq / (mean_sq + 1e-06)
    gap_qq = gap_rr - 2.0 * d * gap_rq + d * d * coef_ref[2]
    shift = gap_qq / (mean_sq + 1e-06) / count_all
    prev = state_ref[0]
    cur = (state_ref[1] - d * prev) / beta
    inter = (received(recv_ref) - d * state_ref[2]) / beta
    resid = (gap_ref[...] - shift) * cur + inter - beta * prev
    out_ref[0] = cur
    out_ref[1] = resid
    coef_out[0] = alpha
    coef_out[1] = beta
    coef_out[2] = shift
    coef_out[3] = square
    dims = msg_ref.shape[:1] + msg_ref.shape[2:]
    msg_ref[:, 0, :] = jnp.full(dims, jnp.sum(cur * resid), F32)
    msg_ref[:, 1, :] = jnp.full(dims, jnp.sum(resid * resid), F32)


def finish_kernel(count_all, msgs_ref, state_ref, coef_ref, out_ref, coeffs_ref):
    sums = jnp.sum(msgs_ref[...], axis=0)
    alpha, d, mean_sq = shifted(count_all, coef_ref[2], coef_ref[3], sums[0, 0], sums[1, 0])
    beta = jnp.sqrt(mean_sq + 1e-06)
    own = (state_ref[1] - d * state_ref[0]) / beta
    coeffs_ref[0] = coef_ref[0]
    coeffs_ref[1] = alpha
    coeffs_ref[2] = coef_ref[1]
    coeffs_ref[3] = beta
    for kl in range(out_ref.shape[0]):
        tile = own[kl // 2 * ROWS : (kl // 2 + 1) * ROWS, :]
        other = pltpu.roll(tile, HALF, axis=1)
        left, right = (tile, other) if kl % 2 == 0 else (other, tile)
        low = lax.broadcasted_iota(jnp.int32, (1, LANES), 1) < HALF
        for j in range(ROWS // 2):
            row = jnp.where(low, left[2 * j : 2 * j + 1], right[2 * j + 1 : 2 * j + 2])
            out_ref[pl.ds(kl, 1), pl.ds(j * LANES, LANES)] = row


def shape_of(dims, kind=F32):
    return jax.ShapeDtypeStruct(dims, kind)


def call(kernel, name, out_shape, in_specs, out_specs, scratch=(), mib=58, flops=0, moved=0):
    return pl.pallas_call(
        kernel,
        out_shape=out_shape,
        in_specs=in_specs,
        out_specs=out_specs,
        scratch_shapes=list(scratch),
        compiler_params=pltpu.CompilerParams(vmem_limit_bytes=mib * MIB),
        cost_estimate=pl.CostEstimate(flops=flops, bytes_accessed=moved, transcendentals=0),
        name=name,
    )


def dma(*dims):
    return pltpu.SemaphoreType.DMA(dims)


def swap(block, axis, d):
    return lax.ppermute(block, axis, [(i, i ^ d) for i in range(lax.axis_size(axis))])


def line_gather(block, axis):
    n = lax.axis_size(axis)
    flows = [[], []]
    for hop in range(3, n):
        up = [(i, i + hop) for i in range(n - hop)]
        down = [(i, j) for j, i in up]
        if hop == n - 1:
            both = lax.ppermute(block, axis, up + down)
            block, both = lax.optimization_barrier((block, both))
            far = (both, both)
        else:
            far = (lax.ppermute(block, axis, up), lax.ppermute(block, axis, down))
        for flow, part in zip(flows, far):
            flow.append(part)
    for side, way in enumerate((-1, 1)):
        moving, flow = block, []
        for hop in range(1, min(n, 3)):
            senders = [i for i in range(n) if 0 <= i + way * (hop - 1) < n and 0 <= i - way < n]
            moving = lax.ppermute(moving, axis, [(i, i - way) for i in senders])
            flow.append(moving)
        flows[side] = flow + flows[side]
    return flows


def plane_pieces(own_piece, others):
    def move(block, d):
        return swap(block, "band", d)

    rows = own_piece.shape[0]
    half = rows // 2
    by_x, by_y = move(own_piece, 2), move(own_piece, 4)
    by_x, by_y, others = lax.optimization_barrier((by_x, by_y, others))
    diag = [move(by_x[:half], 4), move(by_y[half:], 2)]
    near = move(jnp.concatenate([own_piece, by_x, by_y], axis=0), 1)
    far = move(jnp.concatenate(diag, axis=0), 1)
    arrays = [own_piece, near, by_x, by_y, diag[0], diag[1], far]
    parts = (
        ((0, 0, rows),),
        ((1, 0, rows),),
        ((2, 0, rows),),
        ((1, rows, rows),),
        ((3, 0, rows),),
        ((1, 2 * rows, rows),),
        ((4, 0, half), (5, 0, half)),
        ((6, 0, rows),),
    )
    return arrays, parts, others


def kernel_path(start_vec, val_energy, cond_energy, val_orb, cond_orb, coulomb, screened):
    n_ka = lax.axis_size("ka")
    n_band = lax.axis_size("band")
    devices = n_ka * n_band
    ka, band = lax.axis_index("ka"), lax.axis_index("band")
    k_dev = start_vec.shape[0]
    nv_blk = val_orb.shape[1]
    n_cond = cond_orb.shape[1]
    npt_all = cond_orb.shape[2]
    k_points = k_dev * n_ka
    pairs = k_points // 2
    mu_blk, nu_blk = screened.shape
    own = coulomb.shape[0]
    count_all = k_points * nv_blk * n_band * n_cond
    scale = 1.0 / (npt_all * math.sqrt(count_all))
    piece_rows = k_points * nv_blk

    block = ((k_dev + 1) // 2 * ROWS, LANES)
    msg_shape = shape_of((devices,) + block, BF)
    wide = nu_blk + LANES
    cut_lanes = n_cond // ROWS * own
    start_own, gap, *payloads = call(
        functools.partial(pack_kernel, n_ka, nu_blk),
        "pack",
        (shape_of(block), shape_of(block))
        + (shape_of((k_dev, nv_blk, wide + cut_lanes), BF),) * n_ka,
        [ANY] * 5,
        (VMEM,) * (2 + n_ka),
        [
            pltpu.VMEM(start_vec.shape, F32),
            pltpu.VMEM(cond_energy.shape, F32),
            pltpu.SMEM(val_energy.shape, F32),
            pltpu.VMEM((n_ka, k_dev, n_cond, own), BF),
            dma(3),
            dma(2, n_ka),
        ],
    )(start_vec, cond_energy, val_energy, val_orb, cond_orb)
    base, payloads = lax.optimization_barrier((band * mu_blk, payloads))
    got = [payloads[0]] + [swap(payloads[j], "ka", j) for j in range(1, n_ka)]
    val_cut = jnp.concatenate([part[:, :, :wide] for part in got], axis=0)
    val_cut = val_cut.reshape(piece_rows, wide)
    cond_local = lax.dynamic_slice_in_dim(cond_orb, base, mu_blk, 2)
    cond_local = cond_local.reshape(k_dev * n_cond, mu_blk)
    below, above = line_gather(cond_local, "ka")

    chunk, tile = 1024, 1024
    rows_all, conds_all = k_points * nv_blk * n_band, k_points * n_cond
    scr_turned = call(
        functools.partial(turn_kernel, tile // 2),
        "turn",
        shape_of((nu_blk, mu_blk), BF),
        [ANY],
        ANY,
        [pltpu.VMEM((mu_blk, nu_blk), BF), pltpu.VMEM((nu_blk, mu_blk), BF)]
        + [dma(2 * nu_blk // tile)] * 2,
        moved=8 * MIB,
    )(screened)
    pieces, parts, (scr_turned, below[0], above[0]) = plane_pieces(
        val_cut, (scr_turned, below[0], above[0])
    )
    val_rows, val_turned, val_own, cond_own, msgs = call(
        functools.partial(order_kernel, parts, n_ka),
        "order",
        (
            shape_of((rows_all, nu_blk), BF),
            shape_of((nu_blk, rows_all), BF),
            shape_of((rows_all, own), BF),
            shape_of((conds_all, own), BF),
            msg_shape,
        ),
        [ANY] * (n_ka + len(pieces)),
        (ANY, ANY, ANY, VMEM, VMEM),
        [
            pltpu.VMEM((n_band, piece_rows, nu_blk), BF),
            pltpu.VMEM((n_band, piece_rows, LANES), BF),
            pltpu.VMEM((rows_all, nu_blk), BF),
            pltpu.VMEM((nu_blk, rows_all), BF),
            pltpu.VMEM((n_ka, k_dev, nv_blk, cut_lanes), BF),
            dma(2, sum(len(piece) for piece in parts)),
            dma(3, pairs),
            dma(n_ka),
        ],
        moved=9 * MIB,
    )(*got, *pieces)

    msgs, below, above = lax.optimization_barrier((msgs, below, above))
    cond_pts = [cond_local] + below + above
    cfg = (n_ka, n_band, k_dev)
    quads = k_points // 4
    state, coef = None, None
    for step in range(STEPS):
        first = step == 0
        qx, rho = call(
            functools.partial(density_kernel, cfg),
            "density",
            (
                shape_of((quads, 2 * LANES, 2 * LANES), BF),
                shape_of((devices, own // LANES, LANES)),
            ),
            [ANY] * 3,
            (VMEM, VMEM),
            [
                pltpu.VMEM((quads, 2 * LANES, 2 * LANES), F32),
                pltpu.VMEM((devices,) + block, BF),
                pltpu.VMEM((rows_all, own), BF),
                pltpu.VMEM((conds_all, own), BF),
                dma(3),
            ],
        )(msgs, val_own, cond_own)
        density = exchange_all(rho)
        direct = call(
            functools.partial(direct_kernel, n_ka, tile, scale),
            "direct",
            shape_of((pairs, LANES, LANES)),
            [ANY] * (4 + len(cond_pts)),
            VMEM,
            [
                pltpu.VMEM((quads, 2 * LANES, 2 * LANES), BF),
                pltpu.VMEM((nu_blk, rows_all), BF),
                pltpu.VMEM((n_ka, k_dev * n_cond, mu_blk), BF),
                pltpu.VMEM((nu_blk, mu_blk), BF),
                pltpu.VMEM((rows_all, nu_blk), BF),
                pltpu.VMEM((nu_blk, conds_all), BF),
                pltpu.VMEM((nu_blk, mu_blk), BF),
                pltpu.VMEM((rows_all, mu_blk), BF),
                dma(1),
                dma(len(cond_pts)),
                dma(1),
                dma(2, nu_blk // tile),
            ],
            flops=4 * mu_blk * nu_blk * conds_all,
            moved=12 * MIB,
        )(val_turned, scr_turned, val_rows, qx, *cond_pts)
        summed = call(
            functools.partial(exchange_kernel, cfg, chunk, scale),
            "exchange",
            msg_shape,
            [ANY] * 5,
            VMEM,
            [
                pltpu.VMEM((devices, own // LANES, LANES), F32),
                pltpu.VMEM((pairs, LANES, LANES), F32),
                pltpu.VMEM((own, npt_all), BF),
                pltpu.VMEM((conds_all, own), BF),
                pltpu.VMEM((rows_all, own), BF),
                pltpu.VMEM((pairs, LANES, LANES), F32),
                pltpu.VMEM((devices,) + block, F32),
                dma(npt_all // chunk),
                dma(4),
            ],
        )(density, direct, coulomb, val_own, cond_own)
        recv = exchange_all(summed)
        if first:
            state, coef, message = call(
                functools.partial(first_owner_kernel, count_all),
                "first_owner",
                (shape_of((3,) + block), shape_of((3,)), msg_shape),
                [VMEM] * 4,
                (VMEM, SMEM, VMEM),
                mib=8,
            )(recv, msgs, gap, start_own)
        else:
            state, coef, message = call(
                functools.partial(second_owner_kernel, count_all),
                "second_owner",
                (shape_of((2,) + block), shape_of((4,)), shape_of((devices, 2, LANES))),
                [VMEM] * 4 + [SMEM],
                (VMEM, SMEM, VMEM),
                mib=8,
            )(recv, msgs, gap, state, coef)
        msgs = exchange_all(message)
    return call(
        functools.partial(finish_kernel, count_all),
        "finish",
        (shape_of(start_vec.shape), shape_of((2 * STEPS,))),
        [VMEM] * 2 + [SMEM],
        (VMEM, SMEM),
        mib=8,
    )(msgs, state, coef)


def array_path(start_vec, val_energy, cond_energy, val_orb, cond_orb, coulomb, screened):
    n_ka = lax.axis_size("ka")
    n_band = lax.axis_size("band")
    devices = n_ka * n_band
    ka, band = lax.axis_index("ka"), lax.axis_index("band")
    me = ka * n_band + band
    k_dev, pair_blk = start_vec.shape
    nv_blk = val_orb.shape[1]
    n_cond = cond_orb.shape[1]
    n_val = nv_blk * n_band
    npt_all = cond_orb.shape[2]
    k_points = k_dev * n_ka
    mu_blk, nu_blk = screened.shape
    own_pts = coulomb.shape[0]
    count_all = k_points * n_val * n_cond
    kernel_scale = 1.0 / (npt_all * math.sqrt(count_all))

    start_all = gather_all(start_vec, devices)
    val_cut = lax.all_to_all(
        val_orb.reshape(k_dev, nv_blk, n_ka, nu_blk).transpose(2, 0, 1, 3),
        "ka", split_axis=0, concat_axis=0, tiled=True,
    ).reshape(k_points, nv_blk, nu_blk)
    val_pts = lax.all_gather(val_cut, "band", axis=1, tiled=True)
    cond_local = lax.dynamic_slice_in_dim(cond_orb, band * mu_blk, mu_blk, 2)
    cond_pts = lax.all_gather(cond_local, "ka", axis=0, tiled=True)
    cond_rows = cond_orb.reshape(k_dev, n_cond, n_ka, n_band, own_pts)
    cond_rows = lax.dynamic_index_in_dim(cond_rows, band, 3, keepdims=False)
    cond_own = lax.all_to_all(
        cond_rows.transpose(2, 0, 1, 3), "ka", split_axis=0, concat_axis=0, tiled=True
    ).reshape(k_points, n_cond, own_pts)
    val_own = lax.dynamic_slice_in_dim(val_pts, band * own_pts, own_pts, 2)

    energy_gap = (cond_energy[:, None, :] - val_energy[:, :, None]).reshape(k_dev, pair_blk)
    start_sq = jnp.sum(start_all * start_all)
    current = start_all / jnp.sqrt(start_sq / count_all + 1e-06)
    previous = jnp.zeros_like(current)
    beta_val = jnp.float32(0.0)
    alphas = []
    betas = []
    for turn_index in range(STEPS):
        full_vec = (
            current.astype(BF)
            .reshape(n_ka, n_band, k_dev, nv_blk, n_cond)
            .transpose(0, 2, 1, 3, 4)
            .reshape(k_points, n_val, n_cond)
        )
        mixed_f = jnp.einsum("kvc,kvn->kcn", full_vec, val_pts, preferred_element_type=F32)
        mixed_own = lax.dynamic_slice_in_dim(mixed_f, band * own_pts, own_pts, 2)
        density_own = jnp.sum(mixed_own * cond_own.astype(F32), axis=(0, 1))
        density = gather_all(density_own.astype(BF), devices).reshape(npt_all)
        mixed_val = mixed_f.astype(BF)
        amp = jnp.einsum("kcm,kcn->mn", cond_pts, mixed_val, preferred_element_type=F32)
        kern = (screened.astype(F32) * amp * kernel_scale).astype(BF)
        folded = jnp.einsum("mn,kvn->kvm", kern, val_pts, preferred_element_type=F32).astype(BF)
        direct_part = jnp.einsum("kcm,kvm->kvc", cond_pts, folded, preferred_element_type=F32)
        potential = kernel_scale * jnp.dot(coulomb, density, preferred_element_type=F32)
        weighted = (val_own.astype(F32) * potential).astype(BF)
        exchange = jnp.einsum("kvp,kcp->kvc", weighted, cond_own, preferred_element_type=F32)
        part = 2.0 * exchange - direct_part
        arranged = (
            part.reshape(n_ka, k_dev, n_band, nv_blk, n_cond)
            .transpose(0, 2, 1, 3, 4)
            .reshape(devices, k_dev, pair_blk)
        )
        inter_own = jnp.sum(exchange_all(arranged), axis=0)
        current_own = lax.dynamic_index_in_dim(current, me, 0, keepdims=False)
        resid_vec = gather_all(energy_gap * current_own + inter_own, devices)
        resid_vec = resid_vec - beta_val * previous
        alpha_val = jnp.sum(current * resid_vec) / count_all
        resid_vec = resid_vec - alpha_val * current
        beta_val = jnp.sqrt(jnp.sum(resid_vec * resid_vec) / count_all + 1e-06)
        previous = current
        current = resid_vec / beta_val
        alphas.append(alpha_val)
        betas.append(beta_val)
    coeffs = jnp.stack(alphas + betas)
    return (lax.dynamic_index_in_dim(current, me, 0, keepdims=False), coeffs)


def per_device(*args):
    start_vec, _, _, val_orb, cond_orb, coulomb, screened = args
    n_ka, n_band = lax.axis_size("ka"), lax.axis_size("band")
    fits = (
        n_band == 8
        and n_ka & (n_ka - 1) == 0
        and start_vec.shape[0] % 2 == 1
        and val_orb.shape[1] == ROWS
        and cond_orb.shape[1] == HALF
        and start_vec.shape[0] * n_ka % 4 == 0
        and coulomb.shape[0] % LANES == 0
        and coulomb.shape[1] % 1024 == 0
        and screened.shape[0] % 512 == 0
        and screened.shape[1] % 1024 == 0
        and screened.shape[0] * screened.shape[1] <= 2 * MIB
    )
    return (kernel_path if fits else array_path)(*args)


def solution(mesh):
    in_specs = (
        P("ka", "band"),
        P("ka", "band"),
        P("ka", None),
        P("ka", "band", None),
        P("ka", None, None),
        P(("ka", "band"), None),
        P("band", "ka"),
    )
    out_specs = (P("ka", "band"), P())
    return jax.shard_map(
        per_device, mesh=mesh, in_specs=in_specs, out_specs=out_specs, check_vma=False
    )
```

```python
import functools
import math

import jax
import jax.numpy as jnp
from jax import lax
from jax.experimental import pallas as pl
from jax.experimental.pallas import tpu as pltpu
from jax.sharding import PartitionSpec as P

STEPS = 2
AXES = ("ka", "band")
BF, F32 = jnp.bfloat16, jnp.float32
LANES = 128
HALF = 64
ROWS = 8
MIB = 1 << 20

VMEM = pl.BlockSpec(memory_space=pltpu.VMEM)
SMEM = pl.BlockSpec(memory_space=pltpu.SMEM)
ANY = pl.BlockSpec(memory_space=pl.ANY)


def gather_all(block, devices):
    wide = jnp.broadcast_to(block[None], (devices,) + block.shape)
    return exchange_all(wide)


def exchange_all(parts):
    return lax.all_to_all(parts, AXES, split_axis=0, concat_axis=0, tiled=True)


def dot_nt(lhs, rhs):
    return lax.dot_general(lhs, rhs, (((1,), (1,)), ((), ())), preferred_element_type=F32)


def dot_tn(lhs, rhs):
    return lax.dot_general(lhs, rhs, (((0,), (0,)), ((), ())), preferred_element_type=F32)


def lane_half(tile, have, want):
    if have != want:
        tile = pltpu.roll(tile, HALF, axis=1)
    lane = lax.broadcasted_iota(jnp.int32, tile.shape, 1)
    keep = lane < HALF if want == 0 else lane >= HALF
    return jnp.where(keep, tile, 0.0)


def with_sums(block, sums):
    row = lax.broadcasted_iota(jnp.int32, block.shape, 0)
    lane = lax.broadcasted_iota(jnp.int32, block.shape, 1)
    free = row == block.shape[0] - ROWS
    for i, total in enumerate(sums):
        rest = jnp.full(block.shape, total, F32)
        for part in range(3):
            piece = rest.astype(BF).astype(F32)
            block = jnp.where(free & (lane == HALF + 3 * i + part), piece, block)
            rest = rest - piece
    return block


def read_sums(msgs_ref, count):
    rows = msgs_ref.shape[1]
    tile = jnp.sum(msgs_ref[...].astype(F32), axis=0)[rows - ROWS :, :]
    row = lax.broadcasted_iota(jnp.int32, tile.shape, 0)
    lane = lax.broadcasted_iota(jnp.int32, tile.shape, 1)
    out = []
    for i in range(count):
        mine = (row == 0) & (lane >= HALF + 3 * i) & (lane < HALF + 3 * i + 3)
        out.append(jnp.sum(jnp.where(mine, tile, 0.0)))
    return out


def piece_copies(refs, parts, column, width, dest, sems):
    copies = []
    for d, piece in enumerate(parts):
        row = 0
        for ref, start, rows in piece:
            copies.append(
                pltpu.make_async_copy(
                    refs[ref].at[pl.ds(start, rows), pl.ds(column, width)],
                    dest.at[d, pl.ds(row, rows), :],
                    sems.at[len(copies)],
                )
            )
            row += rows
    return copies


def start_all(copies):
    for copy in copies:
        copy.start()


def wait_all(copies):
    for copy in copies:
        copy.wait()


def device_at(n_band, j, d):
    ka = jnp.bitwise_xor(lax.axis_index("ka"), j)
    return ka * n_band + jnp.bitwise_xor(lax.axis_index("band"), d)


def pair_rows(ref, kp):
    part = ref[:, kp * 2 * ROWS : (kp + 1) * 2 * ROWS, :]
    return part.reshape(part.shape[0] * 2 * ROWS, part.shape[2])


def pack_kernel(n_ka, nu, *refs):
    start_in, cond_in, val_in, val_ref, orb_ref = refs[:5]
    own_ref, gap_ref, outs, refs = refs[5], refs[6], refs[7 : 7 + n_ka], refs[7 + n_ka :]
    start_ref, cond_ref, energy_ref, cuts, sems, cut_sems = refs
    own = cuts.shape[-1]
    ins = ((start_in, start_ref), (cond_in, cond_ref), (val_in, energy_ref))
    small = [pltpu.make_async_copy(ref, to, sems.at[i]) for i, (ref, to) in enumerate(ins)]
    k_dev = val_ref.shape[0]
    val_copies, cut_copies = [], []
    for j in range(n_ka):
        at = pl.multiple_of(jnp.bitwise_xor(lax.axis_index("ka"), j) * nu, nu)
        point = pl.multiple_of(at + lax.axis_index("band") * own, LANES)
        val_copies.append(
            pltpu.make_async_copy(
                val_ref.at[:, :, pl.ds(at, nu)], outs[j].at[:, :, pl.ds(0, nu)], cut_sems.at[0, j]
            )
        )
        cut_copies.append(
            pltpu.make_async_copy(
                orb_ref.at[:, :, pl.ds(point, own)], cuts.at[j], cut_sems.at[1, j]
            )
        )
    start_all(small + cut_copies + val_copies)
    wait_all(small)
    own_ref[...] = jnp.zeros_like(own_ref)
    gap_ref[...] = jnp.zeros_like(gap_ref)
    cond = jnp.concatenate([cond_ref[...], cond_ref[...]], axis=1)
    for kl in range(k_dev):
        half = kl % 2
        for v in range(ROWS):
            at = pl.ds(kl // 2 * ROWS + v, 1)
            row = start_ref[pl.ds(kl, 1), pl.ds(v // 2 * LANES, LANES)]
            own_ref[at, :] = own_ref[at, :] + lane_half(row, v % 2, half)
            gap = cond[kl : kl + 1, :] - energy_ref[kl, v]
            gap_ref[at, :] = gap_ref[at, :] + lane_half(gap, half, half)
    mine = own_ref[...]
    square = mine * mine
    block = with_sums(mine, [jnp.sum(square), jnp.sum(gap_ref[...] * square)])
    for j in range(n_ka):
        for g in range(k_dev):
            head = jnp.zeros((ROWS, LANES), F32)
            if (g + 1) * ROWS <= block.shape[0]:
                head = block[g * ROWS : (g + 1) * ROWS, :]
            outs[j][g, :, nu : nu + LANES] = head.astype(BF)
        cut_copies[j].wait()
        for kl in range(k_dev):
            cut = cuts[j, kl].astype(F32)
            wide = [cut[q * ROWS : (q + 1) * ROWS, :] for q in range(cut.shape[0] // ROWS)]
            outs[j][kl, :, nu + LANES :] = jnp.concatenate(wide, axis=1).astype(BF)
    wait_all(val_copies)


def turn_kernel(tile, scr_ref, out_ref, scrs, turned, in_sems, out_sems):
    nu = scr_ref.shape[1]
    ins, outs = [], []
    for j in range(nu // tile):
        at = pl.ds(j * tile, tile)
        ins.append(pltpu.make_async_copy(scr_ref.at[:, at], scrs.at[:, at], in_sems.at[j]))
        outs.append(pltpu.make_async_copy(turned.at[at, :], out_ref.at[at, :], out_sems.at[j]))
    start_all(ins)
    for j in range(nu // tile):
        ins[j].wait()
        turned[j * tile : (j + 1) * tile, :] = scrs[:, j * tile : (j + 1) * tile].T
        outs[j].start()
    wait_all(outs)


def order_kernel(parts, n_ka, *refs):
    got_refs, val_refs, refs = refs[:n_ka], refs[n_ka:-13], refs[-13:]
    rows_out, turned_out, own_out, cond_out, msgs_out = refs[:5]
    vals, heads, ordered, turned, cuts, val_sems, out_sems, cut_sems = refs[5:]
    own = own_out.shape[1]
    nu = ordered.shape[1]
    copies = piece_copies(val_refs, parts, 0, nu, vals, val_sems.at[0])
    head_copies = piece_copies(val_refs, parts, nu, LANES, heads, val_sems.at[1])
    cut_copies = [
        pltpu.make_async_copy(
            ref.at[:, :, pl.ds(nu + LANES, cuts.shape[-1])], cuts.at[j], cut_sems.at[j]
        )
        for j, ref in enumerate(got_refs)
    ]
    start_all(copies + head_copies + cut_copies)
    wait_all(cut_copies)
    k_dev, points = cuts.shape[1], cuts.shape[-1] // own
    for j in range(n_ka):
        for kl in range(k_dev):
            cut = cuts[j, kl].astype(F32)
            tall = [cut[:, q * own : (q + 1) * own] for q in range(points)]
            at = (j * k_dev + kl) * points * ROWS
            cond_out[at : at + points * ROWS, :] = jnp.concatenate(tall, axis=0).astype(BF)
    wait_all(copies)
    n_band, group = vals.shape[0], vals.shape[0] * 2 * ROWS
    column = pl.multiple_of(lax.axis_index("band") * own, LANES)
    outs = []
    for kp in range(ordered.shape[0] // group):
        at = slice(kp * group, (kp + 1) * group)
        ordered[at, :] = pair_rows(vals, kp)
        turned[:, at] = ordered[at, :].T
        at = pl.ds(kp * group, group)
        outs += [
            pltpu.make_async_copy(ordered.at[at, :], rows_out.at[at, :], out_sems.at[0, kp]),
            pltpu.make_async_copy(turned.at[:, at], turned_out.at[:, at], out_sems.at[1, kp]),
            pltpu.make_async_copy(
                ordered.at[at, pl.ds(column, own)], own_out.at[at, :], out_sems.at[2, kp]
            ),
        ]
        start_all(outs[-3:])
    wait_all(head_copies)
    rows = msgs_out.shape[1]
    step = heads.shape[1] // n_ka
    for d in range(n_band):
        head = heads[d].astype(F32)
        for j in range(n_ka):
            msgs_out[device_at(n_band, j, d)] = head[j * step : j * step + rows, :].astype(BF)
    wait_all(outs)


def density_kernel(cfg, *refs):
    n_ka, n_band, k_dev = cfg
    k_points = n_ka * k_dev
    msgs_ref, vown_ref, cond_ref, qx_ref, rho_ref, xs, msgs, vown, conds, sems = refs
    own = vown_ref.shape[1]
    msg_copy = pltpu.make_async_copy(msgs_ref, msgs, sems.at[0])
    copies = [
        pltpu.make_async_copy(vown_ref, vown, sems.at[1]),
        pltpu.make_async_copy(cond_ref, conds, sems.at[2]),
    ]
    start_all([msg_copy] + copies)
    xs[...] = jnp.zeros_like(xs)
    msg_copy.wait()
    for d in range(n_band):
        for k in range(k_points):
            j, kl = divmod(k, k_dev)
            tile = msgs[device_at(n_band, j, d), :, :].astype(F32)
            tile = tile[kl // 2 * ROWS : (kl // 2 + 1) * ROWS, :]
            base = k // 2 % 2 * LANES
            at = pl.ds(base + d * 2 * ROWS + k % 2 * ROWS, ROWS)
            xs[k // 4, at, pl.ds(base, LANES)] = lane_half(tile, kl % 2, k % 2)
    qx_ref[...] = xs[...].astype(BF)
    wait_all(copies)
    rho = jnp.zeros((1, own), F32)
    quad = 2 * LANES
    for kq in range(k_points // 4):
        at = slice(kq * quad, (kq + 1) * quad)
        mixed = dot_tn(qx_ref[kq], vown[at, :])
        rho = rho + jnp.sum(mixed * conds[at, :].astype(F32), axis=0, keepdims=True)
    for r in range(own // LANES):
        part = rho[:, r * LANES : (r + 1) * LANES]
        rho_ref[:, r, :] = jnp.broadcast_to(part, (rho_ref.shape[0], LANES))


def direct_kernel(n_ka, tile, scale, *refs):
    turned_ref, scr_ref, rows_ref, qx_ref, refs = refs[0], refs[1], refs[2], refs[3], refs[4:]
    hops = [(0, 0)] + [(way, hop) for way in (-1, 1) for hop in range(1, n_ka)]
    cond_refs, refs = refs[: len(hops)], refs[len(hops) :]
    di_ref, qx, turned, conds, scrs, vals, mixed, kern, folded = refs[:9]
    qx_sem, cond_sems, row_sem, chunk_sems = refs[9:]
    nu, mu = scr_ref.shape
    quad = 2 * LANES
    qx_copy = pltpu.make_async_copy(qx_ref, qx, qx_sem.at[0])
    ka = lax.axis_index("ka")

    def each_cond(act):
        for i, (way, hop) in enumerate(hops):
            origin = ka + way * hop
            pl.when((origin >= 0) & (origin < n_ka))(
                lambda i=i, origin=origin: act(
                    pltpu.make_async_copy(
                        cond_refs[i], conds.at[jnp.bitwise_xor(ka, origin)], cond_sems.at[i]
                    )
                )
            )

    turned_copies, scr_copies = [], []
    for i in range(nu // tile):
        at = pl.ds(i * tile, tile)
        turned_copies.append(
            pltpu.make_async_copy(turned_ref.at[at, :], turned.at[at, :], chunk_sems.at[0, i])
        )
        scr_copies.append(
            pltpu.make_async_copy(scr_ref.at[at, :], scrs.at[at, :], chunk_sems.at[1, i])
        )
    row_copy = pltpu.make_async_copy(rows_ref, vals, row_sem.at[0])
    start_all([qx_copy, turned_copies[0]])
    each_cond(lambda copy: copy.start())
    scr_copies[0].start()
    for i in range(1, nu // tile):
        start_all([turned_copies[i], scr_copies[i]])
    row_copy.start()
    qx_copy.wait()
    for i in range(nu // tile):
        rows = slice(i * tile, (i + 1) * tile)
        turned_copies[i].wait()
        for kq in range(qx.shape[0]):
            cols = slice(kq * quad, (kq + 1) * quad)
            mixed[rows, cols] = jnp.dot(
                turned[rows, cols], qx[kq], preferred_element_type=F32
            ).astype(BF)
        if i == 0:
            each_cond(lambda copy: copy.wait())
            cond_rows = conds[...].reshape(-1, mu)
        scr_copies[i].wait()
        amp = jnp.dot(mixed[rows, :], cond_rows, preferred_element_type=F32)
        kern[rows, :] = (scrs[rows, :].astype(F32) * amp * scale).astype(BF)
    row_copy.wait()
    folded[...] = jnp.dot(vals[...], kern[...], preferred_element_type=F32).astype(BF)
    for kp in range(di_ref.shape[0]):
        at = slice(kp * LANES, (kp + 1) * LANES)
        di_ref[kp] = dot_nt(folded[at, :], cond_rows[at, :])


def exchange_kernel(cfg, chunk, scale, *refs):
    n_ka, n_band, k_dev = cfg
    k_points = n_ka * k_dev
    rhos, di_ref, coul_ref, vown_ref, cond_ref, msg_ref = refs[:6]
    di, coul, conds, vown, part, msg, coul_sems, sems = refs[6:]
    own, npt = coul_ref.shape
    coul_copies = [
        pltpu.make_async_copy(
            coul_ref.at[:, pl.ds(i * chunk, chunk)], coul.at[:, pl.ds(i * chunk, chunk)], coul_sems.at[i]
        )
        for i in range(npt // chunk)
    ]
    copies = [
        pltpu.make_async_copy(vown_ref, vown, sems.at[0]),
        pltpu.make_async_copy(di_ref, di, sems.at[1]),
        pltpu.make_async_copy(cond_ref, conds, sems.at[2]),
    ]
    start_all(coul_copies + copies)
    acc = jnp.zeros((own, LANES), F32)
    per_dev = own // LANES
    for i in range(npt // chunk):
        coul_copies[i].wait()
        for j in range(i * chunk // LANES, (i + 1) * chunk // LANES):
            rho = rhos[j // per_dev, pl.ds(j % per_dev, 1), :].astype(BF).astype(F32)
            acc = acc + coul[:, j * LANES : (j + 1) * LANES].astype(F32) * rho
    potential = scale * jnp.sum(acc.T, axis=0, keepdims=True)
    wait_all(copies)
    for kp in range(k_points // 2):
        at = slice(kp * LANES, (kp + 1) * LANES)
        weighted = (vown[at, :].astype(F32) * potential).astype(BF)
        part[kp] = 2.0 * dot_nt(weighted, conds[at, :]) - di[kp]
    for d in range(n_band):
        for j in range(n_ka):
            for g in range((k_dev + 1) // 2):
                tile = None
                for kl in range(2 * g, min(2 * g + 2, k_dev)):
                    k = j * k_dev + kl
                    piece = part[k // 2, pl.ds(d * 2 * ROWS + k % 2 * ROWS, ROWS), :]
                    piece = lane_half(piece, k % 2, kl % 2)
                    tile = piece if tile is None else tile + piece
                msg[device_at(n_band, j, d), pl.ds(g * ROWS, ROWS), :] = tile
    msg_ref[...] = msg[...].astype(BF)


def received(recv_ref):
    return jnp.sum(recv_ref[...].astype(F32), axis=0)


def shifted(count_all, shift, square, cross_sum, square_sum):
    alpha = shift * square + cross_sum / count_all
    d = alpha - shift
    mean_sq = (square_sum - 2.0 * d * cross_sum) / count_all + d * d * square
    mean_sq = jnp.maximum(mean_sq, 0.0)
    return alpha, d, mean_sq


def first_owner_kernel(count_all, recv_ref, msgs_ref, gap_ref, own_ref, state_ref, coef_ref, msg_ref):
    start_sq, gap_sq = read_sums(msgs_ref, 2)
    norm = start_sq / count_all
    inv = 1.0 / jnp.sqrt(norm + 1e-06)
    square = norm / (norm + 1e-06)
    shift = gap_sq / jnp.maximum(start_sq, 1e-30)
    cur = own_ref[...] * inv
    inter = received(recv_ref) * inv
    gap = gap_ref[...]
    resid = (gap - shift) * cur + inter
    state_ref[0] = cur
    state_ref[1] = resid
    state_ref[2] = inter
    coef_ref[0] = shift
    coef_ref[1] = square
    coef_ref[2] = gap_sq * inv * inv
    sums = [
        jnp.sum(cur * resid),
        jnp.sum(resid * resid),
        jnp.sum(gap * resid * resid),
        jnp.sum(gap * resid * cur),
    ]
    msg_ref[...] = jnp.broadcast_to(with_sums(resid, sums).astype(BF)[None], msg_ref.shape)


def second_owner_kernel(count_all, recv_ref, msgs_ref, gap_ref, state_ref, coef_ref, out_ref, coef_out, msg_ref):
    cross, total, gap_rr, gap_rq = read_sums(msgs_ref, 4)
    alpha, d, mean_sq = shifted(count_all, coef_ref[0], coef_ref[1], cross, total)
    beta = jnp.sqrt(mean_sq + 1e-06)
    square = mean_sq / (mean_sq + 1e-06)
    gap_qq = gap_rr - 2.0 * d * gap_rq + d * d * coef_ref[2]
    shift = gap_qq / (mean_sq + 1e-06) / count_all
    prev = state_ref[0]
    cur = (state_ref[1] - d * prev) / beta
    inter = (received(recv_ref) - d * state_ref[2]) / beta
    resid = (gap_ref[...] - shift) * cur + inter - beta * prev
    out_ref[0] = cur
    out_ref[1] = resid
    coef_out[0] = alpha
    coef_out[1] = beta
    coef_out[2] = shift
    coef_out[3] = square
    dims = msg_ref.shape[:1] + msg_ref.shape[2:]
    msg_ref[:, 0, :] = jnp.full(dims, jnp.sum(cur * resid), F32)
    msg_ref[:, 1, :] = jnp.full(dims, jnp.sum(resid * resid), F32)


def finish_kernel(count_all, msgs_ref, state_ref, coef_ref, out_ref, coeffs_ref):
    sums = jnp.sum(msgs_ref[...], axis=0)
    alpha, d, mean_sq = shifted(count_all, coef_ref[2], coef_ref[3], sums[0, 0], sums[1, 0])
    beta = jnp.sqrt(mean_sq + 1e-06)
    own = (state_ref[1] - d * state_ref[0]) / beta
    coeffs_ref[0] = coef_ref[0]
    coeffs_ref[1] = alpha
    coeffs_ref[2] = coef_ref[1]
    coeffs_ref[3] = beta
    for kl in range(out_ref.shape[0]):
        tile = own[kl // 2 * ROWS : (kl // 2 + 1) * ROWS, :]
        other = pltpu.roll(tile, HALF, axis=1)
        left, right = (tile, other) if kl % 2 == 0 else (other, tile)
        low = lax.broadcasted_iota(jnp.int32, (1, LANES), 1) < HALF
        for j in range(ROWS // 2):
            row = jnp.where(low, left[2 * j : 2 * j + 1], right[2 * j + 1 : 2 * j + 2])
            out_ref[pl.ds(kl, 1), pl.ds(j * LANES, LANES)] = row


def shape_of(dims, kind=F32):
    return jax.ShapeDtypeStruct(dims, kind)


def call(kernel, name, out_shape, in_specs, out_specs, scratch=(), mib=58, flops=0, moved=0):
    return pl.pallas_call(
        kernel,
        out_shape=out_shape,
        in_specs=in_specs,
        out_specs=out_specs,
        scratch_shapes=list(scratch),
        compiler_params=pltpu.CompilerParams(vmem_limit_bytes=mib * MIB),
        cost_estimate=pl.CostEstimate(flops=flops, bytes_accessed=moved, transcendentals=0),
        name=name,
    )


def dma(*dims):
    return pltpu.SemaphoreType.DMA(dims)


def swap(block, axis, d):
    return lax.ppermute(block, axis, [(i, i ^ d) for i in range(lax.axis_size(axis))])


def line_gather(block, axis):
    n = lax.axis_size(axis)
    flows = []
    for way in (-1, 1):
        moving, flow = block, []
        for hop in range(1, n):
            senders = [i for i in range(n) if 0 <= i + way * (hop - 1) < n and 0 <= i - way < n]
            moving = lax.ppermute(moving, axis, [(i, i - way) for i in senders])
            flow.append(moving)
        flows.append(flow)
    return flows


def plane_pieces(own_piece, others):
    def move(block, d):
        return swap(block, "band", d)

    rows = own_piece.shape[0]
    half = rows // 2
    by_x, by_y, core = move(own_piece, 2), move(own_piece, 4), move(own_piece, 1)
    by_x, by_y, core, others = lax.optimization_barrier((by_x, by_y, core, others))
    diag = [move(by_x[:half], 4), move(by_y[half:], 2)]
    near_x, near_y = move(by_x, 1), move(by_y, 1)
    far = move(jnp.concatenate(diag, axis=0), 1)
    arrays = [own_piece, core, by_x, near_x, by_y, near_y, diag[0], diag[1], far]
    parts = tuple(((i, 0, rows),) for i in range(6))
    parts += (((6, 0, half), (7, 0, half)), ((8, 0, rows),))
    return arrays, parts, others


def kernel_path(start_vec, val_energy, cond_energy, val_orb, cond_orb, coulomb, screened):
    n_ka = lax.axis_size("ka")
    n_band = lax.axis_size("band")
    devices = n_ka * n_band
    ka, band = lax.axis_index("ka"), lax.axis_index("band")
    k_dev = start_vec.shape[0]
    nv_blk = val_orb.shape[1]
    n_cond = cond_orb.shape[1]
    npt_all = cond_orb.shape[2]
    k_points = k_dev * n_ka
    pairs = k_points // 2
    mu_blk, nu_blk = screened.shape
    own = coulomb.shape[0]
    count_all = k_points * nv_blk * n_band * n_cond
    scale = 1.0 / (npt_all * math.sqrt(count_all))
    piece_rows = k_points * nv_blk

    block = ((k_dev + 1) // 2 * ROWS, LANES)
    msg_shape = shape_of((devices,) + block, BF)
    wide = nu_blk + LANES
    cut_lanes = n_cond // ROWS * own
    start_own, gap, *payloads = call(
        functools.partial(pack_kernel, n_ka, nu_blk),
        "pack",
        (shape_of(block), shape_of(block))
        + (shape_of((k_dev, nv_blk, wide + cut_lanes), BF),) * n_ka,
        [ANY] * 5,
        (VMEM,) * (2 + n_ka),
        [
            pltpu.VMEM(start_vec.shape, F32),
            pltpu.VMEM(cond_energy.shape, F32),
            pltpu.SMEM(val_energy.shape, F32),
            pltpu.VMEM((n_ka, k_dev, n_cond, own), BF),
            dma(3),
            dma(2, n_ka),
        ],
    )(start_vec, cond_energy, val_energy, val_orb, cond_orb)
    base, payloads = lax.optimization_barrier((band * mu_blk, payloads))
    got = [payloads[0]] + [swap(payloads[j], "ka", j) for j in range(1, n_ka)]
    val_cut = jnp.concatenate([part[:, :, :wide] for part in got], axis=0)
    val_cut = val_cut.reshape(piece_rows, wide)
    cond_local = lax.dynamic_slice_in_dim(cond_orb, base, mu_blk, 2)
    cond_local = cond_local.reshape(k_dev * n_cond, mu_blk)
    below, above = line_gather(cond_local, "ka")

    chunk, tile = 1024, nu_blk
    rows_all, conds_all = k_points * nv_blk * n_band, k_points * n_cond
    scr_turned = call(
        functools.partial(turn_kernel, nu_blk // 4),
        "turn",
        shape_of((nu_blk, mu_blk), BF),
        [ANY],
        ANY,
        [pltpu.VMEM((mu_blk, nu_blk), BF), pltpu.VMEM((nu_blk, mu_blk), BF)]
        + [dma(4)] * 2,
        moved=8 * MIB,
    )(screened)
    val_cut, below[0], above[0] = lax.optimization_barrier((val_cut, below[0], above[0]))
    pieces, parts, (scr_turned, below[1], above[1]) = plane_pieces(
        val_cut, (scr_turned, below[1], above[1])
    )
    val_rows, val_turned, val_own, cond_own, msgs = call(
        functools.partial(order_kernel, parts, n_ka),
        "order",
        (
            shape_of((rows_all, nu_blk), BF),
            shape_of((nu_blk, rows_all), BF),
            shape_of((rows_all, own), BF),
            shape_of((conds_all, own), BF),
            msg_shape,
        ),
        [ANY] * (n_ka + len(pieces)),
        (ANY, ANY, ANY, VMEM, VMEM),
        [
            pltpu.VMEM((n_band, piece_rows, nu_blk), BF),
            pltpu.VMEM((n_band, piece_rows, LANES), BF),
            pltpu.VMEM((rows_all, nu_blk), BF),
            pltpu.VMEM((nu_blk, rows_all), BF),
            pltpu.VMEM((n_ka, k_dev, nv_blk, cut_lanes), BF),
            dma(2, sum(len(piece) for piece in parts)),
            dma(3, pairs),
            dma(n_ka),
        ],
        moved=9 * MIB,
    )(*got, *pieces)

    cond_pts = [cond_local] + below + above
    cfg = (n_ka, n_band, k_dev)
    quads = k_points // 4
    state, coef = None, None
    for step in range(STEPS):
        first = step == 0
        qx, rho = call(
            functools.partial(density_kernel, cfg),
            "density",
            (
                shape_of((quads, 2 * LANES, 2 * LANES), BF),
                shape_of((devices, own // LANES, LANES)),
            ),
            [ANY] * 3,
            (VMEM, VMEM),
            [
                pltpu.VMEM((quads, 2 * LANES, 2 * LANES), F32),
                pltpu.VMEM((devices,) + block, BF),
                pltpu.VMEM((rows_all, own), BF),
                pltpu.VMEM((conds_all, own), BF),
                dma(3),
            ],
        )(msgs, val_own, cond_own)
        density = exchange_all(rho)
        direct = call(
            functools.partial(direct_kernel, n_ka, tile, scale),
            "direct",
            shape_of((pairs, LANES, LANES)),
            [ANY] * (4 + len(cond_pts)),
            VMEM,
            [
                pltpu.VMEM((quads, 2 * LANES, 2 * LANES), BF),
                pltpu.VMEM((nu_blk, rows_all), BF),
                pltpu.VMEM((n_ka, k_dev * n_cond, mu_blk), BF),
                pltpu.VMEM((nu_blk, mu_blk), BF),
                pltpu.VMEM((rows_all, nu_blk), BF),
                pltpu.VMEM((nu_blk, conds_all), BF),
                pltpu.VMEM((nu_blk, mu_blk), BF),
                pltpu.VMEM((rows_all, mu_blk), BF),
                dma(1),
                dma(len(cond_pts)),
                dma(1),
                dma(2, nu_blk // tile),
            ],
            flops=4 * mu_blk * nu_blk * conds_all,
            moved=12 * MIB,
        )(val_turned, scr_turned, val_rows, qx, *cond_pts)
        summed = call(
            functools.partial(exchange_kernel, cfg, chunk, scale),
            "exchange",
            msg_shape,
            [VMEM] + [ANY] * 4,
            VMEM,
            [
                pltpu.VMEM((pairs, LANES, LANES), F32),
                pltpu.VMEM((own, npt_all), BF),
                pltpu.VMEM((conds_all, own), BF),
                pltpu.VMEM((rows_all, own), BF),
                pltpu.VMEM((pairs, LANES, LANES), F32),
                pltpu.VMEM((devices,) + block, F32),
                dma(npt_all // chunk),
                dma(3),
            ],
        )(density, direct, coulomb, val_own, cond_own)
        recv = exchange_all(summed)
        if first:
            state, coef, message = call(
                functools.partial(first_owner_kernel, count_all),
                "first_owner",
                (shape_of((3,) + block), shape_of((3,)), msg_shape),
                [VMEM] * 4,
                (VMEM, SMEM, VMEM),
                mib=8,
            )(recv, msgs, gap, start_own)
        else:
            state, coef, message = call(
                functools.partial(second_owner_kernel, count_all),
                "second_owner",
                (shape_of((2,) + block), shape_of((4,)), shape_of((devices, 2, LANES))),
                [VMEM] * 4 + [SMEM],
                (VMEM, SMEM, VMEM),
                mib=8,
            )(recv, msgs, gap, state, coef)
        msgs = exchange_all(message)
    return call(
        functools.partial(finish_kernel, count_all),
        "finish",
        (shape_of(start_vec.shape), shape_of((2 * STEPS,))),
        [VMEM] * 2 + [SMEM],
        (VMEM, SMEM),
        mib=8,
    )(msgs, state, coef)


def array_path(start_vec, val_energy, cond_energy, val_orb, cond_orb, coulomb, screened):
    n_ka = lax.axis_size("ka")
    n_band = lax.axis_size("band")
    devices = n_ka * n_band
    ka, band = lax.axis_index("ka"), lax.axis_index("band")
    me = ka * n_band + band
    k_dev, pair_blk = start_vec.shape
    nv_blk = val_orb.shape[1]
    n_cond = cond_orb.shape[1]
    n_val = nv_blk * n_band
    npt_all = cond_orb.shape[2]
    k_points = k_dev * n_ka
    mu_blk, nu_blk = screened.shape
    own_pts = coulomb.shape[0]
    count_all = k_points * n_val * n_cond
    kernel_scale = 1.0 / (npt_all * math.sqrt(count_all))

    start_all = gather_all(start_vec, devices)
    val_cut = lax.all_to_all(
        val_orb.reshape(k_dev, nv_blk, n_ka, nu_blk).transpose(2, 0, 1, 3),
        "ka", split_axis=0, concat_axis=0, tiled=True,
    ).reshape(k_points, nv_blk, nu_blk)
    val_pts = lax.all_gather(val_cut, "band", axis=1, tiled=True)
    cond_local = lax.dynamic_slice_in_dim(cond_orb, band * mu_blk, mu_blk, 2)
    cond_pts = lax.all_gather(cond_local, "ka", axis=0, tiled=True)
    cond_rows = cond_orb.reshape(k_dev, n_cond, n_ka, n_band, own_pts)
    cond_rows = lax.dynamic_index_in_dim(cond_rows, band, 3, keepdims=False)
    cond_own = lax.all_to_all(
        cond_rows.transpose(2, 0, 1, 3), "ka", split_axis=0, concat_axis=0, tiled=True
    ).reshape(k_points, n_cond, own_pts)
    val_own = lax.dynamic_slice_in_dim(val_pts, band * own_pts, own_pts, 2)

    energy_gap = (cond_energy[:, None, :] - val_energy[:, :, None]).reshape(k_dev, pair_blk)
    start_sq = jnp.sum(start_all * start_all)
    current = start_all / jnp.sqrt(start_sq / count_all + 1e-06)
    previous = jnp.zeros_like(current)
    beta_val = jnp.float32(0.0)
    alphas = []
    betas = []
    for turn_index in range(STEPS):
        full_vec = (
            current.astype(BF)
            .reshape(n_ka, n_band, k_dev, nv_blk, n_cond)
            .transpose(0, 2, 1, 3, 4)
            .reshape(k_points, n_val, n_cond)
        )
        mixed_f = jnp.einsum("kvc,kvn->kcn", full_vec, val_pts, preferred_element_type=F32)
        mixed_own = lax.dynamic_slice_in_dim(mixed_f, band * own_pts, own_pts, 2)
        density_own = jnp.sum(mixed_own * cond_own.astype(F32), axis=(0, 1))
        density = gather_all(density_own.astype(BF), devices).reshape(npt_all)
        mixed_val = mixed_f.astype(BF)
        amp = jnp.einsum("kcm,kcn->mn", cond_pts, mixed_val, preferred_element_type=F32)
        kern = (screened.astype(F32) * amp * kernel_scale).astype(BF)
        folded = jnp.einsum("mn,kvn->kvm", kern, val_pts, preferred_element_type=F32).astype(BF)
        direct_part = jnp.einsum("kcm,kvm->kvc", cond_pts, folded, preferred_element_type=F32)
        potential = kernel_scale * jnp.dot(coulomb, density, preferred_element_type=F32)
        weighted = (val_own.astype(F32) * potential).astype(BF)
        exchange = jnp.einsum("kvp,kcp->kvc", weighted, cond_own, preferred_element_type=F32)
        part = 2.0 * exchange - direct_part
        arranged = (
            part.reshape(n_ka, k_dev, n_band, nv_blk, n_cond)
            .transpose(0, 2, 1, 3, 4)
            .reshape(devices, k_dev, pair_blk)
        )
        inter_own = jnp.sum(exchange_all(arranged), axis=0)
        current_own = lax.dynamic_index_in_dim(current, me, 0, keepdims=False)
        resid_vec = gather_all(energy_gap * current_own + inter_own, devices)
        resid_vec = resid_vec - beta_val * previous
        alpha_val = jnp.sum(current * resid_vec) / count_all
        resid_vec = resid_vec - alpha_val * current
        beta_val = jnp.sqrt(jnp.sum(resid_vec * resid_vec) / count_all + 1e-06)
        previous = current
        current = resid_vec / beta_val
        alphas.append(alpha_val)
        betas.append(beta_val)
    coeffs = jnp.stack(alphas + betas)
    return (lax.dynamic_index_in_dim(current, me, 0, keepdims=False), coeffs)


def per_device(*args):
    start_vec, _, _, val_orb, cond_orb, coulomb, screened = args
    n_ka, n_band = lax.axis_size("ka"), lax.axis_size("band")
    fits = (
        n_band == 8
        and n_ka & (n_ka - 1) == 0
        and start_vec.shape[0] % 2 == 1
        and val_orb.shape[1] == ROWS
        and cond_orb.shape[1] == HALF
        and start_vec.shape[0] * n_ka % 4 == 0
        and coulomb.shape[0] % LANES == 0
        and coulomb.shape[1] % 1024 == 0
        and screened.shape[0] % 512 == 0
        and screened.shape[1] % 1024 == 0
        and screened.shape[0] * screened.shape[1] <= 2 * MIB
    )
    return (kernel_path if fits else array_path)(*args)


def solution(mesh):
    in_specs = (
        P("ka", "band"),
        P("ka", "band"),
        P("ka", None),
        P("ka", "band", None),
        P("ka", None, None),
        P(("ka", "band"), None),
        P("band", "ka"),
    )
    out_specs = (P("ka", "band"), P())
    return jax.shard_map(
        per_device, mesh=mesh, in_specs=in_specs, out_specs=out_specs, check_vma=False
    )
```

```python
import functools
import math

import jax
import jax.numpy as jnp
from jax import lax
from jax.experimental import pallas as pl
from jax.experimental.pallas import tpu as pltpu
from jax.sharding import PartitionSpec as P

STEPS = 2
AXES = ("ka", "band")
BF, F32 = jnp.bfloat16, jnp.float32
LANES = 128
HALF = 64
ROWS = 8
MIB = 1 << 20

VMEM = pl.BlockSpec(memory_space=pltpu.VMEM)
SMEM = pl.BlockSpec(memory_space=pltpu.SMEM)
ANY = pl.BlockSpec(memory_space=pl.ANY)


def gather_all(block, devices):
    wide = jnp.broadcast_to(block[None], (devices,) + block.shape)
    return exchange_all(wide)


def exchange_all(parts):
    return lax.all_to_all(parts, AXES, split_axis=0, concat_axis=0, tiled=True)


def dot_nt(lhs, rhs):
    return lax.dot_general(lhs, rhs, (((1,), (1,)), ((), ())), preferred_element_type=F32)


def dot_tn(lhs, rhs):
    return lax.dot_general(lhs, rhs, (((0,), (0,)), ((), ())), preferred_element_type=F32)


def lane_half(tile, have, want):
    if have != want:
        tile = pltpu.roll(tile, HALF, axis=1)
    lane = lax.broadcasted_iota(jnp.int32, tile.shape, 1)
    keep = lane < HALF if want == 0 else lane >= HALF
    return jnp.where(keep, tile, 0.0)


def with_sums(block, sums):
    row = lax.broadcasted_iota(jnp.int32, block.shape, 0)
    lane = lax.broadcasted_iota(jnp.int32, block.shape, 1)
    free = row == block.shape[0] - ROWS
    for i, total in enumerate(sums):
        rest = jnp.full(block.shape, total, F32)
        for part in range(3):
            piece = rest.astype(BF).astype(F32)
            block = jnp.where(free & (lane == HALF + 3 * i + part), piece, block)
            rest = rest - piece
    return block


def read_sums(msgs_ref, count):
    rows = msgs_ref.shape[1]
    tile = jnp.sum(msgs_ref[...].astype(F32), axis=0)[rows - ROWS :, :]
    row = lax.broadcasted_iota(jnp.int32, tile.shape, 0)
    lane = lax.broadcasted_iota(jnp.int32, tile.shape, 1)
    out = []
    for i in range(count):
        mine = (row == 0) & (lane >= HALF + 3 * i) & (lane < HALF + 3 * i + 3)
        out.append(jnp.sum(jnp.where(mine, tile, 0.0)))
    return out


def piece_copies(refs, parts, column, width, dest, sems):
    copies = []
    for d, piece in enumerate(parts):
        row = 0
        for ref, start, rows in piece:
            copies.append(
                pltpu.make_async_copy(
                    refs[ref].at[pl.ds(start, rows), pl.ds(column, width)],
                    dest.at[d, pl.ds(row, rows), :],
                    sems.at[len(copies)],
                )
            )
            row += rows
    return copies


def start_all(copies):
    for copy in copies:
        copy.start()


def wait_all(copies):
    for copy in copies:
        copy.wait()


def device_at(n_band, j, d):
    ka = jnp.bitwise_xor(lax.axis_index("ka"), j)
    return ka * n_band + jnp.bitwise_xor(lax.axis_index("band"), d)


def pair_rows(ref, kp):
    part = ref[:, kp * 2 * ROWS : (kp + 1) * 2 * ROWS, :]
    return part.reshape(part.shape[0] * 2 * ROWS, part.shape[2])


def pack_kernel(n_ka, nu, *refs):
    start_in, cond_in, val_in, val_ref, orb_ref = refs[:5]
    own_ref, gap_ref, outs, refs = refs[5], refs[6], refs[7 : 7 + n_ka], refs[7 + n_ka :]
    start_ref, cond_ref, energy_ref, cuts, sems, cut_sems = refs
    own = cuts.shape[-1]
    ins = ((start_in, start_ref), (cond_in, cond_ref), (val_in, energy_ref))
    small = [pltpu.make_async_copy(ref, to, sems.at[i]) for i, (ref, to) in enumerate(ins)]
    k_dev = val_ref.shape[0]
    val_copies, cut_copies = [], []
    for j in range(n_ka):
        at = pl.multiple_of(jnp.bitwise_xor(lax.axis_index("ka"), j) * nu, nu)
        point = pl.multiple_of(at + lax.axis_index("band") * own, LANES)
        val_copies.append(
            pltpu.make_async_copy(
                val_ref.at[:, :, pl.ds(at, nu)], outs[j].at[:, :, pl.ds(0, nu)], cut_sems.at[0, j]
            )
        )
        cut_copies.append(
            pltpu.make_async_copy(
                orb_ref.at[:, :, pl.ds(point, own)], cuts.at[j], cut_sems.at[1, j]
            )
        )
    start_all(small + cut_copies + val_copies)
    wait_all(small)
    own_ref[...] = jnp.zeros_like(own_ref)
    gap_ref[...] = jnp.zeros_like(gap_ref)
    cond = jnp.concatenate([cond_ref[...], cond_ref[...]], axis=1)
    for kl in range(k_dev):
        half = kl % 2
        for v in range(ROWS):
            at = pl.ds(kl // 2 * ROWS + v, 1)
            row = start_ref[pl.ds(kl, 1), pl.ds(v // 2 * LANES, LANES)]
            own_ref[at, :] = own_ref[at, :] + lane_half(row, v % 2, half)
            gap = cond[kl : kl + 1, :] - energy_ref[kl, v]
            gap_ref[at, :] = gap_ref[at, :] + lane_half(gap, half, half)
    mine = own_ref[...]
    square = mine * mine
    block = with_sums(mine, [jnp.sum(square), jnp.sum(gap_ref[...] * square)])
    for j in range(n_ka):
        for g in range(k_dev):
            head = jnp.zeros((ROWS, LANES), F32)
            if (g + 1) * ROWS <= block.shape[0]:
                head = block[g * ROWS : (g + 1) * ROWS, :]
            outs[j][g, :, nu : nu + LANES] = head.astype(BF)
        cut_copies[j].wait()
        for kl in range(k_dev):
            cut = cuts[j, kl].astype(F32)
            wide = [cut[q * ROWS : (q + 1) * ROWS, :] for q in range(cut.shape[0] // ROWS)]
            outs[j][kl, :, nu + LANES :] = jnp.concatenate(wide, axis=1).astype(BF)
    wait_all(val_copies)


def turn_kernel(tile, scr_ref, out_ref, scrs, turned, in_sems, out_sems):
    nu = scr_ref.shape[1]
    ins, outs = [], []
    for j in range(nu // tile):
        at = pl.ds(j * tile, tile)
        ins.append(pltpu.make_async_copy(scr_ref.at[:, at], scrs.at[:, at], in_sems.at[j]))
        outs.append(pltpu.make_async_copy(turned.at[at, :], out_ref.at[at, :], out_sems.at[j]))
    start_all(ins)
    for j in range(nu // tile):
        ins[j].wait()
        turned[j * tile : (j + 1) * tile, :] = scrs[:, j * tile : (j + 1) * tile].T
        outs[j].start()
    wait_all(outs)


def order_kernel(parts, n_ka, *refs):
    got_refs, val_refs, refs = refs[:n_ka], refs[n_ka:-13], refs[-13:]
    rows_out, turned_out, own_out, cond_out, msgs_out = refs[:5]
    vals, heads, ordered, turned, cuts, val_sems, out_sems, cut_sems = refs[5:]
    own = own_out.shape[1]
    nu = ordered.shape[1]
    copies = piece_copies(val_refs, parts, 0, nu, vals, val_sems.at[0])
    head_copies = piece_copies(val_refs, parts, nu, LANES, heads, val_sems.at[1])
    cut_copies = [
        pltpu.make_async_copy(
            ref.at[:, :, pl.ds(nu + LANES, cuts.shape[-1])], cuts.at[j], cut_sems.at[j]
        )
        for j, ref in enumerate(got_refs)
    ]
    start_all(copies + head_copies + cut_copies)
    wait_all(cut_copies)
    k_dev, points = cuts.shape[1], cuts.shape[-1] // own
    for j in range(n_ka):
        for kl in range(k_dev):
            cut = cuts[j, kl].astype(F32)
            tall = [cut[:, q * own : (q + 1) * own] for q in range(points)]
            at = (j * k_dev + kl) * points * ROWS
            cond_out[at : at + points * ROWS, :] = jnp.concatenate(tall, axis=0).astype(BF)
    wait_all(copies)
    n_band, group = vals.shape[0], vals.shape[0] * 2 * ROWS
    column = pl.multiple_of(lax.axis_index("band") * own, LANES)
    outs = []
    for kp in range(ordered.shape[0] // group):
        at = slice(kp * group, (kp + 1) * group)
        ordered[at, :] = pair_rows(vals, kp)
        turned[:, at] = ordered[at, :].T
        at = pl.ds(kp * group, group)
        outs += [
            pltpu.make_async_copy(ordered.at[at, :], rows_out.at[at, :], out_sems.at[0, kp]),
            pltpu.make_async_copy(turned.at[:, at], turned_out.at[:, at], out_sems.at[1, kp]),
            pltpu.make_async_copy(
                ordered.at[at, pl.ds(column, own)], own_out.at[at, :], out_sems.at[2, kp]
            ),
        ]
        start_all(outs[-3:])
    wait_all(head_copies)
    rows = msgs_out.shape[1]
    step = heads.shape[1] // n_ka
    for d in range(n_band):
        head = heads[d].astype(F32)
        for j in range(n_ka):
            msgs_out[device_at(n_band, j, d)] = head[j * step : j * step + rows, :].astype(BF)
    wait_all(outs)


def density_kernel(cfg, *refs):
    n_ka, n_band, k_dev = cfg
    k_points = n_ka * k_dev
    msgs_ref, vown_ref, cond_ref, qx_ref, rho_ref, xs, msgs, vown, conds, sems = refs
    own = vown_ref.shape[1]
    msg_copy = pltpu.make_async_copy(msgs_ref, msgs, sems.at[0])
    copies = [
        pltpu.make_async_copy(vown_ref, vown, sems.at[1]),
        pltpu.make_async_copy(cond_ref, conds, sems.at[2]),
    ]
    start_all([msg_copy] + copies)
    xs[...] = jnp.zeros_like(xs)
    msg_copy.wait()
    for d in range(n_band):
        for k in range(k_points):
            j, kl = divmod(k, k_dev)
            tile = msgs[device_at(n_band, j, d), :, :].astype(F32)
            tile = tile[kl // 2 * ROWS : (kl // 2 + 1) * ROWS, :]
            base = k // 2 % 2 * LANES
            at = pl.ds(base + d * 2 * ROWS + k % 2 * ROWS, ROWS)
            xs[k // 4, at, pl.ds(base, LANES)] = lane_half(tile, kl % 2, k % 2)
    qx_ref[...] = xs[...].astype(BF)
    wait_all(copies)
    rho = jnp.zeros((1, own), F32)
    quad = 2 * LANES
    for kq in range(k_points // 4):
        at = slice(kq * quad, (kq + 1) * quad)
        mixed = dot_tn(qx_ref[kq], vown[at, :])
        rho = rho + jnp.sum(mixed * conds[at, :].astype(F32), axis=0, keepdims=True)
    for r in range(own // LANES):
        part = rho[:, r * LANES : (r + 1) * LANES]
        rho_ref[:, r, :] = jnp.broadcast_to(part, (rho_ref.shape[0], LANES))


def direct_kernel(n_ka, tile, scale, *refs):
    turned_ref, scr_ref, rows_ref, qx_ref, refs = refs[0], refs[1], refs[2], refs[3], refs[4:]
    cond_ref, refs = refs[0], refs[1:]
    di_ref, qx, turned, conds, scrs, vals, mixed, kern, folded = refs[:9]
    qx_sem, cond_sems, row_sem, chunk_sems = refs[9:]
    nu, mu = scr_ref.shape
    quad = 2 * LANES
    qx_copy = pltpu.make_async_copy(qx_ref, qx, qx_sem.at[0])
    cond_copies = [
        pltpu.make_async_copy(
            cond_ref.at[jnp.bitwise_xor(lax.axis_index("ka"), j)], conds.at[j], cond_sems.at[j]
        )
        for j in range(n_ka)
    ]
    turned_copies, scr_copies = [], []
    for i in range(nu // tile):
        at = pl.ds(i * tile, tile)
        turned_copies.append(
            pltpu.make_async_copy(turned_ref.at[at, :], turned.at[at, :], chunk_sems.at[0, i])
        )
        scr_copies.append(
            pltpu.make_async_copy(scr_ref.at[at, :], scrs.at[at, :], chunk_sems.at[1, i])
        )
    row_copy = pltpu.make_async_copy(rows_ref, vals, row_sem.at[0])
    start_all([qx_copy, turned_copies[0]] + cond_copies + [scr_copies[0]])
    for i in range(1, nu // tile):
        start_all([turned_copies[i], scr_copies[i]])
    row_copy.start()
    qx_copy.wait()
    for i in range(nu // tile):
        rows = slice(i * tile, (i + 1) * tile)
        turned_copies[i].wait()
        for kq in range(qx.shape[0]):
            cols = slice(kq * quad, (kq + 1) * quad)
            mixed[rows, cols] = jnp.dot(
                turned[rows, cols], qx[kq], preferred_element_type=F32
            ).astype(BF)
        if i == 0:
            wait_all(cond_copies)
            cond_rows = conds[...].reshape(-1, mu)
        scr_copies[i].wait()
        amp = jnp.dot(mixed[rows, :], cond_rows, preferred_element_type=F32)
        kern[rows, :] = (scrs[rows, :].astype(F32) * amp * scale).astype(BF)
    row_copy.wait()
    folded[...] = jnp.dot(vals[...], kern[...], preferred_element_type=F32).astype(BF)
    for kp in range(di_ref.shape[0]):
        at = slice(kp * LANES, (kp + 1) * LANES)
        di_ref[kp] = dot_nt(folded[at, :], cond_rows[at, :])


def exchange_kernel(cfg, chunk, scale, *refs):
    n_ka, n_band, k_dev = cfg
    k_points = n_ka * k_dev
    rho_ref, di_ref, coul_ref, vown_ref, cond_ref, msg_ref = refs[:6]
    rhos, di, coul, conds, vown, part, msg, coul_sems, sems = refs[6:]
    rho_copy = pltpu.make_async_copy(rho_ref, rhos, sems.at[3])
    own, npt = coul_ref.shape
    coul_copies = [
        pltpu.make_async_copy(
            coul_ref.at[:, pl.ds(i * chunk, chunk)], coul.at[:, pl.ds(i * chunk, chunk)], coul_sems.at[i]
        )
        for i in range(npt // chunk)
    ]
    copies = [
        pltpu.make_async_copy(vown_ref, vown, sems.at[0]),
        pltpu.make_async_copy(di_ref, di, sems.at[1]),
        pltpu.make_async_copy(cond_ref, conds, sems.at[2]),
    ]
    start_all([rho_copy] + coul_copies + copies)
    rho_copy.wait()
    acc = jnp.zeros((own, LANES), F32)
    per_dev = own // LANES
    for i in range(npt // chunk):
        coul_copies[i].wait()
        for j in range(i * chunk // LANES, (i + 1) * chunk // LANES):
            rho = rhos[j // per_dev, pl.ds(j % per_dev, 1), :].astype(BF).astype(F32)
            acc = acc + coul[:, j * LANES : (j + 1) * LANES].astype(F32) * rho
    potential = scale * jnp.sum(acc.T, axis=0, keepdims=True)
    wait_all(copies)
    for kp in range(k_points // 2):
        at = slice(kp * LANES, (kp + 1) * LANES)
        weighted = (vown[at, :].astype(F32) * potential).astype(BF)
        part[kp] = 2.0 * dot_nt(weighted, conds[at, :]) - di[kp]
    for d in range(n_band):
        for j in range(n_ka):
            for g in range((k_dev + 1) // 2):
                tile = None
                for kl in range(2 * g, min(2 * g + 2, k_dev)):
                    k = j * k_dev + kl
                    piece = part[k // 2, pl.ds(d * 2 * ROWS + k % 2 * ROWS, ROWS), :]
                    piece = lane_half(piece, k % 2, kl % 2)
                    tile = piece if tile is None else tile + piece
                msg[device_at(n_band, j, d), pl.ds(g * ROWS, ROWS), :] = tile
    msg_ref[...] = msg[...].astype(BF)


def received(recv_ref):
    return jnp.sum(recv_ref[...].astype(F32), axis=0)


def shifted(count_all, shift, square, cross_sum, square_sum):
    alpha = shift * square + cross_sum / count_all
    d = alpha - shift
    mean_sq = (square_sum - 2.0 * d * cross_sum) / count_all + d * d * square
    mean_sq = jnp.maximum(mean_sq, 0.0)
    return alpha, d, mean_sq


def first_owner_kernel(count_all, recv_ref, msgs_ref, gap_ref, own_ref, state_ref, coef_ref, msg_ref):
    start_sq, gap_sq = read_sums(msgs_ref, 2)
    norm = start_sq / count_all
    inv = 1.0 / jnp.sqrt(norm + 1e-06)
    square = norm / (norm + 1e-06)
    shift = gap_sq / jnp.maximum(start_sq, 1e-30)
    cur = own_ref[...] * inv
    inter = received(recv_ref) * inv
    gap = gap_ref[...]
    resid = (gap - shift) * cur + inter
    state_ref[0] = cur
    state_ref[1] = resid
    state_ref[2] = inter
    coef_ref[0] = shift
    coef_ref[1] = square
    coef_ref[2] = gap_sq * inv * inv
    sums = [
        jnp.sum(cur * resid),
        jnp.sum(resid * resid),
        jnp.sum(gap * resid * resid),
        jnp.sum(gap * resid * cur),
    ]
    msg_ref[...] = jnp.broadcast_to(with_sums(resid, sums).astype(BF)[None], msg_ref.shape)


def second_owner_kernel(count_all, recv_ref, msgs_ref, gap_ref, state_ref, coef_ref, out_ref, coef_out, msg_ref):
    cross, total, gap_rr, gap_rq = read_sums(msgs_ref, 4)
    alpha, d, mean_sq = shifted(count_all, coef_ref[0], coef_ref[1], cross, total)
    beta = jnp.sqrt(mean_sq + 1e-06)
    square = mean_sq / (mean_sq + 1e-06)
    gap_qq = gap_rr - 2.0 * d * gap_rq + d * d * coef_ref[2]
    shift = gap_qq / (mean_sq + 1e-06) / count_all
    prev = state_ref[0]
    cur = (state_ref[1] - d * prev) / beta
    inter = (received(recv_ref) - d * state_ref[2]) / beta
    resid = (gap_ref[...] - shift) * cur + inter - beta * prev
    out_ref[0] = cur
    out_ref[1] = resid
    coef_out[0] = alpha
    coef_out[1] = beta
    coef_out[2] = shift
    coef_out[3] = square
    dims = msg_ref.shape[:1] + msg_ref.shape[2:]
    msg_ref[:, 0, :] = jnp.full(dims, jnp.sum(cur * resid), F32)
    msg_ref[:, 1, :] = jnp.full(dims, jnp.sum(resid * resid), F32)


def finish_kernel(count_all, msgs_ref, state_ref, coef_ref, out_ref, coeffs_ref):
    sums = jnp.sum(msgs_ref[...], axis=0)
    alpha, d, mean_sq = shifted(count_all, coef_ref[2], coef_ref[3], sums[0, 0], sums[1, 0])
    beta = jnp.sqrt(mean_sq + 1e-06)
    own = (state_ref[1] - d * state_ref[0]) / beta
    coeffs_ref[0] = coef_ref[0]
    coeffs_ref[1] = alpha
    coeffs_ref[2] = coef_ref[1]
    coeffs_ref[3] = beta
    for kl in range(out_ref.shape[0]):
        tile = own[kl // 2 * ROWS : (kl // 2 + 1) * ROWS, :]
        other = pltpu.roll(tile, HALF, axis=1)
        left, right = (tile, other) if kl % 2 == 0 else (other, tile)
        low = lax.broadcasted_iota(jnp.int32, (1, LANES), 1) < HALF
        for j in range(ROWS // 2):
            row = jnp.where(low, left[2 * j : 2 * j + 1], right[2 * j + 1 : 2 * j + 2])
            out_ref[pl.ds(kl, 1), pl.ds(j * LANES, LANES)] = row


def shape_of(dims, kind=F32):
    return jax.ShapeDtypeStruct(dims, kind)


def call(kernel, name, out_shape, in_specs, out_specs, scratch=(), mib=58, flops=0, moved=0):
    return pl.pallas_call(
        kernel,
        out_shape=out_shape,
        in_specs=in_specs,
        out_specs=out_specs,
        scratch_shapes=list(scratch),
        compiler_params=pltpu.CompilerParams(vmem_limit_bytes=mib * MIB),
        cost_estimate=pl.CostEstimate(flops=flops, bytes_accessed=moved, transcendentals=0),
        name=name,
    )


def dma(*dims):
    return pltpu.SemaphoreType.DMA(dims)


def swap(block, axis, d):
    return lax.ppermute(block, axis, [(i, i ^ d) for i in range(lax.axis_size(axis))])


def plane_pieces(own_piece, others):
    def move(block, d):
        return swap(block, "band", d)

    rows = own_piece.shape[0]
    half = rows // 2
    by_x, by_y, core = move(own_piece, 2), move(own_piece, 4), move(own_piece, 1)
    by_x, by_y, core, others = lax.optimization_barrier((by_x, by_y, core, others))
    diag = [move(by_x[:half], 4), move(by_y[half:], 2)]
    near_x, near_y = move(by_x, 1), move(by_y, 1)
    far = move(jnp.concatenate(diag, axis=0), 1)
    arrays = [own_piece, core, by_x, near_x, by_y, near_y, diag[0], diag[1], far]
    parts = tuple(((i, 0, rows),) for i in range(6))
    parts += (((6, 0, half), (7, 0, half)), ((8, 0, rows),))
    return arrays, parts, others


def kernel_path(start_vec, val_energy, cond_energy, val_orb, cond_orb, coulomb, screened):
    n_ka = lax.axis_size("ka")
    n_band = lax.axis_size("band")
    devices = n_ka * n_band
    ka, band = lax.axis_index("ka"), lax.axis_index("band")
    k_dev = start_vec.shape[0]
    nv_blk = val_orb.shape[1]
    n_cond = cond_orb.shape[1]
    npt_all = cond_orb.shape[2]
    k_points = k_dev * n_ka
    pairs = k_points // 2
    mu_blk, nu_blk = screened.shape
    own = coulomb.shape[0]
    count_all = k_points * nv_blk * n_band * n_cond
    scale = 1.0 / (npt_all * math.sqrt(count_all))
    piece_rows = k_points * nv_blk

    block = ((k_dev + 1) // 2 * ROWS, LANES)
    msg_shape = shape_of((devices,) + block, BF)
    wide = nu_blk + LANES
    cut_lanes = n_cond // ROWS * own
    start_own, gap, *payloads = call(
        functools.partial(pack_kernel, n_ka, nu_blk),
        "pack",
        (shape_of(block), shape_of(block))
        + (shape_of((k_dev, nv_blk, wide + cut_lanes), BF),) * n_ka,
        [ANY] * 5,
        (VMEM,) * (2 + n_ka),
        [
            pltpu.VMEM(start_vec.shape, F32),
            pltpu.VMEM(cond_energy.shape, F32),
            pltpu.SMEM(val_energy.shape, F32),
            pltpu.VMEM((n_ka, k_dev, n_cond, own), BF),
            dma(3),
            dma(2, n_ka),
        ],
    )(start_vec, cond_energy, val_energy, val_orb, cond_orb)
    base, payloads = lax.optimization_barrier((band * mu_blk, payloads))
    got = [payloads[0]] + [swap(payloads[j], "ka", j) for j in range(1, n_ka)]
    val_cut = jnp.concatenate([part[:, :, :wide] for part in got], axis=0)
    val_cut = val_cut.reshape(piece_rows, wide)
    cond_local = lax.dynamic_slice_in_dim(cond_orb, base, mu_blk, 2)
    cond_local = cond_local.reshape(k_dev * n_cond, mu_blk)
    cond_wide = jnp.broadcast_to(cond_local[None], (n_ka,) + cond_local.shape)
    cond_pts = lax.all_to_all(cond_wide, "ka", split_axis=0, concat_axis=0, tiled=True)

    chunk, tile = 1024, nu_blk
    rows_all, conds_all = k_points * nv_blk * n_band, k_points * n_cond
    scr_turned = call(
        functools.partial(turn_kernel, nu_blk // 4),
        "turn",
        shape_of((nu_blk, mu_blk), BF),
        [ANY],
        ANY,
        [pltpu.VMEM((mu_blk, nu_blk), BF), pltpu.VMEM((nu_blk, mu_blk), BF)]
        + [dma(4)] * 2,
        moved=8 * MIB,
    )(screened)
    pieces, parts, scr_turned = plane_pieces(val_cut, scr_turned)
    val_rows, val_turned, val_own, cond_own, msgs = call(
        functools.partial(order_kernel, parts, n_ka),
        "order",
        (
            shape_of((rows_all, nu_blk), BF),
            shape_of((nu_blk, rows_all), BF),
            shape_of((rows_all, own), BF),
            shape_of((conds_all, own), BF),
            msg_shape,
        ),
        [ANY] * (n_ka + len(pieces)),
        (ANY, ANY, ANY, VMEM, VMEM),
        [
            pltpu.VMEM((n_band, piece_rows, nu_blk), BF),
            pltpu.VMEM((n_band, piece_rows, LANES), BF),
            pltpu.VMEM((rows_all, nu_blk), BF),
            pltpu.VMEM((nu_blk, rows_all), BF),
            pltpu.VMEM((n_ka, k_dev, nv_blk, cut_lanes), BF),
            dma(2, sum(len(piece) for piece in parts)),
            dma(3, pairs),
            dma(n_ka),
        ],
        moved=9 * MIB,
    )(*got, *pieces)

    cfg = (n_ka, n_band, k_dev)
    quads = k_points // 4
    state, coef = None, None
    for step in range(STEPS):
        first = step == 0
        qx, rho = call(
            functools.partial(density_kernel, cfg),
            "density",
            (
                shape_of((quads, 2 * LANES, 2 * LANES), BF),
                shape_of((devices, own // LANES, LANES)),
            ),
            [ANY] * 3,
            (VMEM, VMEM),
            [
                pltpu.VMEM((quads, 2 * LANES, 2 * LANES), F32),
                pltpu.VMEM((devices,) + block, BF),
                pltpu.VMEM((rows_all, own), BF),
                pltpu.VMEM((conds_all, own), BF),
                dma(3),
            ],
        )(msgs, val_own, cond_own)
        density = exchange_all(rho)
        direct = call(
            functools.partial(direct_kernel, n_ka, tile, scale),
            "direct",
            shape_of((pairs, LANES, LANES)),
            [ANY] * 5,
            VMEM,
            [
                pltpu.VMEM((quads, 2 * LANES, 2 * LANES), BF),
                pltpu.VMEM((nu_blk, rows_all), BF),
                pltpu.VMEM((n_ka, k_dev * n_cond, mu_blk), BF),
                pltpu.VMEM((nu_blk, mu_blk), BF),
                pltpu.VMEM((rows_all, nu_blk), BF),
                pltpu.VMEM((nu_blk, conds_all), BF),
                pltpu.VMEM((nu_blk, mu_blk), BF),
                pltpu.VMEM((rows_all, mu_blk), BF),
                dma(1),
                dma(n_ka),
                dma(1),
                dma(2, nu_blk // tile),
            ],
            flops=4 * mu_blk * nu_blk * conds_all,
            moved=12 * MIB,
        )(val_turned, scr_turned, val_rows, qx, cond_pts)
        summed = call(
            functools.partial(exchange_kernel, cfg, chunk, scale),
            "exchange",
            msg_shape,
            [ANY] * 5,
            VMEM,
            [
                pltpu.VMEM((devices, own // LANES, LANES), F32),
                pltpu.VMEM((pairs, LANES, LANES), F32),
                pltpu.VMEM((own, npt_all), BF),
                pltpu.VMEM((conds_all, own), BF),
                pltpu.VMEM((rows_all, own), BF),
                pltpu.VMEM((pairs, LANES, LANES), F32),
                pltpu.VMEM((devices,) + block, F32),
                dma(npt_all // chunk),
                dma(4),
            ],
        )(density, direct, coulomb, val_own, cond_own)
        recv = exchange_all(summed)
        if first:
            state, coef, message = call(
                functools.partial(first_owner_kernel, count_all),
                "first_owner",
                (shape_of((3,) + block), shape_of((3,)), msg_shape),
                [VMEM] * 4,
                (VMEM, SMEM, VMEM),
                mib=8,
            )(recv, msgs, gap, start_own)
        else:
            state, coef, message = call(
                functools.partial(second_owner_kernel, count_all),
                "second_owner",
                (shape_of((2,) + block), shape_of((4,)), shape_of((devices, 2, LANES))),
                [VMEM] * 4 + [SMEM],
                (VMEM, SMEM, VMEM),
                mib=8,
            )(recv, msgs, gap, state, coef)
        msgs = exchange_all(message)
    return call(
        functools.partial(finish_kernel, count_all),
        "finish",
        (shape_of(start_vec.shape), shape_of((2 * STEPS,))),
        [VMEM] * 2 + [SMEM],
        (VMEM, SMEM),
        mib=8,
    )(msgs, state, coef)


def array_path(start_vec, val_energy, cond_energy, val_orb, cond_orb, coulomb, screened):
    n_ka = lax.axis_size("ka")
    n_band = lax.axis_size("band")
    devices = n_ka * n_band
    ka, band = lax.axis_index("ka"), lax.axis_index("band")
    me = ka * n_band + band
    k_dev, pair_blk = start_vec.shape
    nv_blk = val_orb.shape[1]
    n_cond = cond_orb.shape[1]
    n_val = nv_blk * n_band
    npt_all = cond_orb.shape[2]
    k_points = k_dev * n_ka
    mu_blk, nu_blk = screened.shape
    own_pts = coulomb.shape[0]
    count_all = k_points * n_val * n_cond
    kernel_scale = 1.0 / (npt_all * math.sqrt(count_all))

    start_all = gather_all(start_vec, devices)
    val_cut = lax.all_to_all(
        val_orb.reshape(k_dev, nv_blk, n_ka, nu_blk).transpose(2, 0, 1, 3),
        "ka", split_axis=0, concat_axis=0, tiled=True,
    ).reshape(k_points, nv_blk, nu_blk)
    val_pts = lax.all_gather(val_cut, "band", axis=1, tiled=True)
    cond_local = lax.dynamic_slice_in_dim(cond_orb, band * mu_blk, mu_blk, 2)
    cond_pts = lax.all_gather(cond_local, "ka", axis=0, tiled=True)
    cond_rows = cond_orb.reshape(k_dev, n_cond, n_ka, n_band, own_pts)
    cond_rows = lax.dynamic_index_in_dim(cond_rows, band, 3, keepdims=False)
    cond_own = lax.all_to_all(
        cond_rows.transpose(2, 0, 1, 3), "ka", split_axis=0, concat_axis=0, tiled=True
    ).reshape(k_points, n_cond, own_pts)
    val_own = lax.dynamic_slice_in_dim(val_pts, band * own_pts, own_pts, 2)

    energy_gap = (cond_energy[:, None, :] - val_energy[:, :, None]).reshape(k_dev, pair_blk)
    start_sq = jnp.sum(start_all * start_all)
    current = start_all / jnp.sqrt(start_sq / count_all + 1e-06)
    previous = jnp.zeros_like(current)
    beta_val = jnp.float32(0.0)
    alphas = []
    betas = []
    for turn_index in range(STEPS):
        full_vec = (
            current.astype(BF)
            .reshape(n_ka, n_band, k_dev, nv_blk, n_cond)
            .transpose(0, 2, 1, 3, 4)
            .reshape(k_points, n_val, n_cond)
        )
        mixed_f = jnp.einsum("kvc,kvn->kcn", full_vec, val_pts, preferred_element_type=F32)
        mixed_own = lax.dynamic_slice_in_dim(mixed_f, band * own_pts, own_pts, 2)
        density_own = jnp.sum(mixed_own * cond_own.astype(F32), axis=(0, 1))
        density = gather_all(density_own.astype(BF), devices).reshape(npt_all)
        mixed_val = mixed_f.astype(BF)
        amp = jnp.einsum("kcm,kcn->mn", cond_pts, mixed_val, preferred_element_type=F32)
        kern = (screened.astype(F32) * amp * kernel_scale).astype(BF)
        folded = jnp.einsum("mn,kvn->kvm", kern, val_pts, preferred_element_type=F32).astype(BF)
        direct_part = jnp.einsum("kcm,kvm->kvc", cond_pts, folded, preferred_element_type=F32)
        potential = kernel_scale * jnp.dot(coulomb, density, preferred_element_type=F32)
        weighted = (val_own.astype(F32) * potential).astype(BF)
        exchange = jnp.einsum("kvp,kcp->kvc", weighted, cond_own, preferred_element_type=F32)
        part = 2.0 * exchange - direct_part
        arranged = (
            part.reshape(n_ka, k_dev, n_band, nv_blk, n_cond)
            .transpose(0, 2, 1, 3, 4)
            .reshape(devices, k_dev, pair_blk)
        )
        inter_own = jnp.sum(exchange_all(arranged), axis=0)
        current_own = lax.dynamic_index_in_dim(current, me, 0, keepdims=False)
        resid_vec = gather_all(energy_gap * current_own + inter_own, devices)
        resid_vec = resid_vec - beta_val * previous
        alpha_val = jnp.sum(current * resid_vec) / count_all
        resid_vec = resid_vec - alpha_val * current
        beta_val = jnp.sqrt(jnp.sum(resid_vec * resid_vec) / count_all + 1e-06)
        previous = current
        current = resid_vec / beta_val
        alphas.append(alpha_val)
        betas.append(beta_val)
    coeffs = jnp.stack(alphas + betas)
    return (lax.dynamic_index_in_dim(current, me, 0, keepdims=False), coeffs)


def per_device(*args):
    start_vec, _, _, val_orb, cond_orb, coulomb, screened = args
    n_ka, n_band = lax.axis_size("ka"), lax.axis_size("band")
    fits = (
        n_band == 8
        and n_ka & (n_ka - 1) == 0
        and start_vec.shape[0] % 2 == 1
        and val_orb.shape[1] == ROWS
        and cond_orb.shape[1] == HALF
        and start_vec.shape[0] * n_ka % 4 == 0
        and coulomb.shape[0] % LANES == 0
        and coulomb.shape[1] % 1024 == 0
        and screened.shape[0] % 512 == 0
        and screened.shape[1] % 1024 == 0
        and screened.shape[0] * screened.shape[1] <= 2 * MIB
    )
    return (kernel_path if fits else array_path)(*args)


def solution(mesh):
    in_specs = (
        P("ka", "band"),
        P("ka", "band"),
        P("ka", None),
        P("ka", "band", None),
        P("ka", None, None),
        P(("ka", "band"), None),
        P("band", "ka"),
    )
    out_specs = (P("ka", "band"), P())
    return jax.shard_map(
        per_device, mesh=mesh, in_specs=in_specs, out_specs=out_specs, check_vma=False
    )
```

```python
import functools
import math

import jax
import jax.numpy as jnp
from jax import lax
from jax.experimental import pallas as pl
from jax.experimental.pallas import tpu as pltpu
from jax.sharding import PartitionSpec as P

STEPS = 2
AXES = ("ka", "band")
BF, F32 = jnp.bfloat16, jnp.float32
LANES = 128
HALF = 64
ROWS = 8
MIB = 1 << 20

VMEM = pl.BlockSpec(memory_space=pltpu.VMEM)
SMEM = pl.BlockSpec(memory_space=pltpu.SMEM)
ANY = pl.BlockSpec(memory_space=pl.ANY)


def gather_all(block, devices):
    wide = jnp.broadcast_to(block[None], (devices,) + block.shape)
    return exchange_all(wide)


def exchange_all(parts):
    return lax.all_to_all(parts, AXES, split_axis=0, concat_axis=0, tiled=True)


def dot_nt(lhs, rhs):
    return lax.dot_general(lhs, rhs, (((1,), (1,)), ((), ())), preferred_element_type=F32)


def dot_tn(lhs, rhs):
    return lax.dot_general(lhs, rhs, (((0,), (0,)), ((), ())), preferred_element_type=F32)


def lane_half(tile, have, want):
    if have != want:
        tile = pltpu.roll(tile, HALF, axis=1)
    lane = lax.broadcasted_iota(jnp.int32, tile.shape, 1)
    keep = lane < HALF if want == 0 else lane >= HALF
    return jnp.where(keep, tile, 0.0)


def with_sums(block, sums):
    row = lax.broadcasted_iota(jnp.int32, block.shape, 0)
    lane = lax.broadcasted_iota(jnp.int32, block.shape, 1)
    free = row == block.shape[0] - ROWS
    for i, total in enumerate(sums):
        rest = jnp.full(block.shape, total, F32)
        for part in range(3):
            piece = rest.astype(BF).astype(F32)
            block = jnp.where(free & (lane == HALF + 3 * i + part), piece, block)
            rest = rest - piece
    return block


def read_sums(msgs_ref, count):
    rows = msgs_ref.shape[1]
    tile = jnp.sum(msgs_ref[...].astype(F32), axis=0)[rows - ROWS :, :]
    row = lax.broadcasted_iota(jnp.int32, tile.shape, 0)
    lane = lax.broadcasted_iota(jnp.int32, tile.shape, 1)
    out = []
    for i in range(count):
        mine = (row == 0) & (lane >= HALF + 3 * i) & (lane < HALF + 3 * i + 3)
        out.append(jnp.sum(jnp.where(mine, tile, 0.0), keepdims=True))
    return out


def piece_copies(refs, parts, column, width, dest, sems):
    copies = []
    for d, piece in enumerate(parts):
        row = 0
        for ref, start, rows in piece:
            copies.append(
                pltpu.make_async_copy(
                    refs[ref].at[pl.ds(start, rows), pl.ds(column, width)],
                    dest.at[d, pl.ds(row, rows), :],
                    sems.at[len(copies)],
                )
            )
            row += rows
    return copies


def start_all(copies):
    for copy in copies:
        copy.start()


def wait_all(copies):
    for copy in copies:
        copy.wait()


def device_at(n_band, j, d):
    ka = jnp.bitwise_xor(lax.axis_index("ka"), j)
    return ka * n_band + jnp.bitwise_xor(lax.axis_index("band"), d)


def pair_rows(ref, kp):
    part = ref[:, kp * 2 * ROWS : (kp + 1) * 2 * ROWS, :]
    return part.reshape(part.shape[0] * 2 * ROWS, part.shape[2])


def pack_kernel(n_ka, nu, *refs):
    start_in, cond_in, val_in, val_ref, orb_ref = refs[:5]
    own_ref, gap_ref, outs, refs = refs[5], refs[6], refs[7 : 7 + n_ka], refs[7 + n_ka :]
    start_ref, cond_ref, energy_ref, cuts, sems, cut_sems = refs
    own = cuts.shape[-1]
    ins = ((start_in, start_ref), (cond_in, cond_ref), (val_in, energy_ref))
    small = [pltpu.make_async_copy(ref, to, sems.at[i]) for i, (ref, to) in enumerate(ins)]
    k_dev = val_ref.shape[0]
    val_copies, cut_copies = [], []
    for j in range(n_ka):
        at = pl.multiple_of(jnp.bitwise_xor(lax.axis_index("ka"), j) * nu, nu)
        point = pl.multiple_of(at + lax.axis_index("band") * own, LANES)
        val_copies.append(
            pltpu.make_async_copy(
                val_ref.at[:, :, pl.ds(at, nu)], outs[j].at[:, :, pl.ds(0, nu)], cut_sems.at[0, j]
            )
        )
        cut_copies.append(
            pltpu.make_async_copy(
                orb_ref.at[:, :, pl.ds(point, own)], cuts.at[j], cut_sems.at[1, j]
            )
        )
    start_all(small + cut_copies + val_copies)
    wait_all(small)
    own_ref[...] = jnp.zeros_like(own_ref)
    gap_ref[...] = jnp.zeros_like(gap_ref)
    cond = jnp.concatenate([cond_ref[...], cond_ref[...]], axis=1)
    for kl in range(k_dev):
        half = kl % 2
        for v in range(ROWS):
            at = pl.ds(kl // 2 * ROWS + v, 1)
            row = start_ref[pl.ds(kl, 1), pl.ds(v // 2 * LANES, LANES)]
            own_ref[at, :] = own_ref[at, :] + lane_half(row, v % 2, half)
            gap = cond[kl : kl + 1, :] - energy_ref[kl, v]
            gap_ref[at, :] = gap_ref[at, :] + lane_half(gap, half, half)
    mine = own_ref[...]
    square = mine * mine
    block = with_sums(mine, [jnp.sum(square), jnp.sum(gap_ref[...] * square)])
    for j in range(n_ka):
        for g in range(k_dev):
            head = jnp.zeros((ROWS, LANES), F32)
            if (g + 1) * ROWS <= block.shape[0]:
                head = block[g * ROWS : (g + 1) * ROWS, :]
            outs[j][g, :, nu : nu + LANES] = head.astype(BF)
        cut_copies[j].wait()
        for kl in range(k_dev):
            cut = cuts[j, kl].astype(F32)
            wide = [cut[q * ROWS : (q + 1) * ROWS, :] for q in range(cut.shape[0] // ROWS)]
            outs[j][kl, :, nu + LANES :] = jnp.concatenate(wide, axis=1).astype(BF)
    wait_all(val_copies)


def turn_kernel(tile, scr_ref, out_ref, scrs, turned, in_sems, out_sems):
    nu = scr_ref.shape[1]
    ins, outs = [], []
    for j in range(nu // tile):
        at = pl.ds(j * tile, tile)
        ins.append(pltpu.make_async_copy(scr_ref.at[:, at], scrs.at[:, at], in_sems.at[j]))
        outs.append(pltpu.make_async_copy(turned.at[at, :], out_ref.at[at, :], out_sems.at[j]))
    start_all(ins)
    for j in range(nu // tile):
        ins[j].wait()
        turned[j * tile : (j + 1) * tile, :] = scrs[:, j * tile : (j + 1) * tile].T
        outs[j].start()
    wait_all(outs)


def order_kernel(parts, n_ka, *refs):
    got_refs, val_refs, refs = refs[:n_ka], refs[n_ka:-13], refs[-13:]
    rows_out, turned_out, own_out, cond_out, msgs_out = refs[:5]
    vals, heads, ordered, turned, cuts, val_sems, out_sems, cut_sems = refs[5:]
    own = own_out.shape[1]
    nu = ordered.shape[1]
    copies = piece_copies(val_refs, parts, 0, nu, vals, val_sems.at[0])
    head_copies = piece_copies(val_refs, parts, nu, LANES, heads, val_sems.at[1])
    cut_copies = [
        pltpu.make_async_copy(
            ref.at[:, :, pl.ds(nu + LANES, cuts.shape[-1])], cuts.at[j], cut_sems.at[j]
        )
        for j, ref in enumerate(got_refs)
    ]
    start_all(copies + head_copies + cut_copies)
    wait_all(cut_copies)
    k_dev, points = cuts.shape[1], cuts.shape[-1] // own
    for j in range(n_ka):
        for kl in range(k_dev):
            cut = cuts[j, kl].astype(F32)
            tall = [cut[:, q * own : (q + 1) * own] for q in range(points)]
            at = (j * k_dev + kl) * points * ROWS
            cond_out[at : at + points * ROWS, :] = jnp.concatenate(tall, axis=0).astype(BF)
    wait_all(copies)
    n_band, group = vals.shape[0], vals.shape[0] * 2 * ROWS
    column = pl.multiple_of(lax.axis_index("band") * own, LANES)
    outs = []
    for kp in range(ordered.shape[0] // group):
        at = slice(kp * group, (kp + 1) * group)
        ordered[at, :] = pair_rows(vals, kp)
        turned[:, at] = ordered[at, :].T
        at = pl.ds(kp * group, group)
        outs += [
            pltpu.make_async_copy(ordered.at[at, :], rows_out.at[at, :], out_sems.at[0, kp]),
            pltpu.make_async_copy(turned.at[:, at], turned_out.at[:, at], out_sems.at[1, kp]),
            pltpu.make_async_copy(
                ordered.at[at, pl.ds(column, own)], own_out.at[at, :], out_sems.at[2, kp]
            ),
        ]
        start_all(outs[-3:])
    wait_all(head_copies)
    rows = msgs_out.shape[1]
    step = heads.shape[1] // n_ka
    for d in range(n_band):
        head = heads[d].astype(F32)
        for j in range(n_ka):
            msgs_out[device_at(n_band, j, d)] = head[j * step : j * step + rows, :].astype(BF)
    wait_all(outs)


def density_kernel(cfg, *refs):
    n_ka, n_band, k_dev = cfg
    k_points = n_ka * k_dev
    msgs_ref, vown_ref, cond_ref, qx_ref, rho_ref, xs, msgs, vown, conds, sems = refs
    own = vown_ref.shape[1]
    msg_copy = pltpu.make_async_copy(msgs_ref, msgs, sems.at[0])
    copies = [
        pltpu.make_async_copy(vown_ref, vown, sems.at[1]),
        pltpu.make_async_copy(cond_ref, conds, sems.at[2]),
    ]
    start_all([msg_copy] + copies)
    xs[...] = jnp.zeros_like(xs)
    msg_copy.wait()
    for d in range(n_band):
        for k in range(k_points):
            j, kl = divmod(k, k_dev)
            tile = msgs[device_at(n_band, j, d), :, :].astype(F32)
            tile = tile[kl // 2 * ROWS : (kl // 2 + 1) * ROWS, :]
            base = k // 2 % 2 * LANES
            at = pl.ds(base + d * 2 * ROWS + k % 2 * ROWS, ROWS)
            xs[k // 4, at, pl.ds(base, LANES)] = lane_half(tile, kl % 2, k % 2)
    qx_ref[...] = xs[...].astype(BF)
    wait_all(copies)
    rho = jnp.zeros((1, own), F32)
    quad = 2 * LANES
    for kq in range(k_points // 4):
        at = slice(kq * quad, (kq + 1) * quad)
        mixed = dot_tn(qx_ref[kq], vown[at, :])
        rho = rho + jnp.sum(mixed * conds[at, :].astype(F32), axis=0, keepdims=True)
    for r in range(own // LANES):
        part = rho[:, r * LANES : (r + 1) * LANES]
        rho_ref[:, r, :] = jnp.broadcast_to(part, (rho_ref.shape[0], LANES))


def direct_kernel(n_ka, tile, scale, *refs):
    turned_ref, scr_ref, rows_ref, qx_ref, refs = refs[0], refs[1], refs[2], refs[3], refs[4:]
    cond_refs, refs = refs[:n_ka], refs[n_ka:]
    di_ref, qx, turned, conds, scrs, vals, mixed, kern, folded = refs[:9]
    qx_sem, cond_sems, row_sem, chunk_sems = refs[9:]
    nu, mu = scr_ref.shape
    quad = 2 * LANES
    qx_copy = pltpu.make_async_copy(qx_ref, qx, qx_sem.at[0])
    cond_copies = [
        pltpu.make_async_copy(ref, conds.at[j], cond_sems.at[j]) for j, ref in enumerate(cond_refs)
    ]
    turned_copies, scr_copies = [], []
    for i in range(nu // tile):
        at = pl.ds(i * tile, tile)
        turned_copies.append(
            pltpu.make_async_copy(turned_ref.at[at, :], turned.at[at, :], chunk_sems.at[0, i])
        )
        scr_copies.append(
            pltpu.make_async_copy(scr_ref.at[at, :], scrs.at[at, :], chunk_sems.at[1, i])
        )
    row_copy = pltpu.make_async_copy(rows_ref, vals, row_sem.at[0])
    start_all([qx_copy, turned_copies[0]] + cond_copies + [scr_copies[0]])
    for i in range(1, nu // tile):
        start_all([turned_copies[i], scr_copies[i]])
    row_copy.start()
    qx_copy.wait()
    for i in range(nu // tile):
        rows = slice(i * tile, (i + 1) * tile)
        turned_copies[i].wait()
        for kq in range(qx.shape[0]):
            cols = slice(kq * quad, (kq + 1) * quad)
            mixed[rows, cols] = jnp.dot(
                turned[rows, cols], qx[kq], preferred_element_type=F32
            ).astype(BF)
        if i == 0:
            wait_all(cond_copies)
            cond_rows = conds[...].reshape(-1, mu)
        scr_copies[i].wait()
        amp = jnp.dot(mixed[rows, :], cond_rows, preferred_element_type=F32)
        kern[rows, :] = (scrs[rows, :].astype(F32) * amp * scale).astype(BF)
    row_copy.wait()
    folded[...] = jnp.dot(vals[...], kern[...], preferred_element_type=F32).astype(BF)
    for kp in range(di_ref.shape[0]):
        at = slice(kp * LANES, (kp + 1) * LANES)
        di_ref[kp] = dot_nt(folded[at, :], cond_rows[at, :])


def exchange_kernel(cfg, chunk, scale, *refs):
    n_ka, n_band, k_dev = cfg
    k_points = n_ka * k_dev
    rho_ref, di_ref, coul_ref, vown_ref, cond_ref, msg_ref = refs[:6]
    rhos, di, coul, conds, vown, part, msg, coul_sems, sems = refs[6:]
    rho_copy = pltpu.make_async_copy(rho_ref, rhos, sems.at[3])
    own, npt = coul_ref.shape
    coul_copies = [
        pltpu.make_async_copy(
            coul_ref.at[:, pl.ds(i * chunk, chunk)], coul.at[:, pl.ds(i * chunk, chunk)], coul_sems.at[i]
        )
        for i in range(npt // chunk)
    ]
    copies = [
        pltpu.make_async_copy(vown_ref, vown, sems.at[0]),
        pltpu.make_async_copy(di_ref, di, sems.at[1]),
        pltpu.make_async_copy(cond_ref, conds, sems.at[2]),
    ]
    start_all([rho_copy] + coul_copies + copies)
    rho_copy.wait()
    acc = jnp.zeros((own, LANES), F32)
    per_dev = own // LANES
    for i in range(npt // chunk):
        coul_copies[i].wait()
        for j in range(i * chunk // LANES, (i + 1) * chunk // LANES):
            rho = rhos[j // per_dev, pl.ds(j % per_dev, 1), :].astype(BF).astype(F32)
            acc = acc + coul[:, j * LANES : (j + 1) * LANES].astype(F32) * rho
    potential = scale * jnp.sum(acc.T, axis=0, keepdims=True)
    wait_all(copies)
    for kp in range(k_points // 2):
        at = slice(kp * LANES, (kp + 1) * LANES)
        weighted = (vown[at, :].astype(F32) * potential).astype(BF)
        part[kp] = 2.0 * dot_nt(weighted, conds[at, :]) - di[kp]
    for d in range(n_band):
        for j in range(n_ka):
            for g in range((k_dev + 1) // 2):
                tile = None
                for kl in range(2 * g, min(2 * g + 2, k_dev)):
                    k = j * k_dev + kl
                    piece = part[k // 2, pl.ds(d * 2 * ROWS + k % 2 * ROWS, ROWS), :]
                    piece = lane_half(piece, k % 2, kl % 2)
                    tile = piece if tile is None else tile + piece
                msg[device_at(n_band, j, d), pl.ds(g * ROWS, ROWS), :] = tile
    msg_ref[...] = msg[...].astype(BF)


def received(recv_ref):
    return jnp.sum(recv_ref[...].astype(F32), axis=0)


def shifted(count_all, shift, square, cross_sum, square_sum):
    alpha = shift * square + cross_sum / count_all
    d = alpha - shift
    mean_sq = (square_sum - 2.0 * d * cross_sum) / count_all + d * d * square
    mean_sq = jnp.maximum(mean_sq, 0.0)
    return alpha, d, mean_sq


def first_owner_kernel(count_all, recv_ref, msgs_ref, gap_ref, own_ref, state_ref, coef_ref, msg_ref):
    start_sq, gap_sq = read_sums(msgs_ref, 2)
    norm = start_sq / count_all
    inv = 1.0 / jnp.sqrt(norm + 1e-06)
    square = norm / (norm + 1e-06)
    shift = gap_sq / jnp.maximum(start_sq, 1e-30)
    cur = own_ref[...] * inv
    inter = received(recv_ref) * inv
    gap = gap_ref[...]
    resid = (gap - shift) * cur + inter
    state_ref[0] = cur
    state_ref[1] = resid
    state_ref[2] = inter
    coef_ref[0] = shift[0, 0]
    coef_ref[1] = square[0, 0]
    coef_ref[2] = (gap_sq * inv * inv)[0, 0]
    sums = [
        jnp.sum(cur * resid),
        jnp.sum(resid * resid),
        jnp.sum(gap * resid * resid),
        jnp.sum(gap * resid * cur),
    ]
    msg_ref[...] = jnp.broadcast_to(with_sums(resid, sums).astype(BF)[None], msg_ref.shape)


def second_owner_kernel(count_all, recv_ref, msgs_ref, gap_ref, state_ref, coef_ref, out_ref, coef_out, msg_ref):
    cross, total, gap_rr, gap_rq = read_sums(msgs_ref, 4)
    alpha, d, mean_sq = shifted(count_all, coef_ref[0], coef_ref[1], cross, total)
    beta = jnp.sqrt(mean_sq + 1e-06)
    square = mean_sq / (mean_sq + 1e-06)
    gap_qq = gap_rr - 2.0 * d * gap_rq + d * d * coef_ref[2]
    shift = gap_qq / (mean_sq + 1e-06) / count_all
    prev = state_ref[0]
    cur = (state_ref[1] - d * prev) / beta
    inter = (received(recv_ref) - d * state_ref[2]) / beta
    resid = (gap_ref[...] - shift) * cur + inter - beta * prev
    out_ref[0] = cur
    out_ref[1] = resid
    coef_out[0] = alpha[0, 0]
    coef_out[1] = beta[0, 0]
    coef_out[2] = shift[0, 0]
    coef_out[3] = square[0, 0]
    dims = msg_ref.shape[:1] + msg_ref.shape[2:]
    msg_ref[:, 0, :] = jnp.full(dims, jnp.sum(cur * resid), F32)
    msg_ref[:, 1, :] = jnp.full(dims, jnp.sum(resid * resid), F32)


def finish_kernel(count_all, msgs_ref, state_ref, coef_ref, out_ref, coeffs_ref):
    sums = jnp.sum(msgs_ref[...], axis=0)
    alpha, d, mean_sq = shifted(count_all, coef_ref[2], coef_ref[3], sums[0:1, 0:1], sums[1:2, 0:1])
    beta = jnp.sqrt(mean_sq + 1e-06)
    own = (state_ref[1] - d * state_ref[0]) / beta
    coeffs_ref[0] = coef_ref[0]
    coeffs_ref[1] = alpha[0, 0]
    coeffs_ref[2] = coef_ref[1]
    coeffs_ref[3] = beta[0, 0]
    for kl in range(out_ref.shape[0]):
        tile = own[kl // 2 * ROWS : (kl // 2 + 1) * ROWS, :]
        other = pltpu.roll(tile, HALF, axis=1)
        left, right = (tile, other) if kl % 2 == 0 else (other, tile)
        low = lax.broadcasted_iota(jnp.int32, (1, LANES), 1) < HALF
        for j in range(ROWS // 2):
            row = jnp.where(low, left[2 * j : 2 * j + 1], right[2 * j + 1 : 2 * j + 2])
            out_ref[pl.ds(kl, 1), pl.ds(j * LANES, LANES)] = row


def shape_of(dims, kind=F32):
    return jax.ShapeDtypeStruct(dims, kind)


def call(kernel, name, out_shape, in_specs, out_specs, scratch=(), mib=58, flops=0, moved=0):
    return pl.pallas_call(
        kernel,
        out_shape=out_shape,
        in_specs=in_specs,
        out_specs=out_specs,
        scratch_shapes=list(scratch),
        compiler_params=pltpu.CompilerParams(vmem_limit_bytes=mib * MIB),
        cost_estimate=pl.CostEstimate(flops=flops, bytes_accessed=moved, transcendentals=0),
        name=name,
    )


def dma(*dims):
    return pltpu.SemaphoreType.DMA(dims)


def swap(block, axis, d):
    return lax.ppermute(block, axis, [(i, i ^ d) for i in range(lax.axis_size(axis))])


def plane_pieces(own_piece, others):
    def move(block, d):
        return swap(block, "band", d)

    rows = own_piece.shape[0]
    half = rows // 2
    by_x, by_y, core = move(own_piece, 2), move(own_piece, 4), move(own_piece, 1)
    by_x, by_y, core, others = lax.optimization_barrier((by_x, by_y, core, others))
    diag = [move(by_x[:half], 4), move(by_y[half:], 2)]
    near_x, near_y = move(by_x, 1), move(by_y, 1)
    far = [move(part, 1) for part in diag]
    arrays = [own_piece, core, by_x, near_x, by_y, near_y] + diag + far
    parts = tuple(((i, 0, rows),) for i in range(6))
    parts += (((6, 0, half), (7, 0, half)), ((8, 0, half), (9, 0, half)))
    return arrays, parts, others


def kernel_path(start_vec, val_energy, cond_energy, val_orb, cond_orb, coulomb, screened):
    n_ka = lax.axis_size("ka")
    n_band = lax.axis_size("band")
    devices = n_ka * n_band
    ka, band = lax.axis_index("ka"), lax.axis_index("band")
    k_dev = start_vec.shape[0]
    nv_blk = val_orb.shape[1]
    n_cond = cond_orb.shape[1]
    npt_all = cond_orb.shape[2]
    k_points = k_dev * n_ka
    pairs = k_points // 2
    mu_blk, nu_blk = screened.shape
    own = coulomb.shape[0]
    count_all = k_points * nv_blk * n_band * n_cond
    scale = 1.0 / (npt_all * math.sqrt(count_all))
    piece_rows = k_points * nv_blk

    block = ((k_dev + 1) // 2 * ROWS, LANES)
    msg_shape = shape_of((devices,) + block, BF)
    wide = nu_blk + LANES
    cut_lanes = n_cond // ROWS * own
    start_own, gap, *payloads = call(
        functools.partial(pack_kernel, n_ka, nu_blk),
        "pack",
        (shape_of(block), shape_of(block))
        + (shape_of((k_dev, nv_blk, wide + cut_lanes), BF),) * n_ka,
        [ANY] * 5,
        (VMEM,) * (2 + n_ka),
        [
            pltpu.VMEM(start_vec.shape, F32),
            pltpu.VMEM(cond_energy.shape, F32),
            pltpu.SMEM(val_energy.shape, F32),
            pltpu.VMEM((n_ka, k_dev, n_cond, own), BF),
            dma(3),
            dma(2, n_ka),
        ],
    )(start_vec, cond_energy, val_energy, val_orb, cond_orb)
    base, payloads = lax.optimization_barrier((band * mu_blk, payloads))
    got = [payloads[0]] + [swap(payloads[j], "ka", j) for j in range(1, n_ka)]
    val_cut = jnp.concatenate([part[:, :, :wide] for part in got], axis=0)
    val_cut = val_cut.reshape(piece_rows, wide)
    cond_local = lax.dynamic_slice_in_dim(cond_orb, base, mu_blk, 2)
    cond_local = cond_local.reshape(k_dev * n_cond, mu_blk)
    cond_pts = [cond_local] + [swap(cond_local, "ka", j) for j in range(1, n_ka)]

    chunk, tile = 1024, nu_blk
    rows_all, conds_all = k_points * nv_blk * n_band, k_points * n_cond
    scr_turned = call(
        functools.partial(turn_kernel, nu_blk // 4),
        "turn",
        shape_of((nu_blk, mu_blk), BF),
        [ANY],
        ANY,
        [pltpu.VMEM((mu_blk, nu_blk), BF), pltpu.VMEM((nu_blk, mu_blk), BF)]
        + [dma(4)] * 2,
        moved=8 * MIB,
    )(screened)
    pieces, parts, scr_turned = plane_pieces(val_cut, scr_turned)
    pieces, cond_pts[1:-1] = lax.optimization_barrier((pieces, cond_pts[1:-1]))
    val_rows, val_turned, val_own, cond_own, msgs = call(
        functools.partial(order_kernel, parts, n_ka),
        "order",
        (
            shape_of((rows_all, nu_blk), BF),
            shape_of((nu_blk, rows_all), BF),
            shape_of((rows_all, own), BF),
            shape_of((conds_all, own), BF),
            msg_shape,
        ),
        [ANY] * (n_ka + len(pieces)),
        (ANY, ANY, ANY, VMEM, VMEM),
        [
            pltpu.VMEM((n_band, piece_rows, nu_blk), BF),
            pltpu.VMEM((n_band, piece_rows, LANES), BF),
            pltpu.VMEM((rows_all, nu_blk), BF),
            pltpu.VMEM((nu_blk, rows_all), BF),
            pltpu.VMEM((n_ka, k_dev, nv_blk, cut_lanes), BF),
            dma(2, sum(len(piece) for piece in parts)),
            dma(3, pairs),
            dma(n_ka),
        ],
        moved=9 * MIB,
    )(*got, *pieces)

    cfg = (n_ka, n_band, k_dev)
    quads = k_points // 4
    state, coef = None, None
    for step in range(STEPS):
        first = step == 0
        qx, rho = call(
            functools.partial(density_kernel, cfg),
            "density",
            (
                shape_of((quads, 2 * LANES, 2 * LANES), BF),
                shape_of((devices, own // LANES, LANES)),
            ),
            [ANY] * 3,
            (VMEM, VMEM),
            [
                pltpu.VMEM((quads, 2 * LANES, 2 * LANES), F32),
                pltpu.VMEM((devices,) + block, BF),
                pltpu.VMEM((rows_all, own), BF),
                pltpu.VMEM((conds_all, own), BF),
                dma(3),
            ],
        )(msgs, val_own, cond_own)
        density = exchange_all(rho)
        direct = call(
            functools.partial(direct_kernel, n_ka, tile, scale),
            "direct",
            shape_of((pairs, LANES, LANES)),
            [ANY] * (4 + n_ka),
            VMEM,
            [
                pltpu.VMEM((quads, 2 * LANES, 2 * LANES), BF),
                pltpu.VMEM((nu_blk, rows_all), BF),
                pltpu.VMEM((n_ka, k_dev * n_cond, mu_blk), BF),
                pltpu.VMEM((nu_blk, mu_blk), BF),
                pltpu.VMEM((rows_all, nu_blk), BF),
                pltpu.VMEM((nu_blk, conds_all), BF),
                pltpu.VMEM((nu_blk, mu_blk), BF),
                pltpu.VMEM((rows_all, mu_blk), BF),
                dma(1),
                dma(n_ka),
                dma(1),
                dma(2, nu_blk // tile),
            ],
            flops=4 * mu_blk * nu_blk * conds_all,
            moved=12 * MIB,
        )(val_turned, scr_turned, val_rows, qx, *cond_pts)
        summed = call(
            functools.partial(exchange_kernel, cfg, chunk, scale),
            "exchange",
            msg_shape,
            [ANY] * 5,
            VMEM,
            [
                pltpu.VMEM((devices, own // LANES, LANES), F32),
                pltpu.VMEM((pairs, LANES, LANES), F32),
                pltpu.VMEM((own, npt_all), BF),
                pltpu.VMEM((conds_all, own), BF),
                pltpu.VMEM((rows_all, own), BF),
                pltpu.VMEM((pairs, LANES, LANES), F32),
                pltpu.VMEM((devices,) + block, F32),
                dma(npt_all // chunk),
                dma(4),
            ],
        )(density, direct, coulomb, val_own, cond_own)
        recv = exchange_all(summed)
        if first:
            state, coef, message = call(
                functools.partial(first_owner_kernel, count_all),
                "first_owner",
                (shape_of((3,) + block), shape_of((3,)), msg_shape),
                [VMEM] * 4,
                (VMEM, SMEM, VMEM),
                mib=8,
            )(recv, msgs, gap, start_own)
        else:
            state, coef, message = call(
                functools.partial(second_owner_kernel, count_all),
                "second_owner",
                (shape_of((2,) + block), shape_of((4,)), shape_of((devices, 2, LANES))),
                [VMEM] * 4 + [SMEM],
                (VMEM, SMEM, VMEM),
                mib=8,
            )(recv, msgs, gap, state, coef)
        msgs = exchange_all(message)
    return call(
        functools.partial(finish_kernel, count_all),
        "finish",
        (shape_of(start_vec.shape), shape_of((2 * STEPS,))),
        [VMEM] * 2 + [SMEM],
        (VMEM, SMEM),
        mib=8,
    )(msgs, state, coef)


def array_path(start_vec, val_energy, cond_energy, val_orb, cond_orb, coulomb, screened):
    n_ka = lax.axis_size("ka")
    n_band = lax.axis_size("band")
    devices = n_ka * n_band
    ka, band = lax.axis_index("ka"), lax.axis_index("band")
    me = ka * n_band + band
    k_dev, pair_blk = start_vec.shape
    nv_blk = val_orb.shape[1]
    n_cond = cond_orb.shape[1]
    n_val = nv_blk * n_band
    npt_all = cond_orb.shape[2]
    k_points = k_dev * n_ka
    mu_blk, nu_blk = screened.shape
    own_pts = coulomb.shape[0]
    count_all = k_points * n_val * n_cond
    kernel_scale = 1.0 / (npt_all * math.sqrt(count_all))

    start_all = gather_all(start_vec, devices)
    val_cut = lax.all_to_all(
        val_orb.reshape(k_dev, nv_blk, n_ka, nu_blk).transpose(2, 0, 1, 3),
        "ka", split_axis=0, concat_axis=0, tiled=True,
    ).reshape(k_points, nv_blk, nu_blk)
    val_pts = lax.all_gather(val_cut, "band", axis=1, tiled=True)
    cond_local = lax.dynamic_slice_in_dim(cond_orb, band * mu_blk, mu_blk, 2)
    cond_pts = lax.all_gather(cond_local, "ka", axis=0, tiled=True)
    cond_rows = cond_orb.reshape(k_dev, n_cond, n_ka, n_band, own_pts)
    cond_rows = lax.dynamic_index_in_dim(cond_rows, band, 3, keepdims=False)
    cond_own = lax.all_to_all(
        cond_rows.transpose(2, 0, 1, 3), "ka", split_axis=0, concat_axis=0, tiled=True
    ).reshape(k_points, n_cond, own_pts)
    val_own = lax.dynamic_slice_in_dim(val_pts, band * own_pts, own_pts, 2)

    energy_gap = (cond_energy[:, None, :] - val_energy[:, :, None]).reshape(k_dev, pair_blk)
    start_sq = jnp.sum(start_all * start_all)
    current = start_all / jnp.sqrt(start_sq / count_all + 1e-06)
    previous = jnp.zeros_like(current)
    beta_val = jnp.float32(0.0)
    alphas = []
    betas = []
    for turn_index in range(STEPS):
        full_vec = (
            current.astype(BF)
            .reshape(n_ka, n_band, k_dev, nv_blk, n_cond)
            .transpose(0, 2, 1, 3, 4)
            .reshape(k_points, n_val, n_cond)
        )
        mixed_f = jnp.einsum("kvc,kvn->kcn", full_vec, val_pts, preferred_element_type=F32)
        mixed_own = lax.dynamic_slice_in_dim(mixed_f, band * own_pts, own_pts, 2)
        density_own = jnp.sum(mixed_own * cond_own.astype(F32), axis=(0, 1))
        density = gather_all(density_own.astype(BF), devices).reshape(npt_all)
        mixed_val = mixed_f.astype(BF)
        amp = jnp.einsum("kcm,kcn->mn", cond_pts, mixed_val, preferred_element_type=F32)
        kern = (screened.astype(F32) * amp * kernel_scale).astype(BF)
        folded = jnp.einsum("mn,kvn->kvm", kern, val_pts, preferred_element_type=F32).astype(BF)
        direct_part = jnp.einsum("kcm,kvm->kvc", cond_pts, folded, preferred_element_type=F32)
        potential = kernel_scale * jnp.dot(coulomb, density, preferred_element_type=F32)
        weighted = (val_own.astype(F32) * potential).astype(BF)
        exchange = jnp.einsum("kvp,kcp->kvc", weighted, cond_own, preferred_element_type=F32)
        part = 2.0 * exchange - direct_part
        arranged = (
            part.reshape(n_ka, k_dev, n_band, nv_blk, n_cond)
            .transpose(0, 2, 1, 3, 4)
            .reshape(devices, k_dev, pair_blk)
        )
        inter_own = jnp.sum(exchange_all(arranged), axis=0)
        current_own = lax.dynamic_index_in_dim(current, me, 0, keepdims=False)
        resid_vec = gather_all(energy_gap * current_own + inter_own, devices)
        resid_vec = resid_vec - beta_val * previous
        alpha_val = jnp.sum(current * resid_vec) / count_all
        resid_vec = resid_vec - alpha_val * current
        beta_val = jnp.sqrt(jnp.sum(resid_vec * resid_vec) / count_all + 1e-06)
        previous = current
        current = resid_vec / beta_val
        alphas.append(alpha_val)
        betas.append(beta_val)
    coeffs = jnp.stack(alphas + betas)
    return (lax.dynamic_index_in_dim(current, me, 0, keepdims=False), coeffs)


def per_device(*args):
    start_vec, _, _, val_orb, cond_orb, coulomb, screened = args
    n_ka, n_band = lax.axis_size("ka"), lax.axis_size("band")
    fits = (
        n_band == 8
        and n_ka & (n_ka - 1) == 0
        and start_vec.shape[0] % 2 == 1
        and val_orb.shape[1] == ROWS
        and cond_orb.shape[1] == HALF
        and start_vec.shape[0] * n_ka % 4 == 0
        and coulomb.shape[0] % LANES == 0
        and coulomb.shape[1] % 1024 == 0
        and screened.shape[0] % 512 == 0
        and screened.shape[1] % 1024 == 0
        and screened.shape[0] * screened.shape[1] <= 2 * MIB
    )
    return (kernel_path if fits else array_path)(*args)


def solution(mesh):
    in_specs = (
        P("ka", "band"),
        P("ka", "band"),
        P("ka", None),
        P("ka", "band", None),
        P("ka", None, None),
        P(("ka", "band"), None),
        P("band", "ka"),
    )
    out_specs = (P("ka", "band"), P())
    return jax.shard_map(
        per_device, mesh=mesh, in_specs=in_specs, out_specs=out_specs, check_vma=False
    )
```

```python
import functools
import math

import jax
import jax.numpy as jnp
from jax import lax
from jax.experimental import pallas as pl
from jax.experimental.pallas import tpu as pltpu
from jax.sharding import PartitionSpec as P

STEPS = 2
AXES = ("ka", "band")
BF, F32 = jnp.bfloat16, jnp.float32
LANES = 128
HALF = 64
ROWS = 8
MIB = 1 << 20

VMEM = pl.BlockSpec(memory_space=pltpu.VMEM)
SMEM = pl.BlockSpec(memory_space=pltpu.SMEM)
ANY = pl.BlockSpec(memory_space=pl.ANY)


def gather_all(block, devices):
    wide = jnp.broadcast_to(block[None], (devices,) + block.shape)
    return exchange_all(wide)


def exchange_all(parts):
    return lax.all_to_all(parts, AXES, split_axis=0, concat_axis=0, tiled=True)


def dot_nt(lhs, rhs):
    return lax.dot_general(lhs, rhs, (((1,), (1,)), ((), ())), preferred_element_type=F32)


def dot_tn(lhs, rhs):
    return lax.dot_general(lhs, rhs, (((0,), (0,)), ((), ())), preferred_element_type=F32)


def lane_half(tile, have, want):
    if have != want:
        tile = pltpu.roll(tile, HALF, axis=1)
    lane = lax.broadcasted_iota(jnp.int32, tile.shape, 1)
    keep = lane < HALF if want == 0 else lane >= HALF
    return jnp.where(keep, tile, 0.0)


def with_sums(block, sums):
    row = lax.broadcasted_iota(jnp.int32, block.shape, 0)
    lane = lax.broadcasted_iota(jnp.int32, block.shape, 1)
    free = row == block.shape[0] - ROWS
    for i, total in enumerate(sums):
        rest = jnp.full(block.shape, total, F32)
        for part in range(3):
            piece = rest.astype(BF).astype(F32)
            block = jnp.where(free & (lane == HALF + 3 * i + part), piece, block)
            rest = rest - piece
    return block


def read_sums(msgs_ref, count):
    rows = msgs_ref.shape[1]
    tile = jnp.sum(msgs_ref[...].astype(F32), axis=0)[rows - ROWS :, :]
    row = lax.broadcasted_iota(jnp.int32, tile.shape, 0)
    lane = lax.broadcasted_iota(jnp.int32, tile.shape, 1)
    out = []
    for i in range(count):
        mine = (row == 0) & (lane >= HALF + 3 * i) & (lane < HALF + 3 * i + 3)
        out.append(jnp.sum(jnp.where(mine, tile, 0.0), keepdims=True))
    return out


def piece_copies(refs, parts, column, width, dest, sems):
    copies = []
    for d, piece in enumerate(parts):
        row = 0
        for ref, start, rows in piece:
            copies.append(
                pltpu.make_async_copy(
                    refs[ref].at[pl.ds(start, rows), pl.ds(column, width)],
                    dest.at[d, pl.ds(row, rows), :],
                    sems.at[len(copies)],
                )
            )
            row += rows
    return copies


def start_all(copies):
    for copy in copies:
        copy.start()


def wait_all(copies):
    for copy in copies:
        copy.wait()


def device_at(n_band, j, d):
    ka = jnp.bitwise_xor(lax.axis_index("ka"), j)
    return ka * n_band + jnp.bitwise_xor(lax.axis_index("band"), d)


def own_copies(ref, dest, sems):
    return [
        pltpu.make_async_copy(
            ref.at[jnp.bitwise_xor(lax.axis_index("ka"), j)], dest.at[j], sems.at[j]
        )
        for j in range(dest.shape[0])
    ]


def pair_rows(ref, kp):
    part = ref[:, kp * 2 * ROWS : (kp + 1) * 2 * ROWS, :]
    return part.reshape(part.shape[0] * 2 * ROWS, part.shape[2])


def pack_kernel(n_ka, nu, *refs):
    start_in, cond_in, val_in, val_ref = refs[:4]
    own_ref, gap_ref, outs, refs = refs[4], refs[5], refs[6 : 6 + n_ka], refs[6 + n_ka :]
    start_ref, cond_ref, energy_ref, sems, val_sems = refs
    ins = ((start_in, start_ref), (cond_in, cond_ref), (val_in, energy_ref))
    small = [pltpu.make_async_copy(ref, to, sems.at[i]) for i, (ref, to) in enumerate(ins)]
    k_dev = val_ref.shape[0]
    val_copies = []
    for j in range(n_ka):
        at = pl.multiple_of(jnp.bitwise_xor(lax.axis_index("ka"), j) * nu, nu)
        val_copies.append(
            pltpu.make_async_copy(
                val_ref.at[:, :, pl.ds(at, nu)], outs[j].at[:, :, pl.ds(0, nu)], val_sems.at[j]
            )
        )
    start_all(small + val_copies)
    wait_all(small)
    own_ref[...] = jnp.zeros_like(own_ref)
    gap_ref[...] = jnp.zeros_like(gap_ref)
    cond = jnp.concatenate([cond_ref[...], cond_ref[...]], axis=1)
    for kl in range(k_dev):
        half = kl % 2
        for v in range(ROWS):
            at = pl.ds(kl // 2 * ROWS + v, 1)
            row = start_ref[pl.ds(kl, 1), pl.ds(v // 2 * LANES, LANES)]
            own_ref[at, :] = own_ref[at, :] + lane_half(row, v % 2, half)
            gap = cond[kl : kl + 1, :] - energy_ref[kl, v]
            gap_ref[at, :] = gap_ref[at, :] + lane_half(gap, half, half)
    mine = own_ref[...]
    square = mine * mine
    block = with_sums(mine, [jnp.sum(square), jnp.sum(gap_ref[...] * square)])
    for j in range(n_ka):
        for g in range(k_dev):
            head = jnp.zeros((ROWS, LANES), F32)
            if (g + 1) * ROWS <= block.shape[0]:
                head = block[g * ROWS : (g + 1) * ROWS, :]
            outs[j][g, :, nu:] = head.astype(BF)
    wait_all(val_copies)


def cut_kernel(cond_ref, out_ref, sems):
    n_ka, _, own = out_ref.shape
    k_dev, n_cond, npt = cond_ref.shape
    copies = []
    for z in range(n_ka):
        at = z * (npt // n_ka) + lax.axis_index("band") * own
        for kl in range(k_dev):
            copies.append(
                pltpu.make_async_copy(
                    cond_ref.at[kl, :, pl.ds(pl.multiple_of(at, LANES), own)],
                    out_ref.at[z, pl.ds(kl * n_cond, n_cond), :],
                    sems.at[len(copies)],
                )
            )
    start_all(copies)
    wait_all(copies)


def turn_kernel(tile, scr_ref, out_ref, scrs, turned, in_sems, out_sems):
    nu = scr_ref.shape[1]
    ins, outs = [], []
    for j in range(nu // tile):
        at = pl.ds(j * tile, tile)
        ins.append(pltpu.make_async_copy(scr_ref.at[:, at], scrs.at[:, at], in_sems.at[j]))
        outs.append(pltpu.make_async_copy(turned.at[at, :], out_ref.at[at, :], out_sems.at[j]))
    start_all(ins)
    for j in range(nu // tile):
        ins[j].wait()
        turned[j * tile : (j + 1) * tile, :] = scrs[:, j * tile : (j + 1) * tile].T
        outs[j].start()
    wait_all(outs)


def order_kernel(parts, n_ka, *refs):
    val_refs, refs = refs[:-10], refs[-10:]
    rows_out, turned_out, own_out, msgs_out, vals, heads, ordered, turned, val_sems, out_sems = refs
    own = own_out.shape[1]
    nu = ordered.shape[1]
    copies = piece_copies(val_refs, parts, 0, nu, vals, val_sems.at[0])
    head_copies = piece_copies(val_refs, parts, nu, LANES, heads, val_sems.at[1])
    start_all(copies + head_copies)
    wait_all(copies)
    n_band, group = vals.shape[0], vals.shape[0] * 2 * ROWS
    column = pl.multiple_of(lax.axis_index("band") * own, LANES)
    outs = []
    for kp in range(ordered.shape[0] // group):
        at = slice(kp * group, (kp + 1) * group)
        ordered[at, :] = pair_rows(vals, kp)
        turned[:, at] = ordered[at, :].T
        at = pl.ds(kp * group, group)
        outs += [
            pltpu.make_async_copy(ordered.at[at, :], rows_out.at[at, :], out_sems.at[0, kp]),
            pltpu.make_async_copy(turned.at[:, at], turned_out.at[:, at], out_sems.at[1, kp]),
            pltpu.make_async_copy(
                ordered.at[at, pl.ds(column, own)], own_out.at[at, :], out_sems.at[2, kp]
            ),
        ]
        start_all(outs[-3:])
    wait_all(head_copies)
    rows = msgs_out.shape[1]
    step = heads.shape[1] // n_ka
    for d in range(n_band):
        head = heads[d].astype(F32)
        for j in range(n_ka):
            msgs_out[device_at(n_band, j, d)] = head[j * step : j * step + rows, :].astype(BF)
    wait_all(outs)


def density_kernel(cfg, *refs):
    n_ka, n_band, k_dev = cfg
    k_points = n_ka * k_dev
    msgs_ref, vown_ref, cond_ref, qx_ref, rho_ref, xs, msgs, vown, conds, sems = refs
    own = vown_ref.shape[1]
    msg_copy = pltpu.make_async_copy(msgs_ref, msgs, sems.at[n_ka])
    copies = own_copies(cond_ref, conds, sems)
    copies.append(pltpu.make_async_copy(vown_ref, vown, sems.at[n_ka + 1]))
    start_all([msg_copy] + copies)
    xs[...] = jnp.zeros_like(xs)
    msg_copy.wait()
    for d in range(n_band):
        for k in range(k_points):
            j, kl = divmod(k, k_dev)
            tile = msgs[device_at(n_band, j, d), :, :].astype(F32)
            tile = tile[kl // 2 * ROWS : (kl // 2 + 1) * ROWS, :]
            base = k // 2 % 2 * LANES
            at = pl.ds(base + d * 2 * ROWS + k % 2 * ROWS, ROWS)
            xs[k // 4, at, pl.ds(base, LANES)] = lane_half(tile, kl % 2, k % 2)
    qx_ref[...] = xs[...].astype(BF)
    wait_all(copies)
    cond_rows = conds[...].reshape(-1, own)
    rho = jnp.zeros((1, own), F32)
    quad = 2 * LANES
    for kq in range(k_points // 4):
        at = slice(kq * quad, (kq + 1) * quad)
        mixed = dot_tn(qx_ref[kq], vown[at, :])
        rho = rho + jnp.sum(mixed * cond_rows[at, :].astype(F32), axis=0, keepdims=True)
    for r in range(own // LANES):
        part = rho[:, r * LANES : (r + 1) * LANES]
        rho_ref[:, r, :] = jnp.broadcast_to(part, (rho_ref.shape[0], LANES))


def direct_kernel(n_ka, tile, scale, *refs):
    turned_ref, scr_ref, rows_ref, qx_ref, refs = refs[0], refs[1], refs[2], refs[3], refs[4:]
    cond_refs, refs = refs[:n_ka], refs[n_ka:]
    di_ref, qx, turned, conds, scrs, vals, mixed, kern, folded = refs[:9]
    qx_sem, cond_sems, row_sem, chunk_sems = refs[9:]
    nu, mu = scr_ref.shape
    quad = 2 * LANES
    qx_copy = pltpu.make_async_copy(qx_ref, qx, qx_sem.at[0])
    cond_copies = [
        pltpu.make_async_copy(ref, conds.at[j], cond_sems.at[j]) for j, ref in enumerate(cond_refs)
    ]
    turned_copies, scr_copies = [], []
    for i in range(nu // tile):
        at = pl.ds(i * tile, tile)
        turned_copies.append(
            pltpu.make_async_copy(turned_ref.at[at, :], turned.at[at, :], chunk_sems.at[0, i])
        )
        scr_copies.append(
            pltpu.make_async_copy(scr_ref.at[at, :], scrs.at[at, :], chunk_sems.at[1, i])
        )
    row_copy = pltpu.make_async_copy(rows_ref, vals, row_sem.at[0])
    start_all([qx_copy, turned_copies[0]] + cond_copies + [scr_copies[0]])
    for i in range(1, nu // tile):
        start_all([turned_copies[i], scr_copies[i]])
    row_copy.start()
    qx_copy.wait()
    for i in range(nu // tile):
        rows = slice(i * tile, (i + 1) * tile)
        turned_copies[i].wait()
        for kq in range(qx.shape[0]):
            cols = slice(kq * quad, (kq + 1) * quad)
            mixed[rows, cols] = jnp.dot(
                turned[rows, cols], qx[kq], preferred_element_type=F32
            ).astype(BF)
        if i == 0:
            wait_all(cond_copies)
            cond_rows = conds[...].reshape(-1, mu)
        scr_copies[i].wait()
        amp = jnp.dot(mixed[rows, :], cond_rows, preferred_element_type=F32)
        kern[rows, :] = (scrs[rows, :].astype(F32) * amp).astype(BF)
    row_copy.wait()
    folded[...] = jnp.dot(vals[...], kern[...], preferred_element_type=F32).astype(BF)
    for kq in range(qx.shape[0]):
        at = slice(kq * quad, (kq + 1) * quad)
        both = scale * dot_nt(folded[at, :], cond_rows[at, :])
        di_ref[2 * kq] = both[:LANES, :LANES]
        di_ref[2 * kq + 1] = both[LANES:, LANES:]


def exchange_kernel(cfg, chunk, scale, *refs):
    n_ka, n_band, k_dev = cfg
    k_points = n_ka * k_dev
    rho_ref, di_ref, coul_ref, vown_ref, cond_ref, msg_ref = refs[:6]
    rhos, di, coul, conds, vown, part, msg, coul_sems, sems = refs[6:]
    rho_copy = pltpu.make_async_copy(rho_ref, rhos, sems.at[n_ka])
    own, npt = coul_ref.shape
    coul_copies = [
        pltpu.make_async_copy(
            coul_ref.at[:, pl.ds(i * chunk, chunk)], coul.at[:, pl.ds(i * chunk, chunk)], coul_sems.at[i]
        )
        for i in range(npt // chunk)
    ]
    copies = own_copies(cond_ref, conds, sems)
    copies.append(pltpu.make_async_copy(vown_ref, vown, sems.at[n_ka + 1]))
    copies.append(pltpu.make_async_copy(di_ref, di, sems.at[n_ka + 2]))
    start_all([rho_copy] + coul_copies + copies)
    rho_copy.wait()
    acc = jnp.zeros((own, LANES), F32)
    per_dev = own // LANES
    for i in range(npt // chunk):
        coul_copies[i].wait()
        for j in range(i * chunk // LANES, (i + 1) * chunk // LANES):
            rho = rhos[j // per_dev, pl.ds(j % per_dev, 1), :].astype(BF).astype(F32)
            acc = acc + coul[:, j * LANES : (j + 1) * LANES].astype(F32) * rho
    potential = scale * jnp.sum(acc.T, axis=0, keepdims=True)
    wait_all(copies)
    cond_rows = conds[...].reshape(-1, own)
    for kp in range(k_points // 2):
        at = slice(kp * LANES, (kp + 1) * LANES)
        weighted = (vown[at, :].astype(F32) * potential).astype(BF)
        part[kp] = 2.0 * dot_nt(weighted, cond_rows[at, :]) - di[kp]
    for d in range(n_band):
        for j in range(n_ka):
            for g in range((k_dev + 1) // 2):
                tile = None
                for kl in range(2 * g, min(2 * g + 2, k_dev)):
                    k = j * k_dev + kl
                    piece = part[k // 2, pl.ds(d * 2 * ROWS + k % 2 * ROWS, ROWS), :]
                    piece = lane_half(piece, k % 2, kl % 2)
                    tile = piece if tile is None else tile + piece
                msg[device_at(n_band, j, d), pl.ds(g * ROWS, ROWS), :] = tile
    msg_ref[...] = msg[...].astype(BF)


def write_rows(ref, values):
    for i, value in enumerate(values):
        ref[i : i + 1, :] = jnp.broadcast_to(value, (1, ref.shape[1]))


def received(recv_ref):
    return jnp.sum(recv_ref[...].astype(F32), axis=0)


def shifted(count_all, shift, square, cross_sum, square_sum):
    alpha = shift * square + cross_sum / count_all
    d = alpha - shift
    mean_sq = (square_sum - 2.0 * d * cross_sum) / count_all + d * d * square
    mean_sq = jnp.maximum(mean_sq, 0.0)
    return alpha, d, mean_sq


def first_owner_kernel(count_all, recv_ref, msgs_ref, gap_ref, own_ref, state_ref, coef_ref, msg_ref):
    start_sq, gap_sq = read_sums(msgs_ref, 2)
    norm = start_sq / count_all
    inv = 1.0 / jnp.sqrt(norm + 1e-06)
    square = norm / (norm + 1e-06)
    shift = gap_sq / jnp.maximum(start_sq, 1e-30)
    cur = own_ref[...] * inv
    inter = received(recv_ref) * inv
    gap = gap_ref[...]
    resid = (gap - shift) * cur + inter
    state_ref[0] = cur
    state_ref[1] = resid
    state_ref[2] = inter
    write_rows(coef_ref, (shift, square, gap_sq * inv * inv))
    sums = [
        jnp.sum(cur * resid),
        jnp.sum(resid * resid),
        jnp.sum(gap * resid * resid),
        jnp.sum(gap * resid * cur),
    ]
    msg_ref[...] = jnp.broadcast_to(with_sums(resid, sums).astype(BF)[None], msg_ref.shape)


def second_owner_kernel(count_all, recv_ref, msgs_ref, gap_ref, state_ref, coef_ref, out_ref, coef_out, msg_ref):
    cross, total, gap_rr, gap_rq = read_sums(msgs_ref, 4)
    alpha, d, mean_sq = shifted(count_all, coef_ref[0:1, 0:1], coef_ref[1:2, 0:1], cross, total)
    beta = jnp.sqrt(mean_sq + 1e-06)
    square = mean_sq / (mean_sq + 1e-06)
    gap_qq = gap_rr - 2.0 * d * gap_rq + d * d * coef_ref[2:3, 0:1]
    shift = gap_qq / (mean_sq + 1e-06) / count_all
    prev = state_ref[0]
    cur = (state_ref[1] - d * prev) / beta
    inter = (received(recv_ref) - d * state_ref[2]) / beta
    resid = (gap_ref[...] - shift) * cur + inter - beta * prev
    out_ref[0] = cur
    out_ref[1] = resid
    write_rows(coef_out, (alpha, beta, shift, square))
    dims = msg_ref.shape[:1] + msg_ref.shape[2:]
    msg_ref[:, 0, :] = jnp.full(dims, jnp.sum(cur * resid), F32)
    msg_ref[:, 1, :] = jnp.full(dims, jnp.sum(resid * resid), F32)


def finish_kernel(count_all, msgs_ref, state_ref, coef_ref, out_ref, coeffs_ref):
    sums = jnp.sum(msgs_ref[...], axis=0)
    alpha, d, mean_sq = shifted(count_all, coef_ref[2:3, 0:1], coef_ref[3:4, 0:1], sums[0:1, 0:1], sums[1:2, 0:1])
    beta = jnp.sqrt(mean_sq + 1e-06)
    own = (state_ref[1] - d * state_ref[0]) / beta
    coeffs_ref[0] = coef_ref[0, 0]
    coeffs_ref[1] = alpha[0, 0]
    coeffs_ref[2] = coef_ref[1, 0]
    coeffs_ref[3] = beta[0, 0]
    for kl in range(out_ref.shape[0]):
        tile = own[kl // 2 * ROWS : (kl // 2 + 1) * ROWS, :]
        other = pltpu.roll(tile, HALF, axis=1)
        left, right = (tile, other) if kl % 2 == 0 else (other, tile)
        low = lax.broadcasted_iota(jnp.int32, (1, LANES), 1) < HALF
        for j in range(ROWS // 2):
            row = jnp.where(low, left[2 * j : 2 * j + 1], right[2 * j + 1 : 2 * j + 2])
            out_ref[pl.ds(kl, 1), pl.ds(j * LANES, LANES)] = row


def shape_of(dims, kind=F32):
    return jax.ShapeDtypeStruct(dims, kind)


def call(kernel, name, out_shape, in_specs, out_specs, scratch=(), mib=58, flops=0, moved=0):
    return pl.pallas_call(
        kernel,
        out_shape=out_shape,
        in_specs=in_specs,
        out_specs=out_specs,
        scratch_shapes=list(scratch),
        compiler_params=pltpu.CompilerParams(vmem_limit_bytes=mib * MIB),
        cost_estimate=pl.CostEstimate(flops=flops, bytes_accessed=moved, transcendentals=0),
        name=name,
    )


def dma(*dims):
    return pltpu.SemaphoreType.DMA(dims)


def swap(block, axis, d):
    return lax.ppermute(block, axis, [(i, i ^ d) for i in range(lax.axis_size(axis))])


def plane_pieces(own_piece, others):
    def move(block, d):
        return swap(block, "band", d)

    rows = own_piece.shape[0]
    half = rows // 2
    by_x, by_y, core = move(own_piece, 2), move(own_piece, 4), move(own_piece, 1)
    by_x, by_y, others = lax.optimization_barrier((by_x, by_y, others))
    diag = [move(by_x[:half], 4), move(by_y[half:], 2)]
    near_x, near_y = move(by_x, 1), move(by_y, 1)
    far = [move(part, 1) for part in diag]
    arrays = [own_piece, core, by_x, near_x, by_y, near_y] + diag + far
    parts = tuple(((i, 0, rows),) for i in range(6))
    parts += (((6, 0, half), (7, 0, half)), ((8, 0, half), (9, 0, half)))
    return arrays, parts, others


def kernel_path(start_vec, val_energy, cond_energy, val_orb, cond_orb, coulomb, screened):
    n_ka = lax.axis_size("ka")
    n_band = lax.axis_size("band")
    devices = n_ka * n_band
    ka, band = lax.axis_index("ka"), lax.axis_index("band")
    k_dev = start_vec.shape[0]
    nv_blk = val_orb.shape[1]
    n_cond = cond_orb.shape[1]
    npt_all = cond_orb.shape[2]
    k_points = k_dev * n_ka
    pairs = k_points // 2
    mu_blk, nu_blk = screened.shape
    own = coulomb.shape[0]
    count_all = k_points * nv_blk * n_band * n_cond
    scale = 1.0 / (npt_all * math.sqrt(count_all))
    piece_rows = k_points * nv_blk

    block = ((k_dev + 1) // 2 * ROWS, LANES)
    msg_shape = shape_of((devices,) + block, BF)
    wide = nu_blk + LANES
    start_own, gap, *payloads = call(
        functools.partial(pack_kernel, n_ka, nu_blk),
        "pack",
        (shape_of(block), shape_of(block)) + (shape_of((k_dev, nv_blk, wide), BF),) * n_ka,
        [ANY] * 4,
        (VMEM,) * (2 + n_ka),
        [
            pltpu.VMEM(start_vec.shape, F32),
            pltpu.VMEM(cond_energy.shape, F32),
            pltpu.SMEM(val_energy.shape, F32),
            dma(3),
            dma(n_ka),
        ],
    )(start_vec, cond_energy, val_energy, val_orb)
    base, payloads = lax.optimization_barrier((band * mu_blk, payloads))
    got = [payloads[0]] + [swap(payloads[j], "ka", j) for j in range(1, n_ka)]
    own_rows = k_dev * n_cond
    cuts = call(
        cut_kernel,
        "cut",
        shape_of((n_ka, own_rows, own), BF),
        [ANY],
        VMEM,
        [dma(n_ka * k_dev)],
    )(cond_orb)
    cond_local = lax.dynamic_slice_in_dim(cond_orb, base, mu_blk, 2)
    cond_local = cond_local.reshape(k_dev * n_cond, mu_blk)
    got, cuts, cond_local = lax.optimization_barrier((got, cuts, cond_local))
    val_cut = jnp.concatenate(got, axis=0).reshape(piece_rows, wide)
    cond_pts = [cond_local] + [swap(cond_local, "ka", j) for j in range(1, n_ka)]
    cond_own = lax.all_to_all(cuts, "ka", split_axis=0, concat_axis=0, tiled=True)

    chunk, tile = 1024, nu_blk
    rows_all, conds_all = k_points * nv_blk * n_band, k_points * n_cond
    scr_turned = call(
        functools.partial(turn_kernel, nu_blk // 4),
        "turn",
        shape_of((nu_blk, mu_blk), BF),
        [ANY],
        ANY,
        [pltpu.VMEM((mu_blk, nu_blk), BF), pltpu.VMEM((nu_blk, mu_blk), BF)]
        + [dma(4)] * 2,
        moved=8 * MIB,
    )(screened)
    pieces, parts, scr_turned = plane_pieces(val_cut, scr_turned)
    pieces, cond_pts[1:-1] = lax.optimization_barrier((pieces, cond_pts[1:-1]))
    val_rows, val_turned, val_own, msgs = call(
        functools.partial(order_kernel, parts, n_ka),
        "order",
        (
            shape_of((rows_all, nu_blk), BF),
            shape_of((nu_blk, rows_all), BF),
            shape_of((rows_all, own), BF),
            msg_shape,
        ),
        [ANY] * len(pieces),
        (ANY, ANY, ANY, VMEM),
        [
            pltpu.VMEM((n_band, piece_rows, nu_blk), BF),
            pltpu.VMEM((n_band, piece_rows, LANES), BF),
            pltpu.VMEM((rows_all, nu_blk), BF),
            pltpu.VMEM((nu_blk, rows_all), BF),
            dma(2, sum(len(piece) for piece in parts)),
            dma(3, pairs),
        ],
        moved=9 * MIB,
    )(*pieces)

    cfg = (n_ka, n_band, k_dev)
    quads = k_points // 4
    state, coef = None, None
    for step in range(STEPS):
        first = step == 0
        qx, rho = call(
            functools.partial(density_kernel, cfg),
            "density",
            (
                shape_of((quads, 2 * LANES, 2 * LANES), BF),
                shape_of((devices, own // LANES, LANES)),
            ),
            [ANY] * 3,
            (VMEM, VMEM),
            [
                pltpu.VMEM((quads, 2 * LANES, 2 * LANES), F32),
                pltpu.VMEM((devices,) + block, BF),
                pltpu.VMEM((rows_all, own), BF),
                pltpu.VMEM((n_ka, own_rows, own), BF),
                dma(n_ka + 2),
            ],
        )(msgs, val_own, cond_own)
        density = exchange_all(rho)
        direct = call(
            functools.partial(direct_kernel, n_ka, tile, scale),
            "direct",
            shape_of((pairs, LANES, LANES)),
            [ANY] * (4 + n_ka),
            VMEM,
            [
                pltpu.VMEM((quads, 2 * LANES, 2 * LANES), BF),
                pltpu.VMEM((nu_blk, rows_all), BF),
                pltpu.VMEM((n_ka, k_dev * n_cond, mu_blk), BF),
                pltpu.VMEM((nu_blk, mu_blk), BF),
                pltpu.VMEM((rows_all, nu_blk), BF),
                pltpu.VMEM((nu_blk, conds_all), BF),
                pltpu.VMEM((nu_blk, mu_blk), BF),
                pltpu.VMEM((rows_all, mu_blk), BF),
                dma(1),
                dma(n_ka),
                dma(1),
                dma(2, nu_blk // tile),
            ],
            flops=4 * mu_blk * nu_blk * conds_all,
            moved=12 * MIB,
        )(val_turned, scr_turned, val_rows, qx, *cond_pts)
        summed = call(
            functools.partial(exchange_kernel, cfg, chunk, scale),
            "exchange",
            msg_shape,
            [ANY] * 5,
            VMEM,
            [
                pltpu.VMEM((devices, own // LANES, LANES), F32),
                pltpu.VMEM((pairs, LANES, LANES), F32),
                pltpu.VMEM((own, npt_all), BF),
                pltpu.VMEM((n_ka, own_rows, own), BF),
                pltpu.VMEM((rows_all, own), BF),
                pltpu.VMEM((pairs, LANES, LANES), F32),
                pltpu.VMEM((devices,) + block, F32),
                dma(npt_all // chunk),
                dma(n_ka + 3),
            ],
        )(density, direct, coulomb, val_own, cond_own)
        recv = exchange_all(summed)
        if first:
            state, coef, message = call(
                functools.partial(first_owner_kernel, count_all),
                "first_owner",
                (shape_of((3,) + block), shape_of((ROWS, LANES)), msg_shape),
                [VMEM] * 4,
                (VMEM, VMEM, VMEM),
                mib=8,
            )(recv, msgs, gap, start_own)
        else:
            state, coef, message = call(
                functools.partial(second_owner_kernel, count_all),
                "second_owner",
                (shape_of((2,) + block), shape_of((ROWS, LANES)), shape_of((devices, 2, LANES))),
                [VMEM] * 5,
                (VMEM, VMEM, VMEM),
                mib=8,
            )(recv, msgs, gap, state, coef)
        msgs = exchange_all(message)
    return call(
        functools.partial(finish_kernel, count_all),
        "finish",
        (shape_of(start_vec.shape), shape_of((2 * STEPS,))),
        [VMEM] * 3,
        (VMEM, SMEM),
        mib=8,
    )(msgs, state, coef)


def array_path(start_vec, val_energy, cond_energy, val_orb, cond_orb, coulomb, screened):
    n_ka = lax.axis_size("ka")
    n_band = lax.axis_size("band")
    devices = n_ka * n_band
    ka, band = lax.axis_index("ka"), lax.axis_index("band")
    me = ka * n_band + band
    k_dev, pair_blk = start_vec.shape
    nv_blk = val_orb.shape[1]
    n_cond = cond_orb.shape[1]
    n_val = nv_blk * n_band
    npt_all = cond_orb.shape[2]
    k_points = k_dev * n_ka
    mu_blk, nu_blk = screened.shape
    own_pts = coulomb.shape[0]
    count_all = k_points * n_val * n_cond
    kernel_scale = 1.0 / (npt_all * math.sqrt(count_all))

    start_all = gather_all(start_vec, devices)
    val_cut = lax.all_to_all(
        val_orb.reshape(k_dev, nv_blk, n_ka, nu_blk).transpose(2, 0, 1, 3),
        "ka", split_axis=0, concat_axis=0, tiled=True,
    ).reshape(k_points, nv_blk, nu_blk)
    val_pts = lax.all_gather(val_cut, "band", axis=1, tiled=True)
    cond_local = lax.dynamic_slice_in_dim(cond_orb, band * mu_blk, mu_blk, 2)
    cond_pts = lax.all_gather(cond_local, "ka", axis=0, tiled=True)
    cond_rows = cond_orb.reshape(k_dev, n_cond, n_ka, n_band, own_pts)
    cond_rows = lax.dynamic_index_in_dim(cond_rows, band, 3, keepdims=False)
    cond_own = lax.all_to_all(
        cond_rows.transpose(2, 0, 1, 3), "ka", split_axis=0, concat_axis=0, tiled=True
    ).reshape(k_points, n_cond, own_pts)
    val_own = lax.dynamic_slice_in_dim(val_pts, band * own_pts, own_pts, 2)

    energy_gap = (cond_energy[:, None, :] - val_energy[:, :, None]).reshape(k_dev, pair_blk)
    start_sq = jnp.sum(start_all * start_all)
    current = start_all / jnp.sqrt(start_sq / count_all + 1e-06)
    previous = jnp.zeros_like(current)
    beta_val = jnp.float32(0.0)
    alphas = []
    betas = []
    for turn_index in range(STEPS):
        full_vec = (
            current.astype(BF)
            .reshape(n_ka, n_band, k_dev, nv_blk, n_cond)
            .transpose(0, 2, 1, 3, 4)
            .reshape(k_points, n_val, n_cond)
        )
        mixed_f = jnp.einsum("kvc,kvn->kcn", full_vec, val_pts, preferred_element_type=F32)
        mixed_own = lax.dynamic_slice_in_dim(mixed_f, band * own_pts, own_pts, 2)
        density_own = jnp.sum(mixed_own * cond_own.astype(F32), axis=(0, 1))
        density = gather_all(density_own.astype(BF), devices).reshape(npt_all)
        mixed_val = mixed_f.astype(BF)
        amp = jnp.einsum("kcm,kcn->mn", cond_pts, mixed_val, preferred_element_type=F32)
        kern = (screened.astype(F32) * amp * kernel_scale).astype(BF)
        folded = jnp.einsum("mn,kvn->kvm", kern, val_pts, preferred_element_type=F32).astype(BF)
        direct_part = jnp.einsum("kcm,kvm->kvc", cond_pts, folded, preferred_element_type=F32)
        potential = kernel_scale * jnp.dot(coulomb, density, preferred_element_type=F32)
        weighted = (val_own.astype(F32) * potential).astype(BF)
        exchange = jnp.einsum("kvp,kcp->kvc", weighted, cond_own, preferred_element_type=F32)
        part = 2.0 * exchange - direct_part
        arranged = (
            part.reshape(n_ka, k_dev, n_band, nv_blk, n_cond)
            .transpose(0, 2, 1, 3, 4)
            .reshape(devices, k_dev, pair_blk)
        )
        inter_own = jnp.sum(exchange_all(arranged), axis=0)
        current_own = lax.dynamic_index_in_dim(current, me, 0, keepdims=False)
        resid_vec = gather_all(energy_gap * current_own + inter_own, devices)
        resid_vec = resid_vec - beta_val * previous
        alpha_val = jnp.sum(current * resid_vec) / count_all
        resid_vec = resid_vec - alpha_val * current
        beta_val = jnp.sqrt(jnp.sum(resid_vec * resid_vec) / count_all + 1e-06)
        previous = current
        current = resid_vec / beta_val
        alphas.append(alpha_val)
        betas.append(beta_val)
    coeffs = jnp.stack(alphas + betas)
    return (lax.dynamic_index_in_dim(current, me, 0, keepdims=False), coeffs)


def per_device(*args):
    start_vec, _, _, val_orb, cond_orb, coulomb, screened = args
    n_ka, n_band = lax.axis_size("ka"), lax.axis_size("band")
    fits = (
        n_band == 8
        and n_ka & (n_ka - 1) == 0
        and start_vec.shape[0] % 2 == 1
        and val_orb.shape[1] == ROWS
        and cond_orb.shape[1] == HALF
        and start_vec.shape[0] * n_ka % 4 == 0
        and coulomb.shape[0] % LANES == 0
        and coulomb.shape[1] % 1024 == 0
        and screened.shape[0] % 512 == 0
        and screened.shape[1] % 1024 == 0
        and screened.shape[0] * screened.shape[1] <= 2 * MIB
    )
    return (kernel_path if fits else array_path)(*args)


def solution(mesh):
    in_specs = (
        P("ka", "band"),
        P("ka", "band"),
        P("ka", None),
        P("ka", "band", None),
        P("ka", None, None),
        P(("ka", "band"), None),
        P("band", "ka"),
    )
    out_specs = (P("ka", "band"), P())
    return jax.shard_map(
        per_device, mesh=mesh, in_specs=in_specs, out_specs=out_specs, check_vma=False
    )
```

```python
import functools
import math

import jax
import jax.numpy as jnp
from jax import lax
from jax.experimental import pallas as pl
from jax.experimental.pallas import tpu as pltpu
from jax.sharding import PartitionSpec as P

STEPS = 2
AXES = ("ka", "band")
BF, F32 = jnp.bfloat16, jnp.float32
LANES = 128
HALF = 64
ROWS = 8
MIB = 1 << 20

VMEM = pl.BlockSpec(memory_space=pltpu.VMEM)
SMEM = pl.BlockSpec(memory_space=pltpu.SMEM)
ANY = pl.BlockSpec(memory_space=pl.ANY)


def gather_all(block, devices):
    wide = jnp.broadcast_to(block[None], (devices,) + block.shape)
    return exchange_all(wide)


def exchange_all(parts):
    return lax.all_to_all(parts, AXES, split_axis=0, concat_axis=0, tiled=True)


def dot_nt(lhs, rhs):
    return lax.dot_general(lhs, rhs, (((1,), (1,)), ((), ())), preferred_element_type=F32)


def dot_tn(lhs, rhs):
    return lax.dot_general(lhs, rhs, (((0,), (0,)), ((), ())), preferred_element_type=F32)


def lane_half(tile, have, want):
    if have != want:
        tile = pltpu.roll(tile, HALF, axis=1)
    lane = lax.broadcasted_iota(jnp.int32, tile.shape, 1)
    keep = lane < HALF if want == 0 else lane >= HALF
    return jnp.where(keep, tile, 0.0)


def with_sums(block, sums):
    row = lax.broadcasted_iota(jnp.int32, block.shape, 0)
    lane = lax.broadcasted_iota(jnp.int32, block.shape, 1)
    free = row == block.shape[0] - ROWS
    for i, total in enumerate(sums):
        rest = jnp.full(block.shape, total, F32)
        for part in range(3):
            piece = rest.astype(BF).astype(F32)
            block = jnp.where(free & (lane == HALF + 3 * i + part), piece, block)
            rest = rest - piece
    return block


def read_sums(msgs_ref, count):
    rows = msgs_ref.shape[1]
    tile = jnp.sum(msgs_ref[...].astype(F32), axis=0)[rows - ROWS :, :]
    row = lax.broadcasted_iota(jnp.int32, tile.shape, 0)
    lane = lax.broadcasted_iota(jnp.int32, tile.shape, 1)
    out = []
    for i in range(count):
        mine = (row == 0) & (lane >= HALF + 3 * i) & (lane < HALF + 3 * i + 3)
        out.append(jnp.sum(jnp.where(mine, tile, 0.0), keepdims=True))
    return out


def piece_copies(refs, parts, column, width, dest, sems):
    copies = []
    for d, piece in enumerate(parts):
        row = 0
        for ref, start, rows in piece:
            copies.append(
                pltpu.make_async_copy(
                    refs[ref].at[pl.ds(start, rows), pl.ds(column, width)],
                    dest.at[d, pl.ds(row, rows), :],
                    sems.at[len(copies)],
                )
            )
            row += rows
    return copies


def start_all(copies):
    for copy in copies:
        copy.start()


def wait_all(copies):
    for copy in copies:
        copy.wait()


def device_at(n_band, j, d):
    ka = jnp.bitwise_xor(lax.axis_index("ka"), j)
    return ka * n_band + jnp.bitwise_xor(lax.axis_index("band"), d)


def own_copies(ref, dest, sems):
    return [
        pltpu.make_async_copy(
            ref.at[jnp.bitwise_xor(lax.axis_index("ka"), j)], dest.at[j], sems.at[j]
        )
        for j in range(dest.shape[0])
    ]


def pair_rows(ref, kp):
    part = ref[:, kp * 2 * ROWS : (kp + 1) * 2 * ROWS, :]
    return part.reshape(part.shape[0] * 2 * ROWS, part.shape[2])


def pack_kernel(n_ka, nu, *refs):
    start_in, cond_in, val_in, val_ref = refs[:4]
    own_ref, gap_ref, outs, refs = refs[4], refs[5], refs[6 : 6 + n_ka], refs[6 + n_ka :]
    start_ref, cond_ref, energy_ref, sems, val_sems = refs
    ins = ((start_in, start_ref), (cond_in, cond_ref), (val_in, energy_ref))
    small = [pltpu.make_async_copy(ref, to, sems.at[i]) for i, (ref, to) in enumerate(ins)]
    k_dev = val_ref.shape[0]
    val_copies = []
    for j in range(n_ka):
        at = pl.multiple_of(jnp.bitwise_xor(lax.axis_index("ka"), j) * nu, nu)
        val_copies.append(
            pltpu.make_async_copy(
                val_ref.at[:, :, pl.ds(at, nu)], outs[j].at[:, :, pl.ds(0, nu)], val_sems.at[j]
            )
        )
    start_all(small + val_copies)
    wait_all(small)
    own_ref[...] = jnp.zeros_like(own_ref)
    gap_ref[...] = jnp.zeros_like(gap_ref)
    cond = jnp.concatenate([cond_ref[...], cond_ref[...]], axis=1)
    for kl in range(k_dev):
        half = kl % 2
        for v in range(ROWS):
            at = pl.ds(kl // 2 * ROWS + v, 1)
            row = start_ref[pl.ds(kl, 1), pl.ds(v // 2 * LANES, LANES)]
            own_ref[at, :] = own_ref[at, :] + lane_half(row, v % 2, half)
            gap = cond[kl : kl + 1, :] - energy_ref[kl, v]
            gap_ref[at, :] = gap_ref[at, :] + lane_half(gap, half, half)
    mine = own_ref[...]
    square = mine * mine
    block = with_sums(mine, [jnp.sum(square), jnp.sum(gap_ref[...] * square)])
    for j in range(n_ka):
        for g in range(k_dev):
            head = jnp.zeros((ROWS, LANES), F32)
            if (g + 1) * ROWS <= block.shape[0]:
                head = block[g * ROWS : (g + 1) * ROWS, :]
            outs[j][g, :, nu:] = head.astype(BF)
    wait_all(val_copies)


def cut_kernel(cond_ref, out_ref, sems):
    n_ka, _, own = out_ref.shape
    k_dev, n_cond, npt = cond_ref.shape
    copies = []
    for z in range(n_ka):
        at = z * (npt // n_ka) + lax.axis_index("band") * own
        for kl in range(k_dev):
            copies.append(
                pltpu.make_async_copy(
                    cond_ref.at[kl, :, pl.ds(pl.multiple_of(at, LANES), own)],
                    out_ref.at[z, pl.ds(kl * n_cond, n_cond), :],
                    sems.at[len(copies)],
                )
            )
    start_all(copies)
    wait_all(copies)


def turn_kernel(tile, scr_ref, out_ref, scrs, turned, in_sems, out_sems):
    nu = scr_ref.shape[1]
    ins, outs = [], []
    for j in range(nu // tile):
        at = pl.ds(j * tile, tile)
        ins.append(pltpu.make_async_copy(scr_ref.at[:, at], scrs.at[:, at], in_sems.at[j]))
        outs.append(pltpu.make_async_copy(turned.at[at, :], out_ref.at[at, :], out_sems.at[j]))
    start_all(ins)
    for j in range(nu // tile):
        ins[j].wait()
        turned[j * tile : (j + 1) * tile, :] = scrs[:, j * tile : (j + 1) * tile].T
        outs[j].start()
    wait_all(outs)


def order_kernel(parts, n_ka, *refs):
    val_refs, refs = refs[:-10], refs[-10:]
    rows_out, turned_out, own_out, msgs_out, vals, heads, ordered, turned, val_sems, out_sems = refs
    own = own_out.shape[1]
    nu = ordered.shape[1]
    copies = piece_copies(val_refs, parts, 0, nu, vals, val_sems.at[0])
    head_copies = piece_copies(val_refs, parts, nu, LANES, heads, val_sems.at[1])
    start_all(copies + head_copies)
    wait_all(copies)
    n_band, group = vals.shape[0], vals.shape[0] * 2 * ROWS
    column = pl.multiple_of(lax.axis_index("band") * own, LANES)
    outs = []
    for kp in range(ordered.shape[0] // group):
        at = slice(kp * group, (kp + 1) * group)
        ordered[at, :] = pair_rows(vals, kp)
        turned[:, at] = ordered[at, :].T
        at = pl.ds(kp * group, group)
        outs += [
            pltpu.make_async_copy(ordered.at[at, :], rows_out.at[at, :], out_sems.at[0, kp]),
            pltpu.make_async_copy(turned.at[:, at], turned_out.at[:, at], out_sems.at[1, kp]),
            pltpu.make_async_copy(
                ordered.at[at, pl.ds(column, own)], own_out.at[at, :], out_sems.at[2, kp]
            ),
        ]
        start_all(outs[-3:])
    wait_all(head_copies)
    rows = msgs_out.shape[1]
    step = heads.shape[1] // n_ka
    for d in range(n_band):
        head = heads[d].astype(F32)
        for j in range(n_ka):
            msgs_out[device_at(n_band, j, d)] = head[j * step : j * step + rows, :].astype(BF)
    wait_all(outs)


def density_kernel(cfg, *refs):
    n_ka, n_band, k_dev = cfg
    k_points = n_ka * k_dev
    msgs_ref, vown_ref, cond_ref, qx_ref, rho_ref, xs, msgs, vown, conds, sems = refs
    own = vown_ref.shape[1]
    msg_copy = pltpu.make_async_copy(msgs_ref, msgs, sems.at[n_ka])
    copies = own_copies(cond_ref, conds, sems)
    copies.append(pltpu.make_async_copy(vown_ref, vown, sems.at[n_ka + 1]))
    start_all([msg_copy] + copies)
    xs[...] = jnp.zeros_like(xs)
    msg_copy.wait()
    for d in range(n_band):
        for k in range(k_points):
            j, kl = divmod(k, k_dev)
            tile = msgs[device_at(n_band, j, d), :, :].astype(F32)
            tile = tile[kl // 2 * ROWS : (kl // 2 + 1) * ROWS, :]
            base = k // 2 % 2 * LANES
            at = pl.ds(base + d * 2 * ROWS + k % 2 * ROWS, ROWS)
            xs[k // 4, at, pl.ds(base, LANES)] = lane_half(tile, kl % 2, k % 2)
    qx_ref[...] = xs[...].astype(BF)
    wait_all(copies)
    cond_rows = conds[...].reshape(-1, own)
    rho = jnp.zeros((1, own), F32)
    quad = 2 * LANES
    for kq in range(k_points // 4):
        at = slice(kq * quad, (kq + 1) * quad)
        mixed = dot_tn(qx_ref[kq], vown[at, :])
        rho = rho + jnp.sum(mixed * cond_rows[at, :].astype(F32), axis=0, keepdims=True)
    for r in range(own // LANES):
        part = rho[:, r * LANES : (r + 1) * LANES]
        rho_ref[:, r, :] = jnp.broadcast_to(part, (rho_ref.shape[0], LANES))


def direct_kernel(n_ka, tile, scale, *refs):
    turned_ref, scr_ref, rows_ref, qx_ref, refs = refs[0], refs[1], refs[2], refs[3], refs[4:]
    cond_refs, refs = refs[:n_ka], refs[n_ka:]
    di_ref, qx, turned, conds, scrs, vals, mixed, kern, folded = refs[:9]
    qx_sem, cond_sems, row_sem, chunk_sems = refs[9:]
    nu, mu = scr_ref.shape
    quad = 2 * LANES
    qx_copy = pltpu.make_async_copy(qx_ref, qx, qx_sem.at[0])
    cond_copies = [
        pltpu.make_async_copy(ref, conds.at[j], cond_sems.at[j]) for j, ref in enumerate(cond_refs)
    ]
    turned_copies, scr_copies = [], []
    for i in range(nu // tile):
        at = pl.ds(i * tile, tile)
        turned_copies.append(
            pltpu.make_async_copy(turned_ref.at[at, :], turned.at[at, :], chunk_sems.at[0, i])
        )
        scr_copies.append(
            pltpu.make_async_copy(scr_ref.at[at, :], scrs.at[at, :], chunk_sems.at[1, i])
        )
    row_copy = pltpu.make_async_copy(rows_ref, vals, row_sem.at[0])
    start_all([qx_copy, turned_copies[0]] + cond_copies + [scr_copies[0]])
    for i in range(1, nu // tile):
        start_all([turned_copies[i], scr_copies[i]])
    row_copy.start()
    qx_copy.wait()
    for i in range(nu // tile):
        rows = slice(i * tile, (i + 1) * tile)
        turned_copies[i].wait()
        for kq in range(qx.shape[0]):
            cols = slice(kq * quad, (kq + 1) * quad)
            mixed[rows, cols] = jnp.dot(
                turned[rows, cols], qx[kq], preferred_element_type=F32
            ).astype(BF)
        if i == 0:
            wait_all(cond_copies)
            cond_rows = conds[...].reshape(-1, mu)
        scr_copies[i].wait()
        amp = jnp.dot(mixed[rows, :], cond_rows, preferred_element_type=F32)
        kern[rows, :] = (scrs[rows, :].astype(F32) * amp).astype(BF)
    row_copy.wait()
    folded[...] = jnp.dot(vals[...], kern[...], preferred_element_type=F32).astype(BF)
    for kq in range(qx.shape[0]):
        at = slice(kq * quad, (kq + 1) * quad)
        both = scale * dot_nt(folded[at, :], cond_rows[at, :])
        di_ref[2 * kq] = both[:LANES, :LANES]
        di_ref[2 * kq + 1] = both[LANES:, LANES:]


def exchange_kernel(cfg, chunk, scale, *refs):
    n_ka, n_band, k_dev = cfg
    k_points = n_ka * k_dev
    rho_ref, di_ref, coul_ref, vown_ref, cond_ref, msg_ref = refs[:6]
    rhos, di, coul, conds, vown, part, msg, coul_sems, sems = refs[6:]
    rho_copy = pltpu.make_async_copy(rho_ref, rhos, sems.at[n_ka])
    own, npt = coul_ref.shape
    coul_copies = [
        pltpu.make_async_copy(
            coul_ref.at[:, pl.ds(i * chunk, chunk)], coul.at[:, pl.ds(i * chunk, chunk)], coul_sems.at[i]
        )
        for i in range(npt // chunk)
    ]
    copies = own_copies(cond_ref, conds, sems)
    copies.append(pltpu.make_async_copy(vown_ref, vown, sems.at[n_ka + 1]))
    copies.append(pltpu.make_async_copy(di_ref, di, sems.at[n_ka + 2]))
    start_all([rho_copy] + coul_copies + copies)
    rho_copy.wait()
    acc = jnp.zeros((own, LANES), F32)
    per_dev = own // LANES
    for i in range(npt // chunk):
        coul_copies[i].wait()
        for j in range(i * chunk // LANES, (i + 1) * chunk // LANES):
            rho = rhos[j // per_dev, pl.ds(j % per_dev, 1), :].astype(BF).astype(F32)
            acc = acc + coul[:, j * LANES : (j + 1) * LANES].astype(F32) * rho
    potential = scale * jnp.sum(acc.T, axis=0, keepdims=True)
    wait_all(copies)
    cond_rows = conds[...].reshape(-1, own)
    for kp in range(k_points // 2):
        at = slice(kp * LANES, (kp + 1) * LANES)
        weighted = (vown[at, :].astype(F32) * potential).astype(BF)
        part[kp] = 2.0 * dot_nt(weighted, cond_rows[at, :]) - di[kp]
    for d in range(n_band):
        for j in range(n_ka):
            for g in range((k_dev + 1) // 2):
                tile = None
                for kl in range(2 * g, min(2 * g + 2, k_dev)):
                    k = j * k_dev + kl
                    piece = part[k // 2, pl.ds(d * 2 * ROWS + k % 2 * ROWS, ROWS), :]
                    piece = lane_half(piece, k % 2, kl % 2)
                    tile = piece if tile is None else tile + piece
                msg[device_at(n_band, j, d), pl.ds(g * ROWS, ROWS), :] = tile
    msg_ref[...] = msg[...].astype(BF)


def write_rows(ref, values):
    for i, value in enumerate(values):
        ref[i : i + 1, :] = jnp.broadcast_to(value, (1, ref.shape[1]))


def received(recv_ref):
    return jnp.sum(recv_ref[...].astype(F32), axis=0)


def shifted(count_all, shift, square, cross_sum, square_sum):
    alpha = shift * square + cross_sum / count_all
    d = alpha - shift
    mean_sq = (square_sum - 2.0 * d * cross_sum) / count_all + d * d * square
    mean_sq = jnp.maximum(mean_sq, 0.0)
    return alpha, d, mean_sq


def first_owner_kernel(count_all, recv_ref, msgs_ref, gap_ref, own_ref, state_ref, coef_ref, msg_ref):
    start_sq, gap_sq = read_sums(msgs_ref, 2)
    norm = start_sq / count_all
    inv = 1.0 / jnp.sqrt(norm + 1e-06)
    square = norm / (norm + 1e-06)
    shift = gap_sq / jnp.maximum(start_sq, 1e-30)
    cur = own_ref[...] * inv
    inter = received(recv_ref) * inv
    gap = gap_ref[...]
    resid = (gap - shift) * cur + inter
    state_ref[0] = cur
    state_ref[1] = resid
    state_ref[2] = inter
    write_rows(coef_ref, (shift, square, gap_sq * inv * inv))
    sums = [
        jnp.sum(cur * resid),
        jnp.sum(resid * resid),
        jnp.sum(gap * resid * resid),
        jnp.sum(gap * resid * cur),
    ]
    msg_ref[...] = jnp.broadcast_to(with_sums(resid, sums).astype(BF)[None], msg_ref.shape)


def second_owner_kernel(count_all, recv_ref, msgs_ref, gap_ref, state_ref, coef_ref, out_ref, coef_out, msg_ref):
    cross, total, gap_rr, gap_rq = read_sums(msgs_ref, 4)
    alpha, d, mean_sq = shifted(count_all, coef_ref[0:1, 0:1], coef_ref[1:2, 0:1], cross, total)
    beta = jnp.sqrt(mean_sq + 1e-06)
    square = mean_sq / (mean_sq + 1e-06)
    gap_qq = gap_rr - 2.0 * d * gap_rq + d * d * coef_ref[2:3, 0:1]
    shift = gap_qq / (mean_sq + 1e-06) / count_all
    prev = state_ref[0]
    cur = (state_ref[1] - d * prev) / beta
    inter = (received(recv_ref) - d * state_ref[2]) / beta
    resid = (gap_ref[...] - shift) * cur + inter - beta * prev
    out_ref[0] = cur
    out_ref[1] = resid
    write_rows(coef_out, (alpha, beta, shift, square))
    dims = msg_ref.shape[:1] + msg_ref.shape[2:]
    msg_ref[:, 0, :] = jnp.full(dims, jnp.sum(cur * resid), F32)
    msg_ref[:, 1, :] = jnp.full(dims, jnp.sum(resid * resid), F32)


def finish_kernel(count_all, msgs_ref, state_ref, coef_ref, out_ref, coeffs_ref):
    sums = jnp.sum(msgs_ref[...], axis=0)
    alpha, d, mean_sq = shifted(count_all, coef_ref[2:3, 0:1], coef_ref[3:4, 0:1], sums[0:1, 0:1], sums[1:2, 0:1])
    beta = jnp.sqrt(mean_sq + 1e-06)
    own = (state_ref[1] - d * state_ref[0]) / beta
    coeffs_ref[0] = coef_ref[0, 0]
    coeffs_ref[1] = alpha[0, 0]
    coeffs_ref[2] = coef_ref[1, 0]
    coeffs_ref[3] = beta[0, 0]
    for kl in range(out_ref.shape[0]):
        tile = own[kl // 2 * ROWS : (kl // 2 + 1) * ROWS, :]
        other = pltpu.roll(tile, HALF, axis=1)
        left, right = (tile, other) if kl % 2 == 0 else (other, tile)
        low = lax.broadcasted_iota(jnp.int32, (1, LANES), 1) < HALF
        for j in range(ROWS // 2):
            row = jnp.where(low, left[2 * j : 2 * j + 1], right[2 * j + 1 : 2 * j + 2])
            out_ref[pl.ds(kl, 1), pl.ds(j * LANES, LANES)] = row


def shape_of(dims, kind=F32):
    return jax.ShapeDtypeStruct(dims, kind)


def call(kernel, name, out_shape, in_specs, out_specs, scratch=(), mib=58, flops=0, moved=0):
    return pl.pallas_call(
        kernel,
        out_shape=out_shape,
        in_specs=in_specs,
        out_specs=out_specs,
        scratch_shapes=list(scratch),
        compiler_params=pltpu.CompilerParams(vmem_limit_bytes=mib * MIB),
        cost_estimate=pl.CostEstimate(flops=flops, bytes_accessed=moved, transcendentals=0),
        name=name,
    )


def dma(*dims):
    return pltpu.SemaphoreType.DMA(dims)


def swap(block, axis, d):
    return lax.ppermute(block, axis, [(i, i ^ d) for i in range(lax.axis_size(axis))])


def plane_pieces(own_piece):
    def move(block, d):
        return swap(block, "band", d)

    rows = own_piece.shape[0]
    half = rows // 2
    by_x, by_y, core = move(own_piece, 2), move(own_piece, 4), move(own_piece, 1)
    by_x, by_y, core = lax.optimization_barrier((by_x, by_y, core))
    diag = [move(by_x[:half], 4), move(by_y[half:], 2)]
    near = move(jnp.concatenate([by_x, by_y], axis=0), 1)
    far = move(jnp.concatenate(diag, axis=0), 1)
    arrays = [own_piece, core, by_x, by_y, near] + diag + [far]
    parts = (
        ((0, 0, rows),),
        ((1, 0, rows),),
        ((2, 0, rows),),
        ((4, 0, rows),),
        ((3, 0, rows),),
        ((4, rows, rows),),
        ((5, 0, half), (6, 0, half)),
        ((7, 0, rows),),
    )
    return arrays, parts


def kernel_path(start_vec, val_energy, cond_energy, val_orb, cond_orb, coulomb, screened):
    n_ka = lax.axis_size("ka")
    n_band = lax.axis_size("band")
    devices = n_ka * n_band
    ka, band = lax.axis_index("ka"), lax.axis_index("band")
    k_dev = start_vec.shape[0]
    nv_blk = val_orb.shape[1]
    n_cond = cond_orb.shape[1]
    npt_all = cond_orb.shape[2]
    k_points = k_dev * n_ka
    pairs = k_points // 2
    mu_blk, nu_blk = screened.shape
    own = coulomb.shape[0]
    count_all = k_points * nv_blk * n_band * n_cond
    scale = 1.0 / (npt_all * math.sqrt(count_all))
    piece_rows = k_points * nv_blk

    block = ((k_dev + 1) // 2 * ROWS, LANES)
    msg_shape = shape_of((devices,) + block, BF)
    wide = nu_blk + LANES
    start_own, gap, *payloads = call(
        functools.partial(pack_kernel, n_ka, nu_blk),
        "pack",
        (shape_of(block), shape_of(block)) + (shape_of((k_dev, nv_blk, wide), BF),) * n_ka,
        [ANY] * 4,
        (VMEM,) * (2 + n_ka),
        [
            pltpu.VMEM(start_vec.shape, F32),
            pltpu.VMEM(cond_energy.shape, F32),
            pltpu.SMEM(val_energy.shape, F32),
            dma(3),
            dma(n_ka),
        ],
    )(start_vec, cond_energy, val_energy, val_orb)
    base, payloads = lax.optimization_barrier((band * mu_blk, payloads))
    got = [payloads[0]] + [swap(payloads[j], "ka", j) for j in range(1, n_ka)]
    own_rows = k_dev * n_cond
    cuts = call(
        cut_kernel,
        "cut",
        shape_of((n_ka, own_rows, own), BF),
        [ANY],
        VMEM,
        [dma(n_ka * k_dev)],
    )(cond_orb)
    cond_local = lax.dynamic_slice_in_dim(cond_orb, base, mu_blk, 2)
    cond_local = cond_local.reshape(k_dev * n_cond, mu_blk)
    scr_turned = call(
        functools.partial(turn_kernel, nu_blk // 4),
        "turn",
        shape_of((nu_blk, mu_blk), BF),
        [ANY],
        ANY,
        [pltpu.VMEM((mu_blk, nu_blk), BF), pltpu.VMEM((nu_blk, mu_blk), BF)]
        + [dma(4)] * 2,
        moved=8 * MIB,
    )(screened)
    got, cuts, cond_local, scr_turned = lax.optimization_barrier(
        (got, cuts, cond_local, scr_turned)
    )
    val_cut = jnp.concatenate(got, axis=0).reshape(piece_rows, wide)
    cond_pts = [cond_local] + [swap(cond_local, "ka", j) for j in range(1, n_ka)]
    cond_own = lax.all_to_all(cuts, "ka", split_axis=0, concat_axis=0, tiled=True)

    chunk, tile = 1024, nu_blk
    rows_all, conds_all = k_points * nv_blk * n_band, k_points * n_cond
    pieces, parts = plane_pieces(val_cut)
    pieces, cond_pts[1:-1] = lax.optimization_barrier((pieces, cond_pts[1:-1]))
    val_rows, val_turned, val_own, msgs = call(
        functools.partial(order_kernel, parts, n_ka),
        "order",
        (
            shape_of((rows_all, nu_blk), BF),
            shape_of((nu_blk, rows_all), BF),
            shape_of((rows_all, own), BF),
            msg_shape,
        ),
        [ANY] * len(pieces),
        (ANY, ANY, ANY, VMEM),
        [
            pltpu.VMEM((n_band, piece_rows, nu_blk), BF),
            pltpu.VMEM((n_band, piece_rows, LANES), BF),
            pltpu.VMEM((rows_all, nu_blk), BF),
            pltpu.VMEM((nu_blk, rows_all), BF),
            dma(2, sum(len(piece) for piece in parts)),
            dma(3, pairs),
        ],
        moved=9 * MIB,
    )(*pieces)

    cfg = (n_ka, n_band, k_dev)
    quads = k_points // 4
    state, coef = None, None
    for step in range(STEPS):
        first = step == 0
        qx, rho = call(
            functools.partial(density_kernel, cfg),
            "density",
            (
                shape_of((quads, 2 * LANES, 2 * LANES), BF),
                shape_of((devices, own // LANES, LANES)),
            ),
            [ANY] * 3,
            (VMEM, VMEM),
            [
                pltpu.VMEM((quads, 2 * LANES, 2 * LANES), F32),
                pltpu.VMEM((devices,) + block, BF),
                pltpu.VMEM((rows_all, own), BF),
                pltpu.VMEM((n_ka, own_rows, own), BF),
                dma(n_ka + 2),
            ],
        )(msgs, val_own, cond_own)
        density = exchange_all(rho)
        direct = call(
            functools.partial(direct_kernel, n_ka, tile, scale),
            "direct",
            shape_of((pairs, LANES, LANES)),
            [ANY] * (4 + n_ka),
            VMEM,
            [
                pltpu.VMEM((quads, 2 * LANES, 2 * LANES), BF),
                pltpu.VMEM((nu_blk, rows_all), BF),
                pltpu.VMEM((n_ka, k_dev * n_cond, mu_blk), BF),
                pltpu.VMEM((nu_blk, mu_blk), BF),
                pltpu.VMEM((rows_all, nu_blk), BF),
                pltpu.VMEM((nu_blk, conds_all), BF),
                pltpu.VMEM((nu_blk, mu_blk), BF),
                pltpu.VMEM((rows_all, mu_blk), BF),
                dma(1),
                dma(n_ka),
                dma(1),
                dma(2, nu_blk // tile),
            ],
            flops=4 * mu_blk * nu_blk * conds_all,
            moved=12 * MIB,
        )(val_turned, scr_turned, val_rows, qx, *cond_pts)
        summed = call(
            functools.partial(exchange_kernel, cfg, chunk, scale),
            "exchange",
            msg_shape,
            [ANY] * 5,
            VMEM,
            [
                pltpu.VMEM((devices, own // LANES, LANES), F32),
                pltpu.VMEM((pairs, LANES, LANES), F32),
                pltpu.VMEM((own, npt_all), BF),
                pltpu.VMEM((n_ka, own_rows, own), BF),
                pltpu.VMEM((rows_all, own), BF),
                pltpu.VMEM((pairs, LANES, LANES), F32),
                pltpu.VMEM((devices,) + block, F32),
                dma(npt_all // chunk),
                dma(n_ka + 3),
            ],
        )(density, direct, coulomb, val_own, cond_own)
        recv = exchange_all(summed)
        if first:
            state, coef, message = call(
                functools.partial(first_owner_kernel, count_all),
                "first_owner",
                (shape_of((3,) + block), shape_of((ROWS, LANES)), msg_shape),
                [VMEM] * 4,
                (VMEM, VMEM, VMEM),
                mib=8,
            )(recv, msgs, gap, start_own)
        else:
            state, coef, message = call(
                functools.partial(second_owner_kernel, count_all),
                "second_owner",
                (shape_of((2,) + block), shape_of((ROWS, LANES)), shape_of((devices, 2, LANES))),
                [VMEM] * 5,
                (VMEM, VMEM, VMEM),
                mib=8,
            )(recv, msgs, gap, state, coef)
        msgs = exchange_all(message)
    return call(
        functools.partial(finish_kernel, count_all),
        "finish",
        (shape_of(start_vec.shape), shape_of((2 * STEPS,))),
        [VMEM] * 3,
        (VMEM, SMEM),
        mib=8,
    )(msgs, state, coef)


def array_path(start_vec, val_energy, cond_energy, val_orb, cond_orb, coulomb, screened):
    n_ka = lax.axis_size("ka")
    n_band = lax.axis_size("band")
    devices = n_ka * n_band
    ka, band = lax.axis_index("ka"), lax.axis_index("band")
    me = ka * n_band + band
    k_dev, pair_blk = start_vec.shape
    nv_blk = val_orb.shape[1]
    n_cond = cond_orb.shape[1]
    n_val = nv_blk * n_band
    npt_all = cond_orb.shape[2]
    k_points = k_dev * n_ka
    mu_blk, nu_blk = screened.shape
    own_pts = coulomb.shape[0]
    count_all = k_points * n_val * n_cond
    kernel_scale = 1.0 / (npt_all * math.sqrt(count_all))

    start_all = gather_all(start_vec, devices)
    val_cut = lax.all_to_all(
        val_orb.reshape(k_dev, nv_blk, n_ka, nu_blk).transpose(2, 0, 1, 3),
        "ka", split_axis=0, concat_axis=0, tiled=True,
    ).reshape(k_points, nv_blk, nu_blk)
    val_pts = lax.all_gather(val_cut, "band", axis=1, tiled=True)
    cond_local = lax.dynamic_slice_in_dim(cond_orb, band * mu_blk, mu_blk, 2)
    cond_pts = lax.all_gather(cond_local, "ka", axis=0, tiled=True)
    cond_rows = cond_orb.reshape(k_dev, n_cond, n_ka, n_band, own_pts)
    cond_rows = lax.dynamic_index_in_dim(cond_rows, band, 3, keepdims=False)
    cond_own = lax.all_to_all(
        cond_rows.transpose(2, 0, 1, 3), "ka", split_axis=0, concat_axis=0, tiled=True
    ).reshape(k_points, n_cond, own_pts)
    val_own = lax.dynamic_slice_in_dim(val_pts, band * own_pts, own_pts, 2)

    energy_gap = (cond_energy[:, None, :] - val_energy[:, :, None]).reshape(k_dev, pair_blk)
    start_sq = jnp.sum(start_all * start_all)
    current = start_all / jnp.sqrt(start_sq / count_all + 1e-06)
    previous = jnp.zeros_like(current)
    beta_val = jnp.float32(0.0)
    alphas = []
    betas = []
    for turn_index in range(STEPS):
        full_vec = (
            current.astype(BF)
            .reshape(n_ka, n_band, k_dev, nv_blk, n_cond)
            .transpose(0, 2, 1, 3, 4)
            .reshape(k_points, n_val, n_cond)
        )
        mixed_f = jnp.einsum("kvc,kvn->kcn", full_vec, val_pts, preferred_element_type=F32)
        mixed_own = lax.dynamic_slice_in_dim(mixed_f, band * own_pts, own_pts, 2)
        density_own = jnp.sum(mixed_own * cond_own.astype(F32), axis=(0, 1))
        density = gather_all(density_own.astype(BF), devices).reshape(npt_all)
        mixed_val = mixed_f.astype(BF)
        amp = jnp.einsum("kcm,kcn->mn", cond_pts, mixed_val, preferred_element_type=F32)
        kern = (screened.astype(F32) * amp * kernel_scale).astype(BF)
        folded = jnp.einsum("mn,kvn->kvm", kern, val_pts, preferred_element_type=F32).astype(BF)
        direct_part = jnp.einsum("kcm,kvm->kvc", cond_pts, folded, preferred_element_type=F32)
        potential = kernel_scale * jnp.dot(coulomb, density, preferred_element_type=F32)
        weighted = (val_own.astype(F32) * potential).astype(BF)
        exchange = jnp.einsum("kvp,kcp->kvc", weighted, cond_own, preferred_element_type=F32)
        part = 2.0 * exchange - direct_part
        arranged = (
            part.reshape(n_ka, k_dev, n_band, nv_blk, n_cond)
            .transpose(0, 2, 1, 3, 4)
            .reshape(devices, k_dev, pair_blk)
        )
        inter_own = jnp.sum(exchange_all(arranged), axis=0)
        current_own = lax.dynamic_index_in_dim(current, me, 0, keepdims=False)
        resid_vec = gather_all(energy_gap * current_own + inter_own, devices)
        resid_vec = resid_vec - beta_val * previous
        alpha_val = jnp.sum(current * resid_vec) / count_all
        resid_vec = resid_vec - alpha_val * current
        beta_val = jnp.sqrt(jnp.sum(resid_vec * resid_vec) / count_all + 1e-06)
        previous = current
        current = resid_vec / beta_val
        alphas.append(alpha_val)
        betas.append(beta_val)
    coeffs = jnp.stack(alphas + betas)
    return (lax.dynamic_index_in_dim(current, me, 0, keepdims=False), coeffs)


def per_device(*args):
    start_vec, _, _, val_orb, cond_orb, coulomb, screened = args
    n_ka, n_band = lax.axis_size("ka"), lax.axis_size("band")
    fits = (
        n_band == 8
        and n_ka & (n_ka - 1) == 0
        and start_vec.shape[0] % 2 == 1
        and val_orb.shape[1] == ROWS
        and cond_orb.shape[1] == HALF
        and start_vec.shape[0] * n_ka % 4 == 0
        and coulomb.shape[0] % LANES == 0
        and coulomb.shape[1] % 1024 == 0
        and screened.shape[0] % 512 == 0
        and screened.shape[1] % 1024 == 0
        and screened.shape[0] * screened.shape[1] <= 2 * MIB
    )
    return (kernel_path if fits else array_path)(*args)


def solution(mesh):
    in_specs = (
        P("ka", "band"),
        P("ka", "band"),
        P("ka", None),
        P("ka", "band", None),
        P("ka", None, None),
        P(("ka", "band"), None),
        P("band", "ka"),
    )
    out_specs = (P("ka", "band"), P())
    return jax.shard_map(
        per_device, mesh=mesh, in_specs=in_specs, out_specs=out_specs, check_vma=False
    )
```

```python
import functools
import math

import jax
import jax.numpy as jnp
from jax import lax
from jax.experimental import pallas as pl
from jax.experimental.pallas import tpu as pltpu
from jax.sharding import PartitionSpec as P

STEPS = 2
AXES = ("ka", "band")
BF, F32 = jnp.bfloat16, jnp.float32
LANES = 128
HALF = 64
ROWS = 8
MIB = 1 << 20
VMEM_ALL = 63_400_000

VMEM = pl.BlockSpec(memory_space=pltpu.VMEM)
SMEM = pl.BlockSpec(memory_space=pltpu.SMEM)
ANY = pl.BlockSpec(memory_space=pl.ANY)


def gather_all(block, devices):
    wide = jnp.broadcast_to(block[None], (devices,) + block.shape)
    return exchange_all(wide)


def exchange_all(parts):
    return lax.all_to_all(parts, AXES, split_axis=0, concat_axis=0, tiled=True)


def dot_nt(lhs, rhs):
    return lax.dot_general(lhs, rhs, (((1,), (1,)), ((), ())), preferred_element_type=F32)


def dot_tn(lhs, rhs):
    return lax.dot_general(lhs, rhs, (((0,), (0,)), ((), ())), preferred_element_type=F32)


def lane_half(tile, have, want):
    if have != want:
        tile = pltpu.roll(tile, HALF, axis=1)
    lane = lax.broadcasted_iota(jnp.int32, tile.shape, 1)
    keep = lane < HALF if want == 0 else lane >= HALF
    return jnp.where(keep, tile, 0.0)


def with_sums(block, sums):
    row = lax.broadcasted_iota(jnp.int32, block.shape, 0)
    lane = lax.broadcasted_iota(jnp.int32, block.shape, 1)
    free = row == block.shape[0] - ROWS
    for i, total in enumerate(sums):
        rest = jnp.full(block.shape, total, F32)
        for part in range(3):
            piece = rest.astype(BF).astype(F32)
            block = jnp.where(free & (lane == HALF + 3 * i + part), piece, block)
            rest = rest - piece
    return block


def read_sums(msgs_ref, count):
    rows = msgs_ref.shape[1]
    tile = jnp.sum(msgs_ref[...].astype(F32), axis=0)[rows - ROWS :, :]
    row = lax.broadcasted_iota(jnp.int32, tile.shape, 0)
    lane = lax.broadcasted_iota(jnp.int32, tile.shape, 1)
    out = []
    for i in range(count):
        mine = (row == 0) & (lane >= HALF + 3 * i) & (lane < HALF + 3 * i + 3)
        out.append(jnp.sum(jnp.where(mine, tile, 0.0), keepdims=True))
    return out


def piece_copies(refs, parts, column, width, dest, sems):
    copies = []
    for d, piece in enumerate(parts):
        row = 0
        for ref, start, rows in piece:
            copies.append(
                pltpu.make_async_copy(
                    refs[ref].at[pl.ds(start, rows), pl.ds(column, width)],
                    dest.at[d, pl.ds(row, rows), :],
                    sems.at[len(copies)],
                )
            )
            row += rows
    return copies


def start_all(copies):
    for copy in copies:
        copy.start()


def wait_all(copies):
    for copy in copies:
        copy.wait()


def device_at(n_band, j, d):
    ka = jnp.bitwise_xor(lax.axis_index("ka"), j)
    return ka * n_band + jnp.bitwise_xor(lax.axis_index("band"), d)


def own_copies(ref, dest, sems):
    return [
        pltpu.make_async_copy(
            ref.at[jnp.bitwise_xor(lax.axis_index("ka"), j)], dest.at[j], sems.at[j]
        )
        for j in range(dest.shape[0])
    ]


def pair_rows(ref, kp):
    part = ref[:, kp * 2 * ROWS : (kp + 1) * 2 * ROWS, :]
    return part.reshape(part.shape[0] * 2 * ROWS, part.shape[2])


def pack_kernel(n_ka, nu, *refs):
    start_in, cond_in, val_in, val_ref = refs[:4]
    own_ref, gap_ref, outs, refs = refs[4], refs[5], refs[6 : 6 + n_ka], refs[6 + n_ka :]
    start_ref, cond_ref, energy_ref, sems, val_sems = refs
    ins = ((start_in, start_ref), (cond_in, cond_ref), (val_in, energy_ref))
    small = [pltpu.make_async_copy(ref, to, sems.at[i]) for i, (ref, to) in enumerate(ins)]
    k_dev = val_ref.shape[0]
    val_copies = []
    for j in range(n_ka):
        at = pl.multiple_of(jnp.bitwise_xor(lax.axis_index("ka"), j) * nu, nu)
        val_copies.append(
            pltpu.make_async_copy(
                val_ref.at[:, :, pl.ds(at, nu)], outs[j].at[:, :, pl.ds(0, nu)], val_sems.at[j]
            )
        )
    start_all(small + val_copies)
    wait_all(small)
    own_ref[...] = jnp.zeros_like(own_ref)
    gap_ref[...] = jnp.zeros_like(gap_ref)
    cond = jnp.concatenate([cond_ref[...], cond_ref[...]], axis=1)
    for kl in range(k_dev):
        half = kl % 2
        for v in range(ROWS):
            at = pl.ds(kl // 2 * ROWS + v, 1)
            row = start_ref[pl.ds(kl, 1), pl.ds(v // 2 * LANES, LANES)]
            own_ref[at, :] = own_ref[at, :] + lane_half(row, v % 2, half)
            gap = cond[kl : kl + 1, :] - energy_ref[kl, v]
            gap_ref[at, :] = gap_ref[at, :] + lane_half(gap, half, half)
    mine = own_ref[...]
    square = mine * mine
    block = with_sums(mine, [jnp.sum(square), jnp.sum(gap_ref[...] * square)])
    for j in range(n_ka):
        for g in range(k_dev):
            head = jnp.zeros((ROWS, LANES), F32)
            if (g + 1) * ROWS <= block.shape[0]:
                head = block[g * ROWS : (g + 1) * ROWS, :]
            outs[j][g, :, nu:] = head.astype(BF)
    wait_all(val_copies)


def cut_kernel(cond_ref, out_ref, sems):
    n_ka, _, own = out_ref.shape
    k_dev, n_cond, npt = cond_ref.shape
    copies = []
    for z in range(n_ka):
        at = z * (npt // n_ka) + lax.axis_index("band") * own
        for kl in range(k_dev):
            copies.append(
                pltpu.make_async_copy(
                    cond_ref.at[kl, :, pl.ds(pl.multiple_of(at, LANES), own)],
                    out_ref.at[z, pl.ds(kl * n_cond, n_cond), :],
                    sems.at[len(copies)],
                )
            )
    start_all(copies)
    wait_all(copies)


def turn_kernel(tile, scr_ref, out_ref, scrs, turned, in_sems, out_sems):
    nu = scr_ref.shape[1]
    ins, outs = [], []
    for j in range(nu // tile):
        at = pl.ds(j * tile, tile)
        ins.append(pltpu.make_async_copy(scr_ref.at[:, at], scrs.at[:, at], in_sems.at[j]))
        outs.append(pltpu.make_async_copy(turned.at[at, :], out_ref.at[at, :], out_sems.at[j]))
    start_all(ins)
    for j in range(nu // tile):
        ins[j].wait()
        turned[j * tile : (j + 1) * tile, :] = scrs[:, j * tile : (j + 1) * tile].T
        outs[j].start()
    wait_all(outs)


def order_kernel(parts, n_ka, *refs):
    val_refs, refs = refs[:-10], refs[-10:]
    rows_out, turned_out, own_out, msgs_out, vals, heads, ordered, turned, val_sems, out_sems = refs
    own = own_out.shape[1]
    nu = ordered.shape[1]
    copies = piece_copies(val_refs, parts, 0, nu, vals, val_sems.at[0])
    head_copies = piece_copies(val_refs, parts, nu, LANES, heads, val_sems.at[1])
    start_all(copies + head_copies)
    wait_all(copies)
    n_band, group = vals.shape[0], vals.shape[0] * 2 * ROWS
    column = pl.multiple_of(lax.axis_index("band") * own, LANES)
    outs = []
    for kp in range(ordered.shape[0] // group):
        at = slice(kp * group, (kp + 1) * group)
        ordered[at, :] = pair_rows(vals, kp)
        turned[:, at] = ordered[at, :].T
        at = pl.ds(kp * group, group)
        outs += [
            pltpu.make_async_copy(ordered.at[at, :], rows_out.at[at, :], out_sems.at[0, kp]),
            pltpu.make_async_copy(turned.at[:, at], turned_out.at[:, at], out_sems.at[1, kp]),
            pltpu.make_async_copy(
                ordered.at[at, pl.ds(column, own)], own_out.at[at, :], out_sems.at[2, kp]
            ),
        ]
        start_all(outs[-3:])
    wait_all(head_copies)
    rows = msgs_out.shape[1]
    step = heads.shape[1] // n_ka
    for d in range(n_band):
        head = heads[d].astype(F32)
        for j in range(n_ka):
            msgs_out[device_at(n_band, j, d)] = head[j * step : j * step + rows, :].astype(BF)
    wait_all(outs)


def density_kernel(cfg, *refs):
    n_ka, n_band, k_dev = cfg
    k_points = n_ka * k_dev
    msgs_ref, vown_ref, cond_ref, qx_ref, rho_ref, xs, msgs, vown, conds, sems = refs
    own = vown_ref.shape[1]
    msg_copy = pltpu.make_async_copy(msgs_ref, msgs, sems.at[n_ka])
    copies = own_copies(cond_ref, conds, sems)
    copies.append(pltpu.make_async_copy(vown_ref, vown, sems.at[n_ka + 1]))
    start_all([msg_copy] + copies)
    xs[...] = jnp.zeros_like(xs)
    msg_copy.wait()
    for d in range(n_band):
        for k in range(k_points):
            j, kl = divmod(k, k_dev)
            tile = msgs[device_at(n_band, j, d), :, :].astype(F32)
            tile = tile[kl // 2 * ROWS : (kl // 2 + 1) * ROWS, :]
            base = k // 2 % 2 * LANES
            at = pl.ds(base + d * 2 * ROWS + k % 2 * ROWS, ROWS)
            xs[k // 4, at, pl.ds(base, LANES)] = lane_half(tile, kl % 2, k % 2)
    qx_ref[...] = xs[...].astype(BF)
    wait_all(copies)
    cond_rows = conds[...].reshape(-1, own)
    rho = jnp.zeros((1, own), F32)
    quad = 2 * LANES
    for kq in range(k_points // 4):
        at = slice(kq * quad, (kq + 1) * quad)
        mixed = dot_tn(qx_ref[kq], vown[at, :])
        rho = rho + jnp.sum(mixed * cond_rows[at, :].astype(F32), axis=0, keepdims=True)
    for r in range(own // LANES):
        part = rho[:, r * LANES : (r + 1) * LANES]
        rho_ref[:, r, :] = jnp.broadcast_to(part, (rho_ref.shape[0], LANES))


def direct_kernel(n_ka, tile, scale, *refs):
    turned_ref, scr_ref, rows_ref, qx_ref, refs = refs[0], refs[1], refs[2], refs[3], refs[4:]
    cond_refs, refs = refs[:n_ka], refs[n_ka:]
    di_ref, qx, turned, conds, scrs, vals, mixed, kern, folded = refs[:9]
    qx_sem, cond_sems, row_sem, chunk_sems = refs[9:]
    nu, mu = scr_ref.shape
    quad = 2 * LANES
    qx_copy = pltpu.make_async_copy(qx_ref, qx, qx_sem.at[0])
    cond_copies = [
        pltpu.make_async_copy(ref, conds.at[j], cond_sems.at[j]) for j, ref in enumerate(cond_refs)
    ]
    turned_copies, scr_copies = [], []
    for i in range(nu // tile):
        at = pl.ds(i * tile, tile)
        turned_copies.append(
            pltpu.make_async_copy(turned_ref.at[at, :], turned.at[at, :], chunk_sems.at[0, i])
        )
        scr_copies.append(
            pltpu.make_async_copy(scr_ref.at[at, :], scrs.at[at, :], chunk_sems.at[1, i])
        )
    row_copy = pltpu.make_async_copy(rows_ref, vals, row_sem.at[0])
    start_all([qx_copy, turned_copies[0]] + cond_copies + [scr_copies[0]])
    for i in range(1, nu // tile):
        start_all([turned_copies[i], scr_copies[i]])
    row_copy.start()
    qx_copy.wait()
    for i in range(nu // tile):
        rows = slice(i * tile, (i + 1) * tile)
        turned_copies[i].wait()
        for kq in range(qx.shape[0]):
            cols = slice(kq * quad, (kq + 1) * quad)
            mixed[rows, cols] = jnp.dot(
                turned[rows, cols], qx[kq], preferred_element_type=F32
            ).astype(BF)
        if i == 0:
            wait_all(cond_copies)
            cond_rows = conds[...].reshape(-1, mu)
        scr_copies[i].wait()
        amp = jnp.dot(mixed[rows, :], cond_rows, preferred_element_type=F32)
        kern[rows, :] = (scrs[rows, :].astype(F32) * amp).astype(BF)
    row_copy.wait()
    folded[...] = jnp.dot(vals[...], kern[...], preferred_element_type=F32).astype(BF)
    for kq in range(qx.shape[0]):
        at = slice(kq * quad, (kq + 1) * quad)
        both = scale * dot_nt(folded[at, :], cond_rows[at, :])
        di_ref[2 * kq] = both[:LANES, :LANES]
        di_ref[2 * kq + 1] = both[LANES:, LANES:]


def exchange_kernel(cfg, chunk, scale, *refs):
    n_ka, n_band, k_dev = cfg
    k_points = n_ka * k_dev
    rho_ref, di_ref, coul_ref, vown_ref, cond_ref, msg_ref = refs[:6]
    rhos, di, coul, conds, vown, part, msg, coul_sems, sems = refs[6:]
    rho_copy = pltpu.make_async_copy(rho_ref, rhos, sems.at[n_ka])
    own, npt = coul_ref.shape
    coul_copies = [
        pltpu.make_async_copy(
            coul_ref.at[:, pl.ds(i * chunk, chunk)], coul.at[:, pl.ds(i * chunk, chunk)], coul_sems.at[i]
        )
        for i in range(npt // chunk)
    ]
    copies = own_copies(cond_ref, conds, sems)
    copies.append(pltpu.make_async_copy(vown_ref, vown, sems.at[n_ka + 1]))
    copies.append(pltpu.make_async_copy(di_ref, di, sems.at[n_ka + 2]))
    start_all([rho_copy] + coul_copies + copies)
    rho_copy.wait()
    acc = jnp.zeros((own, LANES), F32)
    per_dev = own // LANES
    for i in range(npt // chunk):
        coul_copies[i].wait()
        for j in range(i * chunk // LANES, (i + 1) * chunk // LANES):
            rho = rhos[j // per_dev, pl.ds(j % per_dev, 1), :].astype(BF).astype(F32)
            acc = acc + coul[:, j * LANES : (j + 1) * LANES].astype(F32) * rho
    potential = scale * jnp.sum(acc.T, axis=0, keepdims=True)
    wait_all(copies)
    cond_rows = conds[...].reshape(-1, own)
    for kp in range(k_points // 2):
        at = slice(kp * LANES, (kp + 1) * LANES)
        weighted = (vown[at, :].astype(F32) * potential).astype(BF)
        part[kp] = 2.0 * dot_nt(weighted, cond_rows[at, :]) - di[kp]
    for d in range(n_band):
        for j in range(n_ka):
            for g in range((k_dev + 1) // 2):
                tile = None
                for kl in range(2 * g, min(2 * g + 2, k_dev)):
                    k = j * k_dev + kl
                    piece = part[k // 2, pl.ds(d * 2 * ROWS + k % 2 * ROWS, ROWS), :]
                    piece = lane_half(piece, k % 2, kl % 2)
                    tile = piece if tile is None else tile + piece
                msg[device_at(n_band, j, d), pl.ds(g * ROWS, ROWS), :] = tile
    msg_ref[...] = msg[...].astype(BF)


def write_rows(ref, values):
    for i, value in enumerate(values):
        ref[i : i + 1, :] = jnp.broadcast_to(value, (1, ref.shape[1]))


def received(recv_ref):
    return jnp.sum(recv_ref[...].astype(F32), axis=0)


def shifted(count_all, shift, square, cross_sum, square_sum):
    alpha = shift * square + cross_sum / count_all
    d = alpha - shift
    mean_sq = (square_sum - 2.0 * d * cross_sum) / count_all + d * d * square
    mean_sq = jnp.maximum(mean_sq, 0.0)
    return alpha, d, mean_sq


def first_owner_kernel(count_all, recv_ref, msgs_ref, gap_ref, own_ref, state_ref, coef_ref, msg_ref):
    start_sq, gap_sq = read_sums(msgs_ref, 2)
    norm = start_sq / count_all
    inv = 1.0 / jnp.sqrt(norm + 1e-06)
    square = norm / (norm + 1e-06)
    shift = gap_sq / jnp.maximum(start_sq, 1e-30)
    cur = own_ref[...] * inv
    inter = received(recv_ref) * inv
    gap = gap_ref[...]
    resid = (gap - shift) * cur + inter
    state_ref[0] = cur
    state_ref[1] = resid
    state_ref[2] = inter
    write_rows(coef_ref, (shift, square, gap_sq * inv * inv))
    sums = [
        jnp.sum(cur * resid),
        jnp.sum(resid * resid),
        jnp.sum(gap * resid * resid),
        jnp.sum(gap * resid * cur),
    ]
    msg_ref[...] = jnp.broadcast_to(with_sums(resid, sums).astype(BF)[None], msg_ref.shape)


def second_owner_kernel(count_all, recv_ref, msgs_ref, gap_ref, state_ref, coef_ref, out_ref, coef_out, msg_ref):
    cross, total, gap_rr, gap_rq = read_sums(msgs_ref, 4)
    alpha, d, mean_sq = shifted(count_all, coef_ref[0:1, 0:1], coef_ref[1:2, 0:1], cross, total)
    beta = jnp.sqrt(mean_sq + 1e-06)
    square = mean_sq / (mean_sq + 1e-06)
    gap_qq = gap_rr - 2.0 * d * gap_rq + d * d * coef_ref[2:3, 0:1]
    shift = gap_qq / (mean_sq + 1e-06) / count_all
    prev = state_ref[0]
    cur = (state_ref[1] - d * prev) / beta
    inter = (received(recv_ref) - d * state_ref[2]) / beta
    resid = (gap_ref[...] - shift) * cur + inter - beta * prev
    out_ref[0] = cur
    out_ref[1] = resid
    write_rows(coef_out, (alpha, beta, shift, square))
    dims = msg_ref.shape[:1] + msg_ref.shape[2:]
    msg_ref[:, 0, :] = jnp.full(dims, jnp.sum(cur * resid), F32)
    msg_ref[:, 1, :] = jnp.full(dims, jnp.sum(resid * resid), F32)


def finish_kernel(count_all, msgs_ref, state_ref, coef_ref, out_ref, coeffs_ref):
    sums = jnp.sum(msgs_ref[...], axis=0)
    alpha, d, mean_sq = shifted(count_all, coef_ref[2:3, 0:1], coef_ref[3:4, 0:1], sums[0:1, 0:1], sums[1:2, 0:1])
    beta = jnp.sqrt(mean_sq + 1e-06)
    own = (state_ref[1] - d * state_ref[0]) / beta
    coeffs_ref[0] = coef_ref[0, 0]
    coeffs_ref[1] = alpha[0, 0]
    coeffs_ref[2] = coef_ref[1, 0]
    coeffs_ref[3] = beta[0, 0]
    for kl in range(out_ref.shape[0]):
        tile = own[kl // 2 * ROWS : (kl // 2 + 1) * ROWS, :]
        other = pltpu.roll(tile, HALF, axis=1)
        left, right = (tile, other) if kl % 2 == 0 else (other, tile)
        low = lax.broadcasted_iota(jnp.int32, (1, LANES), 1) < HALF
        for j in range(ROWS // 2):
            row = jnp.where(low, left[2 * j : 2 * j + 1], right[2 * j + 1 : 2 * j + 2])
            out_ref[pl.ds(kl, 1), pl.ds(j * LANES, LANES)] = row


def shape_of(dims, kind=F32):
    return jax.ShapeDtypeStruct(dims, kind)


def call(kernel, name, out_shape, in_specs, out_specs, scratch=(), mib=None, flops=0, moved=0):
    return pl.pallas_call(
        kernel,
        out_shape=out_shape,
        in_specs=in_specs,
        out_specs=out_specs,
        scratch_shapes=list(scratch),
        compiler_params=pltpu.CompilerParams(vmem_limit_bytes=mib * MIB if mib else VMEM_ALL),
        cost_estimate=pl.CostEstimate(flops=flops, bytes_accessed=moved, transcendentals=0),
        name=name,
    )


def dma(*dims):
    return pltpu.SemaphoreType.DMA(dims)


def swap(block, axis, d):
    return lax.ppermute(block, axis, [(i, i ^ d) for i in range(lax.axis_size(axis))])


def plane_pieces(own_piece, others):
    def move(block, d):
        return swap(block, "band", d)

    rows = own_piece.shape[0]
    half = rows // 2
    by_x, by_y, core = move(own_piece, 2), move(own_piece, 4), move(own_piece, 1)
    by_x, by_y, others = lax.optimization_barrier((by_x, by_y, others))
    diag = [move(by_x[:half], 4), move(by_y[half:], 2)]
    near_x, near_y = move(by_x, 1), move(by_y, 1)
    far = [move(part, 1) for part in diag]
    arrays = [own_piece, core, by_x, near_x, by_y, near_y] + diag + far
    parts = tuple(((i, 0, rows),) for i in range(6))
    parts += (((6, 0, half), (7, 0, half)), ((8, 0, half), (9, 0, half)))
    return arrays, parts, others


def kernel_path(start_vec, val_energy, cond_energy, val_orb, cond_orb, coulomb, screened):
    n_ka = lax.axis_size("ka")
    n_band = lax.axis_size("band")
    devices = n_ka * n_band
    ka, band = lax.axis_index("ka"), lax.axis_index("band")
    k_dev = start_vec.shape[0]
    nv_blk = val_orb.shape[1]
    n_cond = cond_orb.shape[1]
    npt_all = cond_orb.shape[2]
    k_points = k_dev * n_ka
    pairs = k_points // 2
    mu_blk, nu_blk = screened.shape
    own = coulomb.shape[0]
    count_all = k_points * nv_blk * n_band * n_cond
    scale = 1.0 / (npt_all * math.sqrt(count_all))
    piece_rows = k_points * nv_blk

    block = ((k_dev + 1) // 2 * ROWS, LANES)
    msg_shape = shape_of((devices,) + block, BF)
    wide = nu_blk + LANES
    start_own, gap, *payloads = call(
        functools.partial(pack_kernel, n_ka, nu_blk),
        "pack",
        (shape_of(block), shape_of(block)) + (shape_of((k_dev, nv_blk, wide), BF),) * n_ka,
        [ANY] * 4,
        (VMEM,) * (2 + n_ka),
        [
            pltpu.VMEM(start_vec.shape, F32),
            pltpu.VMEM(cond_energy.shape, F32),
            pltpu.SMEM(val_energy.shape, F32),
            dma(3),
            dma(n_ka),
        ],
    )(start_vec, cond_energy, val_energy, val_orb)
    base, payloads = lax.optimization_barrier((band * mu_blk, payloads))
    got = [payloads[0]] + [swap(payloads[j], "ka", j) for j in range(1, n_ka)]
    own_rows = k_dev * n_cond
    cuts = call(
        cut_kernel,
        "cut",
        shape_of((n_ka, own_rows, own), BF),
        [ANY],
        VMEM,
        [dma(n_ka * k_dev)],
    )(cond_orb)
    cond_local = lax.dynamic_slice_in_dim(cond_orb, base, mu_blk, 2)
    cond_local = cond_local.reshape(k_dev * n_cond, mu_blk)
    got, cuts, cond_local = lax.optimization_barrier((got, cuts, cond_local))
    val_cut = jnp.concatenate(got, axis=0).reshape(piece_rows, wide)
    cond_pts = [cond_local] + [swap(cond_local, "ka", j) for j in range(1, n_ka)]
    cond_own = lax.all_to_all(cuts, "ka", split_axis=0, concat_axis=0, tiled=True)

    chunk, tile = 1024, nu_blk
    rows_all, conds_all = k_points * nv_blk * n_band, k_points * n_cond
    scr_turned = call(
        functools.partial(turn_kernel, nu_blk // 4),
        "turn",
        shape_of((nu_blk, mu_blk), BF),
        [ANY],
        ANY,
        [pltpu.VMEM((mu_blk, nu_blk), BF), pltpu.VMEM((nu_blk, mu_blk), BF)]
        + [dma(4)] * 2,
        moved=8 * MIB,
    )(screened)
    pieces, parts, scr_turned = plane_pieces(val_cut, scr_turned)
    pieces, cond_pts[1:-1] = lax.optimization_barrier((pieces, cond_pts[1:-1]))
    val_rows, val_turned, val_own, msgs = call(
        functools.partial(order_kernel, parts, n_ka),
        "order",
        (
            shape_of((rows_all, nu_blk), BF),
            shape_of((nu_blk, rows_all), BF),
            shape_of((rows_all, own), BF),
            msg_shape,
        ),
        [ANY] * len(pieces),
        (ANY, ANY, ANY, VMEM),
        [
            pltpu.VMEM((n_band, piece_rows, nu_blk), BF),
            pltpu.VMEM((n_band, piece_rows, LANES), BF),
            pltpu.VMEM((rows_all, nu_blk), BF),
            pltpu.VMEM((nu_blk, rows_all), BF),
            dma(2, sum(len(piece) for piece in parts)),
            dma(3, pairs),
        ],
        moved=9 * MIB,
    )(*pieces)

    cfg = (n_ka, n_band, k_dev)
    quads = k_points // 4
    state, coef = None, None
    for step in range(STEPS):
        first = step == 0
        qx, rho = call(
            functools.partial(density_kernel, cfg),
            "density",
            (
                shape_of((quads, 2 * LANES, 2 * LANES), BF),
                shape_of((devices, own // LANES, LANES)),
            ),
            [ANY] * 3,
            (VMEM, VMEM),
            [
                pltpu.VMEM((quads, 2 * LANES, 2 * LANES), F32),
                pltpu.VMEM((devices,) + block, BF),
                pltpu.VMEM((rows_all, own), BF),
                pltpu.VMEM((n_ka, own_rows, own), BF),
                dma(n_ka + 2),
            ],
        )(msgs, val_own, cond_own)
        density = exchange_all(rho)
        direct = call(
            functools.partial(direct_kernel, n_ka, tile, scale),
            "direct",
            shape_of((pairs, LANES, LANES)),
            [ANY] * (4 + n_ka),
            VMEM,
            [
                pltpu.VMEM((quads, 2 * LANES, 2 * LANES), BF),
                pltpu.VMEM((nu_blk, rows_all), BF),
                pltpu.VMEM((n_ka, k_dev * n_cond, mu_blk), BF),
                pltpu.VMEM((nu_blk, mu_blk), BF),
                pltpu.VMEM((rows_all, nu_blk), BF),
                pltpu.VMEM((nu_blk, conds_all), BF),
                pltpu.VMEM((nu_blk, mu_blk), BF),
                pltpu.VMEM((rows_all, mu_blk), BF),
                dma(1),
                dma(n_ka),
                dma(1),
                dma(2, nu_blk // tile),
            ],
            flops=4 * mu_blk * nu_blk * conds_all,
            moved=12 * MIB,
        )(val_turned, scr_turned, val_rows, qx, *cond_pts)
        summed = call(
            functools.partial(exchange_kernel, cfg, chunk, scale),
            "exchange",
            msg_shape,
            [ANY] * 5,
            VMEM,
            [
                pltpu.VMEM((devices, own // LANES, LANES), F32),
                pltpu.VMEM((pairs, LANES, LANES), F32),
                pltpu.VMEM((own, npt_all), BF),
                pltpu.VMEM((n_ka, own_rows, own), BF),
                pltpu.VMEM((rows_all, own), BF),
                pltpu.VMEM((pairs, LANES, LANES), F32),
                pltpu.VMEM((devices,) + block, F32),
                dma(npt_all // chunk),
                dma(n_ka + 3),
            ],
        )(density, direct, coulomb, val_own, cond_own)
        recv = exchange_all(summed)
        if first:
            state, coef, message = call(
                functools.partial(first_owner_kernel, count_all),
                "first_owner",
                (shape_of((3,) + block), shape_of((ROWS, LANES)), msg_shape),
                [VMEM] * 4,
                (VMEM, VMEM, VMEM),
                mib=8,
            )(recv, msgs, gap, start_own)
        else:
            state, coef, message = call(
                functools.partial(second_owner_kernel, count_all),
                "second_owner",
                (shape_of((2,) + block), shape_of((ROWS, LANES)), shape_of((devices, 2, LANES))),
                [VMEM] * 5,
                (VMEM, VMEM, VMEM),
                mib=8,
            )(recv, msgs, gap, state, coef)
        msgs = exchange_all(message)
    return call(
        functools.partial(finish_kernel, count_all),
        "finish",
        (shape_of(start_vec.shape), shape_of((2 * STEPS,))),
        [VMEM] * 3,
        (VMEM, SMEM),
        mib=8,
    )(msgs, state, coef)


def array_path(start_vec, val_energy, cond_energy, val_orb, cond_orb, coulomb, screened):
    n_ka = lax.axis_size("ka")
    n_band = lax.axis_size("band")
    devices = n_ka * n_band
    ka, band = lax.axis_index("ka"), lax.axis_index("band")
    me = ka * n_band + band
    k_dev, pair_blk = start_vec.shape
    nv_blk = val_orb.shape[1]
    n_cond = cond_orb.shape[1]
    n_val = nv_blk * n_band
    npt_all = cond_orb.shape[2]
    k_points = k_dev * n_ka
    mu_blk, nu_blk = screened.shape
    own_pts = coulomb.shape[0]
    count_all = k_points * n_val * n_cond
    kernel_scale = 1.0 / (npt_all * math.sqrt(count_all))

    start_all = gather_all(start_vec, devices)
    val_cut = lax.all_to_all(
        val_orb.reshape(k_dev, nv_blk, n_ka, nu_blk).transpose(2, 0, 1, 3),
        "ka", split_axis=0, concat_axis=0, tiled=True,
    ).reshape(k_points, nv_blk, nu_blk)
    val_pts = lax.all_gather(val_cut, "band", axis=1, tiled=True)
    cond_local = lax.dynamic_slice_in_dim(cond_orb, band * mu_blk, mu_blk, 2)
    cond_pts = lax.all_gather(cond_local, "ka", axis=0, tiled=True)
    cond_rows = cond_orb.reshape(k_dev, n_cond, n_ka, n_band, own_pts)
    cond_rows = lax.dynamic_index_in_dim(cond_rows, band, 3, keepdims=False)
    cond_own = lax.all_to_all(
        cond_rows.transpose(2, 0, 1, 3), "ka", split_axis=0, concat_axis=0, tiled=True
    ).reshape(k_points, n_cond, own_pts)
    val_own = lax.dynamic_slice_in_dim(val_pts, band * own_pts, own_pts, 2)

    energy_gap = (cond_energy[:, None, :] - val_energy[:, :, None]).reshape(k_dev, pair_blk)
    start_sq = jnp.sum(start_all * start_all)
    current = start_all / jnp.sqrt(start_sq / count_all + 1e-06)
    previous = jnp.zeros_like(current)
    beta_val = jnp.float32(0.0)
    alphas = []
    betas = []
    for turn_index in range(STEPS):
        full_vec = (
            current.astype(BF)
            .reshape(n_ka, n_band, k_dev, nv_blk, n_cond)
            .transpose(0, 2, 1, 3, 4)
            .reshape(k_points, n_val, n_cond)
        )
        mixed_f = jnp.einsum("kvc,kvn->kcn", full_vec, val_pts, preferred_element_type=F32)
        mixed_own = lax.dynamic_slice_in_dim(mixed_f, band * own_pts, own_pts, 2)
        density_own = jnp.sum(mixed_own * cond_own.astype(F32), axis=(0, 1))
        density = gather_all(density_own.astype(BF), devices).reshape(npt_all)
        mixed_val = mixed_f.astype(BF)
        amp = jnp.einsum("kcm,kcn->mn", cond_pts, mixed_val, preferred_element_type=F32)
        kern = (screened.astype(F32) * amp * kernel_scale).astype(BF)
        folded = jnp.einsum("mn,kvn->kvm", kern, val_pts, preferred_element_type=F32).astype(BF)
        direct_part = jnp.einsum("kcm,kvm->kvc", cond_pts, folded, preferred_element_type=F32)
        potential = kernel_scale * jnp.dot(coulomb, density, preferred_element_type=F32)
        weighted = (val_own.astype(F32) * potential).astype(BF)
        exchange = jnp.einsum("kvp,kcp->kvc", weighted, cond_own, preferred_element_type=F32)
        part = 2.0 * exchange - direct_part
        arranged = (
            part.reshape(n_ka, k_dev, n_band, nv_blk, n_cond)
            .transpose(0, 2, 1, 3, 4)
            .reshape(devices, k_dev, pair_blk)
        )
        inter_own = jnp.sum(exchange_all(arranged), axis=0)
        current_own = lax.dynamic_index_in_dim(current, me, 0, keepdims=False)
        resid_vec = gather_all(energy_gap * current_own + inter_own, devices)
        resid_vec = resid_vec - beta_val * previous
        alpha_val = jnp.sum(current * resid_vec) / count_all
        resid_vec = resid_vec - alpha_val * current
        beta_val = jnp.sqrt(jnp.sum(resid_vec * resid_vec) / count_all + 1e-06)
        previous = current
        current = resid_vec / beta_val
        alphas.append(alpha_val)
        betas.append(beta_val)
    coeffs = jnp.stack(alphas + betas)
    return (lax.dynamic_index_in_dim(current, me, 0, keepdims=False), coeffs)


def per_device(*args):
    start_vec, _, _, val_orb, cond_orb, coulomb, screened = args
    n_ka, n_band = lax.axis_size("ka"), lax.axis_size("band")
    fits = (
        n_band == 8
        and n_ka & (n_ka - 1) == 0
        and start_vec.shape[0] % 2 == 1
        and val_orb.shape[1] == ROWS
        and cond_orb.shape[1] == HALF
        and start_vec.shape[0] * n_ka % 4 == 0
        and coulomb.shape[0] % LANES == 0
        and coulomb.shape[1] % 1024 == 0
        and screened.shape[0] % 512 == 0
        and screened.shape[1] % 1024 == 0
        and screened.shape[0] * screened.shape[1] <= 2 * MIB
    )
    return (kernel_path if fits else array_path)(*args)


def solution(mesh):
    in_specs = (
        P("ka", "band"),
        P("ka", "band"),
        P("ka", None),
        P("ka", "band", None),
        P("ka", None, None),
        P(("ka", "band"), None),
        P("band", "ka"),
    )
    out_specs = (P("ka", "band"), P())
    return jax.shard_map(
        per_device, mesh=mesh, in_specs=in_specs, out_specs=out_specs, check_vma=False
    )
```

```python
import functools
import math

import jax
import jax.numpy as jnp
from jax import lax
from jax.experimental import pallas as pl
from jax.experimental.pallas import tpu as pltpu
from jax.sharding import PartitionSpec as P

STEPS = 2
AXES = ("ka", "band")
BF, F32 = jnp.bfloat16, jnp.float32
LANES = 128
HALF = 64
ROWS = 8
MIB = 1 << 20
VMEM_ALL = 63_400_000

VMEM = pl.BlockSpec(memory_space=pltpu.VMEM)
SMEM = pl.BlockSpec(memory_space=pltpu.SMEM)
ANY = pl.BlockSpec(memory_space=pl.ANY)


def gather_all(block, devices):
    wide = jnp.broadcast_to(block[None], (devices,) + block.shape)
    return exchange_all(wide)


def exchange_all(parts):
    return lax.all_to_all(parts, AXES, split_axis=0, concat_axis=0, tiled=True)


def dot_nt(lhs, rhs):
    return lax.dot_general(lhs, rhs, (((1,), (1,)), ((), ())), preferred_element_type=F32)


def dot_tn(lhs, rhs):
    return lax.dot_general(lhs, rhs, (((0,), (0,)), ((), ())), preferred_element_type=F32)


def lane_half(tile, have, want):
    if have != want:
        tile = pltpu.roll(tile, HALF, axis=1)
    lane = lax.broadcasted_iota(jnp.int32, tile.shape, 1)
    keep = lane < HALF if want == 0 else lane >= HALF
    return jnp.where(keep, tile, 0.0)


def with_sums(block, sums):
    row = lax.broadcasted_iota(jnp.int32, block.shape, 0)
    lane = lax.broadcasted_iota(jnp.int32, block.shape, 1)
    free = row == block.shape[0] - ROWS
    for i, total in enumerate(sums):
        rest = jnp.full(block.shape, total, F32)
        for part in range(3):
            piece = rest.astype(BF).astype(F32)
            block = jnp.where(free & (lane == HALF + 3 * i + part), piece, block)
            rest = rest - piece
    return block


def read_sums(msgs_ref, count):
    rows = msgs_ref.shape[1]
    tile = jnp.sum(msgs_ref[...].astype(F32), axis=0)[rows - ROWS :, :]
    row = lax.broadcasted_iota(jnp.int32, tile.shape, 0)
    lane = lax.broadcasted_iota(jnp.int32, tile.shape, 1)
    out = []
    for i in range(count):
        mine = (row == 0) & (lane >= HALF + 3 * i) & (lane < HALF + 3 * i + 3)
        out.append(jnp.sum(jnp.where(mine, tile, 0.0), keepdims=True))
    return out


def piece_copies(refs, parts, column, width, dest, sems):
    copies = []
    for d, piece in enumerate(parts):
        row = 0
        for ref, start, rows in piece:
            copies.append(
                pltpu.make_async_copy(
                    refs[ref].at[pl.ds(start, rows), pl.ds(column, width)],
                    dest.at[d, pl.ds(row, rows), :],
                    sems.at[len(copies)],
                )
            )
            row += rows
    return copies


def start_all(copies):
    for copy in copies:
        copy.start()


def wait_all(copies):
    for copy in copies:
        copy.wait()


def device_at(n_band, j, d):
    ka = jnp.bitwise_xor(lax.axis_index("ka"), j)
    return ka * n_band + jnp.bitwise_xor(lax.axis_index("band"), d)


def own_copies(ref, dest, sems):
    return [
        pltpu.make_async_copy(
            ref.at[jnp.bitwise_xor(lax.axis_index("ka"), j)], dest.at[j], sems.at[j]
        )
        for j in range(dest.shape[0])
    ]


def pair_rows(ref, kp):
    part = ref[:, kp * 2 * ROWS : (kp + 1) * 2 * ROWS, :]
    return part.reshape(part.shape[0] * 2 * ROWS, part.shape[2])


def pack_kernel(n_ka, nu, *refs):
    start_in, cond_in, val_in, val_ref = refs[:4]
    own_ref, gap_ref, outs, refs = refs[4], refs[5], refs[6 : 6 + n_ka], refs[6 + n_ka :]
    start_ref, cond_ref, energy_ref, sems, val_sems = refs
    ins = ((start_in, start_ref), (cond_in, cond_ref), (val_in, energy_ref))
    small = [pltpu.make_async_copy(ref, to, sems.at[i]) for i, (ref, to) in enumerate(ins)]
    k_dev = val_ref.shape[0]
    val_copies = []
    for j in range(n_ka):
        at = pl.multiple_of(jnp.bitwise_xor(lax.axis_index("ka"), j) * nu, nu)
        val_copies.append(
            pltpu.make_async_copy(
                val_ref.at[:, :, pl.ds(at, nu)], outs[j].at[:, :, pl.ds(0, nu)], val_sems.at[j]
            )
        )
    start_all(small + val_copies)
    wait_all(small)
    own_ref[...] = jnp.zeros_like(own_ref)
    gap_ref[...] = jnp.zeros_like(gap_ref)
    cond = jnp.concatenate([cond_ref[...], cond_ref[...]], axis=1)
    for kl in range(k_dev):
        half = kl % 2
        for v in range(ROWS):
            at = pl.ds(kl // 2 * ROWS + v, 1)
            row = start_ref[pl.ds(kl, 1), pl.ds(v // 2 * LANES, LANES)]
            own_ref[at, :] = own_ref[at, :] + lane_half(row, v % 2, half)
            gap = cond[kl : kl + 1, :] - energy_ref[kl, v]
            gap_ref[at, :] = gap_ref[at, :] + lane_half(gap, half, half)
    mine = own_ref[...]
    square = mine * mine
    block = with_sums(mine, [jnp.sum(square), jnp.sum(gap_ref[...] * square)])
    for j in range(n_ka):
        for g in range(k_dev):
            head = jnp.zeros((ROWS, LANES), F32)
            if (g + 1) * ROWS <= block.shape[0]:
                head = block[g * ROWS : (g + 1) * ROWS, :]
            outs[j][g, :, nu:] = head.astype(BF)
    wait_all(val_copies)


def cut_kernel(cond_ref, out_ref, sems):
    n_ka, _, own = out_ref.shape
    k_dev, n_cond, npt = cond_ref.shape
    copies = []
    for z in range(n_ka):
        at = z * (npt // n_ka) + lax.axis_index("band") * own
        for kl in range(k_dev):
            copies.append(
                pltpu.make_async_copy(
                    cond_ref.at[kl, :, pl.ds(pl.multiple_of(at, LANES), own)],
                    out_ref.at[z, pl.ds(kl * n_cond, n_cond), :],
                    sems.at[len(copies)],
                )
            )
    start_all(copies)
    wait_all(copies)


def turn_kernel(tile, scr_ref, out_ref, scrs, turned, in_sems, out_sems):
    nu = scr_ref.shape[1]
    ins, outs = [], []
    for j in range(nu // tile):
        at = pl.ds(j * tile, tile)
        ins.append(pltpu.make_async_copy(scr_ref.at[:, at], scrs.at[:, at], in_sems.at[j]))
        outs.append(pltpu.make_async_copy(turned.at[at, :], out_ref.at[at, :], out_sems.at[j]))
    start_all(ins)
    for j in range(nu // tile):
        ins[j].wait()
        turned[j * tile : (j + 1) * tile, :] = scrs[:, j * tile : (j + 1) * tile].T
        outs[j].start()
    wait_all(outs)


def order_kernel(parts, n_ka, *refs):
    val_refs, refs = refs[:-10], refs[-10:]
    rows_out, turned_out, own_out, msgs_out, vals, heads, ordered, turned, val_sems, out_sems = refs
    own = own_out.shape[1]
    nu = ordered.shape[1]
    copies = piece_copies(val_refs, parts, 0, nu, vals, val_sems.at[0])
    head_copies = piece_copies(val_refs, parts, nu, LANES, heads, val_sems.at[1])
    start_all(copies + head_copies)
    wait_all(copies)
    n_band, group = vals.shape[0], vals.shape[0] * 2 * ROWS
    column = pl.multiple_of(lax.axis_index("band") * own, LANES)
    outs = []
    for kp in range(ordered.shape[0] // group):
        at = slice(kp * group, (kp + 1) * group)
        ordered[at, :] = pair_rows(vals, kp)
        turned[:, at] = ordered[at, :].T
        at = pl.ds(kp * group, group)
        outs += [
            pltpu.make_async_copy(ordered.at[at, :], rows_out.at[at, :], out_sems.at[0, kp]),
            pltpu.make_async_copy(turned.at[:, at], turned_out.at[:, at], out_sems.at[1, kp]),
            pltpu.make_async_copy(
                ordered.at[at, pl.ds(column, own)], own_out.at[at, :], out_sems.at[2, kp]
            ),
        ]
        start_all(outs[-3:])
    wait_all(head_copies)
    rows = msgs_out.shape[1]
    step = heads.shape[1] // n_ka
    for d in range(n_band):
        head = heads[d].astype(F32)
        for j in range(n_ka):
            msgs_out[device_at(n_band, j, d)] = head[j * step : j * step + rows, :].astype(BF)
    wait_all(outs)


def density_kernel(cfg, *refs):
    n_ka, n_band, k_dev = cfg
    k_points = n_ka * k_dev
    msgs_ref, vown_ref, cond_ref, qx_ref, rho_ref, xs, msgs, vown, conds, sems = refs
    own = vown_ref.shape[1]
    msg_copy = pltpu.make_async_copy(msgs_ref, msgs, sems.at[n_ka])
    copies = own_copies(cond_ref, conds, sems)
    copies.append(pltpu.make_async_copy(vown_ref, vown, sems.at[n_ka + 1]))
    start_all([msg_copy] + copies)
    xs[...] = jnp.zeros_like(xs)
    msg_copy.wait()
    for d in range(n_band):
        for k in range(k_points):
            j, kl = divmod(k, k_dev)
            tile = msgs[device_at(n_band, j, d), :, :].astype(F32)
            tile = tile[kl // 2 * ROWS : (kl // 2 + 1) * ROWS, :]
            base = k // 2 % 2 * LANES
            at = pl.ds(base + d * 2 * ROWS + k % 2 * ROWS, ROWS)
            xs[k // 4, at, pl.ds(base, LANES)] = lane_half(tile, kl % 2, k % 2)
    qx_ref[...] = xs[...].astype(BF)
    wait_all(copies)
    cond_rows = conds[...].reshape(-1, own)
    rho = jnp.zeros((1, own), F32)
    quad = 2 * LANES
    for kq in range(k_points // 4):
        at = slice(kq * quad, (kq + 1) * quad)
        mixed = dot_tn(qx_ref[kq], vown[at, :])
        rho = rho + jnp.sum(mixed * cond_rows[at, :].astype(F32), axis=0, keepdims=True)
    for r in range(own // LANES):
        part = rho[:, r * LANES : (r + 1) * LANES]
        rho_ref[:, r, :] = jnp.broadcast_to(part, (rho_ref.shape[0], LANES))


def direct_kernel(n_ka, tile, scale, *refs):
    turned_ref, scr_ref, rows_ref, qx_ref, refs = refs[0], refs[1], refs[2], refs[3], refs[4:]
    cond_refs, refs = refs[:n_ka], refs[n_ka:]
    di_ref, qx, turned, conds, scrs, vals, mixed, kern, folded = refs[:9]
    qx_sem, cond_sems, row_sem, chunk_sems = refs[9:]
    nu, mu = scr_ref.shape
    quad = 2 * LANES
    qx_copy = pltpu.make_async_copy(qx_ref, qx, qx_sem.at[0])
    cond_copies = [
        pltpu.make_async_copy(ref, conds.at[j], cond_sems.at[j]) for j, ref in enumerate(cond_refs)
    ]
    turned_copies, scr_copies = [], []
    for i in range(nu // tile):
        at = pl.ds(i * tile, tile)
        turned_copies.append(
            pltpu.make_async_copy(turned_ref.at[at, :], turned.at[at, :], chunk_sems.at[0, i])
        )
        scr_copies.append(
            pltpu.make_async_copy(scr_ref.at[at, :], scrs.at[at, :], chunk_sems.at[1, i])
        )
    row_copy = pltpu.make_async_copy(rows_ref, vals, row_sem.at[0])
    start_all([qx_copy, turned_copies[0]] + cond_copies + [scr_copies[0]])
    for i in range(1, nu // tile):
        start_all([turned_copies[i], scr_copies[i]])
    row_copy.start()
    qx_copy.wait()
    for i in range(nu // tile):
        rows = slice(i * tile, (i + 1) * tile)
        turned_copies[i].wait()
        for kq in range(qx.shape[0]):
            cols = slice(kq * quad, (kq + 1) * quad)
            mixed[rows, cols] = jnp.dot(
                turned[rows, cols], qx[kq], preferred_element_type=F32
            ).astype(BF)
        if i == 0:
            wait_all(cond_copies)
            cond_rows = conds[...].reshape(-1, mu)
        scr_copies[i].wait()
        amp = jnp.dot(mixed[rows, :], cond_rows, preferred_element_type=F32)
        kern[rows, :] = (scrs[rows, :].astype(F32) * amp).astype(BF)
    row_copy.wait()
    folded[...] = jnp.dot(vals[...], kern[...], preferred_element_type=F32).astype(BF)
    for kq in range(qx.shape[0]):
        at = slice(kq * quad, (kq + 1) * quad)
        both = scale * dot_nt(folded[at, :], cond_rows[at, :])
        di_ref[2 * kq] = both[:LANES, :LANES]
        di_ref[2 * kq + 1] = both[LANES:, LANES:]


def exchange_kernel(cfg, chunk, scale, *refs):
    n_ka, n_band, k_dev = cfg
    k_points = n_ka * k_dev
    rho_ref, di_ref, coul_ref, vown_ref, cond_ref, msg_ref = refs[:6]
    rhos, di, coul, conds, vown, part, msg, coul_sems, sems = refs[6:]
    rho_copy = pltpu.make_async_copy(rho_ref, rhos, sems.at[n_ka])
    own, npt = coul_ref.shape
    coul_copies = [
        pltpu.make_async_copy(
            coul_ref.at[:, pl.ds(i * chunk, chunk)], coul.at[:, pl.ds(i * chunk, chunk)], coul_sems.at[i]
        )
        for i in range(npt // chunk)
    ]
    copies = own_copies(cond_ref, conds, sems)
    copies.append(pltpu.make_async_copy(vown_ref, vown, sems.at[n_ka + 1]))
    copies.append(pltpu.make_async_copy(di_ref, di, sems.at[n_ka + 2]))
    start_all([rho_copy] + coul_copies + copies)
    rho_copy.wait()
    acc = jnp.zeros((own, LANES), F32)
    per_dev = own // LANES
    for i in range(npt // chunk):
        coul_copies[i].wait()
        for j in range(i * chunk // LANES, (i + 1) * chunk // LANES):
            rho = rhos[j // per_dev, pl.ds(j % per_dev, 1), :].astype(BF).astype(F32)
            acc = acc + coul[:, j * LANES : (j + 1) * LANES].astype(F32) * rho
    potential = scale * jnp.sum(acc.T, axis=0, keepdims=True)
    wait_all(copies)
    cond_rows = conds[...].reshape(-1, own)
    for kp in range(k_points // 2):
        at = slice(kp * LANES, (kp + 1) * LANES)
        weighted = (vown[at, :].astype(F32) * potential).astype(BF)
        part[kp] = 2.0 * dot_nt(weighted, cond_rows[at, :]) - di[kp]
    for d in range(n_band):
        for j in range(n_ka):
            for g in range((k_dev + 1) // 2):
                tile = None
                for kl in range(2 * g, min(2 * g + 2, k_dev)):
                    k = j * k_dev + kl
                    piece = part[k // 2, pl.ds(d * 2 * ROWS + k % 2 * ROWS, ROWS), :]
                    piece = lane_half(piece, k % 2, kl % 2)
                    tile = piece if tile is None else tile + piece
                msg[device_at(n_band, j, d), pl.ds(g * ROWS, ROWS), :] = tile
    msg_ref[...] = msg[...].astype(BF)


def write_rows(ref, values):
    for i, value in enumerate(values):
        ref[i : i + 1, :] = jnp.broadcast_to(value, (1, ref.shape[1]))


def received(recv_ref):
    return jnp.sum(recv_ref[...].astype(F32), axis=0)


def shifted(count_all, shift, square, cross_sum, square_sum):
    alpha = shift * square + cross_sum / count_all
    d = alpha - shift
    mean_sq = (square_sum - 2.0 * d * cross_sum) / count_all + d * d * square
    mean_sq = jnp.maximum(mean_sq, 0.0)
    return alpha, d, mean_sq


def first_owner_kernel(count_all, recv_ref, msgs_ref, gap_ref, own_ref, state_ref, coef_ref, msg_ref):
    start_sq, gap_sq = read_sums(msgs_ref, 2)
    norm = start_sq / count_all
    inv = 1.0 / jnp.sqrt(norm + 1e-06)
    square = norm / (norm + 1e-06)
    shift = gap_sq / jnp.maximum(start_sq, 1e-30)
    cur = own_ref[...] * inv
    inter = received(recv_ref) * inv
    gap = gap_ref[...]
    resid = (gap - shift) * cur + inter
    state_ref[0] = cur
    state_ref[1] = resid
    state_ref[2] = inter
    write_rows(coef_ref, (shift, square, gap_sq * inv * inv))
    sums = [
        jnp.sum(cur * resid),
        jnp.sum(resid * resid),
        jnp.sum(gap * resid * resid),
        jnp.sum(gap * resid * cur),
    ]
    msg_ref[...] = jnp.broadcast_to(with_sums(resid, sums).astype(BF)[None], msg_ref.shape)


def second_owner_kernel(count_all, recv_ref, msgs_ref, gap_ref, state_ref, coef_ref, out_ref, coef_out, msg_ref):
    cross, total, gap_rr, gap_rq = read_sums(msgs_ref, 4)
    alpha, d, mean_sq = shifted(count_all, coef_ref[0:1, 0:1], coef_ref[1:2, 0:1], cross, total)
    beta = jnp.sqrt(mean_sq + 1e-06)
    square = mean_sq / (mean_sq + 1e-06)
    gap_qq = gap_rr - 2.0 * d * gap_rq + d * d * coef_ref[2:3, 0:1]
    shift = gap_qq / (mean_sq + 1e-06) / count_all
    prev = state_ref[0]
    cur = (state_ref[1] - d * prev) / beta
    inter = (received(recv_ref) - d * state_ref[2]) / beta
    resid = (gap_ref[...] - shift) * cur + inter - beta * prev
    out_ref[0] = cur
    out_ref[1] = resid
    write_rows(coef_out, (alpha, beta, shift, square))
    dims = msg_ref.shape[:1] + msg_ref.shape[2:]
    msg_ref[:, 0, :] = jnp.full(dims, jnp.sum(cur * resid), F32)
    msg_ref[:, 1, :] = jnp.full(dims, jnp.sum(resid * resid), F32)


def finish_kernel(count_all, msgs_ref, state_ref, coef_ref, out_ref, coeffs_ref):
    sums = jnp.sum(msgs_ref[...], axis=0)
    alpha, d, mean_sq = shifted(count_all, coef_ref[2:3, 0:1], coef_ref[3:4, 0:1], sums[0:1, 0:1], sums[1:2, 0:1])
    beta = jnp.sqrt(mean_sq + 1e-06)
    own = (state_ref[1] - d * state_ref[0]) / beta
    coeffs_ref[0] = coef_ref[0, 0]
    coeffs_ref[1] = alpha[0, 0]
    coeffs_ref[2] = coef_ref[1, 0]
    coeffs_ref[3] = beta[0, 0]
    for kl in range(out_ref.shape[0]):
        tile = own[kl // 2 * ROWS : (kl // 2 + 1) * ROWS, :]
        other = pltpu.roll(tile, HALF, axis=1)
        left, right = (tile, other) if kl % 2 == 0 else (other, tile)
        low = lax.broadcasted_iota(jnp.int32, (1, LANES), 1) < HALF
        for j in range(ROWS // 2):
            row = jnp.where(low, left[2 * j : 2 * j + 1], right[2 * j + 1 : 2 * j + 2])
            out_ref[pl.ds(kl, 1), pl.ds(j * LANES, LANES)] = row


def shape_of(dims, kind=F32):
    return jax.ShapeDtypeStruct(dims, kind)


def call(kernel, name, out_shape, in_specs, out_specs, scratch=(), mib=None, flops=0, moved=0):
    return pl.pallas_call(
        kernel,
        out_shape=out_shape,
        in_specs=in_specs,
        out_specs=out_specs,
        scratch_shapes=list(scratch),
        compiler_params=pltpu.CompilerParams(vmem_limit_bytes=mib * MIB if mib else VMEM_ALL),
        cost_estimate=pl.CostEstimate(flops=flops, bytes_accessed=moved, transcendentals=0),
        name=name,
    )


def dma(*dims):
    return pltpu.SemaphoreType.DMA(dims)


def swap(block, axis, d):
    return lax.ppermute(block, axis, [(i, i ^ d) for i in range(lax.axis_size(axis))])


def plane_pieces(own_piece, others, after):
    def move(block, d):
        return swap(block, "band", d)

    rows = own_piece.shape[0]
    half = rows // 2
    by_x, by_y, core = move(own_piece, 2), move(own_piece, 4), move(own_piece, 1)
    by_x, by_y, core, others = lax.optimization_barrier((by_x, by_y, core, others))
    diag = [move(by_x[:half], 4), move(by_y[half:], 2)]
    near_x, near_y = move(by_x, 1), move(by_y, 1)
    diag, after = lax.optimization_barrier((diag, after))
    far = [move(part, 1) for part in diag]
    arrays = [own_piece, core, by_x, near_x, by_y, near_y] + diag + far
    parts = tuple(((i, 0, rows),) for i in range(6))
    parts += (((6, 0, half), (7, 0, half)), ((8, 0, half), (9, 0, half)))
    return arrays, parts, others, after


def kernel_path(start_vec, val_energy, cond_energy, val_orb, cond_orb, coulomb, screened):
    n_ka = lax.axis_size("ka")
    n_band = lax.axis_size("band")
    devices = n_ka * n_band
    ka, band = lax.axis_index("ka"), lax.axis_index("band")
    k_dev = start_vec.shape[0]
    nv_blk = val_orb.shape[1]
    n_cond = cond_orb.shape[1]
    npt_all = cond_orb.shape[2]
    k_points = k_dev * n_ka
    pairs = k_points // 2
    mu_blk, nu_blk = screened.shape
    own = coulomb.shape[0]
    count_all = k_points * nv_blk * n_band * n_cond
    scale = 1.0 / (npt_all * math.sqrt(count_all))
    piece_rows = k_points * nv_blk

    block = ((k_dev + 1) // 2 * ROWS, LANES)
    msg_shape = shape_of((devices,) + block, BF)
    wide = nu_blk + LANES
    start_own, gap, *payloads = call(
        functools.partial(pack_kernel, n_ka, nu_blk),
        "pack",
        (shape_of(block), shape_of(block)) + (shape_of((k_dev, nv_blk, wide), BF),) * n_ka,
        [ANY] * 4,
        (VMEM,) * (2 + n_ka),
        [
            pltpu.VMEM(start_vec.shape, F32),
            pltpu.VMEM(cond_energy.shape, F32),
            pltpu.SMEM(val_energy.shape, F32),
            dma(3),
            dma(n_ka),
        ],
    )(start_vec, cond_energy, val_energy, val_orb)
    base, payloads = lax.optimization_barrier((band * mu_blk, payloads))
    got = [payloads[0]] + [swap(payloads[j], "ka", j) for j in range(1, n_ka)]
    own_rows = k_dev * n_cond
    cuts = call(
        cut_kernel,
        "cut",
        shape_of((n_ka, own_rows, own), BF),
        [ANY],
        VMEM,
        [dma(n_ka * k_dev)],
    )(cond_orb)
    cond_local = lax.dynamic_slice_in_dim(cond_orb, base, mu_blk, 2)
    cond_local = cond_local.reshape(k_dev * n_cond, mu_blk)
    got, cuts, cond_local = lax.optimization_barrier((got, cuts, cond_local))
    val_cut = jnp.concatenate(got, axis=0).reshape(piece_rows, wide)
    cond_pts = [cond_local] + [swap(cond_local, "ka", j) for j in range(1, n_ka - 1)]
    cond_own = lax.all_to_all(cuts, "ka", split_axis=0, concat_axis=0, tiled=True)

    chunk, tile = 1024, nu_blk
    rows_all, conds_all = k_points * nv_blk * n_band, k_points * n_cond
    scr_turned = call(
        functools.partial(turn_kernel, nu_blk // 4),
        "turn",
        shape_of((nu_blk, mu_blk), BF),
        [ANY],
        ANY,
        [pltpu.VMEM((mu_blk, nu_blk), BF), pltpu.VMEM((nu_blk, mu_blk), BF)]
        + [dma(4)] * 2,
        moved=8 * MIB,
    )(screened)
    pieces, parts, scr_turned, cond_last = plane_pieces(val_cut, scr_turned, cond_local)
    cond_pts.append(swap(cond_last, "ka", n_ka - 1))
    pieces, cond_pts[1:-1] = lax.optimization_barrier((pieces, cond_pts[1:-1]))
    val_rows, val_turned, val_own, msgs = call(
        functools.partial(order_kernel, parts, n_ka),
        "order",
        (
            shape_of((rows_all, nu_blk), BF),
            shape_of((nu_blk, rows_all), BF),
            shape_of((rows_all, own), BF),
            msg_shape,
        ),
        [ANY] * len(pieces),
        (ANY, ANY, ANY, VMEM),
        [
            pltpu.VMEM((n_band, piece_rows, nu_blk), BF),
            pltpu.VMEM((n_band, piece_rows, LANES), BF),
            pltpu.VMEM((rows_all, nu_blk), BF),
            pltpu.VMEM((nu_blk, rows_all), BF),
            dma(2, sum(len(piece) for piece in parts)),
            dma(3, pairs),
        ],
        moved=9 * MIB,
    )(*pieces)

    cfg = (n_ka, n_band, k_dev)
    quads = k_points // 4
    state, coef = None, None
    for step in range(STEPS):
        first = step == 0
        qx, rho = call(
            functools.partial(density_kernel, cfg),
            "density",
            (
                shape_of((quads, 2 * LANES, 2 * LANES), BF),
                shape_of((devices, own // LANES, LANES)),
            ),
            [ANY] * 3,
            (VMEM, VMEM),
            [
                pltpu.VMEM((quads, 2 * LANES, 2 * LANES), F32),
                pltpu.VMEM((devices,) + block, BF),
                pltpu.VMEM((rows_all, own), BF),
                pltpu.VMEM((n_ka, own_rows, own), BF),
                dma(n_ka + 2),
            ],
        )(msgs, val_own, cond_own)
        density = exchange_all(rho)
        direct = call(
            functools.partial(direct_kernel, n_ka, tile, scale),
            "direct",
            shape_of((pairs, LANES, LANES)),
            [ANY] * (4 + n_ka),
            VMEM,
            [
                pltpu.VMEM((quads, 2 * LANES, 2 * LANES), BF),
                pltpu.VMEM((nu_blk, rows_all), BF),
                pltpu.VMEM((n_ka, k_dev * n_cond, mu_blk), BF),
                pltpu.VMEM((nu_blk, mu_blk), BF),
                pltpu.VMEM((rows_all, nu_blk), BF),
                pltpu.VMEM((nu_blk, conds_all), BF),
                pltpu.VMEM((nu_blk, mu_blk), BF),
                pltpu.VMEM((rows_all, mu_blk), BF),
                dma(1),
                dma(n_ka),
                dma(1),
                dma(2, nu_blk // tile),
            ],
            flops=4 * mu_blk * nu_blk * conds_all,
            moved=12 * MIB,
        )(val_turned, scr_turned, val_rows, qx, *cond_pts)
        summed = call(
            functools.partial(exchange_kernel, cfg, chunk, scale),
            "exchange",
            msg_shape,
            [ANY] * 5,
            VMEM,
            [
                pltpu.VMEM((devices, own // LANES, LANES), F32),
                pltpu.VMEM((pairs, LANES, LANES), F32),
                pltpu.VMEM((own, npt_all), BF),
                pltpu.VMEM((n_ka, own_rows, own), BF),
                pltpu.VMEM((rows_all, own), BF),
                pltpu.VMEM((pairs, LANES, LANES), F32),
                pltpu.VMEM((devices,) + block, F32),
                dma(npt_all // chunk),
                dma(n_ka + 3),
            ],
        )(density, direct, coulomb, val_own, cond_own)
        recv = exchange_all(summed)
        if first:
            state, coef, message = call(
                functools.partial(first_owner_kernel, count_all),
                "first_owner",
                (shape_of((3,) + block), shape_of((ROWS, LANES)), msg_shape),
                [VMEM] * 4,
                (VMEM, VMEM, VMEM),
                mib=8,
            )(recv, msgs, gap, start_own)
        else:
            state, coef, message = call(
                functools.partial(second_owner_kernel, count_all),
                "second_owner",
                (shape_of((2,) + block), shape_of((ROWS, LANES)), shape_of((devices, 2, LANES))),
                [VMEM] * 5,
                (VMEM, VMEM, VMEM),
                mib=8,
            )(recv, msgs, gap, state, coef)
        msgs = exchange_all(message)
    return call(
        functools.partial(finish_kernel, count_all),
        "finish",
        (shape_of(start_vec.shape), shape_of((2 * STEPS,))),
        [VMEM] * 3,
        (VMEM, SMEM),
        mib=8,
    )(msgs, state, coef)


def array_path(start_vec, val_energy, cond_energy, val_orb, cond_orb, coulomb, screened):
    n_ka = lax.axis_size("ka")
    n_band = lax.axis_size("band")
    devices = n_ka * n_band
    ka, band = lax.axis_index("ka"), lax.axis_index("band")
    me = ka * n_band + band
    k_dev, pair_blk = start_vec.shape
    nv_blk = val_orb.shape[1]
    n_cond = cond_orb.shape[1]
    n_val = nv_blk * n_band
    npt_all = cond_orb.shape[2]
    k_points = k_dev * n_ka
    mu_blk, nu_blk = screened.shape
    own_pts = coulomb.shape[0]
    count_all = k_points * n_val * n_cond
    kernel_scale = 1.0 / (npt_all * math.sqrt(count_all))

    start_all = gather_all(start_vec, devices)
    val_cut = lax.all_to_all(
        val_orb.reshape(k_dev, nv_blk, n_ka, nu_blk).transpose(2, 0, 1, 3),
        "ka", split_axis=0, concat_axis=0, tiled=True,
    ).reshape(k_points, nv_blk, nu_blk)
    val_pts = lax.all_gather(val_cut, "band", axis=1, tiled=True)
    cond_local = lax.dynamic_slice_in_dim(cond_orb, band * mu_blk, mu_blk, 2)
    cond_pts = lax.all_gather(cond_local, "ka", axis=0, tiled=True)
    cond_rows = cond_orb.reshape(k_dev, n_cond, n_ka, n_band, own_pts)
    cond_rows = lax.dynamic_index_in_dim(cond_rows, band, 3, keepdims=False)
    cond_own = lax.all_to_all(
        cond_rows.transpose(2, 0, 1, 3), "ka", split_axis=0, concat_axis=0, tiled=True
    ).reshape(k_points, n_cond, own_pts)
    val_own = lax.dynamic_slice_in_dim(val_pts, band * own_pts, own_pts, 2)

    energy_gap = (cond_energy[:, None, :] - val_energy[:, :, None]).reshape(k_dev, pair_blk)
    start_sq = jnp.sum(start_all * start_all)
    current = start_all / jnp.sqrt(start_sq / count_all + 1e-06)
    previous = jnp.zeros_like(current)
    beta_val = jnp.float32(0.0)
    alphas = []
    betas = []
    for turn_index in range(STEPS):
        full_vec = (
            current.astype(BF)
            .reshape(n_ka, n_band, k_dev, nv_blk, n_cond)
            .transpose(0, 2, 1, 3, 4)
            .reshape(k_points, n_val, n_cond)
        )
        mixed_f = jnp.einsum("kvc,kvn->kcn", full_vec, val_pts, preferred_element_type=F32)
        mixed_own = lax.dynamic_slice_in_dim(mixed_f, band * own_pts, own_pts, 2)
        density_own = jnp.sum(mixed_own * cond_own.astype(F32), axis=(0, 1))
        density = gather_all(density_own.astype(BF), devices).reshape(npt_all)
        mixed_val = mixed_f.astype(BF)
        amp = jnp.einsum("kcm,kcn->mn", cond_pts, mixed_val, preferred_element_type=F32)
        kern = (screened.astype(F32) * amp * kernel_scale).astype(BF)
        folded = jnp.einsum("mn,kvn->kvm", kern, val_pts, preferred_element_type=F32).astype(BF)
        direct_part = jnp.einsum("kcm,kvm->kvc", cond_pts, folded, preferred_element_type=F32)
        potential = kernel_scale * jnp.dot(coulomb, density, preferred_element_type=F32)
        weighted = (val_own.astype(F32) * potential).astype(BF)
        exchange = jnp.einsum("kvp,kcp->kvc", weighted, cond_own, preferred_element_type=F32)
        part = 2.0 * exchange - direct_part
        arranged = (
            part.reshape(n_ka, k_dev, n_band, nv_blk, n_cond)
            .transpose(0, 2, 1, 3, 4)
            .reshape(devices, k_dev, pair_blk)
        )
        inter_own = jnp.sum(exchange_all(arranged), axis=0)
        current_own = lax.dynamic_index_in_dim(current, me, 0, keepdims=False)
        resid_vec = gather_all(energy_gap * current_own + inter_own, devices)
        resid_vec = resid_vec - beta_val * previous
        alpha_val = jnp.sum(current * resid_vec) / count_all
        resid_vec = resid_vec - alpha_val * current
        beta_val = jnp.sqrt(jnp.sum(resid_vec * resid_vec) / count_all + 1e-06)
        previous = current
        current = resid_vec / beta_val
        alphas.append(alpha_val)
        betas.append(beta_val)
    coeffs = jnp.stack(alphas + betas)
    return (lax.dynamic_index_in_dim(current, me, 0, keepdims=False), coeffs)


def per_device(*args):
    start_vec, _, _, val_orb, cond_orb, coulomb, screened = args
    n_ka, n_band = lax.axis_size("ka"), lax.axis_size("band")
    fits = (
        n_band == 8
        and n_ka & (n_ka - 1) == 0
        and start_vec.shape[0] % 2 == 1
        and val_orb.shape[1] == ROWS
        and cond_orb.shape[1] == HALF
        and start_vec.shape[0] * n_ka % 4 == 0
        and coulomb.shape[0] % LANES == 0
        and coulomb.shape[1] % 1024 == 0
        and screened.shape[0] % 512 == 0
        and screened.shape[1] % 1024 == 0
        and screened.shape[0] * screened.shape[1] <= 2 * MIB
    )
    return (kernel_path if fits else array_path)(*args)


def solution(mesh):
    in_specs = (
        P("ka", "band"),
        P("ka", "band"),
        P("ka", None),
        P("ka", "band", None),
        P("ka", None, None),
        P(("ka", "band"), None),
        P("band", "ka"),
    )
    out_specs = (P("ka", "band"), P())
    return jax.shard_map(
        per_device, mesh=mesh, in_specs=in_specs, out_specs=out_specs, check_vma=False
    )
```

```python
import functools
import math

import jax
import jax.numpy as jnp
from jax import lax
from jax.experimental import pallas as pl
from jax.experimental.pallas import tpu as pltpu
from jax.sharding import PartitionSpec as P

STEPS = 2
AXES = ("ka", "band")
BF, F32 = jnp.bfloat16, jnp.float32
LANES = 128
HALF = 64
ROWS = 8
MIB = 1 << 20
VMEM_ALL = 63_400_000

VMEM = pl.BlockSpec(memory_space=pltpu.VMEM)
SMEM = pl.BlockSpec(memory_space=pltpu.SMEM)
ANY = pl.BlockSpec(memory_space=pl.ANY)


def gather_all(block, devices):
    wide = jnp.broadcast_to(block[None], (devices,) + block.shape)
    return exchange_all(wide)


def exchange_all(parts):
    return lax.all_to_all(parts, AXES, split_axis=0, concat_axis=0, tiled=True)


def dot_nt(lhs, rhs):
    return lax.dot_general(lhs, rhs, (((1,), (1,)), ((), ())), preferred_element_type=F32)


def dot_tn(lhs, rhs):
    return lax.dot_general(lhs, rhs, (((0,), (0,)), ((), ())), preferred_element_type=F32)


def lane_half(tile, have, want):
    if have != want:
        tile = pltpu.roll(tile, HALF, axis=1)
    lane = lax.broadcasted_iota(jnp.int32, tile.shape, 1)
    keep = lane < HALF if want == 0 else lane >= HALF
    return jnp.where(keep, tile, 0.0)


def with_sums(block, sums):
    row = lax.broadcasted_iota(jnp.int32, block.shape, 0)
    lane = lax.broadcasted_iota(jnp.int32, block.shape, 1)
    free = row == block.shape[0] - ROWS
    for i, total in enumerate(sums):
        rest = jnp.full(block.shape, total, F32)
        for part in range(3):
            piece = rest.astype(BF).astype(F32)
            block = jnp.where(free & (lane == HALF + 3 * i + part), piece, block)
            rest = rest - piece
    return block


def read_sums(msgs_ref, count):
    rows = msgs_ref.shape[1]
    tile = jnp.sum(msgs_ref[...].astype(F32), axis=0)[rows - ROWS :, :]
    row = lax.broadcasted_iota(jnp.int32, tile.shape, 0)
    lane = lax.broadcasted_iota(jnp.int32, tile.shape, 1)
    out = []
    for i in range(count):
        mine = (row == 0) & (lane >= HALF + 3 * i) & (lane < HALF + 3 * i + 3)
        out.append(jnp.sum(jnp.where(mine, tile, 0.0), keepdims=True))
    return out


def piece_copies(refs, parts, column, width, dest, sems):
    copies = []
    for d, piece in enumerate(parts):
        row = 0
        for ref, start, rows in piece:
            copies.append(
                pltpu.make_async_copy(
                    refs[ref].at[pl.ds(start, rows), pl.ds(column, width)],
                    dest.at[d, pl.ds(row, rows), :],
                    sems.at[len(copies)],
                )
            )
            row += rows
    return copies


def start_all(copies):
    for copy in copies:
        copy.start()


def wait_all(copies):
    for copy in copies:
        copy.wait()


def device_at(n_band, j, d):
    ka = jnp.bitwise_xor(lax.axis_index("ka"), j)
    return ka * n_band + jnp.bitwise_xor(lax.axis_index("band"), d)


def own_copies(ref, dest, sems):
    return [
        pltpu.make_async_copy(
            ref.at[jnp.bitwise_xor(lax.axis_index("ka"), j)], dest.at[j], sems.at[j]
        )
        for j in range(dest.shape[0])
    ]


def pair_rows(ref, kp):
    part = ref[:, kp * 2 * ROWS : (kp + 1) * 2 * ROWS, :]
    return part.reshape(part.shape[0] * 2 * ROWS, part.shape[2])


def pack_kernel(n_ka, nu, *refs):
    start_in, cond_in, val_in, val_ref = refs[:4]
    own_ref, gap_ref, outs, refs = refs[4], refs[5], refs[6 : 6 + n_ka], refs[6 + n_ka :]
    start_ref, cond_ref, energy_ref, sems, val_sems = refs
    ins = ((start_in, start_ref), (cond_in, cond_ref), (val_in, energy_ref))
    small = [pltpu.make_async_copy(ref, to, sems.at[i]) for i, (ref, to) in enumerate(ins)]
    k_dev = val_ref.shape[0]
    val_copies = []
    for j in range(n_ka):
        at = pl.multiple_of(jnp.bitwise_xor(lax.axis_index("ka"), j) * nu, nu)
        val_copies.append(
            pltpu.make_async_copy(
                val_ref.at[:, :, pl.ds(at, nu)], outs[j].at[:, :, pl.ds(0, nu)], val_sems.at[j]
            )
        )
    start_all(small + val_copies)
    wait_all(small)
    own_ref[...] = jnp.zeros_like(own_ref)
    gap_ref[...] = jnp.zeros_like(gap_ref)
    cond = jnp.concatenate([cond_ref[...], cond_ref[...]], axis=1)
    for kl in range(k_dev):
        half = kl % 2
        for v in range(ROWS):
            at = pl.ds(kl // 2 * ROWS + v, 1)
            row = start_ref[pl.ds(kl, 1), pl.ds(v // 2 * LANES, LANES)]
            own_ref[at, :] = own_ref[at, :] + lane_half(row, v % 2, half)
            gap = cond[kl : kl + 1, :] - energy_ref[kl, v]
            gap_ref[at, :] = gap_ref[at, :] + lane_half(gap, half, half)
    mine = own_ref[...]
    square = mine * mine
    block = with_sums(mine, [jnp.sum(square), jnp.sum(gap_ref[...] * square)])
    for j in range(n_ka):
        for g in range(k_dev):
            head = jnp.zeros((ROWS, LANES), F32)
            if (g + 1) * ROWS <= block.shape[0]:
                head = block[g * ROWS : (g + 1) * ROWS, :]
            outs[j][g, :, nu:] = head.astype(BF)
    wait_all(val_copies)


def cut_kernel(cond_ref, out_ref, sems):
    n_ka, _, own = out_ref.shape
    k_dev, n_cond, npt = cond_ref.shape
    copies = []
    for z in range(n_ka):
        at = z * (npt // n_ka) + lax.axis_index("band") * own
        for kl in range(k_dev):
            copies.append(
                pltpu.make_async_copy(
                    cond_ref.at[kl, :, pl.ds(pl.multiple_of(at, LANES), own)],
                    out_ref.at[z, pl.ds(kl * n_cond, n_cond), :],
                    sems.at[len(copies)],
                )
            )
    start_all(copies)
    wait_all(copies)


def turn_kernel(tile, scr_ref, out_ref, scrs, turned, in_sems, out_sems):
    nu = scr_ref.shape[1]
    ins, outs = [], []
    for j in range(nu // tile):
        at = pl.ds(j * tile, tile)
        ins.append(pltpu.make_async_copy(scr_ref.at[:, at], scrs.at[:, at], in_sems.at[j]))
        outs.append(pltpu.make_async_copy(turned.at[at, :], out_ref.at[at, :], out_sems.at[j]))
    start_all(ins)
    for j in range(nu // tile):
        ins[j].wait()
        turned[j * tile : (j + 1) * tile, :] = scrs[:, j * tile : (j + 1) * tile].T
        outs[j].start()
    wait_all(outs)


def order_kernel(parts, n_ka, *refs):
    val_refs, refs = refs[:-10], refs[-10:]
    rows_out, turned_out, own_out, msgs_out, vals, heads, ordered, turned, val_sems, out_sems = refs
    own = own_out.shape[1]
    nu = ordered.shape[1]
    copies = piece_copies(val_refs, parts, 0, nu, vals, val_sems.at[0])
    head_copies = piece_copies(val_refs, parts, nu, LANES, heads, val_sems.at[1])
    start_all(copies + head_copies)
    wait_all(copies)
    n_band, group = vals.shape[0], vals.shape[0] * 2 * ROWS
    column = pl.multiple_of(lax.axis_index("band") * own, LANES)
    outs = []
    for kp in range(ordered.shape[0] // group):
        at = slice(kp * group, (kp + 1) * group)
        ordered[at, :] = pair_rows(vals, kp)
        turned[:, at] = ordered[at, :].T
        at = pl.ds(kp * group, group)
        outs += [
            pltpu.make_async_copy(ordered.at[at, :], rows_out.at[at, :], out_sems.at[0, kp]),
            pltpu.make_async_copy(turned.at[:, at], turned_out.at[:, at], out_sems.at[1, kp]),
            pltpu.make_async_copy(
                ordered.at[at, pl.ds(column, own)], own_out.at[at, :], out_sems.at[2, kp]
            ),
        ]
        start_all(outs[-3:])
    wait_all(head_copies)
    rows = msgs_out.shape[1]
    step = heads.shape[1] // n_ka
    for d in range(n_band):
        head = heads[d].astype(F32)
        for j in range(n_ka):
            msgs_out[device_at(n_band, j, d)] = head[j * step : j * step + rows, :].astype(BF)
    wait_all(outs)


def density_kernel(cfg, *refs):
    n_ka, n_band, k_dev = cfg
    k_points = n_ka * k_dev
    msgs_ref, vown_ref, cond_ref, qx_ref, rho_ref, xs, msgs, vown, conds, sems = refs
    own = vown_ref.shape[1]
    msg_copy = pltpu.make_async_copy(msgs_ref, msgs, sems.at[n_ka])
    copies = own_copies(cond_ref, conds, sems)
    copies.append(pltpu.make_async_copy(vown_ref, vown, sems.at[n_ka + 1]))
    start_all([msg_copy] + copies)
    xs[...] = jnp.zeros_like(xs)
    msg_copy.wait()
    for d in range(n_band):
        for k in range(k_points):
            j, kl = divmod(k, k_dev)
            tile = msgs[device_at(n_band, j, d), :, :].astype(F32)
            tile = tile[kl // 2 * ROWS : (kl // 2 + 1) * ROWS, :]
            base = k // 2 % 2 * LANES
            at = pl.ds(base + d * 2 * ROWS + k % 2 * ROWS, ROWS)
            xs[k // 4, at, pl.ds(base, LANES)] = lane_half(tile, kl % 2, k % 2)
    qx_ref[...] = xs[...].astype(BF)
    wait_all(copies)
    cond_rows = conds[...].reshape(-1, own)
    rho = jnp.zeros((1, own), F32)
    quad = 2 * LANES
    for kq in range(k_points // 4):
        at = slice(kq * quad, (kq + 1) * quad)
        mixed = dot_tn(qx_ref[kq], vown[at, :])
        rho = rho + jnp.sum(mixed * cond_rows[at, :].astype(F32), axis=0, keepdims=True)
    for r in range(own // LANES):
        part = rho[:, r * LANES : (r + 1) * LANES]
        rho_ref[:, r, :] = jnp.broadcast_to(part, (rho_ref.shape[0], LANES))


def direct_kernel(n_ka, tile, scale, *refs):
    turned_ref, scr_ref, rows_ref, qx_ref, refs = refs[0], refs[1], refs[2], refs[3], refs[4:]
    cond_refs, refs = refs[:n_ka], refs[n_ka:]
    di_ref, qx, turned, conds, scrs, vals, mixed, kern, folded = refs[:9]
    qx_sem, cond_sems, row_sems, chunk_sems = refs[9:]
    nu, mu = scr_ref.shape
    quad = 2 * LANES
    qx_copy = pltpu.make_async_copy(qx_ref, qx, qx_sem.at[0])
    cond_copies = [
        pltpu.make_async_copy(ref, conds.at[j], cond_sems.at[j]) for j, ref in enumerate(cond_refs)
    ]
    turned_copies = []
    for i in range(nu // tile):
        at = pl.ds(i * tile, tile)
        turned_copies.append(
            pltpu.make_async_copy(turned_ref.at[at, :], turned.at[at, :], chunk_sems.at[i])
        )
    scr_copy = pltpu.make_async_copy(scr_ref, scrs, row_sems.at[0])
    row_copy = pltpu.make_async_copy(rows_ref, vals, row_sems.at[1])
    start_all([qx_copy] + turned_copies + cond_copies + [scr_copy, row_copy])
    qx_copy.wait()
    for i in range(nu // tile):
        rows = slice(i * tile, (i + 1) * tile)
        turned_copies[i].wait()
        for kq in range(qx.shape[0]):
            cols = slice(kq * quad, (kq + 1) * quad)
            mixed[rows, cols] = jnp.dot(
                turned[rows, cols], qx[kq], preferred_element_type=F32
            ).astype(BF)
    wait_all(cond_copies)
    cond_rows = conds[...].reshape(-1, mu)
    scr_copy.wait()
    amp = jnp.dot(mixed[...], cond_rows, preferred_element_type=F32)
    kern[...] = (scrs[...].astype(F32) * amp).astype(BF)
    row_copy.wait()
    folded[...] = jnp.dot(vals[...], kern[...], preferred_element_type=F32).astype(BF)
    for kq in range(qx.shape[0]):
        at = slice(kq * quad, (kq + 1) * quad)
        both = scale * dot_nt(folded[at, :], cond_rows[at, :])
        di_ref[2 * kq] = both[:LANES, :LANES]
        di_ref[2 * kq + 1] = both[LANES:, LANES:]


def exchange_kernel(cfg, chunk, scale, *refs):
    n_ka, n_band, k_dev = cfg
    k_points = n_ka * k_dev
    rho_ref, di_ref, coul_ref, vown_ref, cond_ref, msg_ref = refs[:6]
    rhos, di, coul, conds, vown, part, msg, coul_sems, sems = refs[6:]
    rho_copy = pltpu.make_async_copy(rho_ref, rhos, sems.at[n_ka])
    own, npt = coul_ref.shape
    coul_copies = [
        pltpu.make_async_copy(
            coul_ref.at[:, pl.ds(i * chunk, chunk)], coul.at[:, pl.ds(i * chunk, chunk)], coul_sems.at[i]
        )
        for i in range(npt // chunk)
    ]
    copies = own_copies(cond_ref, conds, sems)
    copies.append(pltpu.make_async_copy(vown_ref, vown, sems.at[n_ka + 1]))
    copies.append(pltpu.make_async_copy(di_ref, di, sems.at[n_ka + 2]))
    start_all([rho_copy] + coul_copies + copies)
    rho_copy.wait()
    acc = jnp.zeros((own, LANES), F32)
    per_dev = own // LANES
    for i in range(npt // chunk):
        coul_copies[i].wait()
        for j in range(i * chunk // LANES, (i + 1) * chunk // LANES):
            rho = rhos[j // per_dev, pl.ds(j % per_dev, 1), :].astype(BF).astype(F32)
            acc = acc + coul[:, j * LANES : (j + 1) * LANES].astype(F32) * rho
    potential = scale * jnp.sum(acc.T, axis=0, keepdims=True)
    wait_all(copies)
    cond_rows = conds[...].reshape(-1, own)
    for kp in range(k_points // 2):
        at = slice(kp * LANES, (kp + 1) * LANES)
        weighted = (vown[at, :].astype(F32) * potential).astype(BF)
        part[kp] = 2.0 * dot_nt(weighted, cond_rows[at, :]) - di[kp]
    for d in range(n_band):
        for j in range(n_ka):
            for g in range((k_dev + 1) // 2):
                tile = None
                for kl in range(2 * g, min(2 * g + 2, k_dev)):
                    k = j * k_dev + kl
                    piece = part[k // 2, pl.ds(d * 2 * ROWS + k % 2 * ROWS, ROWS), :]
                    piece = lane_half(piece, k % 2, kl % 2)
                    tile = piece if tile is None else tile + piece
                msg[device_at(n_band, j, d), pl.ds(g * ROWS, ROWS), :] = tile
    msg_ref[...] = msg[...].astype(BF)


def write_rows(ref, values):
    for i, value in enumerate(values):
        ref[i : i + 1, :] = jnp.broadcast_to(value, (1, ref.shape[1]))


def received(recv_ref):
    return jnp.sum(recv_ref[...].astype(F32), axis=0)


def shifted(count_all, shift, square, cross_sum, square_sum):
    alpha = shift * square + cross_sum / count_all
    d = alpha - shift
    mean_sq = (square_sum - 2.0 * d * cross_sum) / count_all + d * d * square
    mean_sq = jnp.maximum(mean_sq, 0.0)
    return alpha, d, mean_sq


def first_owner_kernel(count_all, recv_ref, msgs_ref, gap_ref, own_ref, state_ref, coef_ref, msg_ref):
    start_sq, gap_sq = read_sums(msgs_ref, 2)
    norm = start_sq / count_all
    inv = 1.0 / jnp.sqrt(norm + 1e-06)
    square = norm / (norm + 1e-06)
    shift = gap_sq / jnp.maximum(start_sq, 1e-30)
    cur = own_ref[...] * inv
    inter = received(recv_ref) * inv
    gap = gap_ref[...]
    resid = (gap - shift) * cur + inter
    state_ref[0] = cur
    state_ref[1] = resid
    state_ref[2] = inter
    write_rows(coef_ref, (shift, square, gap_sq * inv * inv))
    sums = [
        jnp.sum(cur * resid),
        jnp.sum(resid * resid),
        jnp.sum(gap * resid * resid),
        jnp.sum(gap * resid * cur),
    ]
    msg_ref[...] = jnp.broadcast_to(with_sums(resid, sums).astype(BF)[None], msg_ref.shape)


def second_owner_kernel(count_all, recv_ref, msgs_ref, gap_ref, state_ref, coef_ref, out_ref, coef_out, msg_ref):
    cross, total, gap_rr, gap_rq = read_sums(msgs_ref, 4)
    alpha, d, mean_sq = shifted(count_all, coef_ref[0:1, 0:1], coef_ref[1:2, 0:1], cross, total)
    beta = jnp.sqrt(mean_sq + 1e-06)
    square = mean_sq / (mean_sq + 1e-06)
    gap_qq = gap_rr - 2.0 * d * gap_rq + d * d * coef_ref[2:3, 0:1]
    shift = gap_qq / (mean_sq + 1e-06) / count_all
    prev = state_ref[0]
    cur = (state_ref[1] - d * prev) / beta
    inter = (received(recv_ref) - d * state_ref[2]) / beta
    resid = (gap_ref[...] - shift) * cur + inter - beta * prev
    out_ref[0] = cur
    out_ref[1] = resid
    write_rows(coef_out, (alpha, beta, shift, square))
    dims = msg_ref.shape[:1] + msg_ref.shape[2:]
    msg_ref[:, 0, :] = jnp.full(dims, jnp.sum(cur * resid), F32)
    msg_ref[:, 1, :] = jnp.full(dims, jnp.sum(resid * resid), F32)


def finish_kernel(count_all, msgs_ref, state_ref, coef_ref, out_ref, coeffs_ref):
    sums = jnp.sum(msgs_ref[...], axis=0)
    alpha, d, mean_sq = shifted(count_all, coef_ref[2:3, 0:1], coef_ref[3:4, 0:1], sums[0:1, 0:1], sums[1:2, 0:1])
    beta = jnp.sqrt(mean_sq + 1e-06)
    own = (state_ref[1] - d * state_ref[0]) / beta
    coeffs_ref[0] = coef_ref[0, 0]
    coeffs_ref[1] = alpha[0, 0]
    coeffs_ref[2] = coef_ref[1, 0]
    coeffs_ref[3] = beta[0, 0]
    for kl in range(out_ref.shape[0]):
        tile = own[kl // 2 * ROWS : (kl // 2 + 1) * ROWS, :]
        other = pltpu.roll(tile, HALF, axis=1)
        left, right = (tile, other) if kl % 2 == 0 else (other, tile)
        low = lax.broadcasted_iota(jnp.int32, (1, LANES), 1) < HALF
        for j in range(ROWS // 2):
            row = jnp.where(low, left[2 * j : 2 * j + 1], right[2 * j + 1 : 2 * j + 2])
            out_ref[pl.ds(kl, 1), pl.ds(j * LANES, LANES)] = row


def shape_of(dims, kind=F32):
    return jax.ShapeDtypeStruct(dims, kind)


def call(kernel, name, out_shape, in_specs, out_specs, scratch=(), mib=None, flops=0, moved=0):
    return pl.pallas_call(
        kernel,
        out_shape=out_shape,
        in_specs=in_specs,
        out_specs=out_specs,
        scratch_shapes=list(scratch),
        compiler_params=pltpu.CompilerParams(vmem_limit_bytes=mib * MIB if mib else VMEM_ALL),
        cost_estimate=pl.CostEstimate(flops=flops, bytes_accessed=moved, transcendentals=0),
        name=name,
    )


def dma(*dims):
    return pltpu.SemaphoreType.DMA(dims)


def swap(block, axis, d):
    return lax.ppermute(block, axis, [(i, i ^ d) for i in range(lax.axis_size(axis))])


def plane_pieces(own_piece, others):
    def move(block, d):
        return swap(block, "band", d)

    rows = own_piece.shape[0]
    half = rows // 2
    by_x, by_y, core = move(own_piece, 2), move(own_piece, 4), move(own_piece, 1)
    by_x, by_y, others = lax.optimization_barrier((by_x, by_y, others))
    diag = [move(by_x[:half], 4), move(by_y[half:], 2)]
    near_x, near_y = move(by_x, 1), move(by_y, 1)
    far = [move(part, 1) for part in diag]
    arrays = [own_piece, core, by_x, near_x, by_y, near_y] + diag + far
    parts = tuple(((i, 0, rows),) for i in range(6))
    parts += (((6, 0, half), (7, 0, half)), ((8, 0, half), (9, 0, half)))
    return arrays, parts, others


def kernel_path(start_vec, val_energy, cond_energy, val_orb, cond_orb, coulomb, screened):
    n_ka = lax.axis_size("ka")
    n_band = lax.axis_size("band")
    devices = n_ka * n_band
    ka, band = lax.axis_index("ka"), lax.axis_index("band")
    k_dev = start_vec.shape[0]
    nv_blk = val_orb.shape[1]
    n_cond = cond_orb.shape[1]
    npt_all = cond_orb.shape[2]
    k_points = k_dev * n_ka
    pairs = k_points // 2
    mu_blk, nu_blk = screened.shape
    own = coulomb.shape[0]
    count_all = k_points * nv_blk * n_band * n_cond
    scale = 1.0 / (npt_all * math.sqrt(count_all))
    piece_rows = k_points * nv_blk

    block = ((k_dev + 1) // 2 * ROWS, LANES)
    msg_shape = shape_of((devices,) + block, BF)
    wide = nu_blk + LANES
    start_own, gap, *payloads = call(
        functools.partial(pack_kernel, n_ka, nu_blk),
        "pack",
        (shape_of(block), shape_of(block)) + (shape_of((k_dev, nv_blk, wide), BF),) * n_ka,
        [ANY] * 4,
        (VMEM,) * (2 + n_ka),
        [
            pltpu.VMEM(start_vec.shape, F32),
            pltpu.VMEM(cond_energy.shape, F32),
            pltpu.SMEM(val_energy.shape, F32),
            dma(3),
            dma(n_ka),
        ],
    )(start_vec, cond_energy, val_energy, val_orb)
    base, payloads = lax.optimization_barrier((band * mu_blk, payloads))
    got = [payloads[0]] + [swap(payloads[j], "ka", j) for j in range(1, n_ka)]
    own_rows = k_dev * n_cond
    cuts = call(
        cut_kernel,
        "cut",
        shape_of((n_ka, own_rows, own), BF),
        [ANY],
        VMEM,
        [dma(n_ka * k_dev)],
    )(cond_orb)
    cond_local = lax.dynamic_slice_in_dim(cond_orb, base, mu_blk, 2)
    cond_local = cond_local.reshape(k_dev * n_cond, mu_blk)
    got, cuts, cond_local = lax.optimization_barrier((got, cuts, cond_local))
    val_cut = jnp.concatenate(got, axis=0).reshape(piece_rows, wide)
    cond_pts = [cond_local] + [swap(cond_local, "ka", j) for j in range(1, n_ka)]
    cond_own = lax.all_to_all(cuts, "ka", split_axis=0, concat_axis=0, tiled=True)

    chunk, tile = 1024, nu_blk // 4
    rows_all, conds_all = k_points * nv_blk * n_band, k_points * n_cond
    scr_turned = call(
        functools.partial(turn_kernel, nu_blk // 4),
        "turn",
        shape_of((nu_blk, mu_blk), BF),
        [ANY],
        ANY,
        [pltpu.VMEM((mu_blk, nu_blk), BF), pltpu.VMEM((nu_blk, mu_blk), BF)]
        + [dma(4)] * 2,
        moved=8 * MIB,
    )(screened)
    pieces, parts, scr_turned = plane_pieces(val_cut, scr_turned)
    pieces, cond_pts[1:-1] = lax.optimization_barrier((pieces, cond_pts[1:-1]))
    val_rows, val_turned, val_own, msgs = call(
        functools.partial(order_kernel, parts, n_ka),
        "order",
        (
            shape_of((rows_all, nu_blk), BF),
            shape_of((nu_blk, rows_all), BF),
            shape_of((rows_all, own), BF),
            msg_shape,
        ),
        [ANY] * len(pieces),
        (ANY, ANY, ANY, VMEM),
        [
            pltpu.VMEM((n_band, piece_rows, nu_blk), BF),
            pltpu.VMEM((n_band, piece_rows, LANES), BF),
            pltpu.VMEM((rows_all, nu_blk), BF),
            pltpu.VMEM((nu_blk, rows_all), BF),
            dma(2, sum(len(piece) for piece in parts)),
            dma(3, pairs),
        ],
        moved=9 * MIB,
    )(*pieces)

    cfg = (n_ka, n_band, k_dev)
    quads = k_points // 4
    state, coef = None, None
    for step in range(STEPS):
        first = step == 0
        qx, rho = call(
            functools.partial(density_kernel, cfg),
            "density",
            (
                shape_of((quads, 2 * LANES, 2 * LANES), BF),
                shape_of((devices, own // LANES, LANES)),
            ),
            [ANY] * 3,
            (VMEM, VMEM),
            [
                pltpu.VMEM((quads, 2 * LANES, 2 * LANES), F32),
                pltpu.VMEM((devices,) + block, BF),
                pltpu.VMEM((rows_all, own), BF),
                pltpu.VMEM((n_ka, own_rows, own), BF),
                dma(n_ka + 2),
            ],
        )(msgs, val_own, cond_own)
        density = exchange_all(rho)
        direct = call(
            functools.partial(direct_kernel, n_ka, tile, scale),
            "direct",
            shape_of((pairs, LANES, LANES)),
            [ANY] * (4 + n_ka),
            VMEM,
            [
                pltpu.VMEM((quads, 2 * LANES, 2 * LANES), BF),
                pltpu.VMEM((nu_blk, rows_all), BF),
                pltpu.VMEM((n_ka, k_dev * n_cond, mu_blk), BF),
                pltpu.VMEM((nu_blk, mu_blk), BF),
                pltpu.VMEM((rows_all, nu_blk), BF),
                pltpu.VMEM((nu_blk, conds_all), BF),
                pltpu.VMEM((nu_blk, mu_blk), BF),
                pltpu.VMEM((rows_all, mu_blk), BF),
                dma(1),
                dma(n_ka),
                dma(2),
                dma(nu_blk // tile),
            ],
            flops=4 * mu_blk * nu_blk * conds_all,
            moved=12 * MIB,
        )(val_turned, scr_turned, val_rows, qx, *cond_pts)
        summed = call(
            functools.partial(exchange_kernel, cfg, chunk, scale),
            "exchange",
            msg_shape,
            [ANY] * 5,
            VMEM,
            [
                pltpu.VMEM((devices, own // LANES, LANES), F32),
                pltpu.VMEM((pairs, LANES, LANES), F32),
                pltpu.VMEM((own, npt_all), BF),
                pltpu.VMEM((n_ka, own_rows, own), BF),
                pltpu.VMEM((rows_all, own), BF),
                pltpu.VMEM((pairs, LANES, LANES), F32),
                pltpu.VMEM((devices,) + block, F32),
                dma(npt_all // chunk),
                dma(n_ka + 3),
            ],
        )(density, direct, coulomb, val_own, cond_own)
        recv = exchange_all(summed)
        if first:
            state, coef, message = call(
                functools.partial(first_owner_kernel, count_all),
                "first_owner",
                (shape_of((3,) + block), shape_of((ROWS, LANES)), msg_shape),
                [VMEM] * 4,
                (VMEM, VMEM, VMEM),
                mib=8,
            )(recv, msgs, gap, start_own)
        else:
            state, coef, message = call(
                functools.partial(second_owner_kernel, count_all),
                "second_owner",
                (shape_of((2,) + block), shape_of((ROWS, LANES)), shape_of((devices, 2, LANES))),
                [VMEM] * 5,
                (VMEM, VMEM, VMEM),
                mib=8,
            )(recv, msgs, gap, state, coef)
        msgs = exchange_all(message)
    return call(
        functools.partial(finish_kernel, count_all),
        "finish",
        (shape_of(start_vec.shape), shape_of((2 * STEPS,))),
        [VMEM] * 3,
        (VMEM, SMEM),
        mib=8,
    )(msgs, state, coef)


def array_path(start_vec, val_energy, cond_energy, val_orb, cond_orb, coulomb, screened):
    n_ka = lax.axis_size("ka")
    n_band = lax.axis_size("band")
    devices = n_ka * n_band
    ka, band = lax.axis_index("ka"), lax.axis_index("band")
    me = ka * n_band + band
    k_dev, pair_blk = start_vec.shape
    nv_blk = val_orb.shape[1]
    n_cond = cond_orb.shape[1]
    n_val = nv_blk * n_band
    npt_all = cond_orb.shape[2]
    k_points = k_dev * n_ka
    mu_blk, nu_blk = screened.shape
    own_pts = coulomb.shape[0]
    count_all = k_points * n_val * n_cond
    kernel_scale = 1.0 / (npt_all * math.sqrt(count_all))

    start_all = gather_all(start_vec, devices)
    val_cut = lax.all_to_all(
        val_orb.reshape(k_dev, nv_blk, n_ka, nu_blk).transpose(2, 0, 1, 3),
        "ka", split_axis=0, concat_axis=0, tiled=True,
    ).reshape(k_points, nv_blk, nu_blk)
    val_pts = lax.all_gather(val_cut, "band", axis=1, tiled=True)
    cond_local = lax.dynamic_slice_in_dim(cond_orb, band * mu_blk, mu_blk, 2)
    cond_pts = lax.all_gather(cond_local, "ka", axis=0, tiled=True)
    cond_rows = cond_orb.reshape(k_dev, n_cond, n_ka, n_band, own_pts)
    cond_rows = lax.dynamic_index_in_dim(cond_rows, band, 3, keepdims=False)
    cond_own = lax.all_to_all(
        cond_rows.transpose(2, 0, 1, 3), "ka", split_axis=0, concat_axis=0, tiled=True
    ).reshape(k_points, n_cond, own_pts)
    val_own = lax.dynamic_slice_in_dim(val_pts, band * own_pts, own_pts, 2)

    energy_gap = (cond_energy[:, None, :] - val_energy[:, :, None]).reshape(k_dev, pair_blk)
    start_sq = jnp.sum(start_all * start_all)
    current = start_all / jnp.sqrt(start_sq / count_all + 1e-06)
    previous = jnp.zeros_like(current)
    beta_val = jnp.float32(0.0)
    alphas = []
    betas = []
    for turn_index in range(STEPS):
        full_vec = (
            current.astype(BF)
            .reshape(n_ka, n_band, k_dev, nv_blk, n_cond)
            .transpose(0, 2, 1, 3, 4)
            .reshape(k_points, n_val, n_cond)
        )
        mixed_f = jnp.einsum("kvc,kvn->kcn", full_vec, val_pts, preferred_element_type=F32)
        mixed_own = lax.dynamic_slice_in_dim(mixed_f, band * own_pts, own_pts, 2)
        density_own = jnp.sum(mixed_own * cond_own.astype(F32), axis=(0, 1))
        density = gather_all(density_own.astype(BF), devices).reshape(npt_all)
        mixed_val = mixed_f.astype(BF)
        amp = jnp.einsum("kcm,kcn->mn", cond_pts, mixed_val, preferred_element_type=F32)
        kern = (screened.astype(F32) * amp * kernel_scale).astype(BF)
        folded = jnp.einsum("mn,kvn->kvm", kern, val_pts, preferred_element_type=F32).astype(BF)
        direct_part = jnp.einsum("kcm,kvm->kvc", cond_pts, folded, preferred_element_type=F32)
        potential = kernel_scale * jnp.dot(coulomb, density, preferred_element_type=F32)
        weighted = (val_own.astype(F32) * potential).astype(BF)
        exchange = jnp.einsum("kvp,kcp->kvc", weighted, cond_own, preferred_element_type=F32)
        part = 2.0 * exchange - direct_part
        arranged = (
            part.reshape(n_ka, k_dev, n_band, nv_blk, n_cond)
            .transpose(0, 2, 1, 3, 4)
            .reshape(devices, k_dev, pair_blk)
        )
        inter_own = jnp.sum(exchange_all(arranged), axis=0)
        current_own = lax.dynamic_index_in_dim(current, me, 0, keepdims=False)
        resid_vec = gather_all(energy_gap * current_own + inter_own, devices)
        resid_vec = resid_vec - beta_val * previous
        alpha_val = jnp.sum(current * resid_vec) / count_all
        resid_vec = resid_vec - alpha_val * current
        beta_val = jnp.sqrt(jnp.sum(resid_vec * resid_vec) / count_all + 1e-06)
        previous = current
        current = resid_vec / beta_val
        alphas.append(alpha_val)
        betas.append(beta_val)
    coeffs = jnp.stack(alphas + betas)
    return (lax.dynamic_index_in_dim(current, me, 0, keepdims=False), coeffs)


def per_device(*args):
    start_vec, _, _, val_orb, cond_orb, coulomb, screened = args
    n_ka, n_band = lax.axis_size("ka"), lax.axis_size("band")
    fits = (
        n_band == 8
        and n_ka & (n_ka - 1) == 0
        and start_vec.shape[0] % 2 == 1
        and val_orb.shape[1] == ROWS
        and cond_orb.shape[1] == HALF
        and start_vec.shape[0] * n_ka % 4 == 0
        and coulomb.shape[0] % LANES == 0
        and coulomb.shape[1] % 1024 == 0
        and screened.shape[0] % 512 == 0
        and screened.shape[1] % 1024 == 0
        and screened.shape[0] * screened.shape[1] <= 2 * MIB
    )
    return (kernel_path if fits else array_path)(*args)


def solution(mesh):
    in_specs = (
        P("ka", "band"),
        P("ka", "band"),
        P("ka", None),
        P("ka", "band", None),
        P("ka", None, None),
        P(("ka", "band"), None),
        P("band", "ka"),
    )
    out_specs = (P("ka", "band"), P())
    return jax.shard_map(
        per_device, mesh=mesh, in_specs=in_specs, out_specs=out_specs, check_vma=False
    )
```

```python
import functools
import math

import jax
import jax.numpy as jnp
from jax import lax
from jax.experimental import pallas as pl
from jax.experimental.pallas import tpu as pltpu
from jax.sharding import PartitionSpec as P

STEPS = 2
AXES = ("ka", "band")
BF, F32 = jnp.bfloat16, jnp.float32
LANES = 128
HALF = 64
ROWS = 8
MIB = 1 << 20
VMEM_ALL = 63_400_000

VMEM = pl.BlockSpec(memory_space=pltpu.VMEM)
SMEM = pl.BlockSpec(memory_space=pltpu.SMEM)
ANY = pl.BlockSpec(memory_space=pl.ANY)


def gather_all(block, devices):
    wide = jnp.broadcast_to(block[None], (devices,) + block.shape)
    return exchange_all(wide)


def exchange_all(parts):
    return lax.all_to_all(parts, AXES, split_axis=0, concat_axis=0, tiled=True)


def dot_nt(lhs, rhs):
    return lax.dot_general(lhs, rhs, (((1,), (1,)), ((), ())), preferred_element_type=F32)


def dot_tn(lhs, rhs):
    return lax.dot_general(lhs, rhs, (((0,), (0,)), ((), ())), preferred_element_type=F32)


def lane_half(tile, have, want):
    if have != want:
        tile = pltpu.roll(tile, HALF, axis=1)
    lane = lax.broadcasted_iota(jnp.int32, tile.shape, 1)
    keep = lane < HALF if want == 0 else lane >= HALF
    return jnp.where(keep, tile, 0.0)


def with_sums(block, sums):
    row = lax.broadcasted_iota(jnp.int32, block.shape, 0)
    lane = lax.broadcasted_iota(jnp.int32, block.shape, 1)
    free = row == block.shape[0] - ROWS
    for i, total in enumerate(sums):
        rest = jnp.full(block.shape, total, F32)
        for part in range(3):
            piece = rest.astype(BF).astype(F32)
            block = jnp.where(free & (lane == HALF + 3 * i + part), piece, block)
            rest = rest - piece
    return block


def read_sums(msgs_ref, count):
    rows = msgs_ref.shape[1]
    tile = jnp.sum(msgs_ref[...].astype(F32), axis=0)[rows - ROWS :, :]
    row = lax.broadcasted_iota(jnp.int32, tile.shape, 0)
    lane = lax.broadcasted_iota(jnp.int32, tile.shape, 1)
    out = []
    for i in range(count):
        mine = (row == 0) & (lane >= HALF + 3 * i) & (lane < HALF + 3 * i + 3)
        out.append(jnp.sum(jnp.where(mine, tile, 0.0), keepdims=True))
    return out


def piece_copies(refs, parts, column, width, dest, sems):
    copies = []
    for d, piece in enumerate(parts):
        row = 0
        for ref, start, rows in piece:
            copies.append(
                pltpu.make_async_copy(
                    refs[ref].at[pl.ds(start, rows), pl.ds(column, width)],
                    dest.at[d, pl.ds(row, rows), :],
                    sems.at[len(copies)],
                )
            )
            row += rows
    return copies


def start_all(copies):
    for copy in copies:
        copy.start()


def wait_all(copies):
    for copy in copies:
        copy.wait()


def device_at(n_band, j, d):
    ka = jnp.bitwise_xor(lax.axis_index("ka"), j)
    return ka * n_band + jnp.bitwise_xor(lax.axis_index("band"), d)


def own_copies(ref, dest, sems):
    return [
        pltpu.make_async_copy(
            ref.at[jnp.bitwise_xor(lax.axis_index("ka"), j)], dest.at[j], sems.at[j]
        )
        for j in range(dest.shape[0])
    ]


def pair_rows(ref, kp):
    part = ref[:, kp * 2 * ROWS : (kp + 1) * 2 * ROWS, :]
    return part.reshape(part.shape[0] * 2 * ROWS, part.shape[2])


def pack_kernel(n_ka, nu, *refs):
    start_in, cond_in, val_in, val_ref = refs[:4]
    own_ref, gap_ref, outs, refs = refs[4], refs[5], refs[6 : 6 + n_ka], refs[6 + n_ka :]
    start_ref, cond_ref, energy_ref, sems, val_sems = refs
    ins = ((start_in, start_ref), (cond_in, cond_ref), (val_in, energy_ref))
    small = [pltpu.make_async_copy(ref, to, sems.at[i]) for i, (ref, to) in enumerate(ins)]
    k_dev = val_ref.shape[0]
    val_copies = []
    for j in range(n_ka):
        at = pl.multiple_of(jnp.bitwise_xor(lax.axis_index("ka"), j) * nu, nu)
        val_copies.append(
            pltpu.make_async_copy(
                val_ref.at[:, :, pl.ds(at, nu)], outs[j].at[:, :, pl.ds(0, nu)], val_sems.at[j]
            )
        )
    start_all(small + val_copies)
    wait_all(small)
    own_ref[...] = jnp.zeros_like(own_ref)
    gap_ref[...] = jnp.zeros_like(gap_ref)
    cond = jnp.concatenate([cond_ref[...], cond_ref[...]], axis=1)
    for kl in range(k_dev):
        half = kl % 2
        for v in range(ROWS):
            at = pl.ds(kl // 2 * ROWS + v, 1)
            row = start_ref[pl.ds(kl, 1), pl.ds(v // 2 * LANES, LANES)]
            own_ref[at, :] = own_ref[at, :] + lane_half(row, v % 2, half)
            gap = cond[kl : kl + 1, :] - energy_ref[kl, v]
            gap_ref[at, :] = gap_ref[at, :] + lane_half(gap, half, half)
    mine = own_ref[...]
    square = mine * mine
    block = with_sums(mine, [jnp.sum(square), jnp.sum(gap_ref[...] * square)])
    for j in range(n_ka):
        for g in range(k_dev):
            head = jnp.zeros((ROWS, LANES), F32)
            if (g + 1) * ROWS <= block.shape[0]:
                head = block[g * ROWS : (g + 1) * ROWS, :]
            outs[j][g, :, nu:] = head.astype(BF)
    wait_all(val_copies)


def cut_kernel(cond_ref, out_ref, sems):
    n_ka, _, own = out_ref.shape
    k_dev, n_cond, npt = cond_ref.shape
    copies = []
    for z in range(n_ka):
        at = z * (npt // n_ka) + lax.axis_index("band") * own
        for kl in range(k_dev):
            copies.append(
                pltpu.make_async_copy(
                    cond_ref.at[kl, :, pl.ds(pl.multiple_of(at, LANES), own)],
                    out_ref.at[z, pl.ds(kl * n_cond, n_cond), :],
                    sems.at[len(copies)],
                )
            )
    start_all(copies)
    wait_all(copies)


def turn_kernel(tile, scr_ref, out_ref, scrs, turned, in_sems, out_sems):
    nu = scr_ref.shape[1]
    ins, outs = [], []
    for j in range(nu // tile):
        at = pl.ds(j * tile, tile)
        ins.append(pltpu.make_async_copy(scr_ref.at[:, at], scrs.at[:, at], in_sems.at[j]))
        outs.append(pltpu.make_async_copy(turned.at[at, :], out_ref.at[at, :], out_sems.at[j]))
    start_all(ins)
    for j in range(nu // tile):
        ins[j].wait()
        turned[j * tile : (j + 1) * tile, :] = scrs[:, j * tile : (j + 1) * tile].T
        outs[j].start()
    wait_all(outs)


def order_kernel(parts, n_ka, *refs):
    val_refs, refs = refs[:-10], refs[-10:]
    rows_out, turned_out, own_out, msgs_out, vals, heads, ordered, turned, val_sems, out_sems = refs
    own = own_out.shape[1]
    nu = ordered.shape[1]
    copies = piece_copies(val_refs, parts, 0, nu, vals, val_sems.at[0])
    head_copies = piece_copies(val_refs, parts, nu, LANES, heads, val_sems.at[1])
    start_all(copies + head_copies)
    wait_all(copies)
    n_band, group = vals.shape[0], vals.shape[0] * 2 * ROWS
    column = pl.multiple_of(lax.axis_index("band") * own, LANES)
    outs = []
    for kp in range(ordered.shape[0] // group):
        at = slice(kp * group, (kp + 1) * group)
        ordered[at, :] = pair_rows(vals, kp)
        turned[:, at] = ordered[at, :].T
        at = pl.ds(kp * group, group)
        outs += [
            pltpu.make_async_copy(ordered.at[at, :], rows_out.at[at, :], out_sems.at[0, kp]),
            pltpu.make_async_copy(turned.at[:, at], turned_out.at[:, at], out_sems.at[1, kp]),
            pltpu.make_async_copy(
                ordered.at[at, pl.ds(column, own)], own_out.at[at, :], out_sems.at[2, kp]
            ),
        ]
        start_all(outs[-3:])
    wait_all(head_copies)
    rows = msgs_out.shape[1]
    step = heads.shape[1] // n_ka
    for d in range(n_band):
        head = heads[d].astype(F32)
        for j in range(n_ka):
            msgs_out[device_at(n_band, j, d)] = head[j * step : j * step + rows, :].astype(BF)
    wait_all(outs)


def density_kernel(cfg, *refs):
    n_ka, n_band, k_dev = cfg
    k_points = n_ka * k_dev
    msgs_ref, vown_ref, cond_ref, qx_ref, rho_ref, xs, msgs, vown, conds, sems = refs
    own = vown_ref.shape[1]
    msg_copy = pltpu.make_async_copy(msgs_ref, msgs, sems.at[n_ka])
    copies = own_copies(cond_ref, conds, sems)
    copies.append(pltpu.make_async_copy(vown_ref, vown, sems.at[n_ka + 1]))
    start_all([msg_copy] + copies)
    xs[...] = jnp.zeros_like(xs)
    msg_copy.wait()
    for d in range(n_band):
        for k in range(k_points):
            j, kl = divmod(k, k_dev)
            tile = msgs[device_at(n_band, j, d), :, :].astype(F32)
            tile = tile[kl // 2 * ROWS : (kl // 2 + 1) * ROWS, :]
            base = k // 2 % 2 * LANES
            at = pl.ds(base + d * 2 * ROWS + k % 2 * ROWS, ROWS)
            xs[k // 4, at, pl.ds(base, LANES)] = lane_half(tile, kl % 2, k % 2)
    qx_ref[...] = xs[...].astype(BF)
    wait_all(copies)
    cond_rows = conds[...].reshape(-1, own)
    rho = jnp.zeros((1, own), F32)
    quad = 2 * LANES
    for kq in range(k_points // 4):
        at = slice(kq * quad, (kq + 1) * quad)
        mixed = dot_tn(qx_ref[kq], vown[at, :])
        rho = rho + jnp.sum(mixed * cond_rows[at, :].astype(F32), axis=0, keepdims=True)
    for r in range(own // LANES):
        part = rho[:, r * LANES : (r + 1) * LANES]
        rho_ref[:, r, :] = jnp.broadcast_to(part, (rho_ref.shape[0], LANES))


def direct_kernel(n_ka, tile, scale, *refs):
    turned_ref, scr_ref, rows_ref, qx_ref, refs = refs[0], refs[1], refs[2], refs[3], refs[4:]
    cond_refs, refs = refs[:n_ka], refs[n_ka:]
    di_ref, qx, turned, conds, scrs, vals, mixed, kern, folded = refs[:9]
    qx_sem, cond_sems, row_sem, chunk_sems = refs[9:]
    nu, mu = scr_ref.shape
    quad = 2 * LANES
    qx_copy = pltpu.make_async_copy(qx_ref, qx, qx_sem.at[0])
    cond_copies = [
        pltpu.make_async_copy(ref, conds.at[j], cond_sems.at[j]) for j, ref in enumerate(cond_refs)
    ]
    turned_copies, scr_copies = [], []
    for i in range(nu // tile):
        at = pl.ds(i * tile, tile)
        turned_copies.append(
            pltpu.make_async_copy(turned_ref.at[at, :], turned.at[at, :], chunk_sems.at[0, i])
        )
        scr_copies.append(
            pltpu.make_async_copy(scr_ref.at[at, :], scrs.at[at, :], chunk_sems.at[1, i])
        )
    row_copy = pltpu.make_async_copy(rows_ref, vals, row_sem.at[0])
    start_all([qx_copy, turned_copies[0]] + cond_copies + [scr_copies[0]])
    for i in range(1, nu // tile):
        start_all([turned_copies[i], scr_copies[i]])
    row_copy.start()
    qx_copy.wait()
    for i in range(nu // tile):
        rows = slice(i * tile, (i + 1) * tile)
        turned_copies[i].wait()
        for kq in range(qx.shape[0]):
            cols = slice(kq * quad, (kq + 1) * quad)
            mixed[rows, cols] = jnp.dot(
                turned[rows, cols], qx[kq], preferred_element_type=F32
            ).astype(BF)
        if i == 0:
            wait_all(cond_copies)
            cond_rows = conds[...].reshape(-1, mu)
        scr_copies[i].wait()
        amp = jnp.dot(mixed[rows, :], cond_rows, preferred_element_type=F32)
        kern[rows, :] = (scrs[rows, :].astype(F32) * amp).astype(BF)
    row_copy.wait()
    folded[...] = jnp.dot(vals[...], kern[...], preferred_element_type=F32).astype(BF)
    for kq in range(qx.shape[0]):
        at = slice(kq * quad, (kq + 1) * quad)
        both = scale * dot_nt(folded[at, :], cond_rows[at, :])
        di_ref[2 * kq] = both[:LANES, :LANES]
        di_ref[2 * kq + 1] = both[LANES:, LANES:]


def exchange_kernel(cfg, chunk, scale, *refs):
    n_ka, n_band, k_dev = cfg
    k_points = n_ka * k_dev
    rho_ref, di_ref, coul_ref, vown_ref, cond_ref, msg_ref = refs[:6]
    rhos, di, coul, conds, vown, part, msg, coul_sems, sems = refs[6:]
    rho_copy = pltpu.make_async_copy(rho_ref, rhos, sems.at[n_ka])
    own, npt = coul_ref.shape
    coul_copies = [
        pltpu.make_async_copy(
            coul_ref.at[:, pl.ds(i * chunk, chunk)], coul.at[:, pl.ds(i * chunk, chunk)], coul_sems.at[i]
        )
        for i in range(npt // chunk)
    ]
    copies = own_copies(cond_ref, conds, sems)
    copies.append(pltpu.make_async_copy(vown_ref, vown, sems.at[n_ka + 1]))
    copies.append(pltpu.make_async_copy(di_ref, di, sems.at[n_ka + 2]))
    start_all([rho_copy] + coul_copies + copies)
    rho_copy.wait()
    acc = jnp.zeros((own, LANES), F32)
    per_dev = own // LANES
    for i in range(npt // chunk):
        coul_copies[i].wait()
        for j in range(i * chunk // LANES, (i + 1) * chunk // LANES):
            rho = rhos[j // per_dev, pl.ds(j % per_dev, 1), :].astype(BF).astype(F32)
            acc = acc + coul[:, j * LANES : (j + 1) * LANES].astype(F32) * rho
    potential = scale * jnp.sum(acc.T, axis=0, keepdims=True)
    wait_all(copies)
    cond_rows = conds[...].reshape(-1, own)
    quad = 2 * LANES
    for kq in range(k_points // 4):
        at = slice(kq * quad, (kq + 1) * quad)
        weighted = (vown[at, :].astype(F32) * potential).astype(BF)
        both = 2.0 * dot_nt(weighted, cond_rows[at, :])
        part[2 * kq] = both[:LANES, :LANES] - di[2 * kq]
        part[2 * kq + 1] = both[LANES:, LANES:] - di[2 * kq + 1]
    for d in range(n_band):
        for j in range(n_ka):
            for g in range((k_dev + 1) // 2):
                tile = None
                for kl in range(2 * g, min(2 * g + 2, k_dev)):
                    k = j * k_dev + kl
                    piece = part[k // 2, pl.ds(d * 2 * ROWS + k % 2 * ROWS, ROWS), :]
                    piece = lane_half(piece, k % 2, kl % 2)
                    tile = piece if tile is None else tile + piece
                msg[device_at(n_band, j, d), pl.ds(g * ROWS, ROWS), :] = tile
    msg_ref[...] = msg[...].astype(BF)


def write_rows(ref, values):
    for i, value in enumerate(values):
        ref[i : i + 1, :] = jnp.broadcast_to(value, (1, ref.shape[1]))


def received(recv_ref):
    return jnp.sum(recv_ref[...].astype(F32), axis=0)


def shifted(count_all, shift, square, cross_sum, square_sum):
    alpha = shift * square + cross_sum / count_all
    d = alpha - shift
    mean_sq = (square_sum - 2.0 * d * cross_sum) / count_all + d * d * square
    mean_sq = jnp.maximum(mean_sq, 0.0)
    return alpha, d, mean_sq


def first_owner_kernel(count_all, recv_ref, msgs_ref, gap_ref, own_ref, state_ref, coef_ref, msg_ref):
    start_sq, gap_sq = read_sums(msgs_ref, 2)
    norm = start_sq / count_all
    inv = 1.0 / jnp.sqrt(norm + 1e-06)
    square = norm / (norm + 1e-06)
    shift = gap_sq / jnp.maximum(start_sq, 1e-30)
    cur = own_ref[...] * inv
    inter = received(recv_ref) * inv
    gap = gap_ref[...]
    resid = (gap - shift) * cur + inter
    state_ref[0] = cur
    state_ref[1] = resid
    state_ref[2] = inter
    write_rows(coef_ref, (shift, square, gap_sq * inv * inv))
    sums = [
        jnp.sum(cur * resid),
        jnp.sum(resid * resid),
        jnp.sum(gap * resid * resid),
        jnp.sum(gap * resid * cur),
    ]
    msg_ref[...] = jnp.broadcast_to(with_sums(resid, sums).astype(BF)[None], msg_ref.shape)


def second_owner_kernel(count_all, recv_ref, msgs_ref, gap_ref, state_ref, coef_ref, out_ref, coef_out, msg_ref):
    cross, total, gap_rr, gap_rq = read_sums(msgs_ref, 4)
    alpha, d, mean_sq = shifted(count_all, coef_ref[0:1, 0:1], coef_ref[1:2, 0:1], cross, total)
    beta = jnp.sqrt(mean_sq + 1e-06)
    square = mean_sq / (mean_sq + 1e-06)
    gap_qq = gap_rr - 2.0 * d * gap_rq + d * d * coef_ref[2:3, 0:1]
    shift = gap_qq / (mean_sq + 1e-06) / count_all
    prev = state_ref[0]
    cur = (state_ref[1] - d * prev) / beta
    inter = (received(recv_ref) - d * state_ref[2]) / beta
    resid = (gap_ref[...] - shift) * cur + inter - beta * prev
    out_ref[0] = cur
    out_ref[1] = resid
    write_rows(coef_out, (alpha, beta, shift, square))
    dims = msg_ref.shape[:1] + msg_ref.shape[2:]
    msg_ref[:, 0, :] = jnp.full(dims, jnp.sum(cur * resid), F32)
    msg_ref[:, 1, :] = jnp.full(dims, jnp.sum(resid * resid), F32)


def finish_kernel(count_all, msgs_ref, state_ref, coef_ref, out_ref, coeffs_ref):
    sums = jnp.sum(msgs_ref[...], axis=0)
    alpha, d, mean_sq = shifted(count_all, coef_ref[2:3, 0:1], coef_ref[3:4, 0:1], sums[0:1, 0:1], sums[1:2, 0:1])
    beta = jnp.sqrt(mean_sq + 1e-06)
    own = (state_ref[1] - d * state_ref[0]) / beta
    coeffs_ref[0] = coef_ref[0, 0]
    coeffs_ref[1] = alpha[0, 0]
    coeffs_ref[2] = coef_ref[1, 0]
    coeffs_ref[3] = beta[0, 0]
    for kl in range(out_ref.shape[0]):
        tile = own[kl // 2 * ROWS : (kl // 2 + 1) * ROWS, :]
        other = pltpu.roll(tile, HALF, axis=1)
        left, right = (tile, other) if kl % 2 == 0 else (other, tile)
        low = lax.broadcasted_iota(jnp.int32, (1, LANES), 1) < HALF
        for j in range(ROWS // 2):
            row = jnp.where(low, left[2 * j : 2 * j + 1], right[2 * j + 1 : 2 * j + 2])
            out_ref[pl.ds(kl, 1), pl.ds(j * LANES, LANES)] = row


def shape_of(dims, kind=F32):
    return jax.ShapeDtypeStruct(dims, kind)


def call(kernel, name, out_shape, in_specs, out_specs, scratch=(), mib=None, flops=0, moved=0):
    return pl.pallas_call(
        kernel,
        out_shape=out_shape,
        in_specs=in_specs,
        out_specs=out_specs,
        scratch_shapes=list(scratch),
        compiler_params=pltpu.CompilerParams(vmem_limit_bytes=mib * MIB if mib else VMEM_ALL),
        cost_estimate=pl.CostEstimate(flops=flops, bytes_accessed=moved, transcendentals=0),
        name=name,
    )


def dma(*dims):
    return pltpu.SemaphoreType.DMA(dims)


def swap(block, axis, d):
    return lax.ppermute(block, axis, [(i, i ^ d) for i in range(lax.axis_size(axis))])


def plane_pieces(own_piece, others):
    def move(block, d):
        return swap(block, "band", d)

    rows = own_piece.shape[0]
    half = rows // 2
    by_x, by_y, core = move(own_piece, 2), move(own_piece, 4), move(own_piece, 1)
    by_x, by_y, others = lax.optimization_barrier((by_x, by_y, others))
    diag = [move(by_x[:half], 4), move(by_y[half:], 2)]
    near_x, near_y = move(by_x, 1), move(by_y, 1)
    far = [move(part, 1) for part in diag]
    arrays = [own_piece, core, by_x, near_x, by_y, near_y] + diag + far
    parts = tuple(((i, 0, rows),) for i in range(6))
    parts += (((6, 0, half), (7, 0, half)), ((8, 0, half), (9, 0, half)))
    return arrays, parts, others


def kernel_path(start_vec, val_energy, cond_energy, val_orb, cond_orb, coulomb, screened):
    n_ka = lax.axis_size("ka")
    n_band = lax.axis_size("band")
    devices = n_ka * n_band
    ka, band = lax.axis_index("ka"), lax.axis_index("band")
    k_dev = start_vec.shape[0]
    nv_blk = val_orb.shape[1]
    n_cond = cond_orb.shape[1]
    npt_all = cond_orb.shape[2]
    k_points = k_dev * n_ka
    pairs = k_points // 2
    mu_blk, nu_blk = screened.shape
    own = coulomb.shape[0]
    count_all = k_points * nv_blk * n_band * n_cond
    scale = 1.0 / (npt_all * math.sqrt(count_all))
    piece_rows = k_points * nv_blk

    block = ((k_dev + 1) // 2 * ROWS, LANES)
    msg_shape = shape_of((devices,) + block, BF)
    wide = nu_blk + LANES
    start_own, gap, *payloads = call(
        functools.partial(pack_kernel, n_ka, nu_blk),
        "pack",
        (shape_of(block), shape_of(block)) + (shape_of((k_dev, nv_blk, wide), BF),) * n_ka,
        [ANY] * 4,
        (VMEM,) * (2 + n_ka),
        [
            pltpu.VMEM(start_vec.shape, F32),
            pltpu.VMEM(cond_energy.shape, F32),
            pltpu.SMEM(val_energy.shape, F32),
            dma(3),
            dma(n_ka),
        ],
    )(start_vec, cond_energy, val_energy, val_orb)
    base, payloads = lax.optimization_barrier((band * mu_blk, payloads))
    got = [payloads[0]] + [swap(payloads[j], "ka", j) for j in range(1, n_ka)]
    own_rows = k_dev * n_cond
    cuts = call(
        cut_kernel,
        "cut",
        shape_of((n_ka, own_rows, own), BF),
        [ANY],
        VMEM,
        [dma(n_ka * k_dev)],
    )(cond_orb)
    cond_local = lax.dynamic_slice_in_dim(cond_orb, base, mu_blk, 2)
    cond_local = cond_local.reshape(k_dev * n_cond, mu_blk)
    got, cuts, cond_local = lax.optimization_barrier((got, cuts, cond_local))
    val_cut = jnp.concatenate(got, axis=0).reshape(piece_rows, wide)
    cond_pts = [cond_local] + [swap(cond_local, "ka", j) for j in range(1, n_ka)]
    cond_own = lax.all_to_all(cuts, "ka", split_axis=0, concat_axis=0, tiled=True)

    chunk, tile = 1024, nu_blk
    rows_all, conds_all = k_points * nv_blk * n_band, k_points * n_cond
    scr_turned = call(
        functools.partial(turn_kernel, nu_blk // 4),
        "turn",
        shape_of((nu_blk, mu_blk), BF),
        [ANY],
        ANY,
        [pltpu.VMEM((mu_blk, nu_blk), BF), pltpu.VMEM((nu_blk, mu_blk), BF)]
        + [dma(4)] * 2,
        moved=8 * MIB,
    )(screened)
    pieces, parts, scr_turned = plane_pieces(val_cut, scr_turned)
    pieces, cond_pts[1:-1] = lax.optimization_barrier((pieces, cond_pts[1:-1]))
    val_rows, val_turned, val_own, msgs = call(
        functools.partial(order_kernel, parts, n_ka),
        "order",
        (
            shape_of((rows_all, nu_blk), BF),
            shape_of((nu_blk, rows_all), BF),
            shape_of((rows_all, own), BF),
            msg_shape,
        ),
        [ANY] * len(pieces),
        (ANY, ANY, ANY, VMEM),
        [
            pltpu.VMEM((n_band, piece_rows, nu_blk), BF),
            pltpu.VMEM((n_band, piece_rows, LANES), BF),
            pltpu.VMEM((rows_all, nu_blk), BF),
            pltpu.VMEM((nu_blk, rows_all), BF),
            dma(2, sum(len(piece) for piece in parts)),
            dma(3, pairs),
        ],
        moved=9 * MIB,
    )(*pieces)

    cfg = (n_ka, n_band, k_dev)
    quads = k_points // 4
    state, coef = None, None
    for step in range(STEPS):
        first = step == 0
        qx, rho = call(
            functools.partial(density_kernel, cfg),
            "density",
            (
                shape_of((quads, 2 * LANES, 2 * LANES), BF),
                shape_of((devices, own // LANES, LANES)),
            ),
            [ANY] * 3,
            (VMEM, VMEM),
            [
                pltpu.VMEM((quads, 2 * LANES, 2 * LANES), F32),
                pltpu.VMEM((devices,) + block, BF),
                pltpu.VMEM((rows_all, own), BF),
                pltpu.VMEM((n_ka, own_rows, own), BF),
                dma(n_ka + 2),
            ],
        )(msgs, val_own, cond_own)
        density = exchange_all(rho)
        direct = call(
            functools.partial(direct_kernel, n_ka, tile, scale),
            "direct",
            shape_of((pairs, LANES, LANES)),
            [ANY] * (4 + n_ka),
            VMEM,
            [
                pltpu.VMEM((quads, 2 * LANES, 2 * LANES), BF),
                pltpu.VMEM((nu_blk, rows_all), BF),
                pltpu.VMEM((n_ka, k_dev * n_cond, mu_blk), BF),
                pltpu.VMEM((nu_blk, mu_blk), BF),
                pltpu.VMEM((rows_all, nu_blk), BF),
                pltpu.VMEM((nu_blk, conds_all), BF),
                pltpu.VMEM((nu_blk, mu_blk), BF),
                pltpu.VMEM((rows_all, mu_blk), BF),
                dma(1),
                dma(n_ka),
                dma(1),
                dma(2, nu_blk // tile),
            ],
            flops=4 * mu_blk * nu_blk * conds_all,
            moved=12 * MIB,
        )(val_turned, scr_turned, val_rows, qx, *cond_pts)
        summed = call(
            functools.partial(exchange_kernel, cfg, chunk, scale),
            "exchange",
            msg_shape,
            [ANY] * 5,
            VMEM,
            [
                pltpu.VMEM((devices, own // LANES, LANES), F32),
                pltpu.VMEM((pairs, LANES, LANES), F32),
                pltpu.VMEM((own, npt_all), BF),
                pltpu.VMEM((n_ka, own_rows, own), BF),
                pltpu.VMEM((rows_all, own), BF),
                pltpu.VMEM((pairs, LANES, LANES), F32),
                pltpu.VMEM((devices,) + block, F32),
                dma(npt_all // chunk),
                dma(n_ka + 3),
            ],
        )(density, direct, coulomb, val_own, cond_own)
        recv = exchange_all(summed)
        if first:
            state, coef, message = call(
                functools.partial(first_owner_kernel, count_all),
                "first_owner",
                (shape_of((3,) + block), shape_of((ROWS, LANES)), msg_shape),
                [VMEM] * 4,
                (VMEM, VMEM, VMEM),
                mib=8,
            )(recv, msgs, gap, start_own)
        else:
            state, coef, message = call(
                functools.partial(second_owner_kernel, count_all),
                "second_owner",
                (shape_of((2,) + block), shape_of((ROWS, LANES)), shape_of((devices, 2, LANES))),
                [VMEM] * 5,
                (VMEM, VMEM, VMEM),
                mib=8,
            )(recv, msgs, gap, state, coef)
        msgs = exchange_all(message)
    return call(
        functools.partial(finish_kernel, count_all),
        "finish",
        (shape_of(start_vec.shape), shape_of((2 * STEPS,))),
        [VMEM] * 3,
        (VMEM, SMEM),
        mib=8,
    )(msgs, state, coef)


def array_path(start_vec, val_energy, cond_energy, val_orb, cond_orb, coulomb, screened):
    n_ka = lax.axis_size("ka")
    n_band = lax.axis_size("band")
    devices = n_ka * n_band
    ka, band = lax.axis_index("ka"), lax.axis_index("band")
    me = ka * n_band + band
    k_dev, pair_blk = start_vec.shape
    nv_blk = val_orb.shape[1]
    n_cond = cond_orb.shape[1]
    n_val = nv_blk * n_band
    npt_all = cond_orb.shape[2]
    k_points = k_dev * n_ka
    mu_blk, nu_blk = screened.shape
    own_pts = coulomb.shape[0]
    count_all = k_points * n_val * n_cond
    kernel_scale = 1.0 / (npt_all * math.sqrt(count_all))

    start_all = gather_all(start_vec, devices)
    val_cut = lax.all_to_all(
        val_orb.reshape(k_dev, nv_blk, n_ka, nu_blk).transpose(2, 0, 1, 3),
        "ka", split_axis=0, concat_axis=0, tiled=True,
    ).reshape(k_points, nv_blk, nu_blk)
    val_pts = lax.all_gather(val_cut, "band", axis=1, tiled=True)
    cond_local = lax.dynamic_slice_in_dim(cond_orb, band * mu_blk, mu_blk, 2)
    cond_pts = lax.all_gather(cond_local, "ka", axis=0, tiled=True)
    cond_rows = cond_orb.reshape(k_dev, n_cond, n_ka, n_band, own_pts)
    cond_rows = lax.dynamic_index_in_dim(cond_rows, band, 3, keepdims=False)
    cond_own = lax.all_to_all(
        cond_rows.transpose(2, 0, 1, 3), "ka", split_axis=0, concat_axis=0, tiled=True
    ).reshape(k_points, n_cond, own_pts)
    val_own = lax.dynamic_slice_in_dim(val_pts, band * own_pts, own_pts, 2)

    energy_gap = (cond_energy[:, None, :] - val_energy[:, :, None]).reshape(k_dev, pair_blk)
    start_sq = jnp.sum(start_all * start_all)
    current = start_all / jnp.sqrt(start_sq / count_all + 1e-06)
    previous = jnp.zeros_like(current)
    beta_val = jnp.float32(0.0)
    alphas = []
    betas = []
    for turn_index in range(STEPS):
        full_vec = (
            current.astype(BF)
            .reshape(n_ka, n_band, k_dev, nv_blk, n_cond)
            .transpose(0, 2, 1, 3, 4)
            .reshape(k_points, n_val, n_cond)
        )
        mixed_f = jnp.einsum("kvc,kvn->kcn", full_vec, val_pts, preferred_element_type=F32)
        mixed_own = lax.dynamic_slice_in_dim(mixed_f, band * own_pts, own_pts, 2)
        density_own = jnp.sum(mixed_own * cond_own.astype(F32), axis=(0, 1))
        density = gather_all(density_own.astype(BF), devices).reshape(npt_all)
        mixed_val = mixed_f.astype(BF)
        amp = jnp.einsum("kcm,kcn->mn", cond_pts, mixed_val, preferred_element_type=F32)
        kern = (screened.astype(F32) * amp * kernel_scale).astype(BF)
        folded = jnp.einsum("mn,kvn->kvm", kern, val_pts, preferred_element_type=F32).astype(BF)
        direct_part = jnp.einsum("kcm,kvm->kvc", cond_pts, folded, preferred_element_type=F32)
        potential = kernel_scale * jnp.dot(coulomb, density, preferred_element_type=F32)
        weighted = (val_own.astype(F32) * potential).astype(BF)
        exchange = jnp.einsum("kvp,kcp->kvc", weighted, cond_own, preferred_element_type=F32)
        part = 2.0 * exchange - direct_part
        arranged = (
            part.reshape(n_ka, k_dev, n_band, nv_blk, n_cond)
            .transpose(0, 2, 1, 3, 4)
            .reshape(devices, k_dev, pair_blk)
        )
        inter_own = jnp.sum(exchange_all(arranged), axis=0)
        current_own = lax.dynamic_index_in_dim(current, me, 0, keepdims=False)
        resid_vec = gather_all(energy_gap * current_own + inter_own, devices)
        resid_vec = resid_vec - beta_val * previous
        alpha_val = jnp.sum(current * resid_vec) / count_all
        resid_vec = resid_vec - alpha_val * current
        beta_val = jnp.sqrt(jnp.sum(resid_vec * resid_vec) / count_all + 1e-06)
        previous = current
        current = resid_vec / beta_val
        alphas.append(alpha_val)
        betas.append(beta_val)
    coeffs = jnp.stack(alphas + betas)
    return (lax.dynamic_index_in_dim(current, me, 0, keepdims=False), coeffs)


def per_device(*args):
    start_vec, _, _, val_orb, cond_orb, coulomb, screened = args
    n_ka, n_band = lax.axis_size("ka"), lax.axis_size("band")
    fits = (
        n_band == 8
        and n_ka & (n_ka - 1) == 0
        and start_vec.shape[0] % 2 == 1
        and val_orb.shape[1] == ROWS
        and cond_orb.shape[1] == HALF
        and start_vec.shape[0] * n_ka % 4 == 0
        and coulomb.shape[0] % LANES == 0
        and coulomb.shape[1] % 1024 == 0
        and screened.shape[0] % 512 == 0
        and screened.shape[1] % 1024 == 0
        and screened.shape[0] * screened.shape[1] <= 2 * MIB
    )
    return (kernel_path if fits else array_path)(*args)


def solution(mesh):
    in_specs = (
        P("ka", "band"),
        P("ka", "band"),
        P("ka", None),
        P("ka", "band", None),
        P("ka", None, None),
        P(("ka", "band"), None),
        P("band", "ka"),
    )
    out_specs = (P("ka", "band"), P())
    return jax.shard_map(
        per_device, mesh=mesh, in_specs=in_specs, out_specs=out_specs, check_vma=False
    )
```
